32 devices in a mesh: groups: 2 (over x), req: 2 (over core), tp: 8 (over z, y).
Axes of the slice: x: 2, y: 2, z: 4, core: 2. Of those that a mesh axis runs over, the one named last changes fastest.
Arguments:
- hidden_in: bfloat16 [1024, 8192], P(('groups', 'req', 'tp')), parts along dimension 0, may hold values from -6 to 6
- norm_gain: float32 [8192], replicated, may hold values from 0.5 to 1.5
- w_query: bfloat16 [8192, 8192], P(None, 'tp'), may hold values from -0.0625 to 0.0625
- w_keyval: bfloat16 [8192, 2048], P(None, 'tp'), may hold values from -0.15625 to 0.15625
- w_out: bfloat16 [8192, 8192], P('tp'), may hold values from -0.1875 to 0.1875
- pool_cache: bfloat16 [16, 2048, 2, 1024], P(('groups', 'req'), 'tp'), parts along dimension 0
- doc_slot: int32 [16], P(('groups', 'req')), parts along dimension 0, may hold values from 0 to 7, each once
- doc_blocks: int32 [4, 4], P(('groups', 'req')), parts along dimension 0, may hold values from 4 to 16, as said below
- sel_pos: int32 [4, 256], P(('groups', 'req')), parts along dimension 0, may hold values from 0 to 8191, as said below
Outputs:
- attn_out: bfloat16 [1024, 8192], P(('groups', 'req', 'tp')), parts along dimension 0
The draws below stay inside these ranges and needn't reach their ends.
There are 2 independent parts, one for each index of `groups`. The reference program is written for one: setup_inputs(seed, part) draws one part's arguments, and reference() takes and returns one part's arrays. A program takes and returns all parts, laid end to end along the dimension named above; an argument that names none is the same for every part. Nothing has to cross between parts.
Inputs may be any that keep to these rules, and one draw needn't show every extreme that they name: `sel_pos`: each request's positions are distinct and ascending, below the total length of its documents, and include that total minus one. `doc_slot`: every slot of the pool is used by exactly one document. `doc_blocks`: request 0's documents fill their slots.
All inputs are finite; a program needn't handle non-finite values.
Results may differ from the reference program's by a relative error of at most 0.02.
The reference program's roundings to bfloat16 on the way (of `normed`, `keyval`, `queries`, `new_keys`, `weights` and `attention`) count: a program that leaves them out, or rounds other values in their place, can miss the bound.
Values may be sent and summed in bfloat16 or wider, within the bound.
No kernel may reach another device: no remote copies, remote signals or barrier semaphores. Data moves between devices by JAX's collectives and lax.ppermute only.
A program may use at most 256 MiB of HBM per device.

```python
import math
import jax
import jax.numpy as jnp
from jax import lax

D = 8192
HEADS = 64
KVH = 8
HD = 128
DOCS = 4
BLOCK = 128
NBLK = 16
MINB = 4
SEL = 256
SPAN = 2048
N_REQ = 2


def shared_blocks(key):
    blocks = jax.random.randint(jax.random.fold_in(key, 11), (N_REQ, DOCS), MINB, NBLK + 1)
    blocks = blocks.at[0].set(NBLK)
    blocks = blocks.at[N_REQ - 1, 0].set(MINB)
    return blocks.astype(jnp.int32)


def draw_doc_blocks(key, part):
    return shared_blocks(key)


def draw_sel_pos(key, part):
    blocks = shared_blocks(key)
    key = jax.random.fold_in(key, 5)
    totals = jnp.sum(blocks, axis=1) * BLOCK
    places = jnp.arange(DOCS * SPAN, dtype=jnp.int32)

    def one_request(sub_key, total):
        ranking = jax.random.permutation(sub_key, DOCS * SPAN).astype(jnp.int32)
        ranking = jnp.where(places < total, ranking, -1)
        ranking = jnp.where(places == total - 1, DOCS * SPAN, ranking)
        picked = lax.top_k(ranking, SEL)[1]
        return jnp.sort(picked)
    sub_keys = jax.random.split(key, N_REQ)
    return jax.vmap(one_request)(sub_keys, totals).astype(jnp.int32)


def draw_pool_cache(key, part):
    key = jax.random.fold_in(key, 3)
    shape = (N_REQ * DOCS, SPAN, 2, KVH * HD)
    base = jax.random.normal(key, shape, jnp.float32)
    part_scale = jnp.array([2.5, 1.0], jnp.float32)[None, None, :, None]
    return (base * part_scale).astype(jnp.bfloat16)


def block_levels(rng, shape, shards, low, largest):
    loudness = 1.0
    for position, parts in shards:
        heights = jax.random.uniform(jax.random.fold_in(jax.random.fold_in(rng, 6), position), (parts,), jnp.float32, low / len(shards), largest / len(shards))
        loudness = loudness * jnp.repeat(jnp.exp(heights), shape[position] // parts).reshape((-1,) + (1,) * (len(shape) - 1 - position))
    return loudness


def bell_draw(key, dims, spread, bound, shards=(), kind=jnp.bfloat16):
    drawn = jax.random.normal(key, dims, jnp.float32) * spread
    if len(shards) > 0:
        drawn = block_levels(key, dims, shards, -0.22, 0.18) * drawn
    return jnp.clip(drawn, min=-bound, max=bound).astype(kind)


def setup_inputs(seed: int = 0, part: int = 0) -> dict:
    arg_keys = jax.random.split(jax.random.key(seed), 10)
    own_keys = jax.random.split(jax.random.fold_in(arg_keys[9], part), 10)
    return {
        "hidden_in": bell_draw(own_keys[0], (N_REQ * SEL, D), 1.0, 6.0, ((0, 16),)),
        "norm_gain": jnp.clip(1.0 + 0.1 * jax.random.normal(arg_keys[1], (D,), jnp.float32), 0.5, 1.5),
        "w_query": bell_draw(arg_keys[2], (D, HEADS * HD), D ** -0.5, 0.0625, ((1, 8),)),
        "w_keyval": bell_draw(arg_keys[3], (D, 2 * KVH * HD), (D // 6) ** -0.5, 0.15625, ((1, 8),)),
        "w_out": bell_draw(arg_keys[4], (HEADS * HD, D), (D // 8) ** -0.5, 0.1875, ((0, 8),)),
        "pool_cache": draw_pool_cache(jax.random.fold_in(jax.random.fold_in(arg_keys[9], part), 71), part),
        "doc_slot": jax.random.permutation(own_keys[6], N_REQ * DOCS).astype(jnp.int32),
        "doc_blocks": draw_doc_blocks(jax.random.fold_in(jax.random.fold_in(arg_keys[9], part), 71), part),
        "sel_pos": draw_sel_pos(jax.random.fold_in(jax.random.fold_in(arg_keys[9], part), 71), part),
    }


EPSILON = 1e-05
ROPE_BASE = 500000.0
MASKED = -1e+30

def rotate(values, positions):
    half_dim = values.shape[-1] // 2
    inverse = ROPE_BASE ** (-(jnp.arange(half_dim, dtype=jnp.float32) * (2.0 / values.shape[-1])))
    angles = positions.astype(jnp.float32)[:, None] * inverse[None, :]
    cosine = jnp.cos(angles)[:, None, :]
    sine_part = jnp.sin(angles)[:, None, :]
    front_half = values[..., :half_dim]
    back_half = values[..., half_dim:]
    return jnp.concatenate([front_half * cosine - back_half * sine_part, back_half * cosine + front_half * sine_part], axis=-1)

def cache_layout(lengths, first_token, token_count, selected):
    offsets = jnp.cumsum(lengths) - lengths
    slot_tokens = first_token + jnp.arange(token_count, dtype=jnp.int32)
    cache_pos = offsets[:, None] + slot_tokens[None, :]
    is_valid = slot_tokens[None, :] < lengths[:, None]
    replaced = jnp.any(cache_pos[:, :, None] == selected[None, None, :], axis=-1)
    return (cache_pos.reshape(-1), (is_valid & jnp.logical_not(replaced)).reshape(-1))

def reference(hidden_in, norm_gain, w_query, w_keyval, w_out, pool_cache, doc_slot, doc_blocks, sel_pos):
    widened = hidden_in.astype(jnp.float32)
    normed = (widened * lax.rsqrt(lax.optimization_barrier(jnp.mean(widened * widened, axis=-1, keepdims=True)) + EPSILON) * norm_gain).astype(jnp.bfloat16)
    query_raw = jnp.dot(normed, w_query, preferred_element_type=jnp.float32)
    keyval = jnp.dot(normed, w_keyval, preferred_element_type=jnp.float32).astype(jnp.bfloat16)
    group_size = HEADS // KVH
    scale = 1.0 / math.sqrt(HD)
    results = []
    for request in range(N_REQ):
        selected = sel_pos[request]
        queries = rotate(query_raw[request * SEL:(request + 1) * SEL].reshape(SEL, HEADS, HD), selected).astype(jnp.bfloat16)
        fresh_kv = keyval[request * SEL:(request + 1) * SEL]
        new_keys = rotate(fresh_kv[:, :KVH * HD].reshape(SEL, KVH, HD).astype(jnp.float32), selected).astype(jnp.bfloat16)
        new_vals = fresh_kv[:, KVH * HD:].reshape(SEL, KVH, HD)
        doc_cache = pool_cache[doc_slot[request * DOCS:(request + 1) * DOCS]]
        old_keys = doc_cache[:, :, 0].reshape(DOCS * SPAN, KVH, HD)
        old_vals = doc_cache[:, :, 1].reshape(DOCS * SPAN, KVH, HD)
        lengths = doc_blocks[request] * BLOCK
        cache_pos, cache_live = cache_layout(lengths, 0, SPAN, selected)
        key_pos = jnp.concatenate([cache_pos, selected])
        key_live = jnp.concatenate([cache_live, jnp.ones((SEL,), dtype=bool)])
        allowed = key_live[None, :] & (key_pos[None, :] <= selected[:, None])
        all_keys = jnp.concatenate([old_keys, new_keys], axis=0).transpose(1, 0, 2)
        all_vals = jnp.concatenate([old_vals, new_vals], axis=0).transpose(1, 0, 2)
        grouped = queries.reshape(SEL, KVH, group_size, HD).transpose(1, 2, 0, 3)

        def head_attend(operands):
            head_q, head_k, head_v = operands
            scores = jnp.einsum('gqd,nd->gqn', head_q.astype(jnp.float32), head_k.astype(jnp.float32)) * scale
            scores = jnp.where(allowed[None], scores, MASKED)
            row_top = lax.optimization_barrier(jnp.max(scores, axis=-1, keepdims=True))
            weights = jnp.exp(scores - row_top)
            totals = lax.optimization_barrier(jnp.sum(weights, axis=-1))
            rounded = lax.optimization_barrier(weights.astype(jnp.bfloat16)).astype(jnp.float32)
            summed = jnp.einsum('gqn,nd->gqd', rounded, head_v.astype(jnp.float32))
            return summed / totals[..., None]
        attention = lax.map(head_attend, (grouped, all_keys, all_vals))
        attention = attention.transpose(2, 0, 1, 3).reshape(SEL, HEADS * HD).astype(jnp.bfloat16)
        results.append(jnp.dot(attention, w_out, preferred_element_type=jnp.float32))
    return jnp.concatenate(results, axis=0).astype(jnp.bfloat16)
```

```python
import functools
import math

import jax
import jax.numpy as jnp
from jax import lax
from jax.experimental import pallas as pl
from jax.experimental.pallas import tpu as pltpu
from jax.sharding import PartitionSpec as P

HEADS = 64
KVH = 8
HD = 128
DOCS = 4
BLOCK = 128
SEL = 256


EPSILON = 1e-05
ROPE_BASE = 500000.0
MASKED = -1e30
FAR = 1 << 30
GATHER_CHUNKS = 2
REDUCE_CHUNKS = 4
TILE_Q = 64
KEY_CHUNKS = 2
VMEM_BYTES = 40 * 1024 * 1024


def rotation_tables(positions):
    half_dim = HD // 2
    inverse = ROPE_BASE ** (-(jnp.arange(half_dim, dtype=jnp.float32) * (2.0 / HD)))
    angles = positions.astype(jnp.float32)[:, None] * inverse[None, :]
    cosine = jnp.cos(angles)
    sine_part = jnp.sin(angles)
    return (
        jnp.concatenate([cosine, cosine], axis=-1),
        jnp.concatenate([-sine_part, sine_part], axis=-1),
    )


def rotate(values, cosine, sine_part):
    swapped = jnp.concatenate([values[:, HD // 2 :], values[:, : HD // 2]], axis=-1)
    return values * cosine + swapped * sine_part


def project_kernel(n_blocks, has_prev, *refs):
    blocks = refs[:n_blocks]
    wq_ref, wkv_ref = refs[n_blocks : n_blocks + 2]
    rest = refs[n_blocks + 2 :]
    if has_prev:
        prev_q, prev_kv = rest[:2]
        rest = rest[2:]
    out_q, out_kv, total_q, total_kv = rest
    step = pl.program_id(0)

    @pl.when(step == 0)
    def _():
        if has_prev:
            total_q[...] = prev_q[...]
            total_kv[...] = prev_kv[...]
        else:
            total_q[...] = jnp.zeros_like(total_q)
            total_kv[...] = jnp.zeros_like(total_kv)

    rows = jnp.concatenate([b[...] for b in blocks], axis=0) if n_blocks > 1 else blocks[0][...]
    total_q[...] += jnp.dot(rows, wq_ref[...], preferred_element_type=jnp.float32)
    total_kv[...] += jnp.dot(rows, wkv_ref[...], preferred_element_type=jnp.float32)

    @pl.when(step == pl.num_programs(0) - 1)
    def _():
        out_q[...] = total_q[...]
        out_kv[...] = total_kv[...].astype(out_kv.dtype)


def project(blocks, w_query, w_keyval, prev, chunk, last):
    depth = blocks[0].shape[1]
    tile = min(1024, depth)
    steps = depth // tile
    q_cols, kv_cols = w_query.shape[1], w_keyval.shape[1]
    whole = lambda k: (0, 0)
    specs = [pl.BlockSpec((b.shape[0], tile), lambda k: (0, k)) for b in blocks]
    specs += [
        pl.BlockSpec((tile, q_cols), lambda k: (chunk * steps + k, 0)),
        pl.BlockSpec((tile, kv_cols), lambda k: (chunk * steps + k, 0)),
    ]
    operands = list(blocks) + [w_query, w_keyval]
    if prev is not None:
        specs += [pl.BlockSpec((SEL, q_cols), whole), pl.BlockSpec((SEL, kv_cols), whole)]
        operands += list(prev)
    return pl.pallas_call(
        functools.partial(project_kernel, len(blocks), prev is not None),
        grid=(steps,),
        in_specs=specs,
        out_specs=[pl.BlockSpec((SEL, q_cols), whole), pl.BlockSpec((SEL, kv_cols), whole)],
        out_shape=[
            jax.ShapeDtypeStruct((SEL, q_cols), jnp.float32),
            jax.ShapeDtypeStruct((SEL, kv_cols), jnp.bfloat16 if last else jnp.float32),
        ],
        scratch_shapes=[
            pltpu.VMEM((SEL, q_cols), jnp.float32),
            pltpu.VMEM((SEL, kv_cols), jnp.float32),
        ],
        compiler_params=pltpu.CompilerParams(vmem_limit_bytes=VMEM_BYTES),
        cost_estimate=pl.CostEstimate(
            flops=2 * SEL * depth * (q_cols + kv_cols),
            bytes_accessed=2 * depth * (q_cols + kv_cols + SEL) + 8 * SEL * (q_cols + kv_cols),
            transcendentals=0,
        ),
        name="project",
    )(*operands)


def select_kernel(n_dest, n_src, place_ref, slot_ref, head_ref, *refs):
    sources = refs[:n_src]
    outs = refs[n_src : n_src + n_dest]
    sems = refs[n_src + n_dest]
    for doc in range(DOCS):
        for src in range(n_src):

            @pl.when(place_ref[doc] == src)
            def _():
                for dest in range(n_dest):
                    pltpu.make_async_copy(
                        sources[src].at[head_ref[dest], :, slot_ref[doc]],
                        outs[dest].at[:, doc],
                        sems.at[dest, doc],
                    ).start()

    for dest in range(n_dest):
        for doc in range(DOCS):
            pltpu.make_async_copy(
                sources[0].at[0, :, 0], outs[dest].at[:, doc], sems.at[dest, doc]
            ).wait()


def select_docs(sources, place, slot, heads, n_dest):
    tokens = sources[0].shape[3]
    shape = (2, DOCS, tokens, HD)
    smem = pl.BlockSpec(memory_space=pltpu.SMEM)
    anywhere = pl.BlockSpec(memory_space=pl.ANY)
    return pl.pallas_call(
        functools.partial(select_kernel, n_dest, len(sources)),
        in_specs=[smem] * 3 + [anywhere] * len(sources),
        out_specs=[anywhere] * n_dest,
        out_shape=[jax.ShapeDtypeStruct(shape, jnp.bfloat16)] * n_dest,
        scratch_shapes=[pltpu.SemaphoreType.DMA((n_dest, DOCS))],
        cost_estimate=pl.CostEstimate(
            flops=0, bytes_accessed=4 * n_dest * math.prod(shape), transcendentals=0
        ),
        name="select_docs",
    )(place, slot, heads, *sources)


def attend_kernel(
    n_chunks,
    tokens,
    heads_here,
    qmax_ref,
    first_ref,
    q_ref,
    qcos_ref,
    qsin_ref,
    qpos_ref,
    kpos_ref,
    newk_ref,
    newv_ref,
    ncos_ref,
    nsin_ref,
    npos_ref,
    *refs,
):
    chunks = refs[:n_chunks]
    out_ref = refs[n_chunks]
    stored, new_key, q_tile, top, total, summed, sems = refs[n_chunks + 1 :]
    rows = heads_here * TILE_Q
    key_block = KEY_CHUNKS * tokens
    n_blocks = n_chunks // KEY_CHUNKS
    scale = math.log2(math.e) / math.sqrt(HD)

    def fill(chunk):
        return pltpu.make_async_copy(
            chunks[chunk], stored.at[:, :, pl.ds(chunk * tokens, tokens)], sems.at[chunk]
        )

    for chunk in range(n_chunks):
        fill(chunk).start()
    new_key[...] = rotate(newk_ref[...].astype(jnp.float32), ncos_ref[...], nsin_ref[...]).astype(
        jnp.bfloat16
    )

    def visit(keys, values, key_pos, token_pos):
        scores = lax.dot_general(
            q_tile[...], keys, (((1,), (1,)), ((), ())), preferred_element_type=jnp.float32
        )
        allowed = key_pos <= token_pos
        scores = jnp.where(
            allowed[None], scores.reshape(heads_here, TILE_Q, keys.shape[0]) * scale, MASKED
        ).reshape(rows, keys.shape[0])
        old_top = top[:, :1]
        new_top = jnp.maximum(old_top, jnp.max(scores, axis=-1, keepdims=True))
        weights = jnp.exp2(scores - new_top)
        shrink = jnp.exp2(old_top - new_top)
        total[...] = jnp.broadcast_to(
            total[:, :1] * shrink + jnp.sum(weights, axis=-1, keepdims=True), total.shape
        )
        summed[...] = summed[...] * shrink + jnp.dot(
            weights.astype(jnp.bfloat16), values, preferred_element_type=jnp.float32
        )
        top[...] = jnp.broadcast_to(new_top, top.shape)

    for chunk in range(n_chunks):
        fill(chunk).wait()

    @pl.loop(0, SEL // TILE_Q)
    def _(tile):
        start = pl.multiple_of(tile * TILE_Q, TILE_Q)
        here = pl.ds(start, TILE_Q)
        for head in range(heads_here):
            q_tile[head * TILE_Q : (head + 1) * TILE_Q, :] = rotate(
                q_ref[here, head * HD : (head + 1) * HD], qcos_ref[here, :], qsin_ref[here, :]
            ).astype(jnp.bfloat16)
        token_pos = qpos_ref[here, :][:, :1]
        top[...] = jnp.full_like(top, MASKED)
        total[...] = jnp.zeros_like(total)
        summed[...] = jnp.zeros_like(summed)
        visit(new_key[...], newv_ref[...], npos_ref[...], token_pos)

        @pl.loop(0, DOCS * n_blocks)
        def _(index):
            doc = index // n_blocks
            block = index % n_blocks

            @pl.when(first_ref[index] <= qmax_ref[tile])
            def _():
                span = pl.ds(pl.multiple_of(block * key_block, key_block), key_block)
                visit(
                    stored[0, doc, span, :],
                    stored[1, doc, span, :],
                    kpos_ref[pl.ds(index, 1), :],
                    token_pos,
                )

        for head in range(heads_here):
            part = slice(head * TILE_Q, (head + 1) * TILE_Q)
            out_ref[here, head * HD : (head + 1) * HD] = (
                summed[part, :] / total[part, :]
            ).astype(jnp.bfloat16)


def attend(chunks, q_raw, q_pos, key_pos, first_pos, new_k, new_v, selected):
    n_chunks = len(chunks)
    tokens = chunks[0].shape[2]
    heads_here = q_raw.shape[1] // HD
    rows = heads_here * TILE_Q
    q_cos, q_sin = rotation_tables(q_pos)
    n_cos, n_sin = rotation_tables(selected)
    q_max = jnp.max(q_pos.reshape(SEL // TILE_Q, TILE_Q), axis=1)
    smem = pl.BlockSpec(memory_space=pltpu.SMEM)
    vmem = pl.BlockSpec(memory_space=pltpu.VMEM)
    anywhere = pl.BlockSpec(memory_space=pl.ANY)
    pairs = HEADS // KVH * SEL * (DOCS * n_chunks * tokens + SEL) * heads_here // (HEADS // KVH)
    return pl.pallas_call(
        functools.partial(attend_kernel, n_chunks, tokens, heads_here),
        in_specs=[smem] * 2 + [vmem] * 10 + [anywhere] * n_chunks,
        out_specs=vmem,
        out_shape=jax.ShapeDtypeStruct((SEL, heads_here * HD), jnp.bfloat16),
        scratch_shapes=[
            pltpu.VMEM((2, DOCS, n_chunks * tokens, HD), jnp.bfloat16),
            pltpu.VMEM((SEL, HD), jnp.bfloat16),
            pltpu.VMEM((rows, HD), jnp.bfloat16),
            pltpu.VMEM((rows, HD), jnp.float32),
            pltpu.VMEM((rows, HD), jnp.float32),
            pltpu.VMEM((rows, HD), jnp.float32),
            pltpu.SemaphoreType.DMA((n_chunks,)),
        ],
        compiler_params=pltpu.CompilerParams(vmem_limit_bytes=VMEM_BYTES),
        cost_estimate=pl.CostEstimate(
            flops=4 * pairs * HD,
            bytes_accessed=4 * DOCS * n_chunks * tokens * HD,
            transcendentals=pairs,
        ),
        name="attend",
    )(
        q_max,
        first_pos,
        q_raw,
        q_cos,
        q_sin,
        jnp.broadcast_to(q_pos[:, None], (SEL, HD)),
        key_pos,
        new_k,
        new_v,
        n_cos,
        n_sin,
        selected[None, :],
        *chunks,
    )


def out_kernel(rows, x_ref, w_ref, own_ref, other_ref):
    product = jnp.dot(x_ref[...], w_ref[...], preferred_element_type=jnp.float32)
    cols = product.shape[1]
    split = product.reshape(SEL // (2 * rows), 2, rows, cols)
    own_ref[...] = split[:, 0].reshape(SEL // 2, cols)
    other_ref[...] = split[:, 1].reshape(SEL // 2, cols).astype(jnp.bfloat16)


def project_out(attention, w_out, chunk, n_chunks, rows):
    depth = w_out.shape[0]
    width = w_out.shape[1] // n_chunks
    tile = min(512, width)
    steps = width // tile
    return pl.pallas_call(
        functools.partial(out_kernel, rows),
        grid=(steps,),
        in_specs=[
            pl.BlockSpec((SEL, depth), lambda n: (0, 0)),
            pl.BlockSpec((depth, tile), lambda n: (0, chunk * steps + n)),
        ],
        out_specs=[
            pl.BlockSpec((SEL // 2, tile), lambda n: (0, n)),
            pl.BlockSpec((SEL // 2, tile), lambda n: (0, n)),
        ],
        out_shape=[
            jax.ShapeDtypeStruct((SEL // 2, width), jnp.float32),
            jax.ShapeDtypeStruct((SEL // 2, width), jnp.bfloat16),
        ],
        compiler_params=pltpu.CompilerParams(vmem_limit_bytes=VMEM_BYTES),
        cost_estimate=pl.CostEstimate(
            flops=2 * SEL * depth * width,
            bytes_accessed=2 * depth * (width + SEL) + 3 * SEL * width,
            transcendentals=0,
        ),
        name="project_out",
    )(attention, w_out)


def per_device(
    hidden_in, norm_gain, w_query, w_keyval, w_out, pool_cache, doc_slot, doc_blocks, sel_pos
):
    tp_size = lax.axis_size("tp")
    req_size = lax.axis_size("req")
    me = lax.axis_index("tp")
    ring = tp_size // 2
    my_z, my_y = me // 2, me % 2
    rows = hidden_in.shape[0]
    width = hidden_in.shape[1]
    tokens = pool_cache.shape[1]
    slots = pool_cache.shape[0]
    selected = sel_pos[0]
    lengths = doc_blocks[0] * BLOCK
    up = [(((z + 1) % ring) * 2 + y, z * 2 + y) for z in range(ring) for y in range(2)]
    down = [(z * 2 + y, ((z + 1) % ring) * 2 + y) for z in range(ring) for y in range(2)]
    across = [(i, i ^ 1) for i in range(tp_size)]

    widened = hidden_in.astype(jnp.float32)
    normed = (
        widened
        * lax.rsqrt(jnp.mean(widened * widened, axis=-1, keepdims=True) + EPSILON)
        * norm_gain
    ).astype(jnp.bfloat16)

    part = width // GATHER_CHUNKS
    prev = None
    for chunk in range(GATHER_CHUNKS):
        held = normed[:, chunk * part : (chunk + 1) * part]
        blocks = []
        for step in range(ring):
            blocks += [held, lax.ppermute(held, "tp", across)]
            if step + 1 < ring:
                held = lax.ppermute(held, "tp", up)
        if rows % 16:
            blocks = [jnp.concatenate(blocks, axis=0)]
        prev = project(blocks, w_query, w_keyval, prev, chunk, chunk + 1 == GATHER_CHUNKS)
    q_raw, keyval = prev

    by_owner = selected.reshape(ring, 2, rows)
    q_pos = jnp.roll(by_owner, (-my_z, -my_y), axis=(0, 1)).reshape(SEL)

    packed = pool_cache.reshape(slots, tokens, 2, KVH, HD).transpose(3, 2, 0, 1, 4)
    sources = [packed]
    for shift in range(1, req_size):
        sources.append(
            lax.ppermute(packed, "req", [((i + shift) % req_size, i) for i in range(req_size)])
        )
    place = (doc_slot // slots - lax.axis_index("req")) % req_size
    order = jnp.arange(tp_size, dtype=jnp.int32)
    sent = select_docs(
        sources, place, doc_slot % slots, (me ^ order) * KVH // tp_size, tp_size
    )
    chunks = [sent[0]] + [
        lax.ppermute(sent[j], "tp", [(i, i ^ j) for i in range(tp_size)])
        for j in range(1, tp_size)
    ]

    offsets = jnp.cumsum(lengths) - lengths
    slot_tokens = ((me ^ order) * tokens)[:, None] + jnp.arange(tokens, dtype=jnp.int32)[None, :]
    cache_pos = offsets[:, None, None] + slot_tokens[None]
    is_valid = slot_tokens[None] < lengths[:, None, None]
    replaced = jnp.any(cache_pos[..., None] == selected, axis=-1)
    key_pos = jnp.where(is_valid & jnp.logical_not(replaced), cache_pos, FAR)
    key_pos = key_pos.reshape(DOCS * tp_size // KEY_CHUNKS, KEY_CHUNKS * tokens)
    first_pos = jnp.min(key_pos, axis=1)

    natural = jnp.roll(keyval.reshape(ring, 2, rows, -1), (my_z, my_y), axis=(0, 1)).reshape(
        SEL, -1
    )
    if tp_size == KVH:
        half = tp_size // 2
        is_key = me < half
        first, second = natural[:, :HD], natural[:, HD:]
        one = lax.ppermute(
            jnp.where(is_key, first, second),
            "tp",
            [(i, 2 * i if i < half else 2 * (i - half) + 1) for i in range(tp_size)],
        )
        two = lax.ppermute(
            jnp.where(is_key, second, first),
            "tp",
            [(i, 2 * i + 1 if i < half else 2 * (i - half)) for i in range(tp_size)],
        )
        even = my_y == 0
        new_k, new_v = jnp.where(even, one, two), jnp.where(even, two, one)
    else:
        everyone = lax.all_gather(natural, "tp", axis=1, tiled=True)
        my_head = me * KVH // tp_size
        new_k = lax.dynamic_slice_in_dim(everyone, my_head * HD, HD, axis=1)
        new_v = lax.dynamic_slice_in_dim(everyone, (KVH + my_head) * HD, HD, axis=1)

    attention = attend(chunks, q_raw, q_pos, key_pos, first_pos, new_k, new_v, selected)

    finished = []
    for chunk in range(REDUCE_CHUNKS):
        own, other = project_out(attention, w_out, chunk, REDUCE_CHUNKS, rows)
        theirs = lax.ppermute(other, "tp", across)
        held = None
        for step in range(ring - 1, -1, -1):
            here = slice(step * rows, (step + 1) * rows)
            mine = own[here] + theirs[here].astype(jnp.float32)
            if held is not None:
                mine = mine + held.astype(jnp.float32)
            mine = mine.astype(jnp.bfloat16)
            if step:
                held = lax.ppermute(mine, "tp", down)
        finished.append(mine)
    return jnp.concatenate(finished, axis=1)


def solution(mesh):
    placed = (
        P(("groups", "req", "tp"), None),
        P(),
        P(None, "tp"),
        P(None, "tp"),
        P("tp", None),
        P(("groups", "req"), "tp", None, None),
        P(("groups", "req")),
        P(("groups", "req"), None),
        P(("groups", "req"), None),
    )
    return jax.shard_map(
        per_device,
        mesh=mesh,
        in_specs=placed,
        out_specs=P(("groups", "req", "tp"), None),
        check_vma=False,
    )
```

```python
import functools
import math

import jax
import jax.numpy as jnp
from jax import lax
from jax.experimental import pallas as pl
from jax.experimental.pallas import tpu as pltpu
from jax.sharding import PartitionSpec as P

HEADS = 64
KVH = 8
HD = 128
DOCS = 4
BLOCK = 128
SEL = 256


EPSILON = 1e-05
ROPE_BASE = 500000.0
MASKED = -1e30
FAR = 1 << 30
GATHER_CHUNKS = 2
REDUCE_CHUNKS = 2
TILE_COLS = 256
GROUPS = 2


def rotation_tables(positions):
    half_dim = HD // 2
    inverse = ROPE_BASE ** (-(jnp.arange(half_dim, dtype=jnp.float32) * (2.0 / HD)))
    angles = positions.astype(jnp.float32)[:, None] * inverse[None, :]
    cosine = jnp.cos(angles)
    sine_part = jnp.sin(angles)
    return (
        jnp.concatenate([cosine, cosine], axis=-1),
        jnp.concatenate([-sine_part, sine_part], axis=-1),
    )


def rotate(values, cosine, sine_part):
    swapped = jnp.concatenate([values[:, HD // 2 :], values[:, : HD // 2]], axis=-1)
    return values * cosine + swapped * sine_part


def megabytes(count):
    return pltpu.CompilerParams(vmem_limit_bytes=count * 1024 * 1024)


def project_kernel(n_blocks, has_prev, place_ref, *refs):
    blocks = refs[:n_blocks]
    left_ref, right_ref, wq_ref, wkv_ref = refs[n_blocks : n_blocks + 4]
    rest = refs[n_blocks + 4 :]
    if has_prev:
        prev_q, prev_kv = rest[:2]
        rest = rest[2:]
    out_q, out_kv, total_q, total_kv = rest
    step = pl.program_id(0)

    @pl.when(step == 0)
    def _():
        if has_prev:
            total_q[...] = prev_q[...]
            total_kv[...] = prev_kv[...]
        else:
            total_q[...] = jnp.zeros_like(total_q)
            total_kv[...] = jnp.zeros_like(total_kv)

    far = jnp.where(step == 0, left_ref[...], right_ref[...])
    rows = jnp.concatenate([b[...] for b in blocks] + [far], axis=0)
    total_q[...] += jnp.dot(rows, wq_ref[...], preferred_element_type=jnp.float32)
    total_kv[...] += jnp.dot(rows, wkv_ref[...], preferred_element_type=jnp.float32)

    @pl.when(step == 1)
    def _():
        if has_prev:
            count = left_ref.shape[0]
            for block in range(SEL // count):
                here = slice(block * count, (block + 1) * count)
                there = pl.ds(pl.multiple_of(place_ref[block] * count, count), count)
                out_q[there, :] = total_q[here, :]
                out_kv[there, :] = total_kv[here, :]
        else:
            out_q[...] = total_q[...]
            out_kv[...] = total_kv[...]


def project(place, blocks, left, right, w_query, w_keyval, prev, chunk):
    depth = 2 * left.shape[1]
    tile = left.shape[1]
    q_cols, kv_cols = w_query.shape[1], w_keyval.shape[1]
    whole = lambda k: (0, 0)
    specs = [pl.BlockSpec(memory_space=pltpu.SMEM)]
    specs += [pl.BlockSpec((b.shape[0], tile), lambda k: (0, k)) for b in blocks]
    specs += [pl.BlockSpec(left.shape, whole)] * 2
    specs += [
        pl.BlockSpec((tile, q_cols), lambda k: (chunk * 2 + k, 0)),
        pl.BlockSpec((tile, kv_cols), lambda k: (chunk * 2 + k, 0)),
    ]
    operands = [place, *blocks, left, right, w_query, w_keyval]
    if prev is not None:
        specs += [pl.BlockSpec((SEL, q_cols), whole), pl.BlockSpec((SEL, kv_cols), whole)]
        operands += list(prev)
    return pl.pallas_call(
        functools.partial(project_kernel, len(blocks), prev is not None),
        grid=(2,),
        in_specs=specs,
        out_specs=[pl.BlockSpec((SEL, q_cols), whole), pl.BlockSpec((SEL, kv_cols), whole)],
        out_shape=[
            jax.ShapeDtypeStruct((SEL, q_cols), jnp.float32),
            jax.ShapeDtypeStruct((SEL, kv_cols), jnp.float32),
        ],
        scratch_shapes=[
            pltpu.VMEM((SEL, q_cols), jnp.float32),
            pltpu.VMEM((SEL, kv_cols), jnp.float32),
        ],
        compiler_params=megabytes(32),
        cost_estimate=pl.CostEstimate(
            flops=2 * SEL * depth * (q_cols + kv_cols),
            bytes_accessed=2 * depth * (q_cols + kv_cols + SEL) + 8 * SEL * (q_cols + kv_cols),
            transcendentals=0,
        ),
        name="project",
    )(*operands)


def select_kernel(n_dest, n_src, place_ref, slot_ref, head_ref, *refs):
    sources = refs[:n_src]
    outs = refs[n_src : n_src + n_dest]
    sems = refs[n_src + n_dest]
    for doc in range(DOCS):
        for src in range(n_src):

            @pl.when(place_ref[doc] == src)
            def _():
                for dest in range(n_dest):
                    cols = pl.ds(pl.multiple_of(head_ref[dest] * HD, HD), HD)
                    pltpu.make_async_copy(
                        sources[src].at[slot_ref[doc], :, :, cols],
                        outs[dest].at[:, doc],
                        sems.at[dest, doc],
                    ).start()

    for dest in range(n_dest):
        for doc in range(DOCS):
            pltpu.make_async_copy(
                sources[0].at[0, :, :, 0:HD], outs[dest].at[:, doc], sems.at[dest, doc]
            ).wait()


def select_docs(sources, place, slot, heads, n_dest):
    tokens = sources[0].shape[2]
    shape = (2, DOCS, tokens, HD)
    smem = pl.BlockSpec(memory_space=pltpu.SMEM)
    return pl.pallas_call(
        functools.partial(select_kernel, n_dest, len(sources)),
        in_specs=[smem] * 3 + [pl.BlockSpec(memory_space=pl.ANY)] * len(sources),
        out_specs=[pl.BlockSpec(memory_space=pltpu.VMEM)] * n_dest,
        out_shape=[jax.ShapeDtypeStruct(shape, jnp.bfloat16)] * n_dest,
        scratch_shapes=[pltpu.SemaphoreType.DMA((n_dest, DOCS))],
        compiler_params=megabytes(16),
        cost_estimate=pl.CostEstimate(
            flops=0, bytes_accessed=4 * n_dest * math.prod(shape), transcendentals=0
        ),
        name="select_docs",
    )(place, slot, heads, *sources)


def attend_kernel(n_chunks, is_first, is_last, heads_here, first_ref, qmin_ref, qmax_ref, *refs):
    refs = list(refs)
    take = lambda count: [refs.pop(0) for _ in range(count)]
    chunks = take(n_chunks)
    dead_ref, qpos_ref = take(2)
    if is_first:
        q_ref, cos_ref, sin_ref, newk_ref, newv_ref = take(5)
    else:
        queries, old_top, old_total, old_summed = take(4)
    if is_last:
        (out_ref,) = take(1)
        if is_first:
            (queries,) = take(1)
        top, total, summed = take(3)
    else:
        queries, top, total, summed = take(4)
    values = take(1)[0]
    if is_first:
        new_key, new_value = take(2)
    n_tiles = SEL * heads_here // TILE_COLS
    tile_q = TILE_COLS // heads_here
    tokens = chunks[0].shape[2]
    scale = math.log2(math.e) / math.sqrt(HD)

    for chunk in range(n_chunks):
        for doc in range(DOCS):
            values[doc, :, chunk * tokens : (chunk + 1) * tokens] = chunks[chunk][1, doc].T
    if is_first:
        new_key[...] = rotate(
            newk_ref[...].astype(jnp.float32), cos_ref[...], sin_ref[...]
        ).astype(jnp.bfloat16)
        new_value[...] = newv_ref[...].T

    one_row = jnp.where(
        lax.broadcasted_iota(jnp.int32, (HD, TILE_COLS), 0) == 0, 1.0, 0.0
    ).astype(jnp.bfloat16)

    def update(tile, parts):
        best = functools.reduce(
            jnp.maximum, [jnp.max(scores, axis=0, keepdims=True) for scores, _ in parts]
        )
        old = top[tile]
        new = jnp.maximum(old, best)
        shrink = jnp.exp2((old - new) * scale)
        running = total[tile] * shrink
        mixed = summed[tile] * shrink
        for scores, value in parts:
            weights = jnp.exp2((scores - new) * scale)
            running += jnp.sum(weights, axis=0, keepdims=True)
            mixed += jnp.dot(
                value, weights.astype(jnp.bfloat16), preferred_element_type=jnp.float32
            )
        top[tile] = new
        total[tile] = running
        summed[tile] = mixed

    @pl.loop(0, n_tiles)
    def _(tile):
        here = pl.ds(pl.multiple_of(tile * tile_q, tile_q), tile_q)
        if is_first:
            stacked = jnp.concatenate(
                [
                    rotate(
                        q_ref[here, head * HD : (head + 1) * HD], cos_ref[here, :], sin_ref[here, :]
                    )
                    for head in range(heads_here)
                ],
                axis=0,
            )
            queries[tile] = stacked.T.astype(jnp.bfloat16)
            top[tile] = jnp.full(top.shape[1:], MASKED, jnp.float32)
            total[tile] = jnp.zeros(total.shape[1:], jnp.float32)
            summed[tile] = jnp.zeros(summed.shape[1:], jnp.float32)
            scores = jnp.dot(new_key[...], queries[tile], preferred_element_type=jnp.float32)
            key_index = lax.broadcasted_iota(jnp.int32, scores.shape, 0)
            q_index = tile * tile_q + lax.broadcasted_iota(jnp.int32, scores.shape, 1) % tile_q
            scores = jnp.where(key_index <= q_index, scores, MASKED)
            update(tile, [(scores, new_value[...])])
        else:
            top[tile] = old_top[tile]
            total[tile] = old_total[tile]
            summed[tile] = old_summed[tile]

        extended = jnp.concatenate([queries[tile], one_row], axis=0)

        @pl.loop(0, DOCS)
        def _(doc):
            firsts = [first_ref[doc * n_chunks + chunk] for chunk in range(n_chunks)]
            lowest = functools.reduce(jnp.minimum, firsts)
            reach = functools.reduce(jnp.maximum, firsts) + tokens - 1

            def visit(masked):
                parts = []
                for chunk in range(n_chunks):
                    span = slice(chunk * tokens, (chunk + 1) * tokens)
                    keys = jnp.concatenate([chunks[chunk][0, doc], dead_ref[doc, span, :]], axis=1)
                    scores = jnp.dot(keys, extended, preferred_element_type=jnp.float32)
                    if masked:
                        key_pos = firsts[chunk] + lax.broadcasted_iota(jnp.int32, scores.shape, 0)
                        scores = jnp.where(key_pos <= qpos_ref[tile], scores, MASKED)
                    parts.append((scores, values[doc, :, span]))
                update(tile, parts)

            live = lowest <= qmax_ref[tile]
            whole = reach <= qmin_ref[tile]

            @pl.when(live & whole)
            def _():
                visit(False)

            @pl.when(live & jnp.logical_not(whole))
            def _():
                visit(True)

        if is_last:
            finished = (summed[tile] / total[tile]).T.astype(jnp.bfloat16)
            for head in range(heads_here):
                out_ref[here, head * HD : (head + 1) * HD] = finished[
                    head * tile_q : (head + 1) * tile_q, :
                ]


def attend(chunks, dead, first_pos, selected, heads_here, fresh, state, is_last):
    n_chunks = len(chunks)
    tokens = chunks[0].shape[2]
    n_tiles = SEL * heads_here // TILE_COLS
    tile_q = TILE_COLS // heads_here
    is_first = state is None
    by_tile = selected.reshape(n_tiles, tile_q)
    q_pos = jnp.tile(by_tile, (1, heads_here)).reshape(n_tiles, 1, TILE_COLS)
    smem = pl.BlockSpec(memory_space=pltpu.SMEM)
    vmem = pl.BlockSpec(memory_space=pltpu.VMEM)
    operands = [first_pos, by_tile[:, 0], by_tile[:, -1], *chunks, dead, q_pos]
    operands += list(fresh) if is_first else list(state)
    shapes = [
        ((n_tiles, HD, TILE_COLS), jnp.bfloat16),
        ((n_tiles, 1, TILE_COLS), jnp.float32),
        ((n_tiles, 1, TILE_COLS), jnp.float32),
        ((n_tiles, HD, TILE_COLS), jnp.float32),
    ]
    if is_last:
        outs = [((SEL, heads_here * HD), jnp.bfloat16)]
        scratch = shapes if is_first else shapes[1:]
    else:
        outs, scratch = shapes, []
    scratch = scratch + [((DOCS, HD, n_chunks * tokens), jnp.bfloat16)]
    if is_first:
        scratch = scratch + [((SEL, HD), jnp.bfloat16), ((HD, SEL), jnp.bfloat16)]
    pairs = SEL * heads_here * DOCS * n_chunks * tokens // 2
    return pl.pallas_call(
        functools.partial(attend_kernel, n_chunks, is_first, is_last, heads_here),
        in_specs=[smem] * 3 + [vmem] * (len(operands) - 3),
        out_specs=[vmem] * len(outs),
        out_shape=[jax.ShapeDtypeStruct(*s) for s in outs],
        scratch_shapes=[pltpu.VMEM(*s) for s in scratch],
        compiler_params=megabytes(32),
        cost_estimate=pl.CostEstimate(
            flops=4 * pairs * HD,
            bytes_accessed=4 * DOCS * n_chunks * tokens * HD,
            transcendentals=pairs,
        ),
        name="attend",
    )(*operands)


def out_kernel(n_blocks, place_ref, x_ref, w_ref, *refs):
    outs, ordered = refs[:-1], refs[-1]
    rows = SEL // n_blocks
    tiles = pl.num_programs(0)
    step = pl.program_id(0)

    @pl.when(step == 0)
    def _():
        for block in range(n_blocks):
            there = pl.ds(pl.multiple_of(place_ref[block] * rows, rows), rows)
            ordered[block * rows : (block + 1) * rows, :] = x_ref[there, :]

    product = jnp.dot(
        ordered[...].astype(jnp.bfloat16), w_ref[...], preferred_element_type=jnp.float32
    )
    for block in range(n_blocks - 1):
        outs[block][...] = product[block * rows : (block + 1) * rows, :]
    far = product[(n_blocks - 1) * rows :, :].astype(jnp.bfloat16)

    @pl.when(step < tiles // 2)
    def _():
        outs[n_blocks - 1][...] = far

    @pl.when(step >= tiles // 2)
    def _():
        outs[n_blocks][...] = far


def project_out(place, attention, w_out, chunk, n_chunks, n_blocks):
    depth = w_out.shape[0]
    width = w_out.shape[1] // n_chunks
    rows = SEL // n_blocks
    tile = 512
    steps = width // tile
    half = steps // 2
    if rows % 16:
        attention = attention.astype(jnp.float32)
    return pl.pallas_call(
        functools.partial(out_kernel, n_blocks),
        grid=(steps,),
        in_specs=[
            pl.BlockSpec(memory_space=pltpu.SMEM),
            pl.BlockSpec((SEL, depth), lambda n: (0, 0)),
            pl.BlockSpec((depth, tile), lambda n: (0, chunk * steps + n)),
        ],
        out_specs=[pl.BlockSpec((rows, tile), lambda n: (0, n))] * (n_blocks - 1)
        + [
            pl.BlockSpec((rows, tile), lambda n: (0, jnp.minimum(n, half - 1))),
            pl.BlockSpec((rows, tile), lambda n: (0, jnp.maximum(n - half, 0))),
        ],
        out_shape=[jax.ShapeDtypeStruct((rows, width), jnp.float32)] * (n_blocks - 1)
        + [jax.ShapeDtypeStruct((rows, width // 2), jnp.bfloat16)] * 2,
        scratch_shapes=[pltpu.VMEM((SEL, depth), attention.dtype)],
        compiler_params=megabytes(32),
        cost_estimate=pl.CostEstimate(
            flops=2 * SEL * depth * width,
            bytes_accessed=2 * depth * (width + SEL) + 4 * SEL * width,
            transcendentals=0,
        ),
        name="project_out",
    )(place, attention, w_out)


def per_device(
    hidden_in, norm_gain, w_query, w_keyval, w_out, pool_cache, doc_slot, doc_blocks, sel_pos
):
    tp_size = lax.axis_size("tp")
    req_size = lax.axis_size("req")
    me = lax.axis_index("tp")
    rows, width = hidden_in.shape
    slots, tokens = pool_cache.shape[:2]
    heads_here = w_query.shape[1] // HD
    selected = sel_pos[0]
    lengths = doc_blocks[0] * BLOCK

    if tp_size == KVH:
        ring = [*range(0, tp_size, 2), *range(tp_size - 1, 0, -2)]
    else:
        ring = list(range(tp_size))
    far = tp_size // 2
    forth = [(ring[p], ring[(p + 1) % tp_size]) for p in range(tp_size)]
    back = [(dst, src) for src, dst in forth]
    steps = [0] + [sign * k for k in range(1, far) for sign in (-1, 1)] + [far]
    table = [[ring[(ring.index(i) + s) % tp_size] for s in steps] for i in range(tp_size)]
    place = jnp.array(table, jnp.int32)[me]

    widened = hidden_in.astype(jnp.float32)
    normed = (
        widened
        * lax.rsqrt(jnp.mean(widened * widened, axis=-1, keepdims=True) + EPSILON)
        * norm_gain
    ).astype(jnp.bfloat16)
    normed, pool_cache = lax.optimization_barrier((normed, pool_cache))

    part = width // GATHER_CHUNKS
    half = part // 2
    prev = None
    for chunk in range(GATHER_CHUNKS):
        own = normed[:, chunk * part : (chunk + 1) * part]
        before = behind = own
        blocks = [own]
        for _ in range(1, far):
            before = lax.ppermute(before, "tp", forth)
            behind = lax.ppermute(behind, "tp", back)
            blocks += [before, behind]
        left = lax.ppermute(before[:, :half], "tp", forth)
        right = lax.ppermute(behind[:, half:], "tp", back)
        if rows % 16:
            blocks = [jnp.concatenate(blocks, axis=0)]
        prev = project(place, blocks, left, right, w_query, w_keyval, prev, chunk)
    q_raw, keyval = prev

    by_kind = pool_cache.transpose(0, 2, 1, 3)
    sources = [by_kind]
    for shift in range(1, req_size):
        sources.append(
            lax.ppermute(by_kind, "req", [((i + shift) % req_size, i) for i in range(req_size)])
        )
    holder = (doc_slot // slots - lax.axis_index("req")) % req_size
    order = jnp.arange(tp_size, dtype=jnp.int32)
    sent = select_docs(sources, holder, doc_slot % slots, (me ^ order) * KVH // tp_size, tp_size)
    chunks = [sent[0]] + [
        lax.ppermute(sent[j], "tp", [(i, i ^ j) for i in range(tp_size)])
        for j in range(1, tp_size)
    ]

    offsets = jnp.cumsum(lengths) - lengths
    first_slot = (me ^ order) * tokens
    slot_tokens = first_slot[:, None] + jnp.arange(tokens, dtype=jnp.int32)[None, :]
    cache_pos = offsets[:, None, None] + slot_tokens[None]
    is_valid = slot_tokens[None] < lengths[:, None, None]
    replaced = jnp.any(cache_pos[..., None] == selected, axis=-1)
    dead = jnp.where(is_valid & jnp.logical_not(replaced), 0.0, MASKED).astype(jnp.bfloat16)
    dead = jnp.broadcast_to(dead[..., None], (DOCS, tp_size, tokens, HD))
    first_pos = jnp.where(
        first_slot[None] < lengths[:, None], offsets[:, None] + first_slot[None], FAR
    )

    keyval = keyval.astype(jnp.bfloat16)
    if tp_size == KVH:
        middle = tp_size // 2
        is_key = me < middle
        first, second = keyval[:, :HD], keyval[:, HD:]
        one = lax.ppermute(
            jnp.where(is_key, first, second),
            "tp",
            [(i, 2 * i if i < middle else 2 * (i - middle) + 1) for i in range(tp_size)],
        )
        two = lax.ppermute(
            jnp.where(is_key, second, first),
            "tp",
            [(i, 2 * i + 1 if i < middle else 2 * (i - middle)) for i in range(tp_size)],
        )
        even = me % 2 == 0
        new_k, new_v = jnp.where(even, one, two), jnp.where(even, two, one)
    else:
        everyone = lax.all_gather(keyval, "tp", axis=1, tiled=True)
        my_head = me * KVH // tp_size
        new_k = lax.dynamic_slice_in_dim(everyone, my_head * HD, HD, axis=1)
        new_v = lax.dynamic_slice_in_dim(everyone, (KVH + my_head) * HD, HD, axis=1)

    cosine, sine_part = rotation_tables(selected)
    state = None
    size = tp_size // GROUPS
    for group in range(GROUPS):
        span = slice(group * size, (group + 1) * size)
        state = attend(
            chunks[span],
            dead[:, span].reshape(DOCS, size * tokens, HD),
            first_pos[:, span].reshape(-1),
            selected,
            heads_here,
            (q_raw, cosine, sine_part, new_k, new_v),
            state,
            group + 1 == GROUPS,
        )
    (attention,) = state

    finished = []
    for chunk in range(REDUCE_CHUNKS):
        pieces = project_out(place, attention, w_out, chunk, REDUCE_CHUNKS, tp_size)
        total = pieces[0]
        to_forth, to_back = pieces[2 : tp_size - 1 : 2], pieces[1 : tp_size - 1 : 2]
        cut = pieces[-1].shape[1]
        ahead = lax.ppermute(pieces[-2], "tp", forth).astype(jnp.float32)
        astern = lax.ppermute(pieces[-1], "tp", back).astype(jnp.float32)
        for k in range(far - 1, 0, -1):
            up, down = to_forth[k - 1], to_back[k - 1]
            if k == far - 1:
                up = jnp.concatenate([up[:, :cut] + ahead, up[:, cut:]], axis=1)
                down = jnp.concatenate([down[:, :cut], down[:, cut:] + astern], axis=1)
            else:
                up, down = up + ahead, down + astern
            ahead = lax.ppermute(up.astype(jnp.bfloat16), "tp", forth).astype(jnp.float32)
            astern = lax.ppermute(down.astype(jnp.bfloat16), "tp", back).astype(jnp.float32)
        finished.append((total + ahead + astern).astype(jnp.bfloat16))
    return jnp.concatenate(finished, axis=1)


def solution(mesh):
    placed = (
        P(("groups", "req", "tp"), None),
        P(),
        P(None, "tp"),
        P(None, "tp"),
        P("tp", None),
        P(("groups", "req"), "tp", None, None),
        P(("groups", "req")),
        P(("groups", "req"), None),
        P(("groups", "req"), None),
    )
    return jax.shard_map(
        per_device,
        mesh=mesh,
        in_specs=placed,
        out_specs=P(("groups", "req", "tp"), None),
        check_vma=False,
    )
```

```python
import functools
import math

import jax
import jax.numpy as jnp
from jax import lax
from jax.experimental import pallas as pl
from jax.experimental.pallas import tpu as pltpu
from jax.sharding import PartitionSpec as P

HEADS = 64
KVH = 8
HD = 128
DOCS = 4
BLOCK = 128
SEL = 256


EPSILON = 1e-05
ROPE_BASE = 500000.0
MASKED = -1e30
FAR = 1 << 30
GATHER_CHUNKS = 2
REDUCE_CHUNKS = 2
TILE_COLS = 256
PAIR = 2


def rotation_tables(positions):
    half_dim = HD // 2
    inverse = ROPE_BASE ** (-(jnp.arange(half_dim, dtype=jnp.float32) * (2.0 / HD)))
    angles = positions.astype(jnp.float32)[:, None] * inverse[None, :]
    cosine = jnp.cos(angles)
    sine_part = jnp.sin(angles)
    return (
        jnp.concatenate([cosine, cosine], axis=-1),
        jnp.concatenate([-sine_part, sine_part], axis=-1),
    )


def rotate(values, cosine, sine_part):
    swapped = jnp.concatenate([values[:, HD // 2 :], values[:, : HD // 2]], axis=-1)
    return values * cosine + swapped * sine_part


def megabytes(count):
    return pltpu.CompilerParams(vmem_limit_bytes=count * 1024 * 1024)


def project_kernel(n_blocks, has_prev, place_ref, *refs):
    blocks = refs[:n_blocks]
    left_ref, right_ref, wq_ref, wkv_ref = refs[n_blocks : n_blocks + 4]
    rest = refs[n_blocks + 4 :]
    if has_prev:
        prev_q, prev_kv, cos_ref, sin_ref = rest[:4]
        rest = rest[4:]
    out_q, out_kv, total_q, total_kv = rest[:4]
    step = pl.program_id(0)

    @pl.when(step == 0)
    def _():
        if has_prev:
            total_q[...] = prev_q[...]
            total_kv[...] = prev_kv[...]
        else:
            total_q[...] = jnp.zeros_like(total_q)
            total_kv[...] = jnp.zeros_like(total_kv)

    far = jnp.where(step == 0, left_ref[...], right_ref[...])
    rows = jnp.concatenate([b[...] for b in blocks] + [far], axis=0)
    total_q[...] += jnp.dot(rows, wq_ref[...], preferred_element_type=jnp.float32)
    total_kv[...] += jnp.dot(rows, wkv_ref[...], preferred_element_type=jnp.float32)

    @pl.when(step == 1)
    def _():
        if has_prev:
            count = left_ref.shape[0]
            for block in range(SEL // count):
                here = slice(block * count, (block + 1) * count)
                there = pl.ds(pl.multiple_of(place_ref[block] * count, count), count)
                natural = rest[4]
                natural[there, :] = total_q[here, :]
                out_kv[there, :] = total_kv[here, :]
            heads_here = total_q.shape[1] // HD
            tile_q = TILE_COLS // heads_here
            for tile in range(SEL // tile_q):
                here = slice(tile * tile_q, (tile + 1) * tile_q)
                stacked = jnp.concatenate(
                    [
                        rotate(
                            natural[here, head * HD : (head + 1) * HD],
                            cos_ref[here, :],
                            sin_ref[here, :],
                        )
                        for head in range(heads_here)
                    ],
                    axis=0,
                )
                out_q[tile] = stacked.T.astype(jnp.bfloat16)
        else:
            out_q[...] = total_q[...]
            out_kv[...] = total_kv[...]


def project(place, blocks, left, right, w_query, w_keyval, prev, tables, chunk):
    depth = 2 * left.shape[1]
    tile = left.shape[1]
    q_cols, kv_cols = w_query.shape[1], w_keyval.shape[1]
    whole = lambda k: (0, 0)
    specs = [pl.BlockSpec(memory_space=pltpu.SMEM)]
    specs += [pl.BlockSpec((b.shape[0], tile), lambda k: (0, k)) for b in blocks]
    specs += [pl.BlockSpec(left.shape, whole)] * 2
    specs += [
        pl.BlockSpec((tile, q_cols), lambda k: (chunk * 2 + k, 0)),
        pl.BlockSpec((tile, kv_cols), lambda k: (chunk * 2 + k, 0)),
    ]
    operands = [place, *blocks, left, right, w_query, w_keyval]
    if prev is not None:
        specs += [pl.BlockSpec(a.shape, whole) for a in (*prev, *tables)]
        operands += [*prev, *tables]
        q_out = ((SEL * q_cols // (HD * TILE_COLS), HD, TILE_COLS), jnp.bfloat16)
    else:
        q_out = ((SEL, q_cols), jnp.float32)
    return pl.pallas_call(
        functools.partial(project_kernel, len(blocks), prev is not None),
        grid=(2,),
        in_specs=specs,
        out_specs=[
            pl.BlockSpec(q_out[0], lambda k: (0,) * len(q_out[0])),
            pl.BlockSpec((SEL, kv_cols), whole),
        ],
        out_shape=[
            jax.ShapeDtypeStruct(*q_out),
            jax.ShapeDtypeStruct((SEL, kv_cols), jnp.float32),
        ],
        scratch_shapes=[
            pltpu.VMEM((SEL, q_cols), jnp.float32),
            pltpu.VMEM((SEL, kv_cols), jnp.float32),
        ]
        + [pltpu.VMEM((SEL, q_cols), jnp.float32)] * (prev is not None),
        compiler_params=megabytes(32),
        cost_estimate=pl.CostEstimate(
            flops=2 * SEL * depth * (q_cols + kv_cols),
            bytes_accessed=2 * depth * (q_cols + kv_cols + SEL) + 8 * SEL * (q_cols + kv_cols),
            transcendentals=0,
        ),
        name="project",
    )(*operands)


def select_kernel(n_dest, n_src, place_ref, slot_ref, head_ref, *refs):
    sources = refs[:n_src]
    outs = refs[n_src : n_src + n_dest]
    sems = refs[n_src + n_dest]
    for doc in range(DOCS):
        for src in range(n_src):

            @pl.when(place_ref[doc] == src)
            def _():
                for dest in range(n_dest):
                    cols = pl.ds(pl.multiple_of(head_ref[dest] * HD, HD), HD)
                    pltpu.make_async_copy(
                        sources[src].at[slot_ref[doc], :, :, cols],
                        outs[dest].at[:, doc],
                        sems.at[dest, doc],
                    ).start()

    for dest in range(n_dest):
        for doc in range(DOCS):
            pltpu.make_async_copy(
                sources[0].at[0, :, :, 0:HD], outs[dest].at[:, doc], sems.at[dest, doc]
            ).wait()


def select_docs(sources, place, slot, heads, n_dest):
    tokens = sources[0].shape[2]
    shape = (2, DOCS, tokens, HD)
    smem = pl.BlockSpec(memory_space=pltpu.SMEM)
    return pl.pallas_call(
        functools.partial(select_kernel, n_dest, len(sources)),
        in_specs=[smem] * 3 + [pl.BlockSpec(memory_space=pl.ANY)] * len(sources),
        out_specs=[pl.BlockSpec(memory_space=pltpu.VMEM)] * n_dest,
        out_shape=[jax.ShapeDtypeStruct(shape, jnp.bfloat16)] * n_dest,
        scratch_shapes=[pltpu.SemaphoreType.DMA((n_dest, DOCS))],
        compiler_params=megabytes(16),
        cost_estimate=pl.CostEstimate(
            flops=0, bytes_accessed=4 * n_dest * math.prod(shape), transcendentals=0
        ),
        name="select_docs",
    )(place, slot, heads, *sources)


def attend_kernel(n_chunks, with_new, tile_q, first_ref, qmin_ref, qmax_ref, *refs):
    refs = list(refs)
    take = lambda count: [refs.pop(0) for _ in range(count)]
    chunks = take(n_chunks)
    dead_ref, qpos_ref, queries = take(3)
    if with_new:
        cos_ref, sin_ref, newk_ref, newv_ref = take(4)
    top, total, mixed_out, values = take(4)
    if with_new:
        summed = mixed_out
        new_key, new_value = take(2)
    else:
        summed = take(1)[0]
    n_pairs = queries.shape[0] // PAIR
    tokens = chunks[0].shape[2]
    scale = math.log2(math.e) / math.sqrt(HD)

    for chunk in range(n_chunks):
        for doc in range(DOCS):
            values[doc, :, chunk * tokens : (chunk + 1) * tokens] = chunks[chunk][1, doc].T
    if with_new:
        new_key[...] = rotate(
            newk_ref[...].astype(jnp.float32), cos_ref[...], sin_ref[...]
        ).astype(jnp.bfloat16)
        new_value[...] = newv_ref[...].T

    one_row = jnp.where(
        lax.broadcasted_iota(jnp.int32, (HD, TILE_COLS), 0) == 0, 1.0, 0.0
    ).astype(jnp.bfloat16)

    def update(tile, parts):
        best = functools.reduce(
            jnp.maximum, [jnp.max(scores, axis=0, keepdims=True) for scores, _ in parts]
        )
        old = top[tile]
        new = jnp.maximum(old, best)
        shrink = jnp.exp2((old - new) * scale)
        running = total[tile] * shrink
        mixed = summed[tile] * shrink
        for scores, value in parts:
            weights = jnp.exp2((scores - new) * scale)
            running += jnp.sum(weights, axis=0, keepdims=True)
            mixed += jnp.dot(
                value, weights.astype(jnp.bfloat16), preferred_element_type=jnp.float32
            )
        top[tile] = new
        total[tile] = running
        summed[tile] = mixed

    @pl.loop(0, n_pairs)
    def _(pair):
        tiles = [pair * PAIR + i for i in range(PAIR)]
        for tile in tiles:
            top[tile] = jnp.full(top.shape[1:], MASKED, jnp.float32)
            total[tile] = jnp.zeros(total.shape[1:], jnp.float32)
            summed[tile] = jnp.zeros(summed.shape[1:], jnp.float32)
        if with_new:
            fresh = []
            for tile in tiles:
                scores = jnp.dot(new_key[...], queries[tile], preferred_element_type=jnp.float32)
                key_index = lax.broadcasted_iota(jnp.int32, scores.shape, 0)
                q_index = tile * tile_q + lax.broadcasted_iota(jnp.int32, scores.shape, 1) % tile_q
                fresh.append(jnp.where(key_index <= q_index, scores, MASKED))
            for tile, scores in zip(tiles, fresh):
                update(tile, [(scores, new_value[...])])

        @pl.loop(0, DOCS)
        def _(doc):
            firsts = [first_ref[doc * n_chunks + chunk] for chunk in range(n_chunks)]
            lowest = functools.reduce(jnp.minimum, firsts)
            reach = functools.reduce(jnp.maximum, firsts) + tokens - 1

            def visit(masked):
                found = []
                for tile in tiles:
                    extended = jnp.concatenate([queries[tile], one_row], axis=0)
                    parts = []
                    for chunk in range(n_chunks):
                        span = slice(chunk * tokens, (chunk + 1) * tokens)
                        keys = jnp.concatenate(
                            [chunks[chunk][0, doc], dead_ref[doc, span, :]], axis=1
                        )
                        scores = jnp.dot(keys, extended, preferred_element_type=jnp.float32)
                        if masked:
                            key_pos = firsts[chunk] + lax.broadcasted_iota(
                                jnp.int32, scores.shape, 0
                            )
                            scores = jnp.where(key_pos <= qpos_ref[tile], scores, MASKED)
                        parts.append((scores, values[doc, :, span]))
                    found.append(parts)
                for tile, parts in zip(tiles, found):
                    update(tile, parts)

            live = lowest <= qmax_ref[pair]
            whole = reach <= qmin_ref[pair]

            @pl.when(live & whole)
            def _():
                visit(False)

            @pl.when(live & jnp.logical_not(whole))
            def _():
                visit(True)

        if not with_new:
            for tile in tiles:
                mixed_out[tile] = summed[tile].astype(jnp.bfloat16)


def attend(chunks, dead, first_pos, selected, queries, fresh):
    n_chunks = len(chunks)
    tokens = chunks[0].shape[2]
    n_tiles = queries.shape[0]
    tile_q = SEL // n_tiles
    by_pair = selected.reshape(n_tiles // PAIR, PAIR * tile_q)
    q_pos = jnp.tile(selected.reshape(n_tiles, tile_q), (1, TILE_COLS // tile_q))
    q_pos = q_pos.reshape(n_tiles, 1, TILE_COLS)
    smem = pl.BlockSpec(memory_space=pltpu.SMEM)
    vmem = pl.BlockSpec(memory_space=pltpu.VMEM)
    operands = [first_pos, by_pair[:, 0], by_pair[:, -1], *chunks, dead, q_pos, queries, *fresh]
    mixed = ((n_tiles, HD, TILE_COLS), jnp.float32 if fresh else jnp.bfloat16)
    outs = [((n_tiles, 1, TILE_COLS), jnp.float32)] * 2 + [mixed]
    scratch = [((DOCS, HD, n_chunks * tokens), jnp.bfloat16)]
    if fresh:
        scratch += [((SEL, HD), jnp.bfloat16), ((HD, SEL), jnp.bfloat16)]
    else:
        scratch += [(mixed[0], jnp.float32)]
    pairs = SEL * TILE_COLS // tile_q * DOCS * n_chunks * tokens // 2
    return pl.pallas_call(
        functools.partial(attend_kernel, n_chunks, bool(fresh), tile_q),
        in_specs=[smem] * 3 + [vmem] * (len(operands) - 3),
        out_specs=[vmem] * len(outs),
        out_shape=[jax.ShapeDtypeStruct(*s) for s in outs],
        scratch_shapes=[pltpu.VMEM(*s) for s in scratch],
        compiler_params=megabytes(24),
        cost_estimate=pl.CostEstimate(
            flops=4 * pairs * HD,
            bytes_accessed=4 * DOCS * n_chunks * tokens * HD,
            transcendentals=pairs,
        ),
        name="attend",
    )(*operands)


def merge_kernel(*refs):
    top_a, total_a, mixed_a, top_b, total_b, mixed_b, out_ref = refs
    scale = math.log2(math.e) / math.sqrt(HD)
    n_tiles = top_a.shape[0]
    tile_q = SEL // n_tiles
    for tile in range(n_tiles):
        new = jnp.maximum(top_a[tile], top_b[tile])
        part_a = jnp.exp2((top_a[tile] - new) * scale)
        part_b = jnp.exp2((top_b[tile] - new) * scale)
        total = total_a[tile] * part_a + total_b[tile] * part_b
        mixed = mixed_a[tile] * part_a + mixed_b[tile].astype(jnp.float32) * part_b
        finished = (mixed / total).T.astype(jnp.bfloat16)
        for head in range(TILE_COLS // tile_q):
            out_ref[tile * tile_q : (tile + 1) * tile_q, head * HD : (head + 1) * HD] = finished[
                head * tile_q : (head + 1) * tile_q, :
            ]


def merge(mine, theirs):
    n_tiles = mine[0].shape[0]
    shape = (SEL, TILE_COLS * n_tiles // SEL * HD)
    return pl.pallas_call(
        merge_kernel,
        out_shape=jax.ShapeDtypeStruct(shape, jnp.bfloat16),
        compiler_params=megabytes(16),
        cost_estimate=pl.CostEstimate(
            flops=4 * math.prod(shape), bytes_accessed=8 * math.prod(shape), transcendentals=0
        ),
        name="merge",
    )(*mine, *theirs)


def out_kernel(n_blocks, place_ref, x_ref, w_ref, *refs):
    outs, ordered = refs[:-1], refs[-1]
    rows = SEL // n_blocks
    tiles = pl.num_programs(0)
    step = pl.program_id(0)

    @pl.when(step == 0)
    def _():
        for block in range(n_blocks):
            there = pl.ds(pl.multiple_of(place_ref[block] * rows, rows), rows)
            ordered[block * rows : (block + 1) * rows, :] = x_ref[there, :]

    product = jnp.dot(
        ordered[...].astype(jnp.bfloat16), w_ref[...], preferred_element_type=jnp.float32
    )
    for block in range(n_blocks - 1):
        outs[block][...] = product[block * rows : (block + 1) * rows, :]
    far = product[(n_blocks - 1) * rows :, :].astype(jnp.bfloat16)

    @pl.when(step < tiles // 2)
    def _():
        outs[n_blocks - 1][...] = far

    @pl.when(step >= tiles // 2)
    def _():
        outs[n_blocks][...] = far


def project_out(place, attention, w_out, chunk, n_chunks, n_blocks):
    depth = w_out.shape[0]
    width = w_out.shape[1] // n_chunks
    rows = SEL // n_blocks
    tile = 512
    steps = width // tile
    half = steps // 2
    if rows % 16:
        attention = attention.astype(jnp.float32)
    return pl.pallas_call(
        functools.partial(out_kernel, n_blocks),
        grid=(steps,),
        in_specs=[
            pl.BlockSpec(memory_space=pltpu.SMEM),
            pl.BlockSpec((SEL, depth), lambda n: (0, 0)),
            pl.BlockSpec((depth, tile), lambda n: (0, chunk * steps + n)),
        ],
        out_specs=[pl.BlockSpec((rows, tile), lambda n: (0, n))] * (n_blocks - 1)
        + [
            pl.BlockSpec((rows, tile), lambda n: (0, jnp.minimum(n, half - 1))),
            pl.BlockSpec((rows, tile), lambda n: (0, jnp.maximum(n - half, 0))),
        ],
        out_shape=[jax.ShapeDtypeStruct((rows, width), jnp.float32)] * (n_blocks - 1)
        + [jax.ShapeDtypeStruct((rows, width // 2), jnp.bfloat16)] * 2,
        scratch_shapes=[pltpu.VMEM((SEL, depth), attention.dtype)],
        compiler_params=megabytes(32),
        cost_estimate=pl.CostEstimate(
            flops=2 * SEL * depth * width,
            bytes_accessed=2 * depth * (width + SEL) + 4 * SEL * width,
            transcendentals=0,
        ),
        name="project_out",
    )(place, attention, w_out)


def per_device(
    hidden_in, norm_gain, w_query, w_keyval, w_out, pool_cache, doc_slot, doc_blocks, sel_pos
):
    tp_size = lax.axis_size("tp")
    req_size = lax.axis_size("req")
    me = lax.axis_index("tp")
    rows, width = hidden_in.shape
    slots, tokens = pool_cache.shape[:2]
    heads_here = w_query.shape[1] // HD
    selected = sel_pos[0]
    lengths = doc_blocks[0] * BLOCK

    if tp_size == KVH:
        ring = [*range(0, tp_size, 2), *range(tp_size - 1, 0, -2)]
    else:
        ring = list(range(tp_size))
    far = tp_size // 2
    forth = [(ring[p], ring[(p + 1) % tp_size]) for p in range(tp_size)]
    back = [(dst, src) for src, dst in forth]
    steps = [0] + [sign * k for k in range(1, far) for sign in (-1, 1)] + [far]
    table = [[ring[(ring.index(i) + s) % tp_size] for s in steps] for i in range(tp_size)]
    place = jnp.array(table, jnp.int32)[me]

    widened = hidden_in.astype(jnp.float32)
    normed = (
        widened
        * lax.rsqrt(jnp.mean(widened * widened, axis=-1, keepdims=True) + EPSILON)
        * norm_gain
    ).astype(jnp.bfloat16)
    normed, pool_cache = lax.optimization_barrier((normed, pool_cache))

    middle = tp_size // 2
    by_kind = pool_cache.transpose(0, 2, 1, 3)
    sources = [by_kind]
    for shift in range(1, req_size):
        sources.append(
            lax.ppermute(by_kind, "req", [((i + shift) % req_size, i) for i in range(req_size)])
        )
    holder = (doc_slot // slots - lax.axis_index("req")) % req_size
    order = jnp.arange(middle, dtype=jnp.int32)
    takers = jnp.concatenate([me ^ order, me ^ order ^ middle])
    sent = select_docs(sources, holder, doc_slot % slots, takers * KVH // tp_size, tp_size)

    cosine, sine_part = rotation_tables(selected)
    part = width // GATHER_CHUNKS
    half = part // 2
    prev = None
    for chunk in range(GATHER_CHUNKS):
        own = normed[:, chunk * part : (chunk + 1) * part]
        before = behind = own
        blocks = [own]
        for k in range(1, far):
            before = lax.ppermute(before, "tp", forth)
            behind = lax.ppermute(behind, "tp", back)
            if chunk == 0 and k == min(2, far - 1):
                before, behind, *sent = lax.optimization_barrier((before, behind, *sent))
            blocks += [before, behind]
        left = lax.ppermute(before[:, :half], "tp", forth)
        right = lax.ppermute(behind[:, half:], "tp", back)
        if rows % 16:
            blocks = [jnp.concatenate(blocks, axis=0)]
        prev = project(place, blocks, left, right, w_query, w_keyval, prev, (cosine, sine_part), chunk)
    queries, keyval = prev

    chunks = [
        [
            lax.ppermute(sent[slot * middle + j], "tp", [(i, i ^ j) for i in range(tp_size)])
            if j
            else sent[slot * middle]
            for j in range(middle)
        ]
        for slot in range(2)
    ]
    across = [(i, i ^ middle) for i in range(tp_size)]
    their_queries = lax.ppermute(queries, "tp", across)

    offsets = jnp.cumsum(lengths) - lengths
    first_slot = (me ^ order) * tokens
    slot_tokens = first_slot[:, None] + jnp.arange(tokens, dtype=jnp.int32)[None, :]
    cache_pos = offsets[:, None, None] + slot_tokens[None]
    is_valid = slot_tokens[None] < lengths[:, None, None]
    replaced = jnp.any(cache_pos[..., None] == selected, axis=-1)
    dead = jnp.where(is_valid & jnp.logical_not(replaced), 0.0, MASKED).astype(jnp.bfloat16)
    dead = jnp.broadcast_to(dead[..., None], (DOCS, middle, tokens, HD))
    dead = dead.reshape(DOCS, middle * tokens, HD)
    first_pos = jnp.where(
        first_slot[None] < lengths[:, None], offsets[:, None] + first_slot[None], FAR
    ).reshape(-1)

    keyval = keyval.astype(jnp.bfloat16)
    if tp_size == KVH:
        is_key = me < middle
        first, second = keyval[:, :HD], keyval[:, HD:]
        one = lax.ppermute(
            jnp.where(is_key, first, second),
            "tp",
            [(i, 2 * i if i < middle else 2 * (i - middle) + 1) for i in range(tp_size)],
        )
        two = lax.ppermute(
            jnp.where(is_key, second, first),
            "tp",
            [(i, 2 * i + 1 if i < middle else 2 * (i - middle)) for i in range(tp_size)],
        )
        even = me % 2 == 0
        new_k, new_v = jnp.where(even, one, two), jnp.where(even, two, one)
    else:
        everyone = lax.all_gather(keyval, "tp", axis=1, tiled=True)
        my_head = me * KVH // tp_size
        new_k = lax.dynamic_slice_in_dim(everyone, my_head * HD, HD, axis=1)
        new_v = lax.dynamic_slice_in_dim(everyone, (KVH + my_head) * HD, HD, axis=1)

    mine = attend(
        chunks[0], dead, first_pos, selected, queries, [cosine, sine_part, new_k, new_v]
    )
    top, total, mixed = attend(chunks[1], dead, first_pos, selected, their_queries, [])
    stats = lax.ppermute(jnp.concatenate([top, total], axis=1), "tp", across)
    mixed = lax.ppermute(mixed, "tp", across)
    attention = merge(mine, (stats[:, :1], stats[:, 1:], mixed))

    finished = []
    for chunk in range(REDUCE_CHUNKS):
        pieces = project_out(place, attention, w_out, chunk, REDUCE_CHUNKS, tp_size)
        total = pieces[0]
        to_forth, to_back = pieces[2 : tp_size - 1 : 2], pieces[1 : tp_size - 1 : 2]
        cut = pieces[-1].shape[1]
        ahead = lax.ppermute(pieces[-2], "tp", forth).astype(jnp.float32)
        astern = lax.ppermute(pieces[-1], "tp", back).astype(jnp.float32)
        for k in range(far - 1, 0, -1):
            up, down = to_forth[k - 1], to_back[k - 1]
            if k == far - 1:
                up = jnp.concatenate([up[:, :cut] + ahead, up[:, cut:]], axis=1)
                down = jnp.concatenate([down[:, :cut], down[:, cut:] + astern], axis=1)
            else:
                up, down = up + ahead, down + astern
            ahead = lax.ppermute(up.astype(jnp.bfloat16), "tp", forth).astype(jnp.float32)
            astern = lax.ppermute(down.astype(jnp.bfloat16), "tp", back).astype(jnp.float32)
        finished.append((total + ahead + astern).astype(jnp.bfloat16))
    return jnp.concatenate(finished, axis=1)


def solution(mesh):
    placed = (
        P(("groups", "req", "tp"), None),
        P(),
        P(None, "tp"),
        P(None, "tp"),
        P("tp", None),
        P(("groups", "req"), "tp", None, None),
        P(("groups", "req")),
        P(("groups", "req"), None),
        P(("groups", "req"), None),
    )
    return jax.shard_map(
        per_device,
        mesh=mesh,
        in_specs=placed,
        out_specs=P(("groups", "req", "tp"), None),
        check_vma=False,
    )
```

```python
import functools
import math

import jax
import jax.numpy as jnp
from jax import lax
from jax.experimental import pallas as pl
from jax.experimental.pallas import tpu as pltpu
from jax.sharding import PartitionSpec as P

HEADS = 64
KVH = 8
HD = 128
DOCS = 4
BLOCK = 128
SEL = 256


EPSILON = 1e-05
ROPE_BASE = 500000.0
MASKED = -1e30
FAR = 1 << 30
REDUCE_CHUNKS = 2
TILE_COLS = 256
PAIR = 2
STATS = 16
HALVES = 2
DEPTH_TILE = 1024
WIDTH_TILE = 512
SLOTS = 3

QUICK = pl.CostEstimate(flops=1, bytes_accessed=1, transcendentals=0)


def rotation_tables(positions):
    half_dim = HD // 2
    inverse = ROPE_BASE ** (-(jnp.arange(half_dim, dtype=jnp.float32) * (2.0 / HD)))
    angles = positions.astype(jnp.float32)[:, None] * inverse[None, :]
    cosine = jnp.cos(angles)
    sine_part = jnp.sin(angles)
    return (
        jnp.concatenate([cosine, cosine], axis=-1),
        jnp.concatenate([-sine_part, sine_part], axis=-1),
    )


def rotate(values, cosine, sine_part):
    swapped = jnp.concatenate([values[:, HD // 2 :], values[:, : HD // 2]], axis=-1)
    return values * cosine + swapped * sine_part


def megabytes(count):
    return pltpu.CompilerParams(vmem_limit_bytes=count * 1024 * 1024)


def stream(sources, slots, sems, count):
    def copies(step):
        slot = lax.rem(step, SLOTS)
        return [
            pltpu.make_async_copy(source(step), buffer.at[slot], sems.at[i, slot])
            for i, (source, buffer) in enumerate(zip(sources, slots))
        ]

    def start(step):
        for copy in copies(step):
            copy.start()

    def wait(step):
        for copy in copies(step):
            copy.wait()

    return start, wait


def project_kernel(n_blocks, place_ref, *refs):
    blocks = refs[:n_blocks]
    left_ref, right_ref, wq_ref, wkv_ref, cos_ref, sin_ref = refs[n_blocks : n_blocks + 6]
    out_q = refs[n_blocks + 6 : n_blocks + 6 + HALVES]
    *out_kv, total_q, total_kv, natural, natural_kv, wq_slots, wkv_slots, sems = refs[
        n_blocks + 6 + HALVES :
    ]
    depth = wq_ref.shape[0]
    tile = wq_slots.shape[1]
    count = depth // tile
    rows_of = lambda ref: lambda step: ref.at[pl.ds(pl.multiple_of(step * tile, tile), tile), :]
    start, wait = stream([rows_of(wq_ref), rows_of(wkv_ref)], [wq_slots, wkv_slots], sems, count)

    for step in range(SLOTS - 1):
        start(step)
    total_q[...] = jnp.zeros_like(total_q)
    total_kv[...] = jnp.zeros_like(total_kv)
    for side, far_ref in enumerate((left_ref, right_ref)):
        offset = side * count // 2

        @pl.loop(offset, offset + count // 2)
        def _(step):
            @pl.when(step + SLOTS - 1 < count)
            def _():
                start(step + SLOTS - 1)

            wait(step)
            slot = lax.rem(step, SLOTS)
            cols = pl.ds(pl.multiple_of(step * tile, tile), tile)
            far_cols = pl.ds(pl.multiple_of((step - offset) * tile, tile), tile)
            rows = jnp.concatenate([b[:, cols] for b in blocks] + [far_ref[:, far_cols]], axis=0)
            total_q[...] += jnp.dot(rows, wq_slots[slot], preferred_element_type=jnp.float32)
            total_kv[...] += jnp.dot(rows, wkv_slots[slot], preferred_element_type=jnp.float32)

    height = left_ref.shape[0]
    for block in range(SEL // height):
        here = slice(block * height, (block + 1) * height)
        there = pl.ds(pl.multiple_of(place_ref[block] * height, height), height)
        natural[there, :] = total_q[here, :]
        natural_kv[there, :] = total_kv[here, :]
    heads_here = total_q.shape[1] // HD
    tile_q = TILE_COLS // heads_here
    per_half = SEL // tile_q // HALVES
    for index in range(SEL // tile_q):
        here = slice(index * tile_q, (index + 1) * tile_q)
        stacked = jnp.concatenate(
            [
                rotate(natural[here, head * HD : (head + 1) * HD], cos_ref[here, :], sin_ref[here, :])
                for head in range(heads_here)
            ],
            axis=0,
        )
        out_q[index // per_half][index % per_half] = stacked.T.astype(jnp.bfloat16)
    if out_kv:
        out_kv[0][...] = natural_kv[...].astype(jnp.bfloat16)
    else:
        for index in range(SEL // HD):
            out_q[-1][per_half + index] = natural_kv[
                index * HD : (index + 1) * HD, :
            ].astype(jnp.bfloat16)


def project(place, blocks, left, right, w_query, w_keyval, tables):
    depth, q_cols = w_query.shape
    kv_cols = w_keyval.shape[1]
    tile = min(DEPTH_TILE, depth // 2)
    vmem = pl.BlockSpec(memory_space=pltpu.VMEM)
    hbm = pl.BlockSpec(memory_space=pltpu.HBM)
    per_half = SEL * q_cols // (HD * TILE_COLS * HALVES)
    behind = SEL // HD if kv_cols == TILE_COLS else 0
    outs = [(per_half, HD, TILE_COLS)] * (HALVES - 1) + [(per_half + behind, HD, TILE_COLS)]
    if not behind:
        outs.append((SEL, kv_cols))
    return pl.pallas_call(
        functools.partial(project_kernel, len(blocks)),
        in_specs=[pl.BlockSpec(memory_space=pltpu.SMEM)]
        + [vmem] * (len(blocks) + 2)
        + [hbm] * 2
        + [vmem] * 2,
        out_specs=[vmem] * len(outs),
        out_shape=[jax.ShapeDtypeStruct(shape, jnp.bfloat16) for shape in outs],
        scratch_shapes=[
            pltpu.VMEM((SEL, q_cols), jnp.float32),
            pltpu.VMEM((SEL, kv_cols), jnp.float32),
            pltpu.VMEM((SEL, q_cols), jnp.float32),
            pltpu.VMEM((SEL, kv_cols), jnp.float32),
            pltpu.VMEM((SLOTS, tile, q_cols), jnp.bfloat16),
            pltpu.VMEM((SLOTS, tile, kv_cols), jnp.bfloat16),
            pltpu.SemaphoreType.DMA((2, SLOTS)),
        ],
        compiler_params=megabytes(32),
        cost_estimate=QUICK,
        name="project",
    )(place, *blocks, left, right, w_query, w_keyval, *tables)


def select_kernel(n_dest, n_src, place_ref, slot_ref, head_ref, *refs):
    sources = refs[:n_src]
    outs = refs[n_src : n_src + n_dest]
    held, sems, out_sems = refs[n_src + n_dest :]
    for doc in range(DOCS):
        for src in range(n_src):

            @pl.when(place_ref[doc] == src)
            def _():
                for dest in range(n_dest):
                    cols = pl.ds(pl.multiple_of(head_ref[dest] * HD, HD), HD)
                    pltpu.make_async_copy(
                        sources[src].at[slot_ref[doc], :, :, cols],
                        held.at[dest, :, doc],
                        sems.at[dest, doc],
                    ).start()

    for dest in range(n_dest):
        for doc in range(DOCS):
            pltpu.make_async_copy(
                sources[0].at[0, :, :, 0:HD], held.at[dest, :, doc], sems.at[dest, doc]
            ).wait()
        pltpu.make_async_copy(held.at[dest], outs[dest], out_sems.at[dest]).start()
    for dest in range(n_dest):
        pltpu.make_async_copy(held.at[dest], outs[dest], out_sems.at[dest]).wait()


def select_docs(sources, place, slot, heads, n_dest):
    tokens = sources[0].shape[2]
    shape = (2, DOCS, tokens, HD)
    smem = pl.BlockSpec(memory_space=pltpu.SMEM)
    return pl.pallas_call(
        functools.partial(select_kernel, n_dest, len(sources)),
        in_specs=[smem] * 3 + [pl.BlockSpec(memory_space=pl.ANY)] * len(sources),
        out_specs=[pl.BlockSpec(memory_space=pltpu.HBM)] * n_dest,
        out_shape=[jax.ShapeDtypeStruct(shape, jnp.bfloat16)] * n_dest,
        scratch_shapes=[
            pltpu.VMEM((n_dest, *shape), jnp.bfloat16),
            pltpu.SemaphoreType.DMA((n_dest, DOCS)),
            pltpu.SemaphoreType.DMA((n_dest,)),
        ],
        compiler_params=megabytes(16),
        cost_estimate=QUICK,
        name="select_docs",
    )(place, slot, heads, *sources)


def split_exact(value):
    pieces = []
    for _ in range(3):
        pieces.append(value.astype(jnp.bfloat16).astype(jnp.float32))
        value = value - pieces[-1]
    return pieces


def attend_kernel(n_chunks, with_new, tile_q, first_token, first_ref, qmin_ref, qmax_ref, *refs):
    refs = list(refs)
    take = lambda count: [refs.pop(0) for _ in range(count)]
    chunks = take(n_chunks)
    dead_ref, qpos_ref, queries = take(3)
    if with_new:
        cos_ref, sin_ref, new_ref = take(3)
    if with_new:
        top, total, summed, values, new_key, new_value = take(6)
    else:
        packed, top, total, summed, values = take(5)
    together = min(PAIR, qpos_ref.shape[0])
    n_pairs = qpos_ref.shape[0] // together
    tokens = chunks[0].shape[2]
    scale = math.log2(math.e) / math.sqrt(HD)

    for chunk in range(n_chunks):
        for doc in range(DOCS):
            values[doc, :, chunk * tokens : (chunk + 1) * tokens] = chunks[chunk][1, doc].T
    if with_new:
        new_key[...] = rotate(
            new_ref[:, :HD].astype(jnp.float32), cos_ref[...], sin_ref[...]
        ).astype(jnp.bfloat16)
        new_value[...] = new_ref[:, HD:].T

    one_row = jnp.where(
        lax.broadcasted_iota(jnp.int32, (HD, TILE_COLS), 0) == 0, 1.0, 0.0
    ).astype(jnp.bfloat16)

    def update(tile, parts):
        best = functools.reduce(
            jnp.maximum, [jnp.max(scores, axis=0, keepdims=True) for scores, _ in parts]
        )
        old = top[tile]
        new = jnp.maximum(old, best)
        shrink = jnp.exp2((old - new) * scale)
        running = total[tile] * shrink
        mixed = summed[tile] * shrink
        for scores, value in parts:
            weights = jnp.exp2((scores - new) * scale)
            running += jnp.sum(weights, axis=0, keepdims=True)
            mixed += jnp.dot(
                value, weights.astype(jnp.bfloat16), preferred_element_type=jnp.float32
            )
        top[tile] = new
        total[tile] = running
        summed[tile] = mixed

    @pl.loop(0, n_pairs)
    def _(pair):
        tiles = [pair * together + i for i in range(together)]
        for tile in tiles:
            top[tile] = jnp.full(top.shape[1:], MASKED, jnp.float32)
            total[tile] = jnp.zeros(total.shape[1:], jnp.float32)
            summed[tile] = jnp.zeros(summed.shape[1:], jnp.float32)
        if with_new:
            fresh = []
            for tile in tiles:
                scores = jnp.dot(new_key[...], queries[tile], preferred_element_type=jnp.float32)
                key_index = lax.broadcasted_iota(jnp.int32, scores.shape, 0)
                q_index = first_token + tile * tile_q + lax.broadcasted_iota(jnp.int32, scores.shape, 1) % tile_q
                fresh.append(jnp.where(key_index <= q_index, scores, MASKED))
            for tile, scores in zip(tiles, fresh):
                update(tile, [(scores, new_value[...])])

        @pl.loop(0, DOCS)
        def _(doc):
            firsts = [first_ref[doc * n_chunks + chunk] for chunk in range(n_chunks)]
            lowest = functools.reduce(jnp.minimum, firsts)
            reach = functools.reduce(jnp.maximum, firsts) + tokens - 1

            def visit(masked):
                found = []
                for tile in tiles:
                    extended = jnp.concatenate([queries[tile], one_row], axis=0)
                    parts = []
                    for chunk in range(n_chunks):
                        span = slice(chunk * tokens, (chunk + 1) * tokens)
                        keys = jnp.concatenate(
                            [chunks[chunk][0, doc], dead_ref[doc, span, :]], axis=1
                        )
                        scores = jnp.dot(keys, extended, preferred_element_type=jnp.float32)
                        if masked:
                            key_pos = firsts[chunk] + lax.broadcasted_iota(
                                jnp.int32, scores.shape, 0
                            )
                            scores = jnp.where(key_pos <= qpos_ref[tile], scores, MASKED)
                        parts.append((scores, values[doc, :, span]))
                    found.append(parts)
                for tile, parts in zip(tiles, found):
                    update(tile, parts)

            live = lowest <= qmax_ref[pair]
            whole = reach <= qmin_ref[pair]

            @pl.when(live & whole)
            def _():
                visit(False)

            @pl.when(live & jnp.logical_not(whole))
            def _():
                visit(True)

        if not with_new:
            for tile in tiles:
                extra = jnp.concatenate(
                    split_exact(top[tile])
                    + split_exact(total[tile])
                    + [jnp.zeros((STATS - 6, TILE_COLS), jnp.float32)],
                    axis=0,
                )
                packed[tile] = jnp.concatenate([summed[tile], extra], axis=0).astype(jnp.bfloat16)


def attend(chunks, dead, first_pos, positions, first_token, queries, n_tiles, fresh):
    n_chunks = len(chunks)
    tokens = chunks[0].shape[2]
    tile_q = positions.shape[0] // n_tiles
    together = min(PAIR, n_tiles)
    by_pair = positions.reshape(n_tiles // together, together * tile_q)
    q_pos = jnp.tile(positions.reshape(n_tiles, tile_q), (1, TILE_COLS // tile_q))
    q_pos = q_pos.reshape(n_tiles, 1, TILE_COLS)
    smem = pl.BlockSpec(memory_space=pltpu.SMEM)
    vmem = pl.BlockSpec(memory_space=pltpu.VMEM)
    operands = [first_pos, by_pair[:, 0], by_pair[:, -1], *chunks, dead, q_pos, queries, *fresh]
    state = [((n_tiles, 1, TILE_COLS), jnp.float32)] * 2
    state += [((n_tiles, HD, TILE_COLS), jnp.float32)]
    values = ((DOCS, HD, n_chunks * tokens), jnp.bfloat16)
    if fresh:
        outs = state
        scratch = [values, ((SEL, HD), jnp.bfloat16), ((HD, SEL), jnp.bfloat16)]
    else:
        outs = [((n_tiles, HD + STATS, TILE_COLS), jnp.bfloat16)]
        scratch = state + [values]
    pairs = n_tiles * TILE_COLS * DOCS * n_chunks * tokens // 2
    return pl.pallas_call(
        functools.partial(attend_kernel, n_chunks, bool(fresh), tile_q, first_token),
        in_specs=[smem] * 3 + [vmem] * (len(operands) - 3),
        out_specs=[vmem] * len(outs),
        out_shape=[jax.ShapeDtypeStruct(*s) for s in outs],
        scratch_shapes=[pltpu.VMEM(*s) for s in scratch],
        compiler_params=megabytes(20),
        cost_estimate=QUICK,
        name="attend",
    )(*operands)


def merge_kernel(*refs):
    out_ref = refs[-1]
    scale = math.log2(math.e) / math.sqrt(HD)
    for half in range(HALVES):
        top_a, total_a, mixed_a, packed = refs[4 * half : 4 * half + 4]
        n_tiles = top_a.shape[0]
        tile_q = SEL // HALVES // n_tiles
        for tile in range(n_tiles):
            extra = packed[tile, HD:, :].astype(jnp.float32)
            top_b = extra[0:1] + (extra[1:2] + extra[2:3])
            total_b = extra[3:4] + (extra[4:5] + extra[5:6])
            new = jnp.maximum(top_a[tile], top_b)
            part_a = jnp.exp2((top_a[tile] - new) * scale)
            part_b = jnp.exp2((top_b - new) * scale)
            total = total_a[tile] * part_a + total_b * part_b
            mixed = mixed_a[tile] * part_a + packed[tile, :HD, :].astype(jnp.float32) * part_b
            finished = (mixed / total).T.astype(jnp.bfloat16)
            here = slice((half * n_tiles + tile) * tile_q, (half * n_tiles + tile + 1) * tile_q)
            for head in range(TILE_COLS // tile_q):
                out_ref[here, head * HD : (head + 1) * HD] = finished[
                    head * tile_q : (head + 1) * tile_q, :
                ]


def merge(mine, theirs):
    n_tiles = mine[0][0].shape[0] * HALVES
    shape = (SEL, TILE_COLS * n_tiles // SEL * HD)
    operands = [a for state, packed in zip(mine, theirs) for a in (*state, packed)]
    return pl.pallas_call(
        merge_kernel,
        out_shape=jax.ShapeDtypeStruct(shape, jnp.bfloat16),
        compiler_params=megabytes(16),
        cost_estimate=QUICK,
        name="merge",
    )(*operands)


def out_kernel(n_blocks, first_col, place_ref, x_ref, w_ref, *refs):
    outs = refs[: n_blocks + 1]
    ordered, slots, sems = refs[n_blocks + 1 :]
    rows = SEL // n_blocks
    tile = slots.shape[2]
    width = outs[0].shape[1]
    count = width // tile
    source = lambda step: w_ref.at[:, pl.ds(pl.multiple_of(first_col + step * tile, tile), tile)]
    start, wait = stream([source], [slots], sems, count)

    for step in range(SLOTS - 1):
        start(step)
    for block in range(n_blocks):
        there = pl.ds(pl.multiple_of(place_ref[block] * rows, rows), rows)
        ordered[block * rows : (block + 1) * rows, :] = x_ref[there, :]
    for side in range(2):
        offset = side * count // 2

        @pl.loop(offset, offset + count // 2)
        def _(step):
            @pl.when(step + SLOTS - 1 < count)
            def _():
                start(step + SLOTS - 1)

            wait(step)
            product = jnp.dot(
                ordered[...].astype(jnp.bfloat16),
                slots[lax.rem(step, SLOTS)],
                preferred_element_type=jnp.float32,
            )
            cols = pl.ds(pl.multiple_of(step * tile, tile), tile)
            far_cols = pl.ds(pl.multiple_of((step - offset) * tile, tile), tile)
            for block in range(n_blocks - 1):
                outs[block][:, cols] = product[block * rows : (block + 1) * rows, :]
            outs[n_blocks - 1 + side][:, far_cols] = product[(n_blocks - 1) * rows :, :].astype(
                jnp.bfloat16
            )


def project_out(place, attention, w_out, chunk, n_chunks, n_blocks):
    depth = w_out.shape[0]
    width = w_out.shape[1] // n_chunks
    rows = SEL // n_blocks
    if rows % 16:
        attention = attention.astype(jnp.float32)
    vmem = pl.BlockSpec(memory_space=pltpu.VMEM)
    return pl.pallas_call(
        functools.partial(out_kernel, n_blocks, chunk * width),
        in_specs=[
            pl.BlockSpec(memory_space=pltpu.SMEM),
            vmem,
            pl.BlockSpec(memory_space=pltpu.HBM),
        ],
        out_specs=[vmem] * (n_blocks + 1),
        out_shape=[jax.ShapeDtypeStruct((rows, width), jnp.float32)] * (n_blocks - 1)
        + [jax.ShapeDtypeStruct((rows, width // 2), jnp.bfloat16)] * 2,
        scratch_shapes=[
            pltpu.VMEM((SEL, depth), attention.dtype),
            pltpu.VMEM((SLOTS, depth, WIDTH_TILE), jnp.bfloat16),
            pltpu.SemaphoreType.DMA((1, SLOTS)),
        ],
        compiler_params=megabytes(50),
        cost_estimate=QUICK,
        name="project_out",
    )(place, attention, w_out)


def per_device(
    hidden_in, norm_gain, w_query, w_keyval, w_out, pool_cache, doc_slot, doc_blocks, sel_pos
):
    tp_size = lax.axis_size("tp")
    req_size = lax.axis_size("req")
    me = lax.axis_index("tp")
    rows, width = hidden_in.shape
    slots, tokens = pool_cache.shape[:2]
    heads_here = w_query.shape[1] // HD
    selected = sel_pos[0]
    lengths = doc_blocks[0] * BLOCK

    if tp_size == KVH:
        ring = [*range(0, tp_size, 2), *range(tp_size - 1, 0, -2)]
    else:
        ring = list(range(tp_size))
    far = tp_size // 2
    forth = [(ring[p], ring[(p + 1) % tp_size]) for p in range(tp_size)]
    back = [(dst, src) for src, dst in forth]
    steps = [0] + [sign * k for k in range(1, far) for sign in (-1, 1)] + [far]
    table = [[ring[(ring.index(i) + s) % tp_size] for s in steps] for i in range(tp_size)]
    place = jnp.array(table, jnp.int32)[me]

    widened = hidden_in.astype(jnp.float32)
    normed = (
        widened
        * lax.rsqrt(jnp.mean(widened * widened, axis=-1, keepdims=True) + EPSILON)
        * norm_gain
    ).astype(jnp.bfloat16)
    normed, pool_cache = lax.optimization_barrier((normed, pool_cache))

    middle = tp_size // 2
    by_kind = pool_cache.transpose(0, 2, 1, 3)
    sources = [by_kind]
    for shift in range(1, req_size):
        sources.append(
            lax.ppermute(by_kind, "req", [((i + shift) % req_size, i) for i in range(req_size)])
        )
    holder = (doc_slot // slots - lax.axis_index("req")) % req_size
    order = jnp.arange(middle, dtype=jnp.int32)
    takers = jnp.concatenate([me ^ order, me ^ order ^ middle])
    sent = select_docs(sources, holder, doc_slot % slots, takers * KVH // tp_size, tp_size)

    cosine, sine_part = rotation_tables(selected)
    before = behind = normed
    blocks = [normed]
    for k in range(1, far):
        before = lax.ppermute(before, "tp", forth)
        behind = lax.ppermute(behind, "tp", back)
        if k == min(2, far - 1):
            before, behind, *sent = lax.optimization_barrier((before, behind, *sent))
        blocks += [before, behind]
    left = lax.ppermute(before[:, : width // 2], "tp", forth)
    right = lax.ppermute(behind[:, width // 2 :], "tp", back)
    if rows % 16:
        blocks = [jnp.concatenate(blocks, axis=0)]
    projected = project(place, blocks, left, right, w_query, w_keyval, (cosine, sine_part))
    chunks = [
        [
            lax.ppermute(sent[slot * middle + j], "tp", [(i, i ^ j) for i in range(tp_size)])
            if j
            else sent[slot * middle]
            for j in range(middle)
        ]
        for slot in range(2)
    ]
    *queries, chunks[1] = lax.optimization_barrier((*projected[:HALVES], chunks[1]))
    n_tiles = queries[0].shape[0]
    across = [(i, i ^ middle) for i in range(tp_size)]
    their_queries = [None] * HALVES
    for part in reversed(range(HALVES)):
        their_queries[part] = lax.ppermute(queries[part], "tp", across)

    offsets = jnp.cumsum(lengths) - lengths
    first_slot = (me ^ order) * tokens
    slot_tokens = first_slot[:, None] + jnp.arange(tokens, dtype=jnp.int32)[None, :]
    cache_pos = offsets[:, None, None] + slot_tokens[None]
    is_valid = slot_tokens[None] < lengths[:, None, None]
    replaced = jnp.any(cache_pos[..., None] == selected, axis=-1)
    dead = jnp.where(is_valid & jnp.logical_not(replaced), 0.0, MASKED).astype(jnp.bfloat16)
    dead = jnp.broadcast_to(dead[..., None], (DOCS, middle, tokens, HD))
    dead = dead.reshape(DOCS, middle * tokens, HD)
    first_pos = jnp.where(
        first_slot[None] < lengths[:, None], offsets[:, None] + first_slot[None], FAR
    ).reshape(-1)

    if tp_size == KVH:
        is_key = me < middle
        here = queries[-1][n_tiles:].reshape(SEL, 2 * HD)
        there = their_queries[-1][n_tiles:].reshape(SEL, 2 * HD)
        keys, vals = jnp.where(is_key, here, there), jnp.where(is_key, there, here)
        new = lax.ppermute(
            jnp.concatenate(
                [
                    jnp.where(is_key, keys[:, :HD], keys[:, HD:]),
                    jnp.where(is_key, vals[:, :HD], vals[:, HD:]),
                ],
                axis=1,
            ),
            "tp",
            [(i, 2 * i if i < middle else 2 * (i - middle) + 1) for i in range(tp_size)],
        )
    else:
        everyone = lax.all_gather(projected[-1], "tp", axis=1, tiled=True)
        my_head = me * KVH // tp_size
        new = jnp.concatenate(
            [
                lax.dynamic_slice_in_dim(everyone, (kind * KVH + my_head) * HD, HD, axis=1)
                for kind in range(2)
            ],
            axis=1,
        )

    size = SEL // HALVES

    def attend_half(part, asked, slot, extra):
        span = slice(part * size, (part + 1) * size)
        return attend(
            chunks[slot], dead, first_pos, selected[span], part * size, asked[part], n_tiles, extra
        )

    theirs = [None] * HALVES
    for part in reversed(range(HALVES)):
        (packed,) = attend_half(part, their_queries, 1, [])
        if part:
            packed, new, their_queries[part - 1] = lax.optimization_barrier(
                (packed, new, their_queries[part - 1])
            )
        theirs[part] = lax.ppermute(packed, "tp", across)
    fresh = [cosine, sine_part, new]
    mine = [attend_half(part, queries, 0, fresh) for part in range(HALVES)]
    attention = merge(mine, theirs)

    finished = []
    for chunk in range(REDUCE_CHUNKS):
        pieces = project_out(place, attention, w_out, chunk, REDUCE_CHUNKS, tp_size)
        total = pieces[0]
        to_forth, to_back = pieces[2 : tp_size - 1 : 2], pieces[1 : tp_size - 1 : 2]
        cut = pieces[-1].shape[1]
        ahead = lax.ppermute(pieces[-2], "tp", forth).astype(jnp.float32)
        astern = lax.ppermute(pieces[-1], "tp", back).astype(jnp.float32)
        for k in range(far - 1, 0, -1):
            up, down = to_forth[k - 1], to_back[k - 1]
            if k == far - 1:
                up = jnp.concatenate([up[:, :cut] + ahead, up[:, cut:]], axis=1)
                down = jnp.concatenate([down[:, :cut], down[:, cut:] + astern], axis=1)
            else:
                up, down = up + ahead, down + astern
            ahead = lax.ppermute(up.astype(jnp.bfloat16), "tp", forth).astype(jnp.float32)
            astern = lax.ppermute(down.astype(jnp.bfloat16), "tp", back).astype(jnp.float32)
        finished.append((total + ahead + astern).astype(jnp.bfloat16))
    return jnp.concatenate(finished, axis=1)


def solution(mesh):
    placed = (
        P(("groups", "req", "tp"), None),
        P(),
        P(None, "tp"),
        P(None, "tp"),
        P("tp", None),
        P(("groups", "req"), "tp", None, None),
        P(("groups", "req")),
        P(("groups", "req"), None),
        P(("groups", "req"), None),
    )
    return jax.shard_map(
        per_device,
        mesh=mesh,
        in_specs=placed,
        out_specs=P(("groups", "req", "tp"), None),
        check_vma=False,
    )
```

```python
import functools
import math

import jax
import jax.numpy as jnp
from jax import lax
from jax.experimental import pallas as pl
from jax.experimental.pallas import tpu as pltpu
from jax.sharding import PartitionSpec as P

HEADS = 64
KVH = 8
HD = 128
DOCS = 4
BLOCK = 128
SEL = 256


EPSILON = 1e-05
ROPE_BASE = 500000.0
MASKED = -1e30
FAR = 1 << 30
CHUNKS = 2
TILE_COLS = 256
PAIR = 2
STATS = 16
HALVES = 2
DEPTH_TILE = 1024
WIDTH_TILE = 1024
SLOTS = 3


def cost(flops, bytes_accessed, transcendentals=0):
    return pl.CostEstimate(
        flops=int(flops), bytes_accessed=int(bytes_accessed), transcendentals=int(transcendentals)
    )


def rotation_tables(positions):
    half_dim = HD // 2
    inverse = ROPE_BASE ** (-(jnp.arange(half_dim, dtype=jnp.float32) * (2.0 / HD)))
    angles = positions.astype(jnp.float32)[:, None] * inverse[None, :]
    cosine = jnp.cos(angles)
    sine_part = jnp.sin(angles)
    return (
        jnp.concatenate([cosine, cosine], axis=-1),
        jnp.concatenate([-sine_part, sine_part], axis=-1),
    )


def rotate(values, cosine, sine_part):
    swapped = jnp.concatenate([values[:, HD // 2 :], values[:, : HD // 2]], axis=-1)
    return values * cosine + swapped * sine_part


def megabytes(count):
    return pltpu.CompilerParams(vmem_limit_bytes=count * 1024 * 1024)


def stream(sources, buffers, sems):
    def copies(step):
        slot = step % SLOTS
        return [
            pltpu.make_async_copy(source(step), buffer.at[slot], sems.at[i, slot])
            for i, (source, buffer) in enumerate(zip(sources, buffers))
        ]

    def start(step):
        for copy in copies(step):
            copy.start()

    def wait(step):
        for copy in copies(step):
            copy.wait()

    return start, wait


def project_kernel(n_blocks, chunk, is_last, place_ref, *refs):
    refs = list(refs)
    take = lambda count: [refs.pop(0) for _ in range(count)]
    blocks = take(n_blocks)
    wq_ref, wkv_ref = take(2)
    if chunk:
        prev_q, prev_kv = take(2)
    if is_last:
        cos_ref, sin_ref = take(2)
        total_q, total_kv, natural, natural_kv = refs[-7:-3]
        outs = refs[:-7]
    else:
        total_q, total_kv = take(2)
    wq_slots, wkv_slots, sems = refs[-3:]
    tile = wq_slots.shape[1]
    depth = blocks[0].shape[1]
    count = depth // tile
    rows_of = lambda ref: lambda step: ref.at[pl.ds(chunk * depth + step * tile, tile), :]
    start, wait = stream([rows_of(wq_ref), rows_of(wkv_ref)], [wq_slots, wkv_slots], sems)

    for step in range(min(SLOTS, count)):
        start(step)
    for step in range(count):
        wait(step)
        slot = step % SLOTS
        cols = slice(step * tile, (step + 1) * tile)
        rows = jnp.concatenate([b[:, cols] for b in blocks], axis=0)
        part_q = jnp.dot(rows, wq_slots[slot], preferred_element_type=jnp.float32)
        part_kv = jnp.dot(rows, wkv_slots[slot], preferred_element_type=jnp.float32)
        if step:
            total_q[...] += part_q
            total_kv[...] += part_kv
        elif chunk:
            total_q[...] = prev_q[...] + part_q
            total_kv[...] = prev_kv[...] + part_kv
        else:
            total_q[...] = part_q
            total_kv[...] = part_kv
        if step + SLOTS < count:
            start(step + SLOTS)

    if is_last:
        height = SEL // place_ref.shape[0]
        for block in range(SEL // height):
            here = slice(block * height, (block + 1) * height)
            there = pl.ds(pl.multiple_of(place_ref[block] * height, height), height)
            natural[there, :] = total_q[here, :]
            natural_kv[there, :] = total_kv[here, :]
        heads_here = total_q.shape[1] // HD
        tile_q = TILE_COLS // heads_here
        per_half = SEL // tile_q // HALVES
        for index in range(SEL // tile_q):
            here = slice(index * tile_q, (index + 1) * tile_q)
            stacked = jnp.concatenate(
                [
                    rotate(
                        natural[here, head * HD : (head + 1) * HD], cos_ref[here, :], sin_ref[here, :]
                    )
                    for head in range(heads_here)
                ],
                axis=0,
            )
            outs[index // per_half][index % per_half] = stacked.T.astype(jnp.bfloat16)
        if len(outs) > HALVES:
            outs[-1][...] = natural_kv[...].astype(jnp.bfloat16)
        else:
            for index in range(SEL // HD):
                outs[-1][per_half + index] = natural_kv[
                    index * HD : (index + 1) * HD, :
                ].astype(jnp.bfloat16)


def project(place, blocks, w_query, w_keyval, prev, tables, chunk):
    depth = blocks[0].shape[1]
    q_cols, kv_cols = w_query.shape[1], w_keyval.shape[1]
    tile = min(DEPTH_TILE, depth)
    is_last = chunk + 1 == CHUNKS
    vmem = pl.BlockSpec(memory_space=pltpu.VMEM)
    hbm = pl.BlockSpec(memory_space=pltpu.HBM)
    total = [((SEL, q_cols), jnp.float32), ((SEL, kv_cols), jnp.float32)]
    scratch = []
    if is_last:
        per_half = SEL * q_cols // (HD * TILE_COLS * HALVES)
        behind = SEL // HD if kv_cols == TILE_COLS else 0
        outs = [(per_half, HD, TILE_COLS)] * (HALVES - 1) + [(per_half + behind, HD, TILE_COLS)]
        if not behind:
            outs.append((SEL, kv_cols))
        outs = [(shape, jnp.bfloat16) for shape in outs]
        scratch = total + total
    else:
        outs = total
    extra = ([] if prev is None else list(prev)) + (list(tables) if is_last else [])
    return pl.pallas_call(
        functools.partial(project_kernel, len(blocks), chunk, is_last),
        in_specs=[pl.BlockSpec(memory_space=pltpu.SMEM)]
        + [vmem] * len(blocks)
        + [hbm] * 2
        + [vmem] * len(extra),
        out_specs=[vmem] * len(outs),
        out_shape=[jax.ShapeDtypeStruct(*o) for o in outs],
        scratch_shapes=[pltpu.VMEM(*x) for x in scratch]
        + [
            pltpu.VMEM((SLOTS, tile, q_cols), jnp.bfloat16),
            pltpu.VMEM((SLOTS, tile, kv_cols), jnp.bfloat16),
            pltpu.SemaphoreType.DMA((2, SLOTS)),
        ],
        compiler_params=megabytes(16),
        cost_estimate=cost(
            2 * SEL * depth * (q_cols + kv_cols), 2 * depth * (q_cols + kv_cols + SEL)
        ),
        name="project",
    )(place, *blocks, w_query, w_keyval, *extra)


def select_kernel(n_dest, n_src, place_ref, slot_ref, head_ref, *refs):
    sources = refs[:n_src]
    outs = refs[n_src : n_src + n_dest]
    held, sems, out_sems = refs[n_src + n_dest :]
    for doc in range(DOCS):
        for src in range(n_src):

            @pl.when(place_ref[doc] == src)
            def _():
                for dest in range(n_dest):
                    cols = pl.ds(pl.multiple_of(head_ref[dest] * HD, HD), HD)
                    pltpu.make_async_copy(
                        sources[src].at[slot_ref[doc], :, :, cols],
                        held.at[dest, :, doc],
                        sems.at[dest, doc],
                    ).start()

    for dest in range(n_dest):
        for doc in range(DOCS):
            pltpu.make_async_copy(
                sources[0].at[0, :, :, 0:HD], held.at[dest, :, doc], sems.at[dest, doc]
            ).wait()
        pltpu.make_async_copy(held.at[dest], outs[dest], out_sems.at[dest]).start()
    for dest in range(n_dest):
        pltpu.make_async_copy(held.at[dest], outs[dest], out_sems.at[dest]).wait()


def select_docs(sources, place, slot, heads, n_dest):
    tokens = sources[0].shape[2]
    shape = (2, DOCS, tokens, HD)
    smem = pl.BlockSpec(memory_space=pltpu.SMEM)
    return pl.pallas_call(
        functools.partial(select_kernel, n_dest, len(sources)),
        in_specs=[smem] * 3 + [pl.BlockSpec(memory_space=pl.ANY)] * len(sources),
        out_specs=[pl.BlockSpec(memory_space=pltpu.HBM)] * n_dest,
        out_shape=[pltpu.HBM(shape, jnp.bfloat16)] * n_dest,
        scratch_shapes=[
            pltpu.VMEM((n_dest, *shape), jnp.bfloat16),
            pltpu.SemaphoreType.DMA((n_dest, DOCS)),
            pltpu.SemaphoreType.DMA((n_dest,)),
        ],
        compiler_params=megabytes(8),
        cost_estimate=cost(0, 4 * n_dest * math.prod(shape)),
        name="select_docs",
    )(place, slot, heads, *sources)


def split_exact(value):
    pieces = []
    for _ in range(3):
        pieces.append(value.astype(jnp.bfloat16).astype(jnp.float32))
        value = value - pieces[-1]
    return pieces


def attend_kernel(n_chunks, with_new, n_tiles, tile_q, first_tile, first_ref, pos_ref, *refs):
    refs = list(refs)
    take = lambda count: [refs.pop(0) for _ in range(count)]
    chunks = take(n_chunks)
    dead_ref, qpos_ref, queries = take(3)
    if with_new:
        cos_ref, sin_ref, new_ref = take(3)
    if with_new:
        top, total, summed, values, new_key, new_value = take(6)
    else:
        packed, top, total, summed, values = take(5)
    together = min(PAIR, n_tiles)
    n_pairs = n_tiles // together
    tokens = chunks[0].shape[2]
    scale = math.log2(math.e) / math.sqrt(HD)

    for chunk in range(n_chunks):
        for doc in range(DOCS):
            values[doc, :, chunk * tokens : (chunk + 1) * tokens] = chunks[chunk][1, doc].T
    if with_new:
        new_key[...] = rotate(
            new_ref[:, :HD].astype(jnp.float32), cos_ref[...], sin_ref[...]
        ).astype(jnp.bfloat16)
        new_value[...] = new_ref[:, HD:].T

    one_row = jnp.where(
        lax.broadcasted_iota(jnp.int32, (HD, TILE_COLS), 0) == 0, 1.0, 0.0
    ).astype(jnp.bfloat16)

    def update(tile, parts):
        best = functools.reduce(
            jnp.maximum, [jnp.max(scores, axis=0, keepdims=True) for scores, _ in parts]
        )
        old = top[tile]
        new = jnp.maximum(old, best)
        shrink = jnp.exp2((old - new) * scale)
        running = total[tile] * shrink
        mixed = summed[tile] * shrink
        for scores, value in parts:
            weights = jnp.exp2((scores - new) * scale)
            running += jnp.sum(weights, axis=0, keepdims=True)
            mixed += jnp.dot(
                value, weights.astype(jnp.bfloat16), preferred_element_type=jnp.float32
            )
        top[tile] = new
        total[tile] = running
        summed[tile] = mixed

    @pl.loop(0, n_pairs)
    def _(pair):
        tiles = [pair * together + i for i in range(together)]
        for tile in tiles:
            top[tile] = jnp.full(top.shape[1:], MASKED, jnp.float32)
            total[tile] = jnp.zeros(total.shape[1:], jnp.float32)
            summed[tile] = jnp.zeros(summed.shape[1:], jnp.float32)
        if with_new:
            fresh = []
            for tile in tiles:
                scores = jnp.dot(new_key[...], queries[tile], preferred_element_type=jnp.float32)
                key_index = lax.broadcasted_iota(jnp.int32, scores.shape, 0)
                q_index = (first_tile + tile) * tile_q + lax.broadcasted_iota(jnp.int32, scores.shape, 1) % tile_q
                fresh.append(jnp.where(key_index <= q_index, scores, MASKED))
            for tile, scores in zip(tiles, fresh):
                update(tile, [(scores, new_value[...])])

        @pl.loop(0, DOCS)
        def _(doc):
            firsts = [first_ref[doc * n_chunks + chunk] for chunk in range(n_chunks)]
            lowest = functools.reduce(jnp.minimum, firsts)
            reach = functools.reduce(jnp.maximum, firsts) + tokens - 1

            def visit(masked):
                found = []
                for tile in tiles:
                    extended = jnp.concatenate([queries[tile], one_row], axis=0)
                    parts = []
                    for chunk in range(n_chunks):
                        span = slice(chunk * tokens, (chunk + 1) * tokens)
                        keys = jnp.concatenate(
                            [chunks[chunk][0, doc], dead_ref[doc, span, :]], axis=1
                        )
                        scores = jnp.dot(keys, extended, preferred_element_type=jnp.float32)
                        if masked:
                            key_pos = firsts[chunk] + lax.broadcasted_iota(
                                jnp.int32, scores.shape, 0
                            )
                            scores = jnp.where(key_pos <= qpos_ref[first_tile + tile], scores, MASKED)
                        parts.append((scores, values[doc, :, span]))
                    found.append(parts)
                for tile, parts in zip(tiles, found):
                    update(tile, parts)

            start = first_tile * tile_q + pair * together * tile_q
            live = lowest <= pos_ref[start + together * tile_q - 1]
            whole = reach <= pos_ref[start]

            @pl.when(live & whole)
            def _():
                visit(False)

            @pl.when(live & jnp.logical_not(whole))
            def _():
                visit(True)

        if not with_new:
            for tile in tiles:
                extra = jnp.concatenate(
                    split_exact(top[tile])
                    + split_exact(total[tile])
                    + [jnp.zeros((STATS - 6, TILE_COLS), jnp.float32)],
                    axis=0,
                )
                packed[tile] = jnp.concatenate([summed[tile], extra], axis=0).astype(jnp.bfloat16)


def attend(chunks, dead, first_pos, selected, q_pos, queries, first_tile, n_tiles, fresh):
    n_chunks = len(chunks)
    tokens = chunks[0].shape[2]
    tile_q = SEL // q_pos.shape[0]
    smem = pl.BlockSpec(memory_space=pltpu.SMEM)
    vmem = pl.BlockSpec(memory_space=pltpu.VMEM)
    operands = [first_pos, selected, *chunks, dead, q_pos, queries, *fresh]
    state = [((n_tiles, 1, TILE_COLS), jnp.float32)] * 2
    state += [((n_tiles, HD, TILE_COLS), jnp.float32)]
    values = ((DOCS, HD, n_chunks * tokens), jnp.bfloat16)
    if fresh:
        outs = state
        scratch = [values, ((SEL, HD), jnp.bfloat16), ((HD, SEL), jnp.bfloat16)]
    else:
        outs = [((n_tiles, HD + STATS, TILE_COLS), jnp.bfloat16)]
        scratch = state + [values]
    pairs = n_tiles * TILE_COLS * DOCS * n_chunks * tokens // 2
    return pl.pallas_call(
        functools.partial(
            attend_kernel, n_chunks, bool(fresh), n_tiles, tile_q, first_tile
        ),
        in_specs=[smem] * 2 + [vmem] * (len(operands) - 2),
        out_specs=[vmem] * len(outs),
        out_shape=[jax.ShapeDtypeStruct(*s) for s in outs],
        scratch_shapes=[pltpu.VMEM(*s) for s in scratch],
        compiler_params=megabytes(16),
        cost_estimate=cost(4 * pairs * HD, 4 * DOCS * n_chunks * tokens * HD, pairs),
        name="attend",
    )(*operands)


def merge_kernel(*refs):
    out_ref = refs[-1]
    scale = math.log2(math.e) / math.sqrt(HD)
    for half in range(HALVES):
        top_a, total_a, mixed_a, packed = refs[4 * half : 4 * half + 4]
        n_tiles = top_a.shape[0]
        tile_q = SEL // HALVES // n_tiles
        for tile in range(n_tiles):
            extra = packed[tile, HD:, :].astype(jnp.float32)
            top_b = extra[0:1] + (extra[1:2] + extra[2:3])
            total_b = extra[3:4] + (extra[4:5] + extra[5:6])
            new = jnp.maximum(top_a[tile], top_b)
            part_a = jnp.exp2((top_a[tile] - new) * scale)
            part_b = jnp.exp2((top_b - new) * scale)
            total = total_a[tile] * part_a + total_b * part_b
            mixed = mixed_a[tile] * part_a + packed[tile, :HD, :].astype(jnp.float32) * part_b
            finished = (mixed / total).T.astype(jnp.bfloat16)
            here = slice((half * n_tiles + tile) * tile_q, (half * n_tiles + tile + 1) * tile_q)
            for head in range(TILE_COLS // tile_q):
                out_ref[here, head * HD : (head + 1) * HD] = finished[
                    head * tile_q : (head + 1) * tile_q, :
                ]


def merge(mine, theirs):
    n_tiles = mine[0][0].shape[0] * HALVES
    shape = (SEL, TILE_COLS * n_tiles // SEL * HD)
    operands = [a for state, packed in zip(mine, theirs) for a in (*state, packed)]
    return pl.pallas_call(
        merge_kernel,
        out_shape=jax.ShapeDtypeStruct(shape, jnp.bfloat16),
        compiler_params=megabytes(16),
        cost_estimate=cost(4 * math.prod(shape), 8 * math.prod(shape)),
        name="merge",
    )(*operands)


def out_kernel(n_blocks, first_col, place_ref, x_ref, w_ref, *refs):
    outs = refs[:n_blocks]
    ordered, slots, sems = refs[n_blocks:]
    rows = SEL // n_blocks
    tile = slots.shape[2]
    count = outs[0].shape[1] // tile
    start, wait = stream(
        [lambda step: w_ref.at[:, pl.ds(first_col + step * tile, tile)]], [slots], sems
    )

    for step in range(min(SLOTS, count)):
        start(step)
    for block in range(n_blocks):
        there = pl.ds(pl.multiple_of(place_ref[block] * rows, rows), rows)
        ordered[block * rows : (block + 1) * rows, :] = x_ref[there, :]
    for step in range(count):
        wait(step)
        product = jnp.dot(
            ordered[...].astype(jnp.bfloat16),
            slots[step % SLOTS],
            preferred_element_type=jnp.float32,
        )
        cols = slice(step * tile, (step + 1) * tile)
        for block, out in enumerate(outs):
            out[:, cols] = product[block * rows : (block + 1) * rows, :].astype(out.dtype)
        if step + SLOTS < count:
            start(step + SLOTS)


def project_out(place, attention, w_out, chunk, kinds):
    depth = w_out.shape[0]
    n_blocks = len(kinds)
    width = w_out.shape[1] // CHUNKS
    rows = SEL // n_blocks
    if rows % 16:
        attention = attention.astype(jnp.float32)
    vmem = pl.BlockSpec(memory_space=pltpu.VMEM)
    return pl.pallas_call(
        functools.partial(out_kernel, n_blocks, chunk * width),
        in_specs=[
            pl.BlockSpec(memory_space=pltpu.SMEM),
            vmem,
            pl.BlockSpec(memory_space=pltpu.HBM),
        ],
        out_specs=[vmem] * n_blocks,
        out_shape=[jax.ShapeDtypeStruct((rows, width), kind) for kind in kinds],
        scratch_shapes=[
            pltpu.VMEM((SEL, depth), attention.dtype),
            pltpu.VMEM((SLOTS, depth, min(WIDTH_TILE, width)), jnp.bfloat16),
            pltpu.SemaphoreType.DMA((1, SLOTS)),
        ],
        compiler_params=megabytes(50),
        cost_estimate=cost(2 * SEL * depth * width, 2 * depth * (width + SEL) + 4 * SEL * width),
        name="project_out",
    )(place, attention, w_out)


def per_device(
    hidden_in, norm_gain, w_query, w_keyval, w_out, pool_cache, doc_slot, doc_blocks, sel_pos
):
    tp_size = lax.axis_size("tp")
    req_size = lax.axis_size("req")
    me = lax.axis_index("tp")
    rows, width = hidden_in.shape
    slots, tokens = pool_cache.shape[:2]
    heads_here = w_query.shape[1] // HD
    selected = sel_pos[0]
    lengths = doc_blocks[0] * BLOCK

    if tp_size == KVH:
        ring = [*range(0, tp_size, 2), *range(tp_size - 1, 0, -2)]
    else:
        ring = list(range(tp_size))
    far = tp_size // 2
    forth = [(ring[p], ring[(p + 1) % tp_size]) for p in range(tp_size)]
    back = [(dst, src) for src, dst in forth]
    steps = [0] + [sign * k for k in range(1, far) for sign in (-1, 1)] + [far]
    table = [[ring[(ring.index(i) + s) % tp_size] for s in steps] for i in range(tp_size)]
    place = jnp.array(table, jnp.int32)[me]

    widened = hidden_in.astype(jnp.float32)
    normed = (
        widened
        * lax.rsqrt(jnp.mean(widened * widened, axis=-1, keepdims=True) + EPSILON)
        * norm_gain
    ).astype(jnp.bfloat16)
    middle = tp_size // 2
    order = jnp.arange(middle, dtype=jnp.int32)
    offsets = jnp.cumsum(lengths) - lengths
    first_slot = (me ^ order) * tokens
    slot_tokens = first_slot[:, None] + jnp.arange(tokens, dtype=jnp.int32)[None, :]
    cache_pos = offsets[:, None, None] + slot_tokens[None]
    is_valid = slot_tokens[None] < lengths[:, None, None]
    replaced = jnp.any(cache_pos[..., None] == selected, axis=-1)
    dead = jnp.where(is_valid & jnp.logical_not(replaced), 0.0, MASKED).astype(jnp.bfloat16)
    dead = jnp.broadcast_to(dead[..., None], (DOCS, middle, tokens, HD))
    dead = dead.reshape(DOCS, middle * tokens, HD)
    first_pos = jnp.where(
        first_slot[None] < lengths[:, None], offsets[:, None] + first_slot[None], FAR
    ).reshape(-1)
    cosine, sine_part = rotation_tables(selected)
    heads_here = w_query.shape[1] // HD
    tile_q = TILE_COLS // heads_here
    q_pos = jnp.tile(selected.reshape(SEL // tile_q, tile_q), (1, heads_here))
    q_pos = q_pos.reshape(SEL // tile_q, 1, TILE_COLS)

    part = width // CHUNKS
    streams = []
    for chunk in range(CHUNKS):
        own = normed[:, chunk * part : (chunk + 1) * part]
        streams.append({"before": [own], "behind": [own]})
    for k in range(1, far + 1):
        for chunk, held in enumerate(streams):
            if k < far or chunk % 2 == 0:
                held["before"].append(lax.ppermute(held["before"][-1], "tp", forth))
            if k < far or chunk % 2 == 1:
                held["behind"].append(lax.ppermute(held["behind"][-1], "tp", back))
        first = streams[0]["before"]
        if k == 1:
            first[-1], pool_cache = lax.optimization_barrier((first[-1], pool_cache))
            by_kind = pool_cache.transpose(0, 2, 1, 3)
            sources = [by_kind]
            for shift in range(1, req_size):
                pairs = [((i + shift) % req_size, i) for i in range(req_size)]
                sources.append(lax.ppermute(by_kind, "req", pairs))
            holder = (doc_slot // slots - lax.axis_index("req")) % req_size
            takers = jnp.concatenate([me ^ order, me ^ order ^ middle]) * KVH // tp_size
        if k == 2:
            first[-1], dead, first_pos, cosine, sine_part, q_pos, takers, holder = (
                lax.optimization_barrier(
                    (first[-1], dead, first_pos, cosine, sine_part, q_pos, takers, holder)
                )
            )
        if k == far - 1:
            sent = select_docs(sources, holder, doc_slot % slots, takers, tp_size)
            first[-1], *sent = lax.optimization_barrier((first[-1], *sent))
    projected = None
    for chunk, held in enumerate(streams):
        blocks = [held["before"][0]]
        for k in range(1, far):
            blocks += [held["before"][k], held["behind"][k]]
        blocks.append(held["behind" if chunk % 2 else "before"][far])
        if rows % 16:
            blocks = [jnp.concatenate(blocks, axis=0)]
        projected = project(
            place, blocks, w_query, w_keyval, projected, (cosine, sine_part), chunk
        )
    chunks = [
        [
            lax.ppermute(sent[slot * middle + j], "tp", [(i, i ^ j) for i in range(tp_size)])
            if j
            else sent[slot * middle]
            for j in range(middle)
        ]
        for slot in range(2)
    ]
    *queries, chunks[1] = lax.optimization_barrier((*projected[:HALVES], chunks[1]))
    n_tiles = queries[0].shape[0]
    across = [(i, i ^ middle) for i in range(tp_size)]
    their_queries = [None] * HALVES
    for part in reversed(range(HALVES)):
        their_queries[part] = lax.ppermute(queries[part], "tp", across)

    if tp_size == KVH:
        is_key = me < middle
        here = queries[-1][n_tiles:].reshape(SEL, 2 * HD)
        there = their_queries[-1][n_tiles:].reshape(SEL, 2 * HD)
        keys, vals = jnp.where(is_key, here, there), jnp.where(is_key, there, here)
        new = lax.ppermute(
            jnp.concatenate(
                [
                    jnp.where(is_key, keys[:, :HD], keys[:, HD:]),
                    jnp.where(is_key, vals[:, :HD], vals[:, HD:]),
                ],
                axis=1,
            ),
            "tp",
            [(i, 2 * i if i < middle else 2 * (i - middle) + 1) for i in range(tp_size)],
        )
    else:
        everyone = lax.all_gather(projected[-1], "tp", axis=1, tiled=True)
        my_head = me * KVH // tp_size
        new = jnp.concatenate(
            [
                lax.dynamic_slice_in_dim(everyone, (kind * KVH + my_head) * HD, HD, axis=1)
                for kind in range(2)
            ],
            axis=1,
        )

    def attend_half(part, asked, slot, extra):
        return attend(
            chunks[slot], dead, first_pos, selected, q_pos, asked[part], part * n_tiles, n_tiles, extra
        )

    theirs = [None] * HALVES
    for part in reversed(range(HALVES)):
        (packed,) = attend_half(part, their_queries, 1, [])
        if part:
            packed, new, their_queries[part - 1] = lax.optimization_barrier(
                (packed, new, their_queries[part - 1])
            )
        theirs[part] = lax.ppermute(packed, "tp", across)
    fresh = [cosine, sine_part, new]
    mine = [attend_half(part, queries, 0, fresh) for part in range(HALVES)]
    attention = merge(mine, theirs)

    finished = []
    for chunk in range(CHUNKS):
        kinds = [jnp.float32] * (tp_size - 1) + [jnp.bfloat16]
        pieces = project_out(place, attention, w_out, chunk, kinds)
        to_forth, to_back = list(pieces[2 : tp_size - 1 : 2]), list(pieces[1 : tp_size - 1 : 2])
        (to_back if chunk % 2 else to_forth).append(pieces[-1])
        total = pieces[0]
        for terms, pairs in ((to_forth, forth), (to_back, back)):
            held = None
            for term in reversed(terms):
                if held is not None:
                    term = term + held.astype(jnp.float32)
                held = lax.ppermute(term.astype(jnp.bfloat16), "tp", pairs)
            total = total + held.astype(jnp.float32)
        finished.append(total.astype(jnp.bfloat16))
    return jnp.concatenate(finished, axis=1)


def solution(mesh):
    placed = (
        P(("groups", "req", "tp"), None),
        P(),
        P(None, "tp"),
        P(None, "tp"),
        P("tp", None),
        P(("groups", "req"), "tp", None, None),
        P(("groups", "req")),
        P(("groups", "req"), None),
        P(("groups", "req"), None),
    )
    return jax.shard_map(
        per_device,
        mesh=mesh,
        in_specs=placed,
        out_specs=P(("groups", "req", "tp"), None),
        check_vma=False,
    )
```

```python
import functools
import math

import jax
import jax.numpy as jnp
from jax import lax
from jax.experimental import pallas as pl
from jax.experimental.pallas import tpu as pltpu
from jax.sharding import PartitionSpec as P

HEADS = 64
KVH = 8
HD = 128
DOCS = 4
BLOCK = 128
SEL = 256


EPSILON = 1e-05
ROPE_BASE = 500000.0
MASKED = -1e30
FAR = 1 << 30
CHUNKS = 2
TILE_COLS = 256
PAIR = 2
STATS = 16
HALVES = 2
DEPTH_TILE = 1024
WIDTH_TILE = 1024
SLOTS = 3


def cost(flops, bytes_accessed, transcendentals=0):
    return pl.CostEstimate(
        flops=int(flops), bytes_accessed=int(bytes_accessed), transcendentals=int(transcendentals)
    )


def rotation_tables(positions):
    half_dim = HD // 2
    inverse = ROPE_BASE ** (-(jnp.arange(half_dim, dtype=jnp.float32) * (2.0 / HD)))
    angles = positions.astype(jnp.float32)[:, None] * inverse[None, :]
    cosine = jnp.cos(angles)
    sine_part = jnp.sin(angles)
    return (
        jnp.concatenate([cosine, cosine], axis=-1),
        jnp.concatenate([-sine_part, sine_part], axis=-1),
    )


def rotate(values, cosine, sine_part):
    swapped = jnp.concatenate([values[:, HD // 2 :], values[:, : HD // 2]], axis=-1)
    return values * cosine + swapped * sine_part


def megabytes(count):
    return pltpu.CompilerParams(vmem_limit_bytes=count * 1024 * 1024)


def stream(sources, buffers, sems):
    def copies(step):
        slot = step % SLOTS
        return [
            pltpu.make_async_copy(source(step), buffer.at[slot], sems.at[i, slot])
            for i, (source, buffer) in enumerate(zip(sources, buffers))
        ]

    def start(step):
        for copy in copies(step):
            copy.start()

    def wait(step):
        for copy in copies(step):
            copy.wait()

    return start, wait


def project_kernel(n_blocks, chunk, is_last, place_ref, *refs):
    refs = list(refs)
    take = lambda count: [refs.pop(0) for _ in range(count)]
    blocks = take(n_blocks)
    wq_ref, wkv_ref = take(2)
    if chunk:
        prev_q, prev_kv = take(2)
    if is_last:
        cos_ref, sin_ref = take(2)
        total_q, total_kv, natural, natural_kv = refs[-7:-3]
        outs = refs[:-7]
    else:
        total_q, total_kv = take(2)
    wq_slots, wkv_slots, sems = refs[-3:]
    tile = wq_slots.shape[1]
    depth = blocks[0].shape[1]
    count = depth // tile
    rows_of = lambda ref: lambda step: ref.at[pl.ds(chunk * depth + step * tile, tile), :]
    start, wait = stream([rows_of(wq_ref), rows_of(wkv_ref)], [wq_slots, wkv_slots], sems)

    for step in range(min(SLOTS, count)):
        start(step)
    for step in range(count):
        wait(step)
        slot = step % SLOTS
        cols = slice(step * tile, (step + 1) * tile)
        rows = jnp.concatenate([b[:, cols] for b in blocks], axis=0)
        part_q = jnp.dot(rows, wq_slots[slot], preferred_element_type=jnp.float32)
        part_kv = jnp.dot(rows, wkv_slots[slot], preferred_element_type=jnp.float32)
        if step:
            total_q[...] += part_q
            total_kv[...] += part_kv
        elif chunk:
            total_q[...] = prev_q[...] + part_q
            total_kv[...] = prev_kv[...] + part_kv
        else:
            total_q[...] = part_q
            total_kv[...] = part_kv
        if step + SLOTS < count:
            start(step + SLOTS)

    if is_last:
        height = SEL // place_ref.shape[0]
        for block in range(SEL // height):
            here = slice(block * height, (block + 1) * height)
            there = pl.ds(pl.multiple_of(place_ref[block] * height, height), height)
            natural[there, :] = total_q[here, :]
            natural_kv[there, :] = total_kv[here, :]
        heads_here = total_q.shape[1] // HD
        tile_q = TILE_COLS // heads_here
        per_half = SEL // tile_q // HALVES
        for index in range(SEL // tile_q):
            here = slice(index * tile_q, (index + 1) * tile_q)
            stacked = jnp.concatenate(
                [
                    rotate(
                        natural[here, head * HD : (head + 1) * HD], cos_ref[here, :], sin_ref[here, :]
                    )
                    for head in range(heads_here)
                ],
                axis=0,
            )
            outs[index // per_half][index % per_half] = stacked.T.astype(jnp.bfloat16)
        if len(outs) > HALVES:
            outs[-1][...] = natural_kv[...].astype(jnp.bfloat16)
        else:
            for index in range(SEL // HD):
                outs[-1][per_half + index] = natural_kv[
                    index * HD : (index + 1) * HD, :
                ].astype(jnp.bfloat16)


def project(place, blocks, w_query, w_keyval, prev, tables, chunk):
    depth = blocks[0].shape[1]
    q_cols, kv_cols = w_query.shape[1], w_keyval.shape[1]
    tile = min(DEPTH_TILE, depth)
    is_last = chunk + 1 == CHUNKS
    vmem = pl.BlockSpec(memory_space=pltpu.VMEM)
    hbm = pl.BlockSpec(memory_space=pltpu.HBM)
    total = [((SEL, q_cols), jnp.float32), ((SEL, kv_cols), jnp.float32)]
    scratch = []
    if is_last:
        per_half = SEL * q_cols // (HD * TILE_COLS * HALVES)
        behind = SEL // HD if kv_cols == TILE_COLS else 0
        outs = [(per_half, HD, TILE_COLS)] * (HALVES - 1) + [(per_half + behind, HD, TILE_COLS)]
        if not behind:
            outs.append((SEL, kv_cols))
        outs = [(shape, jnp.bfloat16) for shape in outs]
        scratch = total + total
    else:
        outs = total
    extra = ([] if prev is None else list(prev)) + (list(tables) if is_last else [])
    return pl.pallas_call(
        functools.partial(project_kernel, len(blocks), chunk, is_last),
        in_specs=[pl.BlockSpec(memory_space=pltpu.SMEM)]
        + [vmem] * len(blocks)
        + [hbm] * 2
        + [vmem] * len(extra),
        out_specs=[vmem] * len(outs),
        out_shape=[jax.ShapeDtypeStruct(*o) for o in outs],
        scratch_shapes=[pltpu.VMEM(*x) for x in scratch]
        + [
            pltpu.VMEM((SLOTS, tile, q_cols), jnp.bfloat16),
            pltpu.VMEM((SLOTS, tile, kv_cols), jnp.bfloat16),
            pltpu.SemaphoreType.DMA((2, SLOTS)),
        ],
        compiler_params=megabytes(16),
        cost_estimate=cost(
            2 * SEL * depth * (q_cols + kv_cols), 2 * depth * (q_cols + kv_cols + SEL)
        ),
        name="project",
    )(place, *blocks, w_query, w_keyval, *extra)


def select_kernel(n_dest, n_src, place_ref, slot_ref, head_ref, *refs):
    sources = refs[:n_src]
    outs = refs[n_src : n_src + n_dest]
    sems = refs[n_src + n_dest]
    for doc in range(DOCS):
        for src in range(n_src):

            @pl.when(place_ref[doc] == src)
            def _():
                for dest in range(n_dest):
                    cols = pl.ds(pl.multiple_of(head_ref[dest] * HD, HD), HD)
                    pltpu.make_async_copy(
                        sources[src].at[slot_ref[doc], :, :, cols],
                        outs[dest].at[:, doc],
                        sems.at[dest, doc],
                    ).start()

    for dest in range(n_dest):
        for doc in range(DOCS):
            pltpu.make_async_copy(
                sources[0].at[0, :, :, 0:HD], outs[dest].at[:, doc], sems.at[dest, doc]
            ).wait()


def select_docs(sources, place, slot, heads, n_dest):
    tokens = sources[0].shape[2]
    shape = (2, DOCS, tokens, HD)
    smem = pl.BlockSpec(memory_space=pltpu.SMEM)
    return pl.pallas_call(
        functools.partial(select_kernel, n_dest, len(sources)),
        in_specs=[smem] * 3 + [pl.BlockSpec(memory_space=pl.ANY)] * len(sources),
        out_specs=[pl.BlockSpec(memory_space=pltpu.VMEM)] * n_dest,
        out_shape=[jax.ShapeDtypeStruct(shape, jnp.bfloat16)] * n_dest,
        scratch_shapes=[pltpu.SemaphoreType.DMA((n_dest, DOCS))],
        compiler_params=megabytes(8),
        cost_estimate=cost(0, 4 * n_dest * math.prod(shape)),
        name="select_docs",
    )(place, slot, heads, *sources)


def split_exact(value):
    pieces = []
    for _ in range(3):
        pieces.append(value.astype(jnp.bfloat16).astype(jnp.float32))
        value = value - pieces[-1]
    return pieces


def attend_kernel(n_chunks, with_new, n_tiles, tile_q, first_tile, first_ref, pos_ref, *refs):
    refs = list(refs)
    take = lambda count: [refs.pop(0) for _ in range(count)]
    chunks = take(n_chunks)
    dead_ref, qpos_ref, queries = take(3)
    if with_new:
        cos_ref, sin_ref, new_ref = take(3)
    if with_new:
        top, total, summed, values, new_key, new_value = take(6)
    else:
        packed, top, total, summed, values = take(5)
    together = min(PAIR, n_tiles)
    n_pairs = n_tiles // together
    tokens = chunks[0].shape[2]
    scale = math.log2(math.e) / math.sqrt(HD)

    for chunk in range(n_chunks):
        for doc in range(DOCS):
            values[doc, :, chunk * tokens : (chunk + 1) * tokens] = chunks[chunk][1, doc].T
    if with_new:
        new_key[...] = rotate(
            new_ref[:, :HD].astype(jnp.float32), cos_ref[...], sin_ref[...]
        ).astype(jnp.bfloat16)
        new_value[...] = new_ref[:, HD:].T

    one_row = jnp.where(
        lax.broadcasted_iota(jnp.int32, (HD, TILE_COLS), 0) == 0, 1.0, 0.0
    ).astype(jnp.bfloat16)

    def update(tile, parts):
        best = functools.reduce(
            jnp.maximum, [jnp.max(scores, axis=0, keepdims=True) for scores, _ in parts]
        )
        old = top[tile]
        new = jnp.maximum(old, best)
        shrink = jnp.exp2((old - new) * scale)
        running = total[tile] * shrink
        mixed = summed[tile] * shrink
        for scores, value in parts:
            weights = jnp.exp2((scores - new) * scale)
            running += jnp.sum(weights, axis=0, keepdims=True)
            mixed += jnp.dot(
                value, weights.astype(jnp.bfloat16), preferred_element_type=jnp.float32
            )
        top[tile] = new
        total[tile] = running
        summed[tile] = mixed

    @pl.loop(0, n_pairs)
    def _(pair):
        tiles = [pair * together + i for i in range(together)]
        for tile in tiles:
            top[tile] = jnp.full(top.shape[1:], MASKED, jnp.float32)
            total[tile] = jnp.zeros(total.shape[1:], jnp.float32)
            summed[tile] = jnp.zeros(summed.shape[1:], jnp.float32)
        if with_new:
            fresh = []
            for tile in tiles:
                scores = jnp.dot(new_key[...], queries[tile], preferred_element_type=jnp.float32)
                key_index = lax.broadcasted_iota(jnp.int32, scores.shape, 0)
                q_index = (first_tile + tile) * tile_q + lax.broadcasted_iota(jnp.int32, scores.shape, 1) % tile_q
                fresh.append(jnp.where(key_index <= q_index, scores, MASKED))
            for tile, scores in zip(tiles, fresh):
                update(tile, [(scores, new_value[...])])

        @pl.loop(0, DOCS)
        def _(doc):
            firsts = [first_ref[doc * n_chunks + chunk] for chunk in range(n_chunks)]
            lowest = functools.reduce(jnp.minimum, firsts)
            reach = functools.reduce(jnp.maximum, firsts) + tokens - 1

            def visit(masked):
                found = []
                for tile in tiles:
                    extended = jnp.concatenate([queries[tile], one_row], axis=0)
                    parts = []
                    for chunk in range(n_chunks):
                        span = slice(chunk * tokens, (chunk + 1) * tokens)
                        keys = jnp.concatenate(
                            [chunks[chunk][0, doc], dead_ref[doc, span, :]], axis=1
                        )
                        scores = jnp.dot(keys, extended, preferred_element_type=jnp.float32)
                        if masked:
                            key_pos = firsts[chunk] + lax.broadcasted_iota(
                                jnp.int32, scores.shape, 0
                            )
                            scores = jnp.where(key_pos <= qpos_ref[first_tile + tile], scores, MASKED)
                        parts.append((scores, values[doc, :, span]))
                    found.append(parts)
                for tile, parts in zip(tiles, found):
                    update(tile, parts)

            start = first_tile * tile_q + pair * together * tile_q
            live = lowest <= pos_ref[start + together * tile_q - 1]
            whole = reach <= pos_ref[start]

            @pl.when(live & whole)
            def _():
                visit(False)

            @pl.when(live & jnp.logical_not(whole))
            def _():
                visit(True)

        if not with_new:
            for tile in tiles:
                extra = jnp.concatenate(
                    split_exact(top[tile])
                    + split_exact(total[tile])
                    + [jnp.zeros((STATS - 6, TILE_COLS), jnp.float32)],
                    axis=0,
                )
                packed[tile] = jnp.concatenate([summed[tile], extra], axis=0).astype(jnp.bfloat16)


def attend(chunks, dead, first_pos, selected, q_pos, queries, first_tile, n_tiles, fresh):
    n_chunks = len(chunks)
    tokens = chunks[0].shape[2]
    tile_q = SEL // q_pos.shape[0]
    smem = pl.BlockSpec(memory_space=pltpu.SMEM)
    vmem = pl.BlockSpec(memory_space=pltpu.VMEM)
    operands = [first_pos, selected, *chunks, dead, q_pos, queries, *fresh]
    state = [((n_tiles, 1, TILE_COLS), jnp.float32)] * 2
    state += [((n_tiles, HD, TILE_COLS), jnp.float32)]
    values = ((DOCS, HD, n_chunks * tokens), jnp.bfloat16)
    if fresh:
        outs = state
        scratch = [values, ((SEL, HD), jnp.bfloat16), ((HD, SEL), jnp.bfloat16)]
    else:
        outs = [((n_tiles, HD + STATS, TILE_COLS), jnp.bfloat16)]
        scratch = state + [values]
    pairs = n_tiles * TILE_COLS * DOCS * n_chunks * tokens // 2
    return pl.pallas_call(
        functools.partial(
            attend_kernel, n_chunks, bool(fresh), n_tiles, tile_q, first_tile
        ),
        in_specs=[smem] * 2 + [vmem] * (len(operands) - 2),
        out_specs=[vmem] * len(outs),
        out_shape=[jax.ShapeDtypeStruct(*s) for s in outs],
        scratch_shapes=[pltpu.VMEM(*s) for s in scratch],
        compiler_params=megabytes(16),
        cost_estimate=cost(4 * pairs * HD, 4 * DOCS * n_chunks * tokens * HD, pairs),
        name="attend",
    )(*operands)


def merge_kernel(*refs):
    out_ref = refs[-1]
    scale = math.log2(math.e) / math.sqrt(HD)
    for half in range(HALVES):
        top_a, total_a, mixed_a, packed = refs[4 * half : 4 * half + 4]
        n_tiles = top_a.shape[0]
        tile_q = SEL // HALVES // n_tiles
        for tile in range(n_tiles):
            extra = packed[tile, HD:, :].astype(jnp.float32)
            top_b = extra[0:1] + (extra[1:2] + extra[2:3])
            total_b = extra[3:4] + (extra[4:5] + extra[5:6])
            new = jnp.maximum(top_a[tile], top_b)
            part_a = jnp.exp2((top_a[tile] - new) * scale)
            part_b = jnp.exp2((top_b - new) * scale)
            total = total_a[tile] * part_a + total_b * part_b
            mixed = mixed_a[tile] * part_a + packed[tile, :HD, :].astype(jnp.float32) * part_b
            finished = (mixed / total).T.astype(jnp.bfloat16)
            here = slice((half * n_tiles + tile) * tile_q, (half * n_tiles + tile + 1) * tile_q)
            for head in range(TILE_COLS // tile_q):
                out_ref[here, head * HD : (head + 1) * HD] = finished[
                    head * tile_q : (head + 1) * tile_q, :
                ]


def merge(mine, theirs):
    n_tiles = mine[0][0].shape[0] * HALVES
    shape = (SEL, TILE_COLS * n_tiles // SEL * HD)
    operands = [a for state, packed in zip(mine, theirs) for a in (*state, packed)]
    return pl.pallas_call(
        merge_kernel,
        out_shape=jax.ShapeDtypeStruct(shape, jnp.bfloat16),
        compiler_params=megabytes(16),
        cost_estimate=cost(4 * math.prod(shape), 8 * math.prod(shape)),
        name="merge",
    )(*operands)


def out_kernel(n_blocks, first_col, place_ref, x_ref, w_ref, *refs):
    outs = refs[:n_blocks]
    ordered, slots, sems = refs[n_blocks:]
    rows = SEL // n_blocks
    tile = slots.shape[2]
    count = outs[0].shape[1] // tile
    start, wait = stream(
        [lambda step: w_ref.at[:, pl.ds(first_col + step * tile, tile)]], [slots], sems
    )

    for step in range(min(SLOTS, count)):
        start(step)
    for block in range(n_blocks):
        there = pl.ds(pl.multiple_of(place_ref[block] * rows, rows), rows)
        ordered[block * rows : (block + 1) * rows, :] = x_ref[there, :]
    for step in range(count):
        wait(step)
        product = jnp.dot(
            ordered[...].astype(jnp.bfloat16),
            slots[step % SLOTS],
            preferred_element_type=jnp.float32,
        )
        cols = slice(step * tile, (step + 1) * tile)
        for block, out in enumerate(outs):
            out[:, cols] = product[block * rows : (block + 1) * rows, :].astype(out.dtype)
        if step + SLOTS < count:
            start(step + SLOTS)


def project_out(place, attention, w_out, chunk, kinds):
    depth = w_out.shape[0]
    n_blocks = len(kinds)
    width = w_out.shape[1] // CHUNKS
    rows = SEL // n_blocks
    if rows % 16:
        attention = attention.astype(jnp.float32)
    vmem = pl.BlockSpec(memory_space=pltpu.VMEM)
    return pl.pallas_call(
        functools.partial(out_kernel, n_blocks, chunk * width),
        in_specs=[
            pl.BlockSpec(memory_space=pltpu.SMEM),
            vmem,
            pl.BlockSpec(memory_space=pltpu.HBM),
        ],
        out_specs=[vmem] * n_blocks,
        out_shape=[jax.ShapeDtypeStruct((rows, width), kind) for kind in kinds],
        scratch_shapes=[
            pltpu.VMEM((SEL, depth), attention.dtype),
            pltpu.VMEM((SLOTS, depth, min(WIDTH_TILE, width)), jnp.bfloat16),
            pltpu.SemaphoreType.DMA((1, SLOTS)),
        ],
        compiler_params=megabytes(16),
        cost_estimate=cost(2 * SEL * depth * width, 2 * depth * (width + SEL) + 4 * SEL * width),
        name="project_out",
    )(place, attention, w_out)


def per_device(
    hidden_in, norm_gain, w_query, w_keyval, w_out, pool_cache, doc_slot, doc_blocks, sel_pos
):
    tp_size = lax.axis_size("tp")
    req_size = lax.axis_size("req")
    me = lax.axis_index("tp")
    rows, width = hidden_in.shape
    slots, tokens = pool_cache.shape[:2]
    heads_here = w_query.shape[1] // HD
    selected = sel_pos[0]
    lengths = doc_blocks[0] * BLOCK

    if tp_size == KVH:
        ring = [*range(0, tp_size, 2), *range(tp_size - 1, 0, -2)]
    else:
        ring = list(range(tp_size))
    far = tp_size // 2
    forth = [(ring[p], ring[(p + 1) % tp_size]) for p in range(tp_size)]
    back = [(dst, src) for src, dst in forth]
    steps = [0] + [sign * k for k in range(1, far) for sign in (-1, 1)] + [far]
    table = [[ring[(ring.index(i) + s) % tp_size] for s in steps] for i in range(tp_size)]
    place = jnp.array(table, jnp.int32)[me]

    widened = hidden_in.astype(jnp.float32)
    normed = (
        widened
        * lax.rsqrt(jnp.mean(widened * widened, axis=-1, keepdims=True) + EPSILON)
        * norm_gain
    ).astype(jnp.bfloat16)
    normed, pool_cache = lax.optimization_barrier((normed, pool_cache))
    w_query, w_keyval, w_out = (
        pltpu.with_memory_space_constraint(w, pltpu.HBM) for w in (w_query, w_keyval, w_out)
    )
    middle = tp_size // 2
    order = jnp.arange(middle, dtype=jnp.int32)
    offsets = jnp.cumsum(lengths) - lengths
    first_slot = (me ^ order) * tokens
    slot_tokens = first_slot[:, None] + jnp.arange(tokens, dtype=jnp.int32)[None, :]
    cache_pos = offsets[:, None, None] + slot_tokens[None]
    is_valid = slot_tokens[None] < lengths[:, None, None]
    replaced = jnp.any(cache_pos[..., None] == selected, axis=-1)
    dead = jnp.where(is_valid & jnp.logical_not(replaced), 0.0, MASKED).astype(jnp.bfloat16)
    dead = jnp.broadcast_to(dead[..., None], (DOCS, middle, tokens, HD))
    dead = dead.reshape(DOCS, middle * tokens, HD)
    first_pos = jnp.where(
        first_slot[None] < lengths[:, None], offsets[:, None] + first_slot[None], FAR
    ).reshape(-1)
    cosine, sine_part = rotation_tables(selected)
    heads_here = w_query.shape[1] // HD
    tile_q = TILE_COLS // heads_here
    q_pos = jnp.tile(selected.reshape(SEL // tile_q, tile_q), (1, heads_here))
    q_pos = q_pos.reshape(SEL // tile_q, 1, TILE_COLS)

    part = width // CHUNKS
    streams = []
    for chunk in range(CHUNKS):
        own = normed[:, chunk * part : (chunk + 1) * part]
        streams.append({"before": [own], "behind": [own]})
    for k in range(1, far + 1):
        for chunk, held in enumerate(streams):
            if k < far or chunk % 2 == 0:
                held["before"].append(lax.ppermute(held["before"][-1], "tp", forth))
            if k < far or chunk % 2 == 1:
                held["behind"].append(lax.ppermute(held["behind"][-1], "tp", back))
        first = streams[0]["before"]
        if k == 1:
            by_kind = pool_cache.transpose(0, 2, 1, 3)
            sources = [by_kind]
            for shift in range(1, req_size):
                pairs = [((i + shift) % req_size, i) for i in range(req_size)]
                sources.append(lax.ppermute(by_kind, "req", pairs))
            holder = (doc_slot // slots - lax.axis_index("req")) % req_size
            takers = jnp.concatenate([me ^ order, me ^ order ^ middle]) * KVH // tp_size
        if k == 2:
            first[-1], dead, first_pos, cosine, sine_part, q_pos, takers, holder = (
                lax.optimization_barrier(
                    (first[-1], dead, first_pos, cosine, sine_part, q_pos, takers, holder)
                )
            )
        if k == far - 1:
            sent = select_docs(sources, holder, doc_slot % slots, takers, tp_size)
            first[-1], *sent = lax.optimization_barrier((first[-1], *sent))
    projected = None
    for chunk, held in enumerate(streams):
        blocks = [held["before"][0]]
        for k in range(1, far):
            blocks += [held["before"][k], held["behind"][k]]
        blocks.append(held["behind" if chunk % 2 else "before"][far])
        if rows % 16:
            blocks = [jnp.concatenate(blocks, axis=0)]
        projected = project(
            place, blocks, w_query, w_keyval, projected, (cosine, sine_part), chunk
        )
    chunks = [
        [
            lax.ppermute(sent[slot * middle + j], "tp", [(i, i ^ j) for i in range(tp_size)])
            if j
            else sent[slot * middle]
            for j in range(middle)
        ]
        for slot in range(2)
    ]
    *queries, chunks[1] = lax.optimization_barrier((*projected[:HALVES], chunks[1]))
    n_tiles = queries[0].shape[0]
    across = [(i, i ^ middle) for i in range(tp_size)]
    their_queries = [None] * HALVES
    for part in reversed(range(HALVES)):
        their_queries[part] = lax.ppermute(queries[part], "tp", across)

    if tp_size == KVH:
        is_key = me < middle
        here = queries[-1][n_tiles:].reshape(SEL, 2 * HD)
        there = their_queries[-1][n_tiles:].reshape(SEL, 2 * HD)
        keys, vals = jnp.where(is_key, here, there), jnp.where(is_key, there, here)
        new = lax.ppermute(
            jnp.concatenate(
                [
                    jnp.where(is_key, keys[:, :HD], keys[:, HD:]),
                    jnp.where(is_key, vals[:, :HD], vals[:, HD:]),
                ],
                axis=1,
            ),
            "tp",
            [(i, 2 * i if i < middle else 2 * (i - middle) + 1) for i in range(tp_size)],
        )
    else:
        everyone = lax.all_gather(projected[-1], "tp", axis=1, tiled=True)
        my_head = me * KVH // tp_size
        new = jnp.concatenate(
            [
                lax.dynamic_slice_in_dim(everyone, (kind * KVH + my_head) * HD, HD, axis=1)
                for kind in range(2)
            ],
            axis=1,
        )

    def attend_half(part, asked, slot, extra):
        return attend(
            chunks[slot], dead, first_pos, selected, q_pos, asked[part], part * n_tiles, n_tiles, extra
        )

    theirs = [None] * HALVES
    for part in reversed(range(HALVES)):
        (packed,) = attend_half(part, their_queries, 1, [])
        if part:
            packed, new, their_queries[part - 1] = lax.optimization_barrier(
                (packed, new, their_queries[part - 1])
            )
        theirs[part] = lax.ppermute(packed, "tp", across)
    fresh = [cosine, sine_part, new]
    mine = [attend_half(part, queries, 0, fresh) for part in range(HALVES)]
    attention = merge(mine, theirs)

    finished = []
    for chunk in range(CHUNKS):
        kinds = [jnp.float32] * (tp_size - 1) + [jnp.bfloat16]
        pieces = project_out(place, attention, w_out, chunk, kinds)
        to_forth, to_back = list(pieces[2 : tp_size - 1 : 2]), list(pieces[1 : tp_size - 1 : 2])
        (to_back if chunk % 2 else to_forth).append(pieces[-1])
        total = pieces[0]
        for terms, pairs in ((to_forth, forth), (to_back, back)):
            held = None
            for term in reversed(terms):
                if held is not None:
                    term = term + held.astype(jnp.float32)
                held = lax.ppermute(term.astype(jnp.bfloat16), "tp", pairs)
            total = total + held.astype(jnp.float32)
        finished.append(total.astype(jnp.bfloat16))
    return jnp.concatenate(finished, axis=1)


def solution(mesh):
    placed = (
        P(("groups", "req", "tp"), None),
        P(),
        P(None, "tp"),
        P(None, "tp"),
        P("tp", None),
        P(("groups", "req"), "tp", None, None),
        P(("groups", "req")),
        P(("groups", "req"), None),
        P(("groups", "req"), None),
    )
    return jax.shard_map(
        per_device,
        mesh=mesh,
        in_specs=placed,
        out_specs=P(("groups", "req", "tp"), None),
        check_vma=False,
    )
```

```python
import functools
import math

import jax
import jax.numpy as jnp
from jax import lax
from jax.experimental import pallas as pl
from jax.experimental.pallas import tpu as pltpu
from jax.sharding import PartitionSpec as P

HEADS = 64
KVH = 8
HD = 128
DOCS = 4
BLOCK = 128
SEL = 256


EPSILON = 1e-05
ROPE_BASE = 500000.0
MASKED = -1e30
FAR = 1 << 30
CHUNKS = 2
TILE_COLS = 256
PAIR = 2
STATS = 16
HALVES = 2
DEPTH_TILE = 1024
WIDTH_TILE = 1024
SLOTS = 3


def cost(flops, bytes_accessed, transcendentals=0):
    return pl.CostEstimate(
        flops=int(flops), bytes_accessed=int(bytes_accessed), transcendentals=int(transcendentals)
    )


def rotation_tables(positions):
    half_dim = HD // 2
    inverse = ROPE_BASE ** (-(jnp.arange(half_dim, dtype=jnp.float32) * (2.0 / HD)))
    angles = positions.astype(jnp.float32)[:, None] * inverse[None, :]
    cosine = jnp.cos(angles)
    sine_part = jnp.sin(angles)
    return (
        jnp.concatenate([cosine, cosine], axis=-1),
        jnp.concatenate([-sine_part, sine_part], axis=-1),
    )


def rotate(values, cosine, sine_part):
    swapped = jnp.concatenate([values[:, HD // 2 :], values[:, : HD // 2]], axis=-1)
    return values * cosine + swapped * sine_part


def megabytes(count):
    return pltpu.CompilerParams(vmem_limit_bytes=count * 1024 * 1024)


def stream(sources, buffers, sems):
    def copies(step):
        slot = step % SLOTS
        return [
            pltpu.make_async_copy(source(step), buffer.at[slot], sems.at[i, slot])
            for i, (source, buffer) in enumerate(zip(sources, buffers))
        ]

    def start(step):
        for copy in copies(step):
            copy.start()

    def wait(step):
        for copy in copies(step):
            copy.wait()

    return start, wait


def project_kernel(n_blocks, chunk, is_last, place_ref, *refs):
    refs = list(refs)
    take = lambda count: [refs.pop(0) for _ in range(count)]
    blocks = take(n_blocks)
    wq_ref, wkv_ref = take(2)
    if chunk:
        prev_q, prev_kv = take(2)
    if is_last:
        cos_ref, sin_ref = take(2)
        total_q, total_kv, natural, natural_kv = refs[-7:-3]
        outs = refs[:-7]
    else:
        total_q, total_kv = take(2)
    wq_slots, wkv_slots, sems = refs[-3:]
    tile = wq_slots.shape[1]
    depth = blocks[0].shape[1]
    count = depth // tile
    rows_of = lambda ref: lambda step: ref.at[pl.ds(chunk * depth + step * tile, tile), :]
    start, wait = stream([rows_of(wq_ref), rows_of(wkv_ref)], [wq_slots, wkv_slots], sems)

    for step in range(min(SLOTS, count)):
        start(step)
    for step in range(count):
        wait(step)
        slot = step % SLOTS
        cols = slice(step * tile, (step + 1) * tile)
        rows = jnp.concatenate([b[:, cols] for b in blocks], axis=0)
        part_q = jnp.dot(rows, wq_slots[slot], preferred_element_type=jnp.float32)
        part_kv = jnp.dot(rows, wkv_slots[slot], preferred_element_type=jnp.float32)
        if step:
            total_q[...] += part_q
            total_kv[...] += part_kv
        elif chunk:
            total_q[...] = prev_q[...] + part_q
            total_kv[...] = prev_kv[...] + part_kv
        else:
            total_q[...] = part_q
            total_kv[...] = part_kv
        if step + SLOTS < count:
            start(step + SLOTS)

    if is_last:
        height = SEL // place_ref.shape[0]
        for block in range(SEL // height):
            here = slice(block * height, (block + 1) * height)
            there = pl.ds(pl.multiple_of(place_ref[block] * height, height), height)
            natural[there, :] = total_q[here, :]
            natural_kv[there, :] = total_kv[here, :]
        heads_here = total_q.shape[1] // HD
        tile_q = TILE_COLS // heads_here
        per_half = SEL // tile_q // HALVES
        for index in range(SEL // tile_q):
            here = slice(index * tile_q, (index + 1) * tile_q)
            stacked = jnp.concatenate(
                [
                    rotate(
                        natural[here, head * HD : (head + 1) * HD], cos_ref[here, :], sin_ref[here, :]
                    )
                    for head in range(heads_here)
                ],
                axis=0,
            )
            outs[index // per_half][index % per_half] = stacked.T.astype(jnp.bfloat16)
        if len(outs) > HALVES:
            outs[-1][...] = natural_kv[...].astype(jnp.bfloat16)
        else:
            for index in range(SEL // HD):
                outs[-1][per_half + index] = natural_kv[
                    index * HD : (index + 1) * HD, :
                ].astype(jnp.bfloat16)


def project(place, blocks, w_query, w_keyval, prev, tables, chunk):
    depth = blocks[0].shape[1]
    q_cols, kv_cols = w_query.shape[1], w_keyval.shape[1]
    tile = min(DEPTH_TILE, depth)
    is_last = chunk + 1 == CHUNKS
    vmem = pl.BlockSpec(memory_space=pltpu.VMEM)
    hbm = pl.BlockSpec(memory_space=pltpu.HBM)
    total = [((SEL, q_cols), jnp.float32), ((SEL, kv_cols), jnp.float32)]
    scratch = []
    if is_last:
        per_half = SEL * q_cols // (HD * TILE_COLS * HALVES)
        behind = SEL // HD if kv_cols == TILE_COLS else 0
        outs = [(per_half, HD, TILE_COLS)] * (HALVES - 1) + [(per_half + behind, HD, TILE_COLS)]
        if not behind:
            outs.append((SEL, kv_cols))
        outs = [(shape, jnp.bfloat16) for shape in outs]
        scratch = total + total
    else:
        outs = total
    extra = ([] if prev is None else list(prev)) + (list(tables) if is_last else [])
    return pl.pallas_call(
        functools.partial(project_kernel, len(blocks), chunk, is_last),
        in_specs=[pl.BlockSpec(memory_space=pltpu.SMEM)]
        + [vmem] * len(blocks)
        + [hbm] * 2
        + [vmem] * len(extra),
        out_specs=[vmem] * len(outs),
        out_shape=[jax.ShapeDtypeStruct(*o) for o in outs],
        scratch_shapes=[pltpu.VMEM(*x) for x in scratch]
        + [
            pltpu.VMEM((SLOTS, tile, q_cols), jnp.bfloat16),
            pltpu.VMEM((SLOTS, tile, kv_cols), jnp.bfloat16),
            pltpu.SemaphoreType.DMA((2, SLOTS)),
        ],
        compiler_params=megabytes(16),
        cost_estimate=cost(
            2 * SEL * depth * (q_cols + kv_cols), 2 * depth * (q_cols + kv_cols + SEL)
        ),
        name="project",
    )(place, *blocks, w_query, w_keyval, *extra)


def select_kernel(n_dest, n_src, place_ref, slot_ref, head_ref, *refs):
    sources = refs[:n_src]
    outs = refs[n_src : n_src + n_dest]
    sems = refs[n_src + n_dest]
    for doc in range(DOCS):
        for src in range(n_src):

            @pl.when(place_ref[doc] == src)
            def _():
                for dest in range(n_dest):
                    cols = pl.ds(pl.multiple_of(head_ref[dest] * HD, HD), HD)
                    pltpu.make_async_copy(
                        sources[src].at[slot_ref[doc], :, :, cols],
                        outs[dest].at[:, doc],
                        sems.at[dest, doc],
                    ).start()

    for dest in range(n_dest):
        for doc in range(DOCS):
            pltpu.make_async_copy(
                sources[0].at[0, :, :, 0:HD], outs[dest].at[:, doc], sems.at[dest, doc]
            ).wait()


def select_docs(sources, place, slot, heads, n_dest):
    tokens = sources[0].shape[2]
    shape = (2, DOCS, tokens, HD)
    smem = pl.BlockSpec(memory_space=pltpu.SMEM)
    return pl.pallas_call(
        functools.partial(select_kernel, n_dest, len(sources)),
        in_specs=[smem] * 3 + [pl.BlockSpec(memory_space=pl.ANY)] * len(sources),
        out_specs=[pl.BlockSpec(memory_space=pltpu.VMEM)] * n_dest,
        out_shape=[jax.ShapeDtypeStruct(shape, jnp.bfloat16)] * n_dest,
        scratch_shapes=[pltpu.SemaphoreType.DMA((n_dest, DOCS))],
        compiler_params=megabytes(8),
        cost_estimate=cost(0, 4 * n_dest * math.prod(shape)),
        name="select_docs",
    )(place, slot, heads, *sources)


def split_exact(value):
    pieces = []
    for _ in range(3):
        pieces.append(value.astype(jnp.bfloat16).astype(jnp.float32))
        value = value - pieces[-1]
    return pieces


def attend_kernel(n_chunks, with_new, n_tiles, tile_q, first_tile, first_ref, pos_ref, *refs):
    refs = list(refs)
    take = lambda count: [refs.pop(0) for _ in range(count)]
    chunks = take(n_chunks)
    dead_ref, qpos_ref, queries = take(3)
    if with_new:
        cos_ref, sin_ref, new_ref = take(3)
    if with_new:
        top, total, summed, values, new_key, new_value = take(6)
    else:
        packed, top, total, summed, values = take(5)
    together = min(PAIR, n_tiles)
    n_pairs = n_tiles // together
    tokens = chunks[0].shape[2]
    scale = math.log2(math.e) / math.sqrt(HD)

    for chunk in range(n_chunks):
        for doc in range(DOCS):
            values[doc, :, chunk * tokens : (chunk + 1) * tokens] = chunks[chunk][1, doc].T
    if with_new:
        new_key[...] = rotate(
            new_ref[:, :HD].astype(jnp.float32), cos_ref[...], sin_ref[...]
        ).astype(jnp.bfloat16)
        new_value[...] = new_ref[:, HD:].T

    one_row = jnp.where(
        lax.broadcasted_iota(jnp.int32, (HD, TILE_COLS), 0) == 0, 1.0, 0.0
    ).astype(jnp.bfloat16)

    def update(tile, parts):
        best = functools.reduce(
            jnp.maximum, [jnp.max(scores, axis=0, keepdims=True) for scores, _ in parts]
        )
        old = top[tile]
        new = jnp.maximum(old, best)
        shrink = jnp.exp2((old - new) * scale)
        running = total[tile] * shrink
        mixed = summed[tile] * shrink
        for scores, value in parts:
            weights = jnp.exp2((scores - new) * scale)
            running += jnp.sum(weights, axis=0, keepdims=True)
            mixed += jnp.dot(
                value, weights.astype(jnp.bfloat16), preferred_element_type=jnp.float32
            )
        top[tile] = new
        total[tile] = running
        summed[tile] = mixed

    @pl.loop(0, n_pairs)
    def _(pair):
        tiles = [pair * together + i for i in range(together)]
        for tile in tiles:
            top[tile] = jnp.full(top.shape[1:], MASKED, jnp.float32)
            total[tile] = jnp.zeros(total.shape[1:], jnp.float32)
            summed[tile] = jnp.zeros(summed.shape[1:], jnp.float32)
        if with_new:
            fresh = []
            for tile in tiles:
                scores = jnp.dot(new_key[...], queries[tile], preferred_element_type=jnp.float32)
                key_index = lax.broadcasted_iota(jnp.int32, scores.shape, 0)
                q_index = (first_tile + tile) * tile_q + lax.broadcasted_iota(jnp.int32, scores.shape, 1) % tile_q
                fresh.append(jnp.where(key_index <= q_index, scores, MASKED))
            for tile, scores in zip(tiles, fresh):
                update(tile, [(scores, new_value[...])])

        @pl.loop(0, DOCS)
        def _(doc):
            firsts = [first_ref[doc * n_chunks + chunk] for chunk in range(n_chunks)]
            lowest = functools.reduce(jnp.minimum, firsts)
            reach = functools.reduce(jnp.maximum, firsts) + tokens - 1

            def visit(masked):
                found = []
                for tile in tiles:
                    extended = jnp.concatenate([queries[tile], one_row], axis=0)
                    parts = []
                    for chunk in range(n_chunks):
                        span = slice(chunk * tokens, (chunk + 1) * tokens)
                        keys = jnp.concatenate(
                            [chunks[chunk][0, doc], dead_ref[doc, span, :]], axis=1
                        )
                        scores = jnp.dot(keys, extended, preferred_element_type=jnp.float32)
                        if masked:
                            key_pos = firsts[chunk] + lax.broadcasted_iota(
                                jnp.int32, scores.shape, 0
                            )
                            scores = jnp.where(key_pos <= qpos_ref[first_tile + tile], scores, MASKED)
                        parts.append((scores, values[doc, :, span]))
                    found.append(parts)
                for tile, parts in zip(tiles, found):
                    update(tile, parts)

            start = first_tile * tile_q + pair * together * tile_q
            live = lowest <= pos_ref[start + together * tile_q - 1]
            whole = reach <= pos_ref[start]

            @pl.when(live & whole)
            def _():
                visit(False)

            @pl.when(live & jnp.logical_not(whole))
            def _():
                visit(True)

        if not with_new:
            for tile in tiles:
                extra = jnp.concatenate(
                    split_exact(top[tile])
                    + split_exact(total[tile])
                    + [jnp.zeros((STATS - 6, TILE_COLS), jnp.float32)],
                    axis=0,
                )
                packed[tile] = jnp.concatenate([summed[tile], extra], axis=0).astype(jnp.bfloat16)


def attend(chunks, dead, first_pos, selected, q_pos, queries, first_tile, n_tiles, fresh):
    n_chunks = len(chunks)
    tokens = chunks[0].shape[2]
    tile_q = SEL // q_pos.shape[0]
    smem = pl.BlockSpec(memory_space=pltpu.SMEM)
    vmem = pl.BlockSpec(memory_space=pltpu.VMEM)
    operands = [first_pos, selected, *chunks, dead, q_pos, queries, *fresh]
    state = [((n_tiles, 1, TILE_COLS), jnp.float32)] * 2
    state += [((n_tiles, HD, TILE_COLS), jnp.float32)]
    values = ((DOCS, HD, n_chunks * tokens), jnp.bfloat16)
    if fresh:
        outs = state
        scratch = [values, ((SEL, HD), jnp.bfloat16), ((HD, SEL), jnp.bfloat16)]
    else:
        outs = [((n_tiles, HD + STATS, TILE_COLS), jnp.bfloat16)]
        scratch = state + [values]
    pairs = n_tiles * TILE_COLS * DOCS * n_chunks * tokens // 2
    return pl.pallas_call(
        functools.partial(
            attend_kernel, n_chunks, bool(fresh), n_tiles, tile_q, first_tile
        ),
        in_specs=[smem] * 2 + [vmem] * (len(operands) - 2),
        out_specs=[vmem] * len(outs),
        out_shape=[jax.ShapeDtypeStruct(*s) for s in outs],
        scratch_shapes=[pltpu.VMEM(*s) for s in scratch],
        compiler_params=megabytes(16),
        cost_estimate=cost(4 * pairs * HD, 4 * DOCS * n_chunks * tokens * HD, pairs),
        name="attend",
    )(*operands)


def pick_kernel(n_tiles, side_ref, here_ref, there_ref, out_ref):
    def pick(keys_ref, values_ref, head):
        cols = slice(head * HD, (head + 1) * HD)
        for index in range(SEL // HD):
            rows = slice(index * HD, (index + 1) * HD)
            out_ref[rows, :HD] = keys_ref[n_tiles + index][:, cols]
            out_ref[rows, HD:] = values_ref[n_tiles + index][:, cols]

    @pl.when(side_ref[0] == 1)
    def _():
        pick(here_ref, there_ref, 0)

    @pl.when(side_ref[0] == 0)
    def _():
        pick(there_ref, here_ref, 1)


def pick_new(side, here, there, n_tiles):
    vmem = pl.BlockSpec(memory_space=pltpu.VMEM)
    return pl.pallas_call(
        functools.partial(pick_kernel, n_tiles),
        in_specs=[pl.BlockSpec(memory_space=pltpu.SMEM), vmem, vmem],
        out_specs=vmem,
        out_shape=jax.ShapeDtypeStruct((SEL, 2 * HD), jnp.bfloat16),
        compiler_params=megabytes(4),
        cost_estimate=cost(0, 8 * SEL * HD),
        name="pick_new",
    )(side, here, there)


def merge_kernel(*refs):
    out_ref = refs[-1]
    scale = math.log2(math.e) / math.sqrt(HD)
    for half in range(HALVES):
        top_a, total_a, mixed_a, packed = refs[4 * half : 4 * half + 4]
        n_tiles = top_a.shape[0]
        tile_q = SEL // HALVES // n_tiles
        for tile in range(n_tiles):
            extra = packed[tile, HD:, :].astype(jnp.float32)
            top_b = extra[0:1] + (extra[1:2] + extra[2:3])
            total_b = extra[3:4] + (extra[4:5] + extra[5:6])
            new = jnp.maximum(top_a[tile], top_b)
            part_a = jnp.exp2((top_a[tile] - new) * scale)
            part_b = jnp.exp2((top_b - new) * scale)
            total = total_a[tile] * part_a + total_b * part_b
            mixed = mixed_a[tile] * part_a + packed[tile, :HD, :].astype(jnp.float32) * part_b
            finished = (mixed / total).T.astype(jnp.bfloat16)
            here = slice((half * n_tiles + tile) * tile_q, (half * n_tiles + tile + 1) * tile_q)
            for head in range(TILE_COLS // tile_q):
                out_ref[here, head * HD : (head + 1) * HD] = finished[
                    head * tile_q : (head + 1) * tile_q, :
                ]


def merge(mine, theirs):
    n_tiles = mine[0][0].shape[0] * HALVES
    shape = (SEL, TILE_COLS * n_tiles // SEL * HD)
    operands = [a for state, packed in zip(mine, theirs) for a in (*state, packed)]
    return pl.pallas_call(
        merge_kernel,
        out_shape=jax.ShapeDtypeStruct(shape, jnp.bfloat16),
        compiler_params=megabytes(16),
        cost_estimate=cost(4 * math.prod(shape), 8 * math.prod(shape)),
        name="merge",
    )(*operands)


def out_kernel(n_blocks, first_col, place_ref, x_ref, w_ref, *refs):
    outs = refs[:n_blocks]
    ordered, slots, sems = refs[n_blocks:]
    rows = SEL // n_blocks
    tile = slots.shape[2]
    count = outs[0].shape[1] // tile
    start, wait = stream(
        [lambda step: w_ref.at[:, pl.ds(first_col + step * tile, tile)]], [slots], sems
    )

    for step in range(min(SLOTS, count)):
        start(step)
    for block in range(n_blocks):
        there = pl.ds(pl.multiple_of(place_ref[block] * rows, rows), rows)
        ordered[block * rows : (block + 1) * rows, :] = x_ref[there, :]
    for step in range(count):
        wait(step)
        product = jnp.dot(
            ordered[...].astype(jnp.bfloat16),
            slots[step % SLOTS],
            preferred_element_type=jnp.float32,
        )
        cols = slice(step * tile, (step + 1) * tile)
        for block, out in enumerate(outs):
            out[:, cols] = product[block * rows : (block + 1) * rows, :].astype(out.dtype)
        if step + SLOTS < count:
            start(step + SLOTS)


def project_out(place, attention, w_out, chunk, kinds):
    depth = w_out.shape[0]
    n_blocks = len(kinds)
    width = w_out.shape[1] // CHUNKS
    rows = SEL // n_blocks
    if rows % 16:
        attention = attention.astype(jnp.float32)
    vmem = pl.BlockSpec(memory_space=pltpu.VMEM)
    return pl.pallas_call(
        functools.partial(out_kernel, n_blocks, chunk * width),
        in_specs=[
            pl.BlockSpec(memory_space=pltpu.SMEM),
            vmem,
            pl.BlockSpec(memory_space=pltpu.HBM),
        ],
        out_specs=[vmem] * n_blocks,
        out_shape=[jax.ShapeDtypeStruct((rows, width), kind) for kind in kinds],
        scratch_shapes=[
            pltpu.VMEM((SEL, depth), attention.dtype),
            pltpu.VMEM((SLOTS, depth, min(WIDTH_TILE, width)), jnp.bfloat16),
            pltpu.SemaphoreType.DMA((1, SLOTS)),
        ],
        compiler_params=megabytes(16),
        cost_estimate=cost(2 * SEL * depth * width, 2 * depth * (width + SEL) + 4 * SEL * width),
        name="project_out",
    )(place, attention, w_out)


def per_device(
    hidden_in, norm_gain, w_query, w_keyval, w_out, pool_cache, doc_slot, doc_blocks, sel_pos
):
    tp_size = lax.axis_size("tp")
    req_size = lax.axis_size("req")
    me = lax.axis_index("tp")
    rows, width = hidden_in.shape
    slots, tokens = pool_cache.shape[:2]
    heads_here = w_query.shape[1] // HD
    selected = sel_pos[0]
    lengths = doc_blocks[0] * BLOCK

    if tp_size == KVH:
        ring = [*range(0, tp_size, 2), *range(tp_size - 1, 0, -2)]
    else:
        ring = list(range(tp_size))
    far = tp_size // 2
    forth = [(ring[p], ring[(p + 1) % tp_size]) for p in range(tp_size)]
    back = [(dst, src) for src, dst in forth]
    steps = [0] + [sign * k for k in range(1, far) for sign in (-1, 1)] + [far]
    table = [[ring[(ring.index(i) + s) % tp_size] for s in steps] for i in range(tp_size)]
    place = jnp.array(table, jnp.int32)[me]

    widened = hidden_in.astype(jnp.float32)
    normed = (
        widened
        * lax.rsqrt(jnp.mean(widened * widened, axis=-1, keepdims=True) + EPSILON)
        * norm_gain
    ).astype(jnp.bfloat16)
    normed, pool_cache = lax.optimization_barrier((normed, pool_cache))
    w_query, w_keyval, w_out = (
        pltpu.with_memory_space_constraint(w, pltpu.HBM) for w in (w_query, w_keyval, w_out)
    )
    middle = tp_size // 2
    order = jnp.arange(middle, dtype=jnp.int32)
    offsets = jnp.cumsum(lengths) - lengths
    first_slot = (me ^ order) * tokens
    slot_tokens = first_slot[:, None] + jnp.arange(tokens, dtype=jnp.int32)[None, :]
    cache_pos = offsets[:, None, None] + slot_tokens[None]
    is_valid = slot_tokens[None] < lengths[:, None, None]
    replaced = jnp.any(cache_pos[..., None] == selected, axis=-1)
    dead = jnp.where(is_valid & jnp.logical_not(replaced), 0.0, MASKED).astype(jnp.bfloat16)
    dead = jnp.broadcast_to(dead[..., None], (DOCS, middle, tokens, HD))
    dead = dead.reshape(DOCS, middle * tokens, HD)
    first_pos = jnp.where(
        first_slot[None] < lengths[:, None], offsets[:, None] + first_slot[None], FAR
    ).reshape(-1)
    cosine, sine_part = rotation_tables(selected)
    heads_here = w_query.shape[1] // HD
    tile_q = TILE_COLS // heads_here
    q_pos = jnp.tile(selected.reshape(SEL // tile_q, tile_q), (1, heads_here))
    q_pos = q_pos.reshape(SEL // tile_q, 1, TILE_COLS)

    part = width // CHUNKS
    streams = []
    for chunk in range(CHUNKS):
        own = normed[:, chunk * part : (chunk + 1) * part]
        streams.append({"before": [own], "behind": [own]})
    for k in range(1, far + 1):
        for chunk, held in enumerate(streams):
            if k < far or chunk % 2 == 0:
                held["before"].append(lax.ppermute(held["before"][-1], "tp", forth))
            if k < far or chunk % 2 == 1:
                held["behind"].append(lax.ppermute(held["behind"][-1], "tp", back))
        first = streams[0]["before"]
        if k == 1:
            by_kind = pool_cache.transpose(0, 2, 1, 3)
            sources = [by_kind]
            for shift in range(1, req_size):
                pairs = [((i + shift) % req_size, i) for i in range(req_size)]
                sources.append(lax.ppermute(by_kind, "req", pairs))
            holder = (doc_slot // slots - lax.axis_index("req")) % req_size
            slot = doc_slot % slots
            side = (me < middle).astype(jnp.int32)[None]
            takers = jnp.concatenate([me ^ order, me ^ order ^ middle]) * KVH // tp_size
        if k == 2:
            first[-1], dead, first_pos, cosine, sine_part, q_pos, takers, holder, slot, place, side = (
                lax.optimization_barrier(
                    (first[-1], dead, first_pos, cosine, sine_part, q_pos, takers, holder, slot)
                    + (place, side)
                )
            )
        if k == far - 1:
            sent = select_docs(sources, holder, slot, takers, tp_size)
            first[-1], *sent = lax.optimization_barrier((first[-1], *sent))
    projected = None
    for chunk, held in enumerate(streams):
        blocks = [held["before"][0]]
        for k in range(1, far):
            blocks += [held["before"][k], held["behind"][k]]
        blocks.append(held["behind" if chunk % 2 else "before"][far])
        if rows % 16:
            blocks = [jnp.concatenate(blocks, axis=0)]
        projected = project(
            place, blocks, w_query, w_keyval, projected, (cosine, sine_part), chunk
        )
    chunks = [
        [
            lax.ppermute(sent[slot * middle + j], "tp", [(i, i ^ j) for i in range(tp_size)])
            if j
            else sent[slot * middle]
            for j in range(middle)
        ]
        for slot in range(2)
    ]
    *queries, chunks[1][1] = lax.optimization_barrier((*projected[:HALVES], chunks[1][1]))
    n_tiles = queries[0].shape[0]
    across = [(i, i ^ middle) for i in range(tp_size)]
    their_queries = [None] * HALVES
    for part in reversed(range(HALVES)):
        their_queries[part] = lax.ppermute(queries[part], "tp", across)

    if tp_size == KVH:
        new = lax.ppermute(
            pick_new(side, queries[-1], their_queries[-1], n_tiles),
            "tp",
            [(i, 2 * i if i < middle else 2 * (i - middle) + 1) for i in range(tp_size)],
        )
    else:
        everyone = lax.all_gather(projected[-1], "tp", axis=1, tiled=True)
        my_head = me * KVH // tp_size
        new = jnp.concatenate(
            [
                lax.dynamic_slice_in_dim(everyone, (kind * KVH + my_head) * HD, HD, axis=1)
                for kind in range(2)
            ],
            axis=1,
        )

    def attend_half(part, asked, slot, extra):
        return attend(
            chunks[slot], dead, first_pos, selected, q_pos, asked[part], part * n_tiles, n_tiles, extra
        )

    theirs = [None] * HALVES
    for part in reversed(range(HALVES)):
        (packed,) = attend_half(part, their_queries, 1, [])
        if part:
            packed, new, their_queries[part - 1] = lax.optimization_barrier(
                (packed, new, their_queries[part - 1])
            )
        theirs[part] = lax.ppermute(packed, "tp", across)
    fresh = [cosine, sine_part, new]
    mine = [attend_half(part, queries, 0, fresh) for part in range(HALVES)]
    attention = merge(mine, theirs)

    finished = []
    for chunk in range(CHUNKS):
        kinds = [jnp.float32] * (tp_size - 1) + [jnp.bfloat16]
        pieces = project_out(place, attention, w_out, chunk, kinds)
        to_forth, to_back = list(pieces[2 : tp_size - 1 : 2]), list(pieces[1 : tp_size - 1 : 2])
        (to_back if chunk % 2 else to_forth).append(pieces[-1])
        total = pieces[0]
        for terms, pairs in ((to_forth, forth), (to_back, back)):
            held = None
            for term in reversed(terms):
                if held is not None:
                    term = term + held.astype(jnp.float32)
                held = lax.ppermute(term.astype(jnp.bfloat16), "tp", pairs)
            total = total + held.astype(jnp.float32)
        finished.append(total.astype(jnp.bfloat16))
    return jnp.concatenate(finished, axis=1)


def solution(mesh):
    placed = (
        P(("groups", "req", "tp"), None),
        P(),
        P(None, "tp"),
        P(None, "tp"),
        P("tp", None),
        P(("groups", "req"), "tp", None, None),
        P(("groups", "req")),
        P(("groups", "req"), None),
        P(("groups", "req"), None),
    )
    return jax.shard_map(
        per_device,
        mesh=mesh,
        in_specs=placed,
        out_specs=P(("groups", "req", "tp"), None),
        check_vma=False,
    )
```

```python
import functools
import math

import jax
import jax.numpy as jnp
from jax import lax
from jax.experimental import pallas as pl
from jax.experimental.pallas import tpu as pltpu
from jax.sharding import PartitionSpec as P

HEADS = 64
KVH = 8
HD = 128
DOCS = 4
BLOCK = 128
SEL = 256


EPSILON = 1e-05
ROPE_BASE = 500000.0
MASKED = -1e30
FAR = 1 << 30
CHUNKS = 2
TILE_COLS = 256
PAIR = 2
STATS = 16
HALVES = 2
DEPTH_TILE = 1024
WIDTH_TILE = 1024
SLOTS = 3


def cost(flops, bytes_accessed, transcendentals=0):
    return pl.CostEstimate(
        flops=int(flops), bytes_accessed=int(bytes_accessed), transcendentals=int(transcendentals)
    )


def rotation_tables(positions):
    half_dim = HD // 2
    inverse = ROPE_BASE ** (-(jnp.arange(half_dim, dtype=jnp.float32) * (2.0 / HD)))
    angles = positions.astype(jnp.float32)[:, None] * inverse[None, :]
    cosine = jnp.cos(angles)
    sine_part = jnp.sin(angles)
    return (
        jnp.concatenate([cosine, cosine], axis=-1),
        jnp.concatenate([-sine_part, sine_part], axis=-1),
    )


def rotate(values, cosine, sine_part):
    swapped = jnp.concatenate([values[:, HD // 2 :], values[:, : HD // 2]], axis=-1)
    return values * cosine + swapped * sine_part


def megabytes(count):
    return pltpu.CompilerParams(vmem_limit_bytes=count * 1024 * 1024)


def stream(sources, buffers, sems):
    def copies(step):
        slot = step % SLOTS
        return [
            pltpu.make_async_copy(source(step), buffer.at[slot], sems.at[i, slot])
            for i, (source, buffer) in enumerate(zip(sources, buffers))
        ]

    def start(step):
        for copy in copies(step):
            copy.start()

    def wait(step):
        for copy in copies(step):
            copy.wait()

    return start, wait


def project_kernel(n_blocks, chunk, is_last, place_ref, *refs):
    refs = list(refs)
    take = lambda count: [refs.pop(0) for _ in range(count)]
    blocks = take(n_blocks)
    wq_ref, wkv_ref = take(2)
    if chunk:
        prev_q, prev_kv = take(2)
    if is_last:
        cos_ref, sin_ref = take(2)
        total_q, total_kv, natural, natural_kv = refs[-7:-3]
        outs = refs[:-7]
    else:
        total_q, total_kv = take(2)
    wq_slots, wkv_slots, sems = refs[-3:]
    tile = wq_slots.shape[1]
    depth = blocks[0].shape[1]
    count = depth // tile
    rows_of = lambda ref: lambda step: ref.at[pl.ds(chunk * depth + step * tile, tile), :]
    start, wait = stream([rows_of(wq_ref), rows_of(wkv_ref)], [wq_slots, wkv_slots], sems)

    for step in range(min(SLOTS, count)):
        start(step)
    for step in range(count):
        wait(step)
        slot = step % SLOTS
        cols = slice(step * tile, (step + 1) * tile)
        rows = jnp.concatenate([b[:, cols] for b in blocks], axis=0)
        part_q = jnp.dot(rows, wq_slots[slot], preferred_element_type=jnp.float32)
        part_kv = jnp.dot(rows, wkv_slots[slot], preferred_element_type=jnp.float32)
        if step:
            total_q[...] += part_q
            total_kv[...] += part_kv
        elif chunk:
            total_q[...] = prev_q[...] + part_q
            total_kv[...] = prev_kv[...] + part_kv
        else:
            total_q[...] = part_q
            total_kv[...] = part_kv
        if step + SLOTS < count:
            start(step + SLOTS)

    if is_last:
        height = SEL // place_ref.shape[0]
        for block in range(SEL // height):
            here = slice(block * height, (block + 1) * height)
            there = pl.ds(pl.multiple_of(place_ref[block] * height, height), height)
            natural[there, :] = total_q[here, :]
            natural_kv[there, :] = total_kv[here, :]
        heads_here = total_q.shape[1] // HD
        tile_q = TILE_COLS // heads_here
        per_half = SEL // tile_q // HALVES
        for index in range(SEL // tile_q):
            here = slice(index * tile_q, (index + 1) * tile_q)
            stacked = jnp.concatenate(
                [
                    rotate(
                        natural[here, head * HD : (head + 1) * HD], cos_ref[here, :], sin_ref[here, :]
                    )
                    for head in range(heads_here)
                ],
                axis=0,
            )
            outs[index // per_half][index % per_half] = stacked.T.astype(jnp.bfloat16)
        if len(outs) > HALVES:
            outs[-1][...] = natural_kv[...].astype(jnp.bfloat16)
        else:
            for index in range(SEL // HD):
                outs[-1][per_half + index] = natural_kv[
                    index * HD : (index + 1) * HD, :
                ].astype(jnp.bfloat16)


def project(place, blocks, w_query, w_keyval, prev, tables, chunk):
    depth = blocks[0].shape[1]
    q_cols, kv_cols = w_query.shape[1], w_keyval.shape[1]
    tile = min(DEPTH_TILE, depth)
    is_last = chunk + 1 == CHUNKS
    vmem = pl.BlockSpec(memory_space=pltpu.VMEM)
    hbm = pl.BlockSpec(memory_space=pltpu.HBM)
    total = [((SEL, q_cols), jnp.float32), ((SEL, kv_cols), jnp.float32)]
    scratch = []
    if is_last:
        per_half = SEL * q_cols // (HD * TILE_COLS * HALVES)
        behind = SEL // HD if kv_cols == TILE_COLS else 0
        outs = [(per_half, HD, TILE_COLS)] * (HALVES - 1) + [(per_half + behind, HD, TILE_COLS)]
        if not behind:
            outs.append((SEL, kv_cols))
        outs = [(shape, jnp.bfloat16) for shape in outs]
        scratch = total + total
    else:
        outs = total
    extra = ([] if prev is None else list(prev)) + (list(tables) if is_last else [])
    return pl.pallas_call(
        functools.partial(project_kernel, len(blocks), chunk, is_last),
        in_specs=[pl.BlockSpec(memory_space=pltpu.SMEM)]
        + [vmem] * len(blocks)
        + [hbm] * 2
        + [vmem] * len(extra),
        out_specs=[vmem] * len(outs),
        out_shape=[jax.ShapeDtypeStruct(*o) for o in outs],
        scratch_shapes=[pltpu.VMEM(*x) for x in scratch]
        + [
            pltpu.VMEM((SLOTS, tile, q_cols), jnp.bfloat16),
            pltpu.VMEM((SLOTS, tile, kv_cols), jnp.bfloat16),
            pltpu.SemaphoreType.DMA((2, SLOTS)),
        ],
        compiler_params=megabytes(16),
        cost_estimate=cost(
            2 * SEL * depth * (q_cols + kv_cols), 2 * depth * (q_cols + kv_cols + SEL)
        ),
        name="project",
    )(place, *blocks, w_query, w_keyval, *extra)


def select_kernel(n_dest, n_src, place_ref, slot_ref, head_ref, *refs):
    sources = refs[:n_src]
    outs = refs[n_src:-1]
    sems = refs[-1]
    targets = [out.at[dest] for out in outs for dest in range(n_dest)]
    for doc in range(DOCS):
        for src in range(n_src):

            @pl.when(place_ref[doc] == src)
            def _():
                for i, target in enumerate(targets):
                    cols = pl.ds(pl.multiple_of(head_ref[i] * HD, HD), HD)
                    pltpu.make_async_copy(
                        sources[src].at[slot_ref[doc], :, :, cols], target.at[:, doc], sems.at[i, doc]
                    ).start()

    for i, target in enumerate(targets):
        for doc in range(DOCS):
            pltpu.make_async_copy(
                sources[0].at[0, :, :, 0:HD], target.at[:, doc], sems.at[i, doc]
            ).wait()


def select_docs(sources, place, slot, heads, n_dest):
    tokens = sources[0].shape[2]
    shape = (n_dest, 2, DOCS, tokens, HD)
    smem = pl.BlockSpec(memory_space=pltpu.SMEM)
    return pl.pallas_call(
        functools.partial(select_kernel, n_dest, len(sources)),
        in_specs=[smem] * 3 + [pl.BlockSpec(memory_space=pl.ANY)] * len(sources),
        out_specs=[pl.BlockSpec(memory_space=pltpu.VMEM)] * 2,
        out_shape=[jax.ShapeDtypeStruct(shape, jnp.bfloat16)] * 2,
        scratch_shapes=[pltpu.SemaphoreType.DMA((2 * n_dest, DOCS))],
        compiler_params=megabytes(8),
        cost_estimate=cost(0, 8 * math.prod(shape)),
        name="select_docs",
    )(place, slot, heads, *sources)


def split_exact(value):
    pieces = []
    for _ in range(3):
        pieces.append(value.astype(jnp.bfloat16).astype(jnp.float32))
        value = value - pieces[-1]
    return pieces


def attend_kernel(n_chunks, with_new, n_tiles, tile_q, first_tile, first_ref, pos_ref, *refs):
    refs = list(refs)
    take = lambda count: [refs.pop(0) for _ in range(count)]
    chunks, dead_ref, qpos_ref, queries = take(4)
    if with_new:
        cos_ref, sin_ref, new_ref = take(3)
    if with_new:
        top, total, summed, values, new_key, new_value = take(6)
    else:
        packed, top, total, summed, values = take(5)
    together = min(PAIR, n_tiles)
    n_pairs = n_tiles // together
    tokens = chunks.shape[3]
    scale = math.log2(math.e) / math.sqrt(HD)

    for chunk in range(n_chunks):
        for doc in range(DOCS):
            values[doc, :, chunk * tokens : (chunk + 1) * tokens] = chunks[chunk, 1, doc].T
    if with_new:
        new_key[...] = rotate(
            new_ref[:, :HD].astype(jnp.float32), cos_ref[...], sin_ref[...]
        ).astype(jnp.bfloat16)
        new_value[...] = new_ref[:, HD:].T

    one_row = jnp.where(
        lax.broadcasted_iota(jnp.int32, (HD, TILE_COLS), 0) == 0, 1.0, 0.0
    ).astype(jnp.bfloat16)

    def update(tile, parts):
        best = functools.reduce(
            jnp.maximum, [jnp.max(scores, axis=0, keepdims=True) for scores, _ in parts]
        )
        old = top[tile]
        new = jnp.maximum(old, best)
        shrink = jnp.exp2((old - new) * scale)
        running = total[tile] * shrink
        mixed = summed[tile] * shrink
        for scores, value in parts:
            weights = jnp.exp2((scores - new) * scale)
            running += jnp.sum(weights, axis=0, keepdims=True)
            mixed += jnp.dot(
                value, weights.astype(jnp.bfloat16), preferred_element_type=jnp.float32
            )
        top[tile] = new
        total[tile] = running
        summed[tile] = mixed

    @pl.loop(0, n_pairs)
    def _(pair):
        tiles = [pair * together + i for i in range(together)]
        for tile in tiles:
            top[tile] = jnp.full(top.shape[1:], MASKED, jnp.float32)
            total[tile] = jnp.zeros(total.shape[1:], jnp.float32)
            summed[tile] = jnp.zeros(summed.shape[1:], jnp.float32)
        if with_new:
            fresh = []
            for tile in tiles:
                scores = jnp.dot(new_key[...], queries[tile], preferred_element_type=jnp.float32)
                key_index = lax.broadcasted_iota(jnp.int32, scores.shape, 0)
                q_index = (first_tile + tile) * tile_q + lax.broadcasted_iota(jnp.int32, scores.shape, 1) % tile_q
                fresh.append(jnp.where(key_index <= q_index, scores, MASKED))
            for tile, scores in zip(tiles, fresh):
                update(tile, [(scores, new_value[...])])

        @pl.loop(0, DOCS)
        def _(doc):
            firsts = [first_ref[doc * n_chunks + chunk] for chunk in range(n_chunks)]
            lowest = functools.reduce(jnp.minimum, firsts)
            reach = functools.reduce(jnp.maximum, firsts) + tokens - 1

            def visit(masked):
                found = []
                for tile in tiles:
                    extended = jnp.concatenate([queries[tile], one_row], axis=0)
                    parts = []
                    for chunk in range(n_chunks):
                        span = slice(chunk * tokens, (chunk + 1) * tokens)
                        keys = jnp.concatenate(
                            [chunks[chunk, 0, doc], dead_ref[doc, span, :]], axis=1
                        )
                        scores = jnp.dot(keys, extended, preferred_element_type=jnp.float32)
                        if masked:
                            key_pos = firsts[chunk] + lax.broadcasted_iota(
                                jnp.int32, scores.shape, 0
                            )
                            scores = jnp.where(key_pos <= qpos_ref[first_tile + tile], scores, MASKED)
                        parts.append((scores, values[doc, :, span]))
                    found.append(parts)
                for tile, parts in zip(tiles, found):
                    update(tile, parts)

            start = first_tile * tile_q + pair * together * tile_q
            live = lowest <= pos_ref[start + together * tile_q - 1]
            whole = reach <= pos_ref[start]

            @pl.when(live & whole)
            def _():
                visit(False)

            @pl.when(live & jnp.logical_not(whole))
            def _():
                visit(True)

        if not with_new:
            for tile in tiles:
                extra = jnp.concatenate(
                    split_exact(top[tile])
                    + split_exact(total[tile])
                    + [jnp.zeros((STATS - 6, TILE_COLS), jnp.float32)],
                    axis=0,
                )
                packed[tile] = jnp.concatenate([summed[tile], extra], axis=0).astype(jnp.bfloat16)


def attend(chunks, dead, first_pos, selected, q_pos, queries, first_tile, n_tiles, fresh):
    n_chunks, tokens = chunks.shape[0], chunks.shape[3]
    tile_q = SEL // q_pos.shape[0]
    smem = pl.BlockSpec(memory_space=pltpu.SMEM)
    vmem = pl.BlockSpec(memory_space=pltpu.VMEM)
    operands = [first_pos, selected, chunks, dead, q_pos, queries, *fresh]
    state = [((n_tiles, 1, TILE_COLS), jnp.float32)] * 2
    state += [((n_tiles, HD, TILE_COLS), jnp.float32)]
    values = ((DOCS, HD, n_chunks * tokens), jnp.bfloat16)
    if fresh:
        outs = state
        scratch = [values, ((SEL, HD), jnp.bfloat16), ((HD, SEL), jnp.bfloat16)]
    else:
        outs = [((n_tiles, HD + STATS, TILE_COLS), jnp.bfloat16)]
        scratch = state + [values]
    pairs = n_tiles * TILE_COLS * DOCS * n_chunks * tokens // 2
    return pl.pallas_call(
        functools.partial(
            attend_kernel, n_chunks, bool(fresh), n_tiles, tile_q, first_tile
        ),
        in_specs=[smem] * 2 + [vmem] * (len(operands) - 2),
        out_specs=[vmem] * len(outs),
        out_shape=[jax.ShapeDtypeStruct(*s) for s in outs],
        scratch_shapes=[pltpu.VMEM(*s) for s in scratch],
        compiler_params=megabytes(16),
        cost_estimate=cost(4 * pairs * HD, 4 * DOCS * n_chunks * tokens * HD, pairs),
        name="attend",
    )(*operands)


def pick_kernel(n_tiles, side_ref, here_ref, there_ref, out_ref):
    def pick(keys_ref, values_ref, head):
        cols = slice(head * HD, (head + 1) * HD)
        for index in range(SEL // HD):
            rows = slice(index * HD, (index + 1) * HD)
            out_ref[rows, :HD] = keys_ref[n_tiles + index][:, cols]
            out_ref[rows, HD:] = values_ref[n_tiles + index][:, cols]

    @pl.when(side_ref[0] == 1)
    def _():
        pick(here_ref, there_ref, 0)

    @pl.when(side_ref[0] == 0)
    def _():
        pick(there_ref, here_ref, 1)


def pick_new(side, here, there, n_tiles):
    vmem = pl.BlockSpec(memory_space=pltpu.VMEM)
    return pl.pallas_call(
        functools.partial(pick_kernel, n_tiles),
        in_specs=[pl.BlockSpec(memory_space=pltpu.SMEM), vmem, vmem],
        out_specs=vmem,
        out_shape=jax.ShapeDtypeStruct((SEL, 2 * HD), jnp.bfloat16),
        compiler_params=megabytes(4),
        cost_estimate=cost(0, 8 * SEL * HD),
        name="pick_new",
    )(side, here, there)


def merge_kernel(*refs):
    out_ref = refs[-1]
    scale = math.log2(math.e) / math.sqrt(HD)
    for half in range(HALVES):
        top_a, total_a, mixed_a, packed = refs[4 * half : 4 * half + 4]
        n_tiles = top_a.shape[0]
        tile_q = SEL // HALVES // n_tiles
        for tile in range(n_tiles):
            extra = packed[tile, HD:, :].astype(jnp.float32)
            top_b = extra[0:1] + (extra[1:2] + extra[2:3])
            total_b = extra[3:4] + (extra[4:5] + extra[5:6])
            new = jnp.maximum(top_a[tile], top_b)
            part_a = jnp.exp2((top_a[tile] - new) * scale)
            part_b = jnp.exp2((top_b - new) * scale)
            total = total_a[tile] * part_a + total_b * part_b
            mixed = mixed_a[tile] * part_a + packed[tile, :HD, :].astype(jnp.float32) * part_b
            finished = (mixed / total).T.astype(jnp.bfloat16)
            here = slice((half * n_tiles + tile) * tile_q, (half * n_tiles + tile + 1) * tile_q)
            for head in range(TILE_COLS // tile_q):
                out_ref[here, head * HD : (head + 1) * HD] = finished[
                    head * tile_q : (head + 1) * tile_q, :
                ]


def merge(mine, theirs):
    n_tiles = mine[0][0].shape[0] * HALVES
    shape = (SEL, TILE_COLS * n_tiles // SEL * HD)
    operands = [a for state, packed in zip(mine, theirs) for a in (*state, packed)]
    return pl.pallas_call(
        merge_kernel,
        out_shape=jax.ShapeDtypeStruct(shape, jnp.bfloat16),
        compiler_params=megabytes(16),
        cost_estimate=cost(4 * math.prod(shape), 8 * math.prod(shape)),
        name="merge",
    )(*operands)


def out_kernel(n_blocks, first_col, place_ref, x_ref, w_ref, *refs):
    outs = refs[:n_blocks]
    ordered, slots, sems = refs[n_blocks:]
    rows = SEL // n_blocks
    tile = slots.shape[2]
    count = outs[0].shape[1] // tile
    start, wait = stream(
        [lambda step: w_ref.at[:, pl.ds(first_col + step * tile, tile)]], [slots], sems
    )

    for step in range(min(SLOTS, count)):
        start(step)
    for block in range(n_blocks):
        there = pl.ds(pl.multiple_of(place_ref[block] * rows, rows), rows)
        ordered[block * rows : (block + 1) * rows, :] = x_ref[there, :]
    for step in range(count):
        wait(step)
        product = jnp.dot(
            ordered[...].astype(jnp.bfloat16),
            slots[step % SLOTS],
            preferred_element_type=jnp.float32,
        )
        cols = slice(step * tile, (step + 1) * tile)
        for block, out in enumerate(outs):
            out[:, cols] = product[block * rows : (block + 1) * rows, :].astype(out.dtype)
        if step + SLOTS < count:
            start(step + SLOTS)


def project_out(place, attention, w_out, chunk, kinds):
    depth = w_out.shape[0]
    n_blocks = len(kinds)
    width = w_out.shape[1] // CHUNKS
    rows = SEL // n_blocks
    if rows % 16:
        attention = attention.astype(jnp.float32)
    vmem = pl.BlockSpec(memory_space=pltpu.VMEM)
    return pl.pallas_call(
        functools.partial(out_kernel, n_blocks, chunk * width),
        in_specs=[
            pl.BlockSpec(memory_space=pltpu.SMEM),
            vmem,
            pl.BlockSpec(memory_space=pltpu.HBM),
        ],
        out_specs=[vmem] * n_blocks,
        out_shape=[jax.ShapeDtypeStruct((rows, width), kind) for kind in kinds],
        scratch_shapes=[
            pltpu.VMEM((SEL, depth), attention.dtype),
            pltpu.VMEM((SLOTS, depth, min(WIDTH_TILE, width)), jnp.bfloat16),
            pltpu.SemaphoreType.DMA((1, SLOTS)),
        ],
        compiler_params=megabytes(16),
        cost_estimate=cost(2 * SEL * depth * width, 2 * depth * (width + SEL) + 4 * SEL * width),
        name="project_out",
    )(place, attention, w_out)


def per_device(
    hidden_in, norm_gain, w_query, w_keyval, w_out, pool_cache, doc_slot, doc_blocks, sel_pos
):
    tp_size = lax.axis_size("tp")
    req_size = lax.axis_size("req")
    me = lax.axis_index("tp")
    rows, width = hidden_in.shape
    slots, tokens = pool_cache.shape[:2]
    heads_here = w_query.shape[1] // HD
    selected = sel_pos[0]
    lengths = doc_blocks[0] * BLOCK

    if tp_size == KVH:
        ring = [*range(0, tp_size, 2), *range(tp_size - 1, 0, -2)]
    else:
        ring = list(range(tp_size))
    far = tp_size // 2
    forth = [(ring[p], ring[(p + 1) % tp_size]) for p in range(tp_size)]
    back = [(dst, src) for src, dst in forth]
    steps = [0] + [sign * k for k in range(1, far) for sign in (-1, 1)] + [far]
    table = [[ring[(ring.index(i) + s) % tp_size] for s in steps] for i in range(tp_size)]
    place = jnp.array(table, jnp.int32)[me]

    widened = hidden_in.astype(jnp.float32)
    normed = (
        widened
        * lax.rsqrt(jnp.mean(widened * widened, axis=-1, keepdims=True) + EPSILON)
        * norm_gain
    ).astype(jnp.bfloat16)
    normed, pool_cache = lax.optimization_barrier((normed, pool_cache))
    w_query, w_keyval, w_out = (
        pltpu.with_memory_space_constraint(w, pltpu.HBM) for w in (w_query, w_keyval, w_out)
    )
    middle = tp_size // 2
    mates = me // middle * middle + jnp.arange(middle, dtype=jnp.int32)
    offsets = jnp.cumsum(lengths) - lengths
    first_slot = mates * tokens
    slot_tokens = first_slot[:, None] + jnp.arange(tokens, dtype=jnp.int32)[None, :]
    cache_pos = offsets[:, None, None] + slot_tokens[None]
    is_valid = slot_tokens[None] < lengths[:, None, None]
    replaced = jnp.any(cache_pos[..., None] == selected, axis=-1)
    dead = jnp.where(is_valid & jnp.logical_not(replaced), 0.0, MASKED).astype(jnp.bfloat16)
    dead = jnp.broadcast_to(dead[..., None], (DOCS, middle, tokens, HD))
    dead = dead.reshape(DOCS, middle * tokens, HD)
    first_pos = jnp.where(
        first_slot[None] < lengths[:, None], offsets[:, None] + first_slot[None], FAR
    ).reshape(-1)
    cosine, sine_part = rotation_tables(selected)
    heads_here = w_query.shape[1] // HD
    tile_q = TILE_COLS // heads_here
    q_pos = jnp.tile(selected.reshape(SEL // tile_q, tile_q), (1, heads_here))
    q_pos = q_pos.reshape(SEL // tile_q, 1, TILE_COLS)

    part = width // CHUNKS
    streams = []
    for chunk in range(CHUNKS):
        own = normed[:, chunk * part : (chunk + 1) * part]
        streams.append({"before": [own], "behind": [own]})
    for k in range(1, far + 1):
        for chunk, held in enumerate(streams):
            if k < far or chunk % 2 == 0:
                held["before"].append(lax.ppermute(held["before"][-1], "tp", forth))
            if k < far or chunk % 2 == 1:
                held["behind"].append(lax.ppermute(held["behind"][-1], "tp", back))
        first = streams[0]["before"]
        if k == 1:
            by_kind = pool_cache.transpose(0, 2, 1, 3)
            sources = [by_kind]
            for shift in range(1, req_size):
                pairs = [((i + shift) % req_size, i) for i in range(req_size)]
                sources.append(lax.ppermute(by_kind, "req", pairs))
            holder = (doc_slot // slots - lax.axis_index("req")) % req_size
            slot = doc_slot % slots
            side = (me < middle).astype(jnp.int32)[None]
            takers = jnp.concatenate([mates, mates ^ middle]) * KVH // tp_size
        if k == 2:
            first[-1], dead, first_pos, cosine, sine_part, q_pos, takers, holder, slot, place, side = (
                lax.optimization_barrier(
                    (first[-1], dead, first_pos, cosine, sine_part, q_pos, takers, holder, slot)
                    + (place, side)
                )
            )
        if k == far - 1:
            sent = select_docs(sources, holder, slot, takers, middle)
            first[-1], *sent = lax.optimization_barrier((first[-1], *sent))
    projected = None
    for chunk, held in enumerate(streams):
        blocks = [held["before"][0]]
        for k in range(1, far):
            blocks += [held["before"][k], held["behind"][k]]
        blocks.append(held["behind" if chunk % 2 else "before"][far])
        if rows % 16:
            blocks = [jnp.concatenate(blocks, axis=0)]
        projected = project(
            place, blocks, w_query, w_keyval, projected, (cosine, sine_part), chunk
        )
    halves = [list(range(middle)), list(range(middle, tp_size))]

    def exchange(keys):
        return lax.all_to_all(keys, "tp", 0, 0, axis_index_groups=halves, tiled=True)

    theirs_kv = exchange(sent[1])
    mine_kv, theirs_kv = lax.optimization_barrier((sent[0], theirs_kv))
    chunks = [exchange(mine_kv), theirs_kv]
    queries = projected[:HALVES]
    n_tiles = queries[0].shape[0]
    across = [(i, i ^ middle) for i in range(tp_size)]
    their_queries = [None] * HALVES
    for part in reversed(range(HALVES)):
        their_queries[part] = lax.ppermute(queries[part], "tp", across)

    if tp_size == KVH:
        new = lax.ppermute(
            pick_new(side, queries[-1], their_queries[-1], n_tiles),
            "tp",
            [(i, 2 * i if i < middle else 2 * (i - middle) + 1) for i in range(tp_size)],
        )
    else:
        everyone = lax.all_gather(projected[-1], "tp", axis=1, tiled=True)
        my_head = me * KVH // tp_size
        new = jnp.concatenate(
            [
                lax.dynamic_slice_in_dim(everyone, (kind * KVH + my_head) * HD, HD, axis=1)
                for kind in range(2)
            ],
            axis=1,
        )

    def attend_half(part, asked, slot, extra):
        return attend(
            chunks[slot], dead, first_pos, selected, q_pos, asked[part], part * n_tiles, n_tiles, extra
        )

    theirs = [None] * HALVES
    for part in reversed(range(HALVES)):
        (packed,) = attend_half(part, their_queries, 1, [])
        if part:
            packed, new, their_queries[part - 1] = lax.optimization_barrier(
                (packed, new, their_queries[part - 1])
            )
        theirs[part] = lax.ppermute(packed, "tp", across)
    fresh = [cosine, sine_part, new]
    mine = [attend_half(part, queries, 0, fresh) for part in range(HALVES)]
    attention = merge(mine, theirs)

    finished = []
    for chunk in range(CHUNKS):
        kinds = [jnp.float32] * (tp_size - 1) + [jnp.bfloat16]
        pieces = project_out(place, attention, w_out, chunk, kinds)
        to_forth, to_back = list(pieces[2 : tp_size - 1 : 2]), list(pieces[1 : tp_size - 1 : 2])
        (to_back if chunk % 2 else to_forth).append(pieces[-1])
        total = pieces[0]
        for terms, pairs in ((to_forth, forth), (to_back, back)):
            held = None
            for term in reversed(terms):
                if held is not None:
                    term = term + held.astype(jnp.float32)
                held = lax.ppermute(term.astype(jnp.bfloat16), "tp", pairs)
            total = total + held.astype(jnp.float32)
        finished.append(total.astype(jnp.bfloat16))
    return jnp.concatenate(finished, axis=1)


def solution(mesh):
    placed = (
        P(("groups", "req", "tp"), None),
        P(),
        P(None, "tp"),
        P(None, "tp"),
        P("tp", None),
        P(("groups", "req"), "tp", None, None),
        P(("groups", "req")),
        P(("groups", "req"), None),
        P(("groups", "req"), None),
    )
    return jax.shard_map(
        per_device,
        mesh=mesh,
        in_specs=placed,
        out_specs=P(("groups", "req", "tp"), None),
        check_vma=False,
    )
```

```python
import functools
import math

import jax
import jax.numpy as jnp
from jax import lax
from jax.experimental import pallas as pl
from jax.experimental.pallas import tpu as pltpu
from jax.sharding import PartitionSpec as P

HEADS = 64
KVH = 8
HD = 128
DOCS = 4
BLOCK = 128
SEL = 256


EPSILON = 1e-05
ROPE_BASE = 500000.0
MASKED = -1e30
FAR = 1 << 30
CHUNKS = 2
TILE_COLS = 256
PAIR = 2
STATS = 16
HALVES = 2
DEPTH_TILE = 1024
WIDTH_TILE = 1024
SLOTS = 3
CUTS = 4


def cost(flops, bytes_accessed, transcendentals=0):
    return pl.CostEstimate(
        flops=int(flops), bytes_accessed=int(bytes_accessed), transcendentals=int(transcendentals)
    )


def rotation_tables(positions):
    half_dim = HD // 2
    inverse = ROPE_BASE ** (-(jnp.arange(half_dim, dtype=jnp.float32) * (2.0 / HD)))
    angles = positions.astype(jnp.float32)[:, None] * inverse[None, :]
    cosine = jnp.cos(angles)
    sine_part = jnp.sin(angles)
    return (
        jnp.concatenate([cosine, cosine], axis=-1),
        jnp.concatenate([-sine_part, sine_part], axis=-1),
    )


def rotate(values, cosine, sine_part):
    swapped = jnp.concatenate([values[:, HD // 2 :], values[:, : HD // 2]], axis=-1)
    return values * cosine + swapped * sine_part


def megabytes(count):
    return pltpu.CompilerParams(vmem_limit_bytes=count * 1024 * 1024)


def stream(sources, buffers, sems):
    def copies(step):
        slot = step % SLOTS
        made = []
        for i, (source, buffer) in enumerate(zip(sources, buffers)):
            rows = buffer.shape[1] // CUTS
            for cut in range(CUTS):
                here = pl.ds(cut * rows, rows)
                made.append(
                    pltpu.make_async_copy(
                        source(step).at[here], buffer.at[slot, here], sems.at[i * CUTS + cut, slot]
                    )
                )
        return made

    def start(step):
        for copy in copies(step):
            copy.start()

    def wait(step):
        for copy in copies(step):
            copy.wait()

    return start, wait


def project_kernel(n_blocks, chunk, is_last, place_ref, *refs):
    refs = list(refs)
    take = lambda count: [refs.pop(0) for _ in range(count)]
    blocks = take(n_blocks)
    wq_ref, wkv_ref = take(2)
    if chunk:
        prev_q, prev_kv = take(2)
    if is_last:
        cos_ref, sin_ref = take(2)
        total_q, total_kv, natural, natural_kv = refs[-7:-3]
        outs = refs[:-7]
    else:
        total_q, total_kv = take(2)
    wq_slots, wkv_slots, sems = refs[-3:]
    tile = wq_slots.shape[1]
    depth = blocks[0].shape[1]
    count = depth // tile
    rows_of = lambda ref: lambda step: ref.at[pl.ds(chunk * depth + step * tile, tile), :]
    start, wait = stream([rows_of(wq_ref), rows_of(wkv_ref)], [wq_slots, wkv_slots], sems)

    for step in range(min(SLOTS, count)):
        start(step)
    for step in range(count):
        wait(step)
        slot = step % SLOTS
        cols = slice(step * tile, (step + 1) * tile)
        rows = jnp.concatenate([b[:, cols] for b in blocks], axis=0)
        part_q = jnp.dot(rows, wq_slots[slot], preferred_element_type=jnp.float32)
        part_kv = jnp.dot(rows, wkv_slots[slot], preferred_element_type=jnp.float32)
        if step:
            total_q[...] += part_q
            total_kv[...] += part_kv
        elif chunk:
            total_q[...] = prev_q[...] + part_q
            total_kv[...] = prev_kv[...] + part_kv
        else:
            total_q[...] = part_q
            total_kv[...] = part_kv
        if step + SLOTS < count:
            start(step + SLOTS)

    if is_last:
        height = SEL // place_ref.shape[0]
        for block in range(SEL // height):
            here = slice(block * height, (block + 1) * height)
            there = pl.ds(pl.multiple_of(place_ref[block] * height, height), height)
            natural[there, :] = total_q[here, :]
            natural_kv[there, :] = total_kv[here, :]
        heads_here = total_q.shape[1] // HD
        tile_q = TILE_COLS // heads_here
        per_half = SEL // tile_q // HALVES
        for index in range(SEL // tile_q):
            here = slice(index * tile_q, (index + 1) * tile_q)
            stacked = jnp.concatenate(
                [
                    rotate(
                        natural[here, head * HD : (head + 1) * HD], cos_ref[here, :], sin_ref[here, :]
                    )
                    for head in range(heads_here)
                ],
                axis=0,
            )
            outs[index // per_half][index % per_half] = stacked.T.astype(jnp.bfloat16)
        if len(outs) > HALVES:
            outs[-1][...] = natural_kv[...].astype(jnp.bfloat16)
        else:
            for index in range(SEL // HD):
                outs[-1][per_half + index] = natural_kv[
                    index * HD : (index + 1) * HD, :
                ].astype(jnp.bfloat16)


def project(place, blocks, w_query, w_keyval, prev, tables, chunk):
    depth = blocks[0].shape[1]
    q_cols, kv_cols = w_query.shape[1], w_keyval.shape[1]
    tile = min(DEPTH_TILE, depth)
    is_last = chunk + 1 == CHUNKS
    vmem = pl.BlockSpec(memory_space=pltpu.VMEM)
    hbm = pl.BlockSpec(memory_space=pltpu.HBM)
    total = [((SEL, q_cols), jnp.float32), ((SEL, kv_cols), jnp.float32)]
    scratch = []
    if is_last:
        per_half = SEL * q_cols // (HD * TILE_COLS * HALVES)
        behind = SEL // HD if kv_cols == TILE_COLS else 0
        outs = [(per_half, HD, TILE_COLS)] * (HALVES - 1) + [(per_half + behind, HD, TILE_COLS)]
        if not behind:
            outs.append((SEL, kv_cols))
        outs = [(shape, jnp.bfloat16) for shape in outs]
        scratch = total + total
    else:
        outs = total
    extra = ([] if prev is None else list(prev)) + (list(tables) if is_last else [])
    return pl.pallas_call(
        functools.partial(project_kernel, len(blocks), chunk, is_last),
        in_specs=[pl.BlockSpec(memory_space=pltpu.SMEM)]
        + [vmem] * len(blocks)
        + [hbm] * 2
        + [vmem] * len(extra),
        out_specs=[vmem] * len(outs),
        out_shape=[jax.ShapeDtypeStruct(*o) for o in outs],
        scratch_shapes=[pltpu.VMEM(*x) for x in scratch]
        + [
            pltpu.VMEM((SLOTS, tile, q_cols), jnp.bfloat16),
            pltpu.VMEM((SLOTS, tile, kv_cols), jnp.bfloat16),
            pltpu.SemaphoreType.DMA((2 * CUTS, SLOTS)),
        ],
        compiler_params=megabytes(16),
        cost_estimate=cost(
            2 * SEL * depth * (q_cols + kv_cols), 2 * depth * (q_cols + kv_cols + SEL)
        ),
        name="project",
    )(place, *blocks, w_query, w_keyval, *extra)


def select_kernel(n_dest, n_src, place_ref, slot_ref, head_ref, *refs):
    sources = refs[:n_src]
    outs = refs[n_src : n_src + n_dest]
    sems = refs[n_src + n_dest]
    for doc in range(DOCS):
        for src in range(n_src):

            @pl.when(place_ref[doc] == src)
            def _():
                for dest in range(n_dest):
                    cols = pl.ds(pl.multiple_of(head_ref[dest] * HD, HD), HD)
                    pltpu.make_async_copy(
                        sources[src].at[slot_ref[doc], :, :, cols],
                        outs[dest].at[:, doc],
                        sems.at[dest, doc],
                    ).start()

    for dest in range(n_dest):
        for doc in range(DOCS):
            pltpu.make_async_copy(
                sources[0].at[0, :, :, 0:HD], outs[dest].at[:, doc], sems.at[dest, doc]
            ).wait()


def select_docs(sources, place, slot, heads, n_dest):
    tokens = sources[0].shape[2]
    shape = (2, DOCS, tokens, HD)
    smem = pl.BlockSpec(memory_space=pltpu.SMEM)
    return pl.pallas_call(
        functools.partial(select_kernel, n_dest, len(sources)),
        in_specs=[smem] * 3 + [pl.BlockSpec(memory_space=pl.ANY)] * len(sources),
        out_specs=[pl.BlockSpec(memory_space=pltpu.VMEM)] * n_dest,
        out_shape=[jax.ShapeDtypeStruct(shape, jnp.bfloat16)] * n_dest,
        scratch_shapes=[pltpu.SemaphoreType.DMA((n_dest, DOCS))],
        compiler_params=megabytes(8),
        cost_estimate=cost(0, 4 * n_dest * math.prod(shape)),
        name="select_docs",
    )(place, slot, heads, *sources)


def split_exact(value):
    pieces = []
    for _ in range(3):
        pieces.append(value.astype(jnp.bfloat16).astype(jnp.float32))
        value = value - pieces[-1]
    return pieces


def attend_kernel(n_chunks, with_new, n_tiles, tile_q, first_tile, first_ref, pos_ref, *refs):
    refs = list(refs)
    take = lambda count: [refs.pop(0) for _ in range(count)]
    chunks = take(n_chunks)
    dead_ref, qpos_ref, queries = take(3)
    if with_new:
        cos_ref, sin_ref, new_ref = take(3)
    if with_new:
        top, total, summed, values, new_key, new_value = take(6)
    else:
        packed, top, total, summed, values = take(5)
    together = min(PAIR, n_tiles)
    n_pairs = n_tiles // together
    tokens = chunks[0].shape[2]
    scale = math.log2(math.e) / math.sqrt(HD)

    for chunk in range(n_chunks):
        for doc in range(DOCS):
            values[doc, :, chunk * tokens : (chunk + 1) * tokens] = chunks[chunk][1, doc].T
    if with_new:
        new_key[...] = rotate(
            new_ref[:, :HD].astype(jnp.float32), cos_ref[...], sin_ref[...]
        ).astype(jnp.bfloat16)
        new_value[...] = new_ref[:, HD:].T

    one_row = jnp.where(
        lax.broadcasted_iota(jnp.int32, (HD, TILE_COLS), 0) == 0, 1.0, 0.0
    ).astype(jnp.bfloat16)

    def update(tile, parts):
        best = functools.reduce(
            jnp.maximum, [jnp.max(scores, axis=0, keepdims=True) for scores, _ in parts]
        )
        old = top[tile]
        new = jnp.maximum(old, best)
        shrink = jnp.exp2((old - new) * scale)
        running = total[tile] * shrink
        mixed = summed[tile] * shrink
        for scores, value in parts:
            weights = jnp.exp2((scores - new) * scale)
            running += jnp.sum(weights, axis=0, keepdims=True)
            mixed += jnp.dot(
                value, weights.astype(jnp.bfloat16), preferred_element_type=jnp.float32
            )
        top[tile] = new
        total[tile] = running
        summed[tile] = mixed

    @pl.loop(0, n_pairs)
    def _(pair):
        tiles = [pair * together + i for i in range(together)]
        for tile in tiles:
            top[tile] = jnp.full(top.shape[1:], MASKED, jnp.float32)
            total[tile] = jnp.zeros(total.shape[1:], jnp.float32)
            summed[tile] = jnp.zeros(summed.shape[1:], jnp.float32)
        if with_new:
            fresh = []
            for tile in tiles:
                scores = jnp.dot(new_key[...], queries[tile], preferred_element_type=jnp.float32)
                key_index = lax.broadcasted_iota(jnp.int32, scores.shape, 0)
                q_index = (first_tile + tile) * tile_q + lax.broadcasted_iota(jnp.int32, scores.shape, 1) % tile_q
                fresh.append(jnp.where(key_index <= q_index, scores, MASKED))
            for tile, scores in zip(tiles, fresh):
                update(tile, [(scores, new_value[...])])

        @pl.loop(0, DOCS)
        def _(doc):
            firsts = [first_ref[doc * n_chunks + chunk] for chunk in range(n_chunks)]
            lowest = functools.reduce(jnp.minimum, firsts)
            reach = functools.reduce(jnp.maximum, firsts) + tokens - 1

            def visit(masked):
                found = []
                for tile in tiles:
                    extended = jnp.concatenate([queries[tile], one_row], axis=0)
                    parts = []
                    for chunk in range(n_chunks):
                        span = slice(chunk * tokens, (chunk + 1) * tokens)
                        keys = jnp.concatenate(
                            [chunks[chunk][0, doc], dead_ref[doc, span, :]], axis=1
                        )
                        scores = jnp.dot(keys, extended, preferred_element_type=jnp.float32)
                        if masked:
                            key_pos = firsts[chunk] + lax.broadcasted_iota(
                                jnp.int32, scores.shape, 0
                            )
                            scores = jnp.where(key_pos <= qpos_ref[first_tile + tile], scores, MASKED)
                        parts.append((scores, values[doc, :, span]))
                    found.append(parts)
                for tile, parts in zip(tiles, found):
                    update(tile, parts)

            start = first_tile * tile_q + pair * together * tile_q
            live = lowest <= pos_ref[start + together * tile_q - 1]
            whole = reach <= pos_ref[start]

            @pl.when(live & whole)
            def _():
                visit(False)

            @pl.when(live & jnp.logical_not(whole))
            def _():
                visit(True)

        if not with_new:
            for tile in tiles:
                extra = jnp.concatenate(
                    split_exact(top[tile])
                    + split_exact(total[tile])
                    + [jnp.zeros((STATS - 6, TILE_COLS), jnp.float32)],
                    axis=0,
                )
                packed[tile] = jnp.concatenate([summed[tile], extra], axis=0).astype(jnp.bfloat16)


def attend(chunks, dead, first_pos, selected, q_pos, queries, first_tile, n_tiles, fresh):
    n_chunks = len(chunks)
    tokens = chunks[0].shape[2]
    tile_q = SEL // q_pos.shape[0]
    smem = pl.BlockSpec(memory_space=pltpu.SMEM)
    vmem = pl.BlockSpec(memory_space=pltpu.VMEM)
    operands = [first_pos, selected, *chunks, dead, q_pos, queries, *fresh]
    state = [((n_tiles, 1, TILE_COLS), jnp.float32)] * 2
    state += [((n_tiles, HD, TILE_COLS), jnp.float32)]
    values = ((DOCS, HD, n_chunks * tokens), jnp.bfloat16)
    if fresh:
        outs = state
        scratch = [values, ((SEL, HD), jnp.bfloat16), ((HD, SEL), jnp.bfloat16)]
    else:
        outs = [((n_tiles, HD + STATS, TILE_COLS), jnp.bfloat16)]
        scratch = state + [values]
    pairs = n_tiles * TILE_COLS * DOCS * n_chunks * tokens // 2
    return pl.pallas_call(
        functools.partial(
            attend_kernel, n_chunks, bool(fresh), n_tiles, tile_q, first_tile
        ),
        in_specs=[smem] * 2 + [vmem] * (len(operands) - 2),
        out_specs=[vmem] * len(outs),
        out_shape=[jax.ShapeDtypeStruct(*s) for s in outs],
        scratch_shapes=[pltpu.VMEM(*s) for s in scratch],
        compiler_params=megabytes(16),
        cost_estimate=cost(4 * pairs * HD, 4 * DOCS * n_chunks * tokens * HD, pairs),
        name="attend",
    )(*operands)


def pick_kernel(n_tiles, side_ref, here_ref, there_ref, out_ref):
    def pick(keys_ref, values_ref, head):
        cols = slice(head * HD, (head + 1) * HD)
        for index in range(SEL // HD):
            rows = slice(index * HD, (index + 1) * HD)
            out_ref[rows, :HD] = keys_ref[n_tiles + index][:, cols]
            out_ref[rows, HD:] = values_ref[n_tiles + index][:, cols]

    @pl.when(side_ref[0] == 1)
    def _():
        pick(here_ref, there_ref, 0)

    @pl.when(side_ref[0] == 0)
    def _():
        pick(there_ref, here_ref, 1)


def pick_new(side, here, there, n_tiles):
    vmem = pl.BlockSpec(memory_space=pltpu.VMEM)
    return pl.pallas_call(
        functools.partial(pick_kernel, n_tiles),
        in_specs=[pl.BlockSpec(memory_space=pltpu.SMEM), vmem, vmem],
        out_specs=vmem,
        out_shape=jax.ShapeDtypeStruct((SEL, 2 * HD), jnp.bfloat16),
        compiler_params=megabytes(4),
        cost_estimate=cost(0, 8 * SEL * HD),
        name="pick_new",
    )(side, here, there)


def merge_kernel(*refs):
    out_ref = refs[-1]
    scale = math.log2(math.e) / math.sqrt(HD)
    for half in range(HALVES):
        top_a, total_a, mixed_a, packed = refs[4 * half : 4 * half + 4]
        n_tiles = top_a.shape[0]
        tile_q = SEL // HALVES // n_tiles
        for tile in range(n_tiles):
            extra = packed[tile, HD:, :].astype(jnp.float32)
            top_b = extra[0:1] + (extra[1:2] + extra[2:3])
            total_b = extra[3:4] + (extra[4:5] + extra[5:6])
            new = jnp.maximum(top_a[tile], top_b)
            part_a = jnp.exp2((top_a[tile] - new) * scale)
            part_b = jnp.exp2((top_b - new) * scale)
            total = total_a[tile] * part_a + total_b * part_b
            mixed = mixed_a[tile] * part_a + packed[tile, :HD, :].astype(jnp.float32) * part_b
            finished = (mixed / total).T.astype(jnp.bfloat16)
            here = slice((half * n_tiles + tile) * tile_q, (half * n_tiles + tile + 1) * tile_q)
            for head in range(TILE_COLS // tile_q):
                out_ref[here, head * HD : (head + 1) * HD] = finished[
                    head * tile_q : (head + 1) * tile_q, :
                ]


def merge(mine, theirs):
    n_tiles = mine[0][0].shape[0] * HALVES
    shape = (SEL, TILE_COLS * n_tiles // SEL * HD)
    operands = [a for state, packed in zip(mine, theirs) for a in (*state, packed)]
    return pl.pallas_call(
        merge_kernel,
        out_shape=jax.ShapeDtypeStruct(shape, jnp.bfloat16),
        compiler_params=megabytes(16),
        cost_estimate=cost(4 * math.prod(shape), 8 * math.prod(shape)),
        name="merge",
    )(*operands)


def out_kernel(n_blocks, first_col, place_ref, x_ref, w_ref, *refs):
    outs = refs[:n_blocks]
    ordered, slots, sems = refs[n_blocks:]
    rows = SEL // n_blocks
    tile = slots.shape[2]
    count = outs[0].shape[1] // tile
    start, wait = stream(
        [lambda step: w_ref.at[:, pl.ds(first_col + step * tile, tile)]], [slots], sems
    )

    for step in range(min(SLOTS, count)):
        start(step)
    for block in range(n_blocks):
        there = pl.ds(pl.multiple_of(place_ref[block] * rows, rows), rows)
        ordered[block * rows : (block + 1) * rows, :] = x_ref[there, :]
    for step in range(count):
        wait(step)
        product = jnp.dot(
            ordered[...].astype(jnp.bfloat16),
            slots[step % SLOTS],
            preferred_element_type=jnp.float32,
        )
        cols = slice(step * tile, (step + 1) * tile)
        for block, out in enumerate(outs):
            out[:, cols] = product[block * rows : (block + 1) * rows, :].astype(out.dtype)
        if step + SLOTS < count:
            start(step + SLOTS)


def project_out(place, attention, w_out, chunk, kinds):
    depth = w_out.shape[0]
    n_blocks = len(kinds)
    width = w_out.shape[1] // CHUNKS
    rows = SEL // n_blocks
    if rows % 16:
        attention = attention.astype(jnp.float32)
    vmem = pl.BlockSpec(memory_space=pltpu.VMEM)
    return pl.pallas_call(
        functools.partial(out_kernel, n_blocks, chunk * width),
        in_specs=[
            pl.BlockSpec(memory_space=pltpu.SMEM),
            vmem,
            pl.BlockSpec(memory_space=pltpu.HBM),
        ],
        out_specs=[vmem] * n_blocks,
        out_shape=[jax.ShapeDtypeStruct((rows, width), kind) for kind in kinds],
        scratch_shapes=[
            pltpu.VMEM((SEL, depth), attention.dtype),
            pltpu.VMEM((SLOTS, depth, min(WIDTH_TILE, width)), jnp.bfloat16),
            pltpu.SemaphoreType.DMA((CUTS, SLOTS)),
        ],
        compiler_params=megabytes(16),
        cost_estimate=cost(2 * SEL * depth * width, 2 * depth * (width + SEL) + 4 * SEL * width),
        name="project_out",
    )(place, attention, w_out)


def per_device(
    hidden_in, norm_gain, w_query, w_keyval, w_out, pool_cache, doc_slot, doc_blocks, sel_pos
):
    tp_size = lax.axis_size("tp")
    req_size = lax.axis_size("req")
    me = lax.axis_index("tp")
    rows, width = hidden_in.shape
    slots, tokens = pool_cache.shape[:2]
    heads_here = w_query.shape[1] // HD
    selected = sel_pos[0]
    lengths = doc_blocks[0] * BLOCK

    if tp_size == KVH:
        ring = [*range(0, tp_size, 2), *range(tp_size - 1, 0, -2)]
    else:
        ring = list(range(tp_size))
    far = tp_size // 2
    forth = [(ring[p], ring[(p + 1) % tp_size]) for p in range(tp_size)]
    back = [(dst, src) for src, dst in forth]
    steps = [0] + [sign * k for k in range(1, far) for sign in (-1, 1)] + [far]
    table = [[ring[(ring.index(i) + s) % tp_size] for s in steps] for i in range(tp_size)]
    place = jnp.array(table, jnp.int32)[me]

    widened = hidden_in.astype(jnp.float32)
    normed = (
        widened
        * lax.rsqrt(jnp.mean(widened * widened, axis=-1, keepdims=True) + EPSILON)
        * norm_gain
    ).astype(jnp.bfloat16)
    normed, pool_cache = lax.optimization_barrier((normed, pool_cache))
    w_query, w_keyval, w_out = (
        pltpu.with_memory_space_constraint(w, pltpu.HBM) for w in (w_query, w_keyval, w_out)
    )
    middle = tp_size // 2
    order = jnp.arange(middle, dtype=jnp.int32)
    offsets = jnp.cumsum(lengths) - lengths
    first_slot = (me ^ order) * tokens
    slot_tokens = first_slot[:, None] + jnp.arange(tokens, dtype=jnp.int32)[None, :]
    cache_pos = offsets[:, None, None] + slot_tokens[None]
    is_valid = slot_tokens[None] < lengths[:, None, None]
    replaced = jnp.any(cache_pos[..., None] == selected, axis=-1)
    dead = jnp.where(is_valid & jnp.logical_not(replaced), 0.0, MASKED).astype(jnp.bfloat16)
    dead = jnp.broadcast_to(dead[..., None], (DOCS, middle, tokens, HD))
    dead = dead.reshape(DOCS, middle * tokens, HD)
    first_pos = jnp.where(
        first_slot[None] < lengths[:, None], offsets[:, None] + first_slot[None], FAR
    ).reshape(-1)
    cosine, sine_part = rotation_tables(selected)
    heads_here = w_query.shape[1] // HD
    tile_q = TILE_COLS // heads_here
    q_pos = jnp.tile(selected.reshape(SEL // tile_q, tile_q), (1, heads_here))
    q_pos = q_pos.reshape(SEL // tile_q, 1, TILE_COLS)

    part = width // CHUNKS
    streams = []
    for chunk in range(CHUNKS):
        own = normed[:, chunk * part : (chunk + 1) * part]
        streams.append({"before": [own], "behind": [own]})
    for k in range(1, far + 1):
        for chunk, held in enumerate(streams):
            if k < far or chunk % 2 == 0:
                held["before"].append(lax.ppermute(held["before"][-1], "tp", forth))
            if k < far or chunk % 2 == 1:
                held["behind"].append(lax.ppermute(held["behind"][-1], "tp", back))
        first = streams[0]["before"]
        if k == 1:
            by_kind = pool_cache.transpose(0, 2, 1, 3)
            sources = [by_kind]
            for shift in range(1, req_size):
                pairs = [((i + shift) % req_size, i) for i in range(req_size)]
                sources.append(lax.ppermute(by_kind, "req", pairs))
            holder = (doc_slot // slots - lax.axis_index("req")) % req_size
            slot = doc_slot % slots
            side = (me < middle).astype(jnp.int32)[None]
            takers = jnp.concatenate([me ^ order, me ^ order ^ middle]) * KVH // tp_size
        if k == 2:
            first[-1], dead, first_pos, cosine, sine_part, q_pos, takers, holder, slot, place, side = (
                lax.optimization_barrier(
                    (first[-1], dead, first_pos, cosine, sine_part, q_pos, takers, holder, slot)
                    + (place, side)
                )
            )
        if k == far - 1:
            sent = select_docs(sources, holder, slot, takers, tp_size)
            first[-1], *sent = lax.optimization_barrier((first[-1], *sent))
    projected = None
    for chunk, held in enumerate(streams):
        blocks = [held["before"][0]]
        for k in range(1, far):
            blocks += [held["before"][k], held["behind"][k]]
        blocks.append(held["behind" if chunk % 2 else "before"][far])
        if rows % 16:
            blocks = [jnp.concatenate(blocks, axis=0)]
        projected = project(
            place, blocks, w_query, w_keyval, projected, (cosine, sine_part), chunk
        )
    def exchange(kept):
        return [
            lax.ppermute(kept[j], "tp", [(i, i ^ j) for i in range(tp_size)]) if j else kept[j]
            for j in range(middle)
        ]

    own, partners = sent[:middle], exchange(sent[middle:])
    own, partners = lax.optimization_barrier((own, partners))
    chunks = [exchange(own), partners]
    queries = projected[:HALVES]
    n_tiles = queries[0].shape[0]
    across = [(i, i ^ middle) for i in range(tp_size)]
    their_queries = [None] * HALVES
    for part in reversed(range(HALVES)):
        their_queries[part] = lax.ppermute(queries[part], "tp", across)

    if tp_size == KVH:
        new = lax.ppermute(
            pick_new(side, queries[-1], their_queries[-1], n_tiles),
            "tp",
            [(i, 2 * i if i < middle else 2 * (i - middle) + 1) for i in range(tp_size)],
        )
    else:
        everyone = lax.all_gather(projected[-1], "tp", axis=1, tiled=True)
        my_head = me * KVH // tp_size
        new = jnp.concatenate(
            [
                lax.dynamic_slice_in_dim(everyone, (kind * KVH + my_head) * HD, HD, axis=1)
                for kind in range(2)
            ],
            axis=1,
        )

    def attend_half(part, asked, slot, extra):
        return attend(
            chunks[slot], dead, first_pos, selected, q_pos, asked[part], part * n_tiles, n_tiles, extra
        )

    theirs = [None] * HALVES
    for part in reversed(range(HALVES)):
        (packed,) = attend_half(part, their_queries, 1, [])
        if part:
            packed, new, their_queries[part - 1] = lax.optimization_barrier(
                (packed, new, their_queries[part - 1])
            )
        theirs[part] = lax.ppermute(packed, "tp", across)
    fresh = [cosine, sine_part, new]
    mine = [attend_half(part, queries, 0, fresh) for part in range(HALVES)]
    attention = merge(mine, theirs)

    finished = []
    for chunk in range(CHUNKS):
        kinds = [jnp.float32] * (tp_size - 1) + [jnp.bfloat16]
        pieces = project_out(place, attention, w_out, chunk, kinds)
        to_forth, to_back = list(pieces[2 : tp_size - 1 : 2]), list(pieces[1 : tp_size - 1 : 2])
        (to_back if chunk % 2 else to_forth).append(pieces[-1])
        total = pieces[0]
        for terms, pairs in ((to_forth, forth), (to_back, back)):
            held = None
            for term in reversed(terms):
                if held is not None:
                    term = term + held.astype(jnp.float32)
                held = lax.ppermute(term.astype(jnp.bfloat16), "tp", pairs)
            total = total + held.astype(jnp.float32)
        finished.append(total.astype(jnp.bfloat16))
    return jnp.concatenate(finished, axis=1)


def solution(mesh):
    placed = (
        P(("groups", "req", "tp"), None),
        P(),
        P(None, "tp"),
        P(None, "tp"),
        P("tp", None),
        P(("groups", "req"), "tp", None, None),
        P(("groups", "req")),
        P(("groups", "req"), None),
        P(("groups", "req"), None),
    )
    return jax.shard_map(
        per_device,
        mesh=mesh,
        in_specs=placed,
        out_specs=P(("groups", "req", "tp"), None),
        check_vma=False,
    )
```

```python
import functools
import math

import jax
import jax.numpy as jnp
from jax import lax
from jax.experimental import pallas as pl
from jax.experimental.pallas import tpu as pltpu
from jax.sharding import PartitionSpec as P

HEADS = 64
KVH = 8
HD = 128
DOCS = 4
BLOCK = 128
SEL = 256


EPSILON = 1e-05
ROPE_BASE = 500000.0
MASKED = -1e30
FAR = 1 << 30
CHUNKS = 2
TILE_COLS = 256
PAIR = 2
STATS = 16
HALVES = 2
DEPTH_TILE = 1024
WIDTH_TILE = 1024
SLOTS = 3
CUTS = 4


def cost(flops, bytes_accessed, transcendentals=0):
    return pl.CostEstimate(
        flops=int(flops), bytes_accessed=int(bytes_accessed), transcendentals=int(transcendentals)
    )


def rotation_tables(positions):
    half_dim = HD // 2
    inverse = ROPE_BASE ** (-(jnp.arange(half_dim, dtype=jnp.float32) * (2.0 / HD)))
    angles = positions.astype(jnp.float32)[:, None] * inverse[None, :]
    cosine = jnp.cos(angles)
    sine_part = jnp.sin(angles)
    return (
        jnp.concatenate([cosine, cosine], axis=-1),
        jnp.concatenate([-sine_part, sine_part], axis=-1),
    )


def rotate(values, cosine, sine_part):
    swapped = jnp.concatenate([values[:, HD // 2 :], values[:, : HD // 2]], axis=-1)
    return values * cosine + swapped * sine_part


def megabytes(count):
    return pltpu.CompilerParams(vmem_limit_bytes=count * 1024 * 1024)


def stream(sources, buffers, sems):
    def copies(step):
        slot = step % SLOTS
        made = []
        for i, (source, buffer) in enumerate(zip(sources, buffers)):
            rows = buffer.shape[1] // CUTS
            for cut in range(CUTS):
                here = pl.ds(cut * rows, rows)
                made.append(
                    pltpu.make_async_copy(
                        source(step).at[here], buffer.at[slot, here], sems.at[i * CUTS + cut, slot]
                    )
                )
        return made

    def start(step):
        for copy in copies(step):
            copy.start()

    def wait(step):
        for copy in copies(step):
            copy.wait()

    return start, wait


def project_kernel(n_blocks, chunk, is_last, place_ref, *refs):
    refs = list(refs)
    take = lambda count: [refs.pop(0) for _ in range(count)]
    blocks = take(n_blocks)
    wq_ref, wkv_ref = take(2)
    if chunk:
        prev_q, prev_kv = take(2)
    if is_last:
        cos_ref, sin_ref = take(2)
        total_q, total_kv, natural, natural_kv = refs[-7:-3]
        outs = refs[:-7]
    else:
        total_q, total_kv = take(2)
    wq_slots, wkv_slots, sems = refs[-3:]
    tile = wq_slots.shape[1]
    depth = blocks[0].shape[1]
    count = depth // tile
    rows_of = lambda ref: lambda step: ref.at[pl.ds(chunk * depth + step * tile, tile), :]
    start, wait = stream([rows_of(wq_ref), rows_of(wkv_ref)], [wq_slots, wkv_slots], sems)

    for step in range(min(SLOTS, count)):
        start(step)
    for step in range(count):
        wait(step)
        slot = step % SLOTS
        cols = slice(step * tile, (step + 1) * tile)
        rows = jnp.concatenate([b[:, cols] for b in blocks], axis=0)
        part_q = jnp.dot(rows, wq_slots[slot], preferred_element_type=jnp.float32)
        part_kv = jnp.dot(rows, wkv_slots[slot], preferred_element_type=jnp.float32)
        if step:
            total_q[...] += part_q
            total_kv[...] += part_kv
        elif chunk:
            total_q[...] = prev_q[...] + part_q
            total_kv[...] = prev_kv[...] + part_kv
        else:
            total_q[...] = part_q
            total_kv[...] = part_kv
        if step + SLOTS < count:
            start(step + SLOTS)

    if is_last:
        height = SEL // place_ref.shape[0]
        for block in range(SEL // height):
            here = slice(block * height, (block + 1) * height)
            there = pl.ds(pl.multiple_of(place_ref[block] * height, height), height)
            natural[there, :] = total_q[here, :]
            natural_kv[there, :] = total_kv[here, :]
        heads_here = total_q.shape[1] // HD
        tile_q = TILE_COLS // heads_here
        per_half = SEL // tile_q // HALVES
        for index in range(SEL // tile_q):
            here = slice(index * tile_q, (index + 1) * tile_q)
            stacked = jnp.concatenate(
                [
                    rotate(
                        natural[here, head * HD : (head + 1) * HD], cos_ref[here, :], sin_ref[here, :]
                    )
                    for head in range(heads_here)
                ],
                axis=0,
            )
            outs[index // per_half][index % per_half] = stacked.T.astype(jnp.bfloat16)
        if len(outs) > HALVES:
            outs[-1][...] = natural_kv[...].astype(jnp.bfloat16)
        else:
            for index in range(SEL // HD):
                outs[-1][per_half + index] = natural_kv[
                    index * HD : (index + 1) * HD, :
                ].astype(jnp.bfloat16)


def project(place, blocks, w_query, w_keyval, prev, tables, chunk):
    depth = blocks[0].shape[1]
    q_cols, kv_cols = w_query.shape[1], w_keyval.shape[1]
    tile = min(DEPTH_TILE, depth)
    is_last = chunk + 1 == CHUNKS
    vmem = pl.BlockSpec(memory_space=pltpu.VMEM)
    hbm = pl.BlockSpec(memory_space=pltpu.HBM)
    total = [((SEL, q_cols), jnp.float32), ((SEL, kv_cols), jnp.float32)]
    scratch = []
    if is_last:
        per_half = SEL * q_cols // (HD * TILE_COLS * HALVES)
        behind = SEL // HD if kv_cols == TILE_COLS else 0
        outs = [(per_half, HD, TILE_COLS)] * (HALVES - 1) + [(per_half + behind, HD, TILE_COLS)]
        if not behind:
            outs.append((SEL, kv_cols))
        outs = [(shape, jnp.bfloat16) for shape in outs]
        scratch = total + total
    else:
        outs = total
    extra = ([] if prev is None else list(prev)) + (list(tables) if is_last else [])
    return pl.pallas_call(
        functools.partial(project_kernel, len(blocks), chunk, is_last),
        in_specs=[pl.BlockSpec(memory_space=pltpu.SMEM)]
        + [vmem] * len(blocks)
        + [hbm] * 2
        + [vmem] * len(extra),
        out_specs=[vmem] * len(outs),
        out_shape=[jax.ShapeDtypeStruct(*o) for o in outs],
        scratch_shapes=[pltpu.VMEM(*x) for x in scratch]
        + [
            pltpu.VMEM((SLOTS, tile, q_cols), jnp.bfloat16),
            pltpu.VMEM((SLOTS, tile, kv_cols), jnp.bfloat16),
            pltpu.SemaphoreType.DMA((2 * CUTS, SLOTS)),
        ],
        compiler_params=megabytes(16),
        cost_estimate=cost(
            2 * SEL * depth * (q_cols + kv_cols), 2 * depth * (q_cols + kv_cols + SEL)
        ),
        name="project",
    )(place, *blocks, w_query, w_keyval, *extra)


def select_kernel(targets_of, n_src, place_ref, slot_ref, head_ref, *refs):
    sources = refs[:n_src]
    outs = refs[n_src:-1]
    sems = refs[-1]
    targets = [
        outs[out] if slot is None else outs[out].at[slot] for out, slot in targets_of
    ]
    for doc in range(DOCS):
        for src in range(n_src):

            @pl.when(place_ref[doc] == src)
            def _():
                for i, target in enumerate(targets):
                    cols = pl.ds(pl.multiple_of(head_ref[i] * HD, HD), HD)
                    pltpu.make_async_copy(
                        sources[src].at[slot_ref[doc], :, :, cols], target.at[:, doc], sems.at[i, doc]
                    ).start()

    for i, target in enumerate(targets):
        for doc in range(DOCS):
            pltpu.make_async_copy(
                sources[0].at[0, :, :, 0:HD], target.at[:, doc], sems.at[i, doc]
            ).wait()


def select_docs(sources, place, slot, heads, targets_of):
    tokens = sources[0].shape[2]
    one = (2, DOCS, tokens, HD)
    n_outs = 1 + max(out for out, _ in targets_of)
    shapes = [one] * n_outs
    for out, index in targets_of:
        if index is not None:
            shapes[out] = (2, *one)
    smem = pl.BlockSpec(memory_space=pltpu.SMEM)
    return pl.pallas_call(
        functools.partial(select_kernel, targets_of, len(sources)),
        in_specs=[smem] * 3 + [pl.BlockSpec(memory_space=pl.ANY)] * len(sources),
        out_specs=[pl.BlockSpec(memory_space=pltpu.VMEM)] * n_outs,
        out_shape=[jax.ShapeDtypeStruct(shape, jnp.bfloat16) for shape in shapes],
        scratch_shapes=[pltpu.SemaphoreType.DMA((len(targets_of), DOCS))],
        compiler_params=megabytes(8),
        cost_estimate=cost(0, 4 * len(targets_of) * math.prod(one)),
        name="select_docs",
    )(place, slot, heads, *sources)


def split_exact(value):
    pieces = []
    for _ in range(3):
        pieces.append(value.astype(jnp.bfloat16).astype(jnp.float32))
        value = value - pieces[-1]
    return pieces


def attend_kernel(slots, offset, packs, has_state, has_new, n_tiles, tile_q, first_tile, *refs):
    refs = list(refs)
    take = lambda count: [refs.pop(0) for _ in range(count)]
    n_chunks = len(slots)
    first_ref, pos_ref = take(2)
    chunks = [ref if slot is None else ref.at[slot] for ref, slot in zip(take(n_chunks), slots)]
    dead_ref, qpos_ref, queries = take(3)
    if has_state:
        old_top, old_total, old_summed = take(3)
    if has_new:
        cos_ref, sin_ref, new_ref = take(3)
    if packs:
        (packed,) = take(1)
    top, total, summed, values = take(4)
    if has_new:
        new_key, new_value = take(2)
    together = min(PAIR, n_tiles)
    n_pairs = n_tiles // together
    all_chunks, tokens = dead_ref.shape[0], dead_ref.shape[2]
    scale = math.log2(math.e) / math.sqrt(HD)

    for chunk in range(n_chunks):
        for doc in range(DOCS):
            values[doc, :, chunk * tokens : (chunk + 1) * tokens] = chunks[chunk][1, doc].T
    if has_new:
        new_key[...] = rotate(
            new_ref[:, :HD].astype(jnp.float32), cos_ref[...], sin_ref[...]
        ).astype(jnp.bfloat16)
        new_value[...] = new_ref[:, HD:].T

    one_row = jnp.where(
        lax.broadcasted_iota(jnp.int32, (HD, TILE_COLS), 0) == 0, 1.0, 0.0
    ).astype(jnp.bfloat16)

    def update(tile, parts):
        best = functools.reduce(
            jnp.maximum, [jnp.max(scores, axis=0, keepdims=True) for scores, _ in parts]
        )
        old = top[tile]
        new = jnp.maximum(old, best)
        shrink = jnp.exp2((old - new) * scale)
        running = total[tile] * shrink
        mixed = summed[tile] * shrink
        for scores, value in parts:
            weights = jnp.exp2((scores - new) * scale)
            running += jnp.sum(weights, axis=0, keepdims=True)
            mixed += jnp.dot(
                value, weights.astype(jnp.bfloat16), preferred_element_type=jnp.float32
            )
        top[tile] = new
        total[tile] = running
        summed[tile] = mixed

    @pl.loop(0, n_pairs)
    def _(pair):
        tiles = [pair * together + i for i in range(together)]
        for tile in tiles:
            if has_state:
                top[tile] = old_top[tile]
                total[tile] = old_total[tile]
                summed[tile] = old_summed[tile]
            else:
                top[tile] = jnp.full(top.shape[1:], MASKED, jnp.float32)
                total[tile] = jnp.zeros(total.shape[1:], jnp.float32)
                summed[tile] = jnp.zeros(summed.shape[1:], jnp.float32)
        if has_new:
            fresh = []
            for tile in tiles:
                scores = jnp.dot(new_key[...], queries[tile], preferred_element_type=jnp.float32)
                key_index = lax.broadcasted_iota(jnp.int32, scores.shape, 0)
                q_index = (first_tile + tile) * tile_q + lax.broadcasted_iota(jnp.int32, scores.shape, 1) % tile_q
                fresh.append(jnp.where(key_index <= q_index, scores, MASKED))
            for tile, scores in zip(tiles, fresh):
                update(tile, [(scores, new_value[...])])

        @pl.loop(0, DOCS)
        def _(doc):
            firsts = [first_ref[doc * all_chunks + offset + chunk] for chunk in range(n_chunks)]
            lowest = functools.reduce(jnp.minimum, firsts)
            reach = functools.reduce(jnp.maximum, firsts) + tokens - 1

            def visit(masked):
                found = []
                for tile in tiles:
                    extended = jnp.concatenate([queries[tile], one_row], axis=0)
                    parts = []
                    for chunk in range(n_chunks):
                        span = slice(chunk * tokens, (chunk + 1) * tokens)
                        keys = jnp.concatenate(
                            [chunks[chunk][0, doc], dead_ref[offset + chunk, doc]], axis=1
                        )
                        scores = jnp.dot(keys, extended, preferred_element_type=jnp.float32)
                        if masked:
                            key_pos = firsts[chunk] + lax.broadcasted_iota(
                                jnp.int32, scores.shape, 0
                            )
                            scores = jnp.where(key_pos <= qpos_ref[first_tile + tile], scores, MASKED)
                        parts.append((scores, values[doc, :, span]))
                    found.append(parts)
                for tile, parts in zip(tiles, found):
                    update(tile, parts)

            start = first_tile * tile_q + pair * together * tile_q
            live = lowest <= pos_ref[start + together * tile_q - 1]
            whole = reach <= pos_ref[start]

            @pl.when(live & whole)
            def _():
                visit(False)

            @pl.when(live & jnp.logical_not(whole))
            def _():
                visit(True)

        if packs:
            for tile in tiles:
                extra = jnp.concatenate(
                    split_exact(top[tile])
                    + split_exact(total[tile])
                    + [jnp.zeros((STATS - 6, TILE_COLS), jnp.float32)],
                    axis=0,
                )
                packed[tile] = jnp.concatenate([summed[tile], extra], axis=0).astype(jnp.bfloat16)


def attend(chunks, offset, metadata, queries, first_tile, n_tiles, state=(), fresh=(), packs=False):
    first_pos, selected, dead, q_pos = metadata
    n_chunks, tokens = len(chunks), dead.shape[2]
    tile_q = SEL // q_pos.shape[0]
    smem = pl.BlockSpec(memory_space=pltpu.SMEM)
    vmem = pl.BlockSpec(memory_space=pltpu.VMEM)
    operands = [first_pos, selected, *[keys for keys, _ in chunks], dead, q_pos, queries]
    operands += [*state, *fresh]
    outs = [((n_tiles, 1, TILE_COLS), jnp.float32)] * 2
    outs += [((n_tiles, HD, TILE_COLS), jnp.float32)]
    scratch = [((DOCS, HD, n_chunks * tokens), jnp.bfloat16)]
    if packs:
        outs, scratch = [((n_tiles, HD + STATS, TILE_COLS), jnp.bfloat16)], outs + scratch
    if fresh:
        scratch = scratch + [((SEL, HD), jnp.bfloat16), ((HD, SEL), jnp.bfloat16)]
    pairs = n_tiles * TILE_COLS * DOCS * n_chunks * tokens // 2
    return pl.pallas_call(
        functools.partial(
            attend_kernel,
            [slot for _, slot in chunks],
            offset,
            packs,
            bool(state),
            bool(fresh),
            n_tiles,
            tile_q,
            first_tile,
        ),
        in_specs=[smem] * 2 + [vmem] * (len(operands) - 2),
        out_specs=[vmem] * len(outs),
        out_shape=[jax.ShapeDtypeStruct(*o) for o in outs],
        scratch_shapes=[pltpu.VMEM(*x) for x in scratch],
        compiler_params=megabytes(16),
        cost_estimate=cost(4 * pairs * HD, 4 * DOCS * n_chunks * tokens * HD, pairs),
        name="attend",
    )(*operands)


def pick_kernel(n_tiles, side_ref, here_ref, there_ref, out_ref):
    def pick(keys_ref, values_ref, head):
        cols = slice(head * HD, (head + 1) * HD)
        for index in range(SEL // HD):
            rows = slice(index * HD, (index + 1) * HD)
            out_ref[rows, :HD] = keys_ref[n_tiles + index][:, cols]
            out_ref[rows, HD:] = values_ref[n_tiles + index][:, cols]

    @pl.when(side_ref[0] == 1)
    def _():
        pick(here_ref, there_ref, 0)

    @pl.when(side_ref[0] == 0)
    def _():
        pick(there_ref, here_ref, 1)


def pick_new(side, here, there, n_tiles):
    vmem = pl.BlockSpec(memory_space=pltpu.VMEM)
    return pl.pallas_call(
        functools.partial(pick_kernel, n_tiles),
        in_specs=[pl.BlockSpec(memory_space=pltpu.SMEM), vmem, vmem],
        out_specs=vmem,
        out_shape=jax.ShapeDtypeStruct((SEL, 2 * HD), jnp.bfloat16),
        compiler_params=megabytes(4),
        cost_estimate=cost(0, 8 * SEL * HD),
        name="pick_new",
    )(side, here, there)


def merge_kernel(*refs):
    out_ref = refs[-1]
    scale = math.log2(math.e) / math.sqrt(HD)
    for half in range(HALVES):
        top_a, total_a, mixed_a, packed = refs[4 * half : 4 * half + 4]
        n_tiles = top_a.shape[0]
        tile_q = SEL // HALVES // n_tiles
        for tile in range(n_tiles):
            extra = packed[tile, HD:, :].astype(jnp.float32)
            top_b = extra[0:1] + (extra[1:2] + extra[2:3])
            total_b = extra[3:4] + (extra[4:5] + extra[5:6])
            new = jnp.maximum(top_a[tile], top_b)
            part_a = jnp.exp2((top_a[tile] - new) * scale)
            part_b = jnp.exp2((top_b - new) * scale)
            total = total_a[tile] * part_a + total_b * part_b
            mixed = mixed_a[tile] * part_a + packed[tile, :HD, :].astype(jnp.float32) * part_b
            finished = (mixed / total).T.astype(jnp.bfloat16)
            here = slice((half * n_tiles + tile) * tile_q, (half * n_tiles + tile + 1) * tile_q)
            for head in range(TILE_COLS // tile_q):
                out_ref[here, head * HD : (head + 1) * HD] = finished[
                    head * tile_q : (head + 1) * tile_q, :
                ]


def merge(mine, theirs):
    n_tiles = mine[0][0].shape[0] * HALVES
    shape = (SEL, TILE_COLS * n_tiles // SEL * HD)
    operands = [a for state, packed in zip(mine, theirs) for a in (*state, packed)]
    return pl.pallas_call(
        merge_kernel,
        out_shape=jax.ShapeDtypeStruct(shape, jnp.bfloat16),
        compiler_params=megabytes(16),
        cost_estimate=cost(4 * math.prod(shape), 8 * math.prod(shape)),
        name="merge",
    )(*operands)


def out_kernel(n_blocks, first_col, place_ref, x_ref, w_ref, *refs):
    outs = refs[:n_blocks]
    ordered, slots, sems = refs[n_blocks:]
    rows = SEL // n_blocks
    tile = slots.shape[2]
    count = outs[0].shape[1] // tile
    start, wait = stream(
        [lambda step: w_ref.at[:, pl.ds(first_col + step * tile, tile)]], [slots], sems
    )

    for step in range(min(SLOTS, count)):
        start(step)
    for block in range(n_blocks):
        there = pl.ds(pl.multiple_of(place_ref[block] * rows, rows), rows)
        ordered[block * rows : (block + 1) * rows, :] = x_ref[there, :]
    for step in range(count):
        wait(step)
        product = jnp.dot(
            ordered[...].astype(jnp.bfloat16),
            slots[step % SLOTS],
            preferred_element_type=jnp.float32,
        )
        cols = slice(step * tile, (step + 1) * tile)
        for block, out in enumerate(outs):
            out[:, cols] = product[block * rows : (block + 1) * rows, :].astype(out.dtype)
        if step + SLOTS < count:
            start(step + SLOTS)


def project_out(place, attention, w_out, chunk, kinds):
    depth = w_out.shape[0]
    n_blocks = len(kinds)
    width = w_out.shape[1] // CHUNKS
    rows = SEL // n_blocks
    if rows % 16:
        attention = attention.astype(jnp.float32)
    vmem = pl.BlockSpec(memory_space=pltpu.VMEM)
    return pl.pallas_call(
        functools.partial(out_kernel, n_blocks, chunk * width),
        in_specs=[
            pl.BlockSpec(memory_space=pltpu.SMEM),
            vmem,
            pl.BlockSpec(memory_space=pltpu.HBM),
        ],
        out_specs=[vmem] * n_blocks,
        out_shape=[jax.ShapeDtypeStruct((rows, width), kind) for kind in kinds],
        scratch_shapes=[
            pltpu.VMEM((SEL, depth), attention.dtype),
            pltpu.VMEM((SLOTS, depth, min(WIDTH_TILE, width)), jnp.bfloat16),
            pltpu.SemaphoreType.DMA((CUTS, SLOTS)),
        ],
        compiler_params=megabytes(16),
        cost_estimate=cost(2 * SEL * depth * width, 2 * depth * (width + SEL) + 4 * SEL * width),
        name="project_out",
    )(place, attention, w_out)


def per_device(
    hidden_in, norm_gain, w_query, w_keyval, w_out, pool_cache, doc_slot, doc_blocks, sel_pos
):
    tp_size = lax.axis_size("tp")
    req_size = lax.axis_size("req")
    me = lax.axis_index("tp")
    rows, width = hidden_in.shape
    slots, tokens = pool_cache.shape[:2]
    heads_here = w_query.shape[1] // HD
    selected = sel_pos[0]
    lengths = doc_blocks[0] * BLOCK

    if tp_size == KVH:
        ring = [*range(0, tp_size, 2), *range(tp_size - 1, 0, -2)]
    else:
        ring = list(range(tp_size))
    far = tp_size // 2
    forth = [(ring[p], ring[(p + 1) % tp_size]) for p in range(tp_size)]
    back = [(dst, src) for src, dst in forth]
    steps = [0] + [sign * k for k in range(1, far) for sign in (-1, 1)] + [far]
    table = [[ring[(ring.index(i) + s) % tp_size] for s in steps] for i in range(tp_size)]
    place = jnp.array(table, jnp.int32)[me]

    widened = hidden_in.astype(jnp.float32)
    normed = (
        widened
        * lax.rsqrt(jnp.mean(widened * widened, axis=-1, keepdims=True) + EPSILON)
        * norm_gain
    ).astype(jnp.bfloat16)
    normed, pool_cache = lax.optimization_barrier((normed, pool_cache))
    w_query, w_keyval, w_out = (
        pltpu.with_memory_space_constraint(w, pltpu.HBM) for w in (w_query, w_keyval, w_out)
    )
    middle = tp_size // 2
    order = jnp.arange(middle, dtype=jnp.int32)
    offsets = jnp.cumsum(lengths) - lengths
    first_slot = (me ^ order) * tokens
    slot_tokens = first_slot[:, None] + jnp.arange(tokens, dtype=jnp.int32)[None, :]
    cache_pos = offsets[:, None, None] + slot_tokens[None]
    is_valid = slot_tokens[None] < lengths[:, None, None]
    replaced = jnp.any(cache_pos[..., None] == selected, axis=-1)
    dead = jnp.where(is_valid & jnp.logical_not(replaced), 0.0, MASKED).astype(jnp.bfloat16)
    dead = jnp.broadcast_to(
        dead.transpose(1, 0, 2)[..., None], (middle, DOCS, tokens, HD)
    )
    first_pos = jnp.where(
        first_slot[None] < lengths[:, None], offsets[:, None] + first_slot[None], FAR
    ).reshape(-1)
    cosine, sine_part = rotation_tables(selected)
    heads_here = w_query.shape[1] // HD
    tile_q = TILE_COLS // heads_here
    q_pos = jnp.tile(selected.reshape(SEL // tile_q, tile_q), (1, heads_here))
    q_pos = q_pos.reshape(SEL // tile_q, 1, TILE_COLS)

    part = width // CHUNKS
    streams = []
    for chunk in range(CHUNKS):
        own = normed[:, chunk * part : (chunk + 1) * part]
        streams.append({"before": [own], "behind": [own]})
    for k in range(1, far + 1):
        for chunk, held in enumerate(streams):
            if k < far or chunk % 2 == 0:
                held["before"].append(lax.ppermute(held["before"][-1], "tp", forth))
            if k < far or chunk % 2 == 1:
                held["behind"].append(lax.ppermute(held["behind"][-1], "tp", back))
        first = streams[0]["before"]
        if k == 1:
            by_kind = pool_cache.transpose(0, 2, 1, 3)
            sources = [by_kind]
            for shift in range(1, req_size):
                pairs = [((i + shift) % req_size, i) for i in range(req_size)]
                sources.append(lax.ppermute(by_kind, "req", pairs))
            holder = (doc_slot // slots - lax.axis_index("req")) % req_size
            slot = doc_slot % slots
            side = (me < middle).astype(jnp.int32)[None]
            takers = jnp.concatenate([me ^ order, me ^ order ^ middle]) * KVH // tp_size
        if k == 2:
            first[-1], dead, first_pos, cosine, sine_part, q_pos, takers, holder, slot, place, side = (
                lax.optimization_barrier(
                    (first[-1], dead, first_pos, cosine, sine_part, q_pos, takers, holder, slot)
                    + (place, side)
                )
            )
        if k == far - 1:
            targets_of = [(0, None), (1, 0)] + [(j, None) for j in range(2, middle)]
            targets_of += [(middle, None), (1, 1)]
            targets_of += [(middle + j - 1, None) for j in range(2, middle)]
            sent = select_docs(sources, holder, slot, takers, targets_of)
            first[-1], *sent = lax.optimization_barrier((first[-1], *sent))
    projected = None
    for chunk, held in enumerate(streams):
        blocks = [held["before"][0]]
        for k in range(1, far):
            blocks += [held["before"][k], held["behind"][k]]
        blocks.append(held["behind" if chunk % 2 else "before"][far])
        if rows % 16:
            blocks = [jnp.concatenate(blocks, axis=0)]
        projected = project(
            place, blocks, w_query, w_keyval, projected, (cosine, sine_part), chunk
        )
    def exchange(keys, j):
        return lax.ppermute(keys, "tp", [(i, i ^ j) for i in range(tp_size)])

    nearest = exchange(sent[1], 1)
    own = [(sent[0], None), (nearest, 0)]
    partners = [(sent[middle], None), (nearest, 1)]
    partners += [(exchange(sent[middle + j - 1], j), None) for j in range(2, middle)]
    leaving = sent[2:middle]
    queries = projected[:HALVES]
    n_tiles = queries[0].shape[0]
    across = [(i, i ^ middle) for i in range(tp_size)]
    their_queries = [None] * HALVES
    for part in reversed(range(HALVES)):
        their_queries[part] = lax.ppermute(queries[part], "tp", across)

    metadata = (first_pos, selected, dead, q_pos)
    near = [
        attend(own, 0, metadata, queries[part], part * n_tiles, n_tiles) for part in range(HALVES)
    ]
    their_queries[-1], *near = lax.optimization_barrier((their_queries[-1], *near))

    if tp_size == KVH:
        new = lax.ppermute(
            pick_new(side, queries[-1], their_queries[-1], n_tiles),
            "tp",
            [(i, 2 * i if i < middle else 2 * (i - middle) + 1) for i in range(tp_size)],
        )
    else:
        everyone = lax.all_gather(projected[-1], "tp", axis=1, tiled=True)
        my_head = me * KVH // tp_size
        new = jnp.concatenate(
            [
                lax.dynamic_slice_in_dim(everyone, (kind * KVH + my_head) * HD, HD, axis=1)
                for kind in range(2)
            ],
            axis=1,
        )

    theirs = [None] * HALVES
    for part in reversed(range(HALVES)):
        (packed,) = attend(
            partners, 0, metadata, their_queries[part], part * n_tiles, n_tiles, packs=True
        )
        if part + 1 == HALVES:
            packed, new, leaving, *their_queries[:part] = lax.optimization_barrier(
                (packed, new, leaving, *their_queries[:part])
            )
            rest = [(exchange(leaving[j - 2], j), None) for j in range(2, middle)]
        theirs[part] = lax.ppermute(packed, "tp", across)
    mine = [
        attend(
            rest,
            2,
            metadata,
            queries[part],
            part * n_tiles,
            n_tiles,
            near[part],
            (cosine, sine_part, new),
        )
        for part in range(HALVES)
    ]
    attention = merge(mine, theirs)

    finished = []
    for chunk in range(CHUNKS):
        kinds = [jnp.float32] * (tp_size - 1) + [jnp.bfloat16]
        pieces = project_out(place, attention, w_out, chunk, kinds)
        to_forth, to_back = list(pieces[2 : tp_size - 1 : 2]), list(pieces[1 : tp_size - 1 : 2])
        (to_back if chunk % 2 else to_forth).append(pieces[-1])
        total = pieces[0]
        for terms, pairs in ((to_forth, forth), (to_back, back)):
            held = None
            for term in reversed(terms):
                if held is not None:
                    term = term + held.astype(jnp.float32)
                held = lax.ppermute(term.astype(jnp.bfloat16), "tp", pairs)
            total = total + held.astype(jnp.float32)
        finished.append(total.astype(jnp.bfloat16))
    return jnp.concatenate(finished, axis=1)


def solution(mesh):
    placed = (
        P(("groups", "req", "tp"), None),
        P(),
        P(None, "tp"),
        P(None, "tp"),
        P("tp", None),
        P(("groups", "req"), "tp", None, None),
        P(("groups", "req")),
        P(("groups", "req"), None),
        P(("groups", "req"), None),
    )
    return jax.shard_map(
        per_device,
        mesh=mesh,
        in_specs=placed,
        out_specs=P(("groups", "req", "tp"), None),
        check_vma=False,
    )
```

```python
import functools
import math

import jax
import jax.numpy as jnp
from jax import lax
from jax.experimental import pallas as pl
from jax.experimental.pallas import tpu as pltpu
from jax.sharding import PartitionSpec as P

HEADS = 64
KVH = 8
HD = 128
DOCS = 4
BLOCK = 128
SEL = 256


EPSILON = 1e-05
ROPE_BASE = 500000.0
MASKED = -1e30
FAR = 1 << 30
CHUNKS = 2
TILE_COLS = 256
PAIR = 2
STATS = 16
HALVES = 1
DEPTH_TILE = 1024
WIDTH_TILE = 1024
SLOTS = 3
CUTS = 4


def cost(flops, bytes_accessed, transcendentals=0):
    return pl.CostEstimate(
        flops=int(flops), bytes_accessed=int(bytes_accessed), transcendentals=int(transcendentals)
    )


def rotation_tables(positions):
    half_dim = HD // 2
    inverse = ROPE_BASE ** (-(jnp.arange(half_dim, dtype=jnp.float32) * (2.0 / HD)))
    angles = positions.astype(jnp.float32)[:, None] * inverse[None, :]
    cosine = jnp.cos(angles)
    sine_part = jnp.sin(angles)
    return (
        jnp.concatenate([cosine, cosine], axis=-1),
        jnp.concatenate([-sine_part, sine_part], axis=-1),
    )


def rotate(values, cosine, sine_part):
    swapped = jnp.concatenate([values[:, HD // 2 :], values[:, : HD // 2]], axis=-1)
    return values * cosine + swapped * sine_part


def megabytes(count):
    return pltpu.CompilerParams(vmem_limit_bytes=count * 1024 * 1024)


def stream(sources, buffers, sems):
    def copies(step):
        slot = step % SLOTS
        made = []
        for i, (source, buffer) in enumerate(zip(sources, buffers)):
            rows = buffer.shape[1] // CUTS
            for cut in range(CUTS):
                here = pl.ds(cut * rows, rows)
                made.append(
                    pltpu.make_async_copy(
                        source(step).at[here], buffer.at[slot, here], sems.at[i * CUTS + cut, slot]
                    )
                )
        return made

    def start(step):
        for copy in copies(step):
            copy.start()

    def wait(step):
        for copy in copies(step):
            copy.wait()

    return start, wait


def project_kernel(n_blocks, n_weights, chunk, is_last, place_ref, *refs):
    refs = list(refs)
    take = lambda count: [refs.pop(0) for _ in range(count)]
    blocks, weights = take(n_blocks), take(n_weights)
    prev = take(n_weights) if chunk else None
    if is_last:
        tables, (out, total, natural) = take(len(refs) - 5), take(3)
        totals = [total]
    else:
        totals = take(n_weights)
    buffers, sems = take(n_weights), refs[0]
    tile = buffers[0].shape[1]
    depth = blocks[0].shape[1]
    count = depth // tile
    rows_of = lambda ref: lambda step: ref.at[pl.ds(chunk * depth + step * tile, tile), :]
    start, wait = stream([rows_of(ref) for ref in weights], buffers, sems)

    for step in range(min(SLOTS, count)):
        start(step)
    for step in range(count):
        wait(step)
        cols = slice(step * tile, (step + 1) * tile)
        rows = jnp.concatenate([b[:, cols] for b in blocks], axis=0)
        for i, (buffer, total) in enumerate(zip(buffers, totals)):
            term = jnp.dot(rows, buffer[step % SLOTS], preferred_element_type=jnp.float32)
            if step:
                total[...] += term
            elif chunk:
                total[...] = prev[i][...] + term
            else:
                total[...] = term
        if step + SLOTS < count:
            start(step + SLOTS)

    if is_last:
        height = SEL // place_ref.shape[0]
        for block in range(SEL // height):
            here = slice(block * height, (block + 1) * height)
            there = pl.ds(pl.multiple_of(place_ref[block] * height, height), height)
            natural[there, :] = totals[0][here, :]
        if not tables:
            out[...] = natural[...].astype(out.dtype)
            return
        cos_ref, sin_ref = tables
        heads_here = natural.shape[1] // HD
        tile_q = TILE_COLS // heads_here
        for index in range(SEL // tile_q):
            here = slice(index * tile_q, (index + 1) * tile_q)
            stacked = jnp.concatenate(
                [
                    rotate(
                        natural[here, head * HD : (head + 1) * HD], cos_ref[here, :], sin_ref[here, :]
                    )
                    for head in range(heads_here)
                ],
                axis=0,
            )
            out[index] = stacked.T.astype(out.dtype)


def project(place, blocks, weights, prev, chunk, tables=()):
    depth = blocks[0].shape[1]
    widths = [w.shape[1] for w in weights]
    tile = min(DEPTH_TILE, depth)
    is_last = chunk + 1 == CHUNKS
    vmem = pl.BlockSpec(memory_space=pltpu.VMEM)
    hbm = pl.BlockSpec(memory_space=pltpu.HBM)
    totals = [((SEL, width), jnp.float32) for width in widths]
    if is_last:
        shape = (SEL * widths[0] // (HD * TILE_COLS), HD, TILE_COLS) if tables else (SEL, widths[0])
        outs, scratch = [(shape, jnp.bfloat16)], totals * 2
    else:
        outs, scratch = totals, []
    return pl.pallas_call(
        functools.partial(project_kernel, len(blocks), len(weights), chunk, is_last),
        in_specs=[pl.BlockSpec(memory_space=pltpu.SMEM)]
        + [vmem] * len(blocks)
        + [hbm] * len(weights)
        + [vmem] * (len(prev) + len(tables)),
        out_specs=[vmem] * len(outs),
        out_shape=[jax.ShapeDtypeStruct(*o) for o in outs],
        scratch_shapes=[pltpu.VMEM(*x) for x in scratch]
        + [pltpu.VMEM((SLOTS, tile, width), jnp.bfloat16) for width in widths]
        + [pltpu.SemaphoreType.DMA((len(weights) * CUTS, SLOTS))],
        compiler_params=megabytes(16),
        cost_estimate=cost(2 * SEL * depth * sum(widths), 2 * depth * (sum(widths) + SEL)),
        name="project",
    )(place, *blocks, *weights, *prev, *tables)


def select_kernel(n_dest, n_src, place_ref, slot_ref, head_ref, *refs):
    sources = refs[:n_src]
    outs = refs[n_src : n_src + n_dest]
    sems = refs[n_src + n_dest]
    for doc in range(DOCS):
        for src in range(n_src):

            @pl.when(place_ref[doc] == src)
            def _():
                for dest in range(n_dest):
                    cols = pl.ds(pl.multiple_of(head_ref[dest] * HD, HD), HD)
                    pltpu.make_async_copy(
                        sources[src].at[slot_ref[doc], :, :, cols],
                        outs[dest].at[:, doc],
                        sems.at[dest, doc],
                    ).start()

    for dest in range(n_dest):
        for doc in range(DOCS):
            pltpu.make_async_copy(
                sources[0].at[0, :, :, 0:HD], outs[dest].at[:, doc], sems.at[dest, doc]
            ).wait()


def select_docs(sources, place, slot, heads, n_dest):
    tokens = sources[0].shape[2]
    shape = (2, DOCS, tokens, HD)
    smem = pl.BlockSpec(memory_space=pltpu.SMEM)
    return pl.pallas_call(
        functools.partial(select_kernel, n_dest, len(sources)),
        in_specs=[smem] * 3 + [pl.BlockSpec(memory_space=pl.ANY)] * len(sources),
        out_specs=[pl.BlockSpec(memory_space=pltpu.VMEM)] * n_dest,
        out_shape=[jax.ShapeDtypeStruct(shape, jnp.bfloat16)] * n_dest,
        scratch_shapes=[pltpu.SemaphoreType.DMA((n_dest, DOCS))],
        compiler_params=megabytes(8),
        cost_estimate=cost(0, 4 * n_dest * math.prod(shape)),
        name="select_docs",
    )(place, slot, heads, *sources)


def split_exact(value):
    pieces = []
    for _ in range(3):
        pieces.append(value.astype(jnp.bfloat16).astype(jnp.float32))
        value = value - pieces[-1]
    return pieces


def attend_kernel(n_chunks, with_new, n_tiles, tile_q, first_tile, first_ref, pos_ref, *refs):
    refs = list(refs)
    take = lambda count: [refs.pop(0) for _ in range(count)]
    chunks = take(n_chunks)
    dead_ref, qpos_ref, queries = take(3)
    if with_new:
        cos_ref, sin_ref, new_ref = take(3)
    if with_new:
        top, total, summed, values, new_key, new_value = take(6)
    else:
        packed, top, total, summed, values = take(5)
    together = min(PAIR, n_tiles)
    n_pairs = n_tiles // together
    tokens = chunks[0].shape[2]
    scale = math.log2(math.e) / math.sqrt(HD)

    for chunk in range(n_chunks):
        for doc in range(DOCS):
            values[doc, :, chunk * tokens : (chunk + 1) * tokens] = chunks[chunk][1, doc].T
    if with_new:
        new_key[...] = rotate(
            new_ref[:, :HD].astype(jnp.float32), cos_ref[...], sin_ref[...]
        ).astype(jnp.bfloat16)
        new_value[...] = new_ref[:, HD:].T

    one_row = jnp.where(
        lax.broadcasted_iota(jnp.int32, (HD, TILE_COLS), 0) == 0, 1.0, 0.0
    ).astype(jnp.bfloat16)

    def update(tile, parts):
        best = functools.reduce(
            jnp.maximum, [jnp.max(scores, axis=0, keepdims=True) for scores, _ in parts]
        )
        old = top[tile]
        new = jnp.maximum(old, best)
        shrink = jnp.exp2((old - new) * scale)
        running = total[tile] * shrink
        mixed = summed[tile] * shrink
        for scores, value in parts:
            weights = jnp.exp2((scores - new) * scale)
            running += jnp.sum(weights, axis=0, keepdims=True)
            mixed += jnp.dot(
                value, weights.astype(jnp.bfloat16), preferred_element_type=jnp.float32
            )
        top[tile] = new
        total[tile] = running
        summed[tile] = mixed

    @pl.loop(0, n_pairs)
    def _(pair):
        tiles = [pair * together + i for i in range(together)]
        for tile in tiles:
            top[tile] = jnp.full(top.shape[1:], MASKED, jnp.float32)
            total[tile] = jnp.zeros(total.shape[1:], jnp.float32)
            summed[tile] = jnp.zeros(summed.shape[1:], jnp.float32)
        if with_new:
            fresh = []
            for tile in tiles:
                scores = jnp.dot(new_key[...], queries[tile], preferred_element_type=jnp.float32)
                key_index = lax.broadcasted_iota(jnp.int32, scores.shape, 0)
                q_index = (first_tile + tile) * tile_q + lax.broadcasted_iota(jnp.int32, scores.shape, 1) % tile_q
                fresh.append(jnp.where(key_index <= q_index, scores, MASKED))
            for tile, scores in zip(tiles, fresh):
                update(tile, [(scores, new_value[...])])

        @pl.loop(0, DOCS)
        def _(doc):
            firsts = [first_ref[doc * n_chunks + chunk] for chunk in range(n_chunks)]
            lowest = functools.reduce(jnp.minimum, firsts)
            reach = functools.reduce(jnp.maximum, firsts) + tokens - 1

            def visit(masked):
                found = []
                for tile in tiles:
                    extended = jnp.concatenate([queries[tile], one_row], axis=0)
                    parts = []
                    for chunk in range(n_chunks):
                        span = slice(chunk * tokens, (chunk + 1) * tokens)
                        keys = jnp.concatenate(
                            [chunks[chunk][0, doc], dead_ref[doc, span, :]], axis=1
                        )
                        scores = jnp.dot(keys, extended, preferred_element_type=jnp.float32)
                        if masked:
                            key_pos = firsts[chunk] + lax.broadcasted_iota(
                                jnp.int32, scores.shape, 0
                            )
                            scores = jnp.where(key_pos <= qpos_ref[first_tile + tile], scores, MASKED)
                        parts.append((scores, values[doc, :, span]))
                    found.append(parts)
                for tile, parts in zip(tiles, found):
                    update(tile, parts)

            start = first_tile * tile_q + pair * together * tile_q
            live = lowest <= pos_ref[start + together * tile_q - 1]
            whole = reach <= pos_ref[start]

            @pl.when(live & whole)
            def _():
                visit(False)

            @pl.when(live & jnp.logical_not(whole))
            def _():
                visit(True)

        if not with_new:
            for tile in tiles:
                extra = jnp.concatenate(
                    split_exact(top[tile])
                    + split_exact(total[tile])
                    + [jnp.zeros((STATS - 6, TILE_COLS), jnp.float32)],
                    axis=0,
                )
                packed[tile] = jnp.concatenate([summed[tile], extra], axis=0).astype(jnp.bfloat16)


def attend(chunks, dead, first_pos, selected, q_pos, queries, first_tile, n_tiles, fresh):
    n_chunks = len(chunks)
    tokens = chunks[0].shape[2]
    tile_q = SEL // q_pos.shape[0]
    smem = pl.BlockSpec(memory_space=pltpu.SMEM)
    vmem = pl.BlockSpec(memory_space=pltpu.VMEM)
    operands = [first_pos, selected, *chunks, dead, q_pos, queries, *fresh]
    state = [((n_tiles, 1, TILE_COLS), jnp.float32)] * 2
    state += [((n_tiles, HD, TILE_COLS), jnp.float32)]
    values = ((DOCS, HD, n_chunks * tokens), jnp.bfloat16)
    if fresh:
        outs = state
        scratch = [values, ((SEL, HD), jnp.bfloat16), ((HD, SEL), jnp.bfloat16)]
    else:
        outs = [((n_tiles, HD + STATS, TILE_COLS), jnp.bfloat16)]
        scratch = state + [values]
    pairs = n_tiles * TILE_COLS * DOCS * n_chunks * tokens // 2
    return pl.pallas_call(
        functools.partial(
            attend_kernel, n_chunks, bool(fresh), n_tiles, tile_q, first_tile
        ),
        in_specs=[smem] * 2 + [vmem] * (len(operands) - 2),
        out_specs=[vmem] * len(outs),
        out_shape=[jax.ShapeDtypeStruct(*s) for s in outs],
        scratch_shapes=[pltpu.VMEM(*s) for s in scratch],
        compiler_params=megabytes(16),
        cost_estimate=cost(4 * pairs * HD, 4 * DOCS * n_chunks * tokens * HD, pairs),
        name="attend",
    )(*operands)


def pick_kernel(side_ref, here_ref, there_ref, out_ref):
    @pl.when(side_ref[0] == 1)
    def _():
        out_ref[:, :HD] = here_ref[:, :HD]
        out_ref[:, HD:] = there_ref[:, :HD]

    @pl.when(side_ref[0] == 0)
    def _():
        out_ref[:, :HD] = there_ref[:, HD:]
        out_ref[:, HD:] = here_ref[:, HD:]


def pick_new(side, here, there):
    vmem = pl.BlockSpec(memory_space=pltpu.VMEM)
    return pl.pallas_call(
        pick_kernel,
        in_specs=[pl.BlockSpec(memory_space=pltpu.SMEM), vmem, vmem],
        out_specs=vmem,
        out_shape=jax.ShapeDtypeStruct((SEL, 2 * HD), jnp.bfloat16),
        compiler_params=megabytes(4),
        cost_estimate=cost(0, 8 * SEL * HD),
        name="pick_new",
    )(side, here, there)


def merge_kernel(*refs):
    out_ref = refs[-1]
    scale = math.log2(math.e) / math.sqrt(HD)
    for half in range(HALVES):
        top_a, total_a, mixed_a, packed = refs[4 * half : 4 * half + 4]
        n_tiles = top_a.shape[0]
        tile_q = SEL // HALVES // n_tiles
        for tile in range(n_tiles):
            extra = packed[tile, HD:, :].astype(jnp.float32)
            top_b = extra[0:1] + (extra[1:2] + extra[2:3])
            total_b = extra[3:4] + (extra[4:5] + extra[5:6])
            new = jnp.maximum(top_a[tile], top_b)
            part_a = jnp.exp2((top_a[tile] - new) * scale)
            part_b = jnp.exp2((top_b - new) * scale)
            total = total_a[tile] * part_a + total_b * part_b
            mixed = mixed_a[tile] * part_a + packed[tile, :HD, :].astype(jnp.float32) * part_b
            finished = (mixed / total).T.astype(jnp.bfloat16)
            here = slice((half * n_tiles + tile) * tile_q, (half * n_tiles + tile + 1) * tile_q)
            for head in range(TILE_COLS // tile_q):
                out_ref[here, head * HD : (head + 1) * HD] = finished[
                    head * tile_q : (head + 1) * tile_q, :
                ]


def merge(mine, theirs):
    n_tiles = mine[0][0].shape[0] * HALVES
    shape = (SEL, TILE_COLS * n_tiles // SEL * HD)
    operands = [a for state, packed in zip(mine, theirs) for a in (*state, packed)]
    return pl.pallas_call(
        merge_kernel,
        out_shape=jax.ShapeDtypeStruct(shape, jnp.bfloat16),
        compiler_params=megabytes(16),
        cost_estimate=cost(4 * math.prod(shape), 8 * math.prod(shape)),
        name="merge",
    )(*operands)


def out_kernel(n_blocks, first_col, place_ref, x_ref, w_ref, *refs):
    outs = refs[:n_blocks]
    ordered, slots, sems = refs[n_blocks:]
    rows = SEL // n_blocks
    tile = slots.shape[2]
    count = outs[0].shape[1] // tile
    start, wait = stream(
        [lambda step: w_ref.at[:, pl.ds(first_col + step * tile, tile)]], [slots], sems
    )

    for step in range(min(SLOTS, count)):
        start(step)
    for block in range(n_blocks):
        there = pl.ds(pl.multiple_of(place_ref[block] * rows, rows), rows)
        ordered[block * rows : (block + 1) * rows, :] = x_ref[there, :]
    for step in range(count):
        wait(step)
        product = jnp.dot(
            ordered[...].astype(jnp.bfloat16),
            slots[step % SLOTS],
            preferred_element_type=jnp.float32,
        )
        cols = slice(step * tile, (step + 1) * tile)
        for block, out in enumerate(outs):
            out[:, cols] = product[block * rows : (block + 1) * rows, :].astype(out.dtype)
        if step + SLOTS < count:
            start(step + SLOTS)


def project_out(place, attention, w_out, chunk, kinds):
    depth = w_out.shape[0]
    n_blocks = len(kinds)
    width = w_out.shape[1] // CHUNKS
    rows = SEL // n_blocks
    if rows % 16:
        attention = attention.astype(jnp.float32)
    vmem = pl.BlockSpec(memory_space=pltpu.VMEM)
    return pl.pallas_call(
        functools.partial(out_kernel, n_blocks, chunk * width),
        in_specs=[
            pl.BlockSpec(memory_space=pltpu.SMEM),
            vmem,
            pl.BlockSpec(memory_space=pltpu.HBM),
        ],
        out_specs=[vmem] * n_blocks,
        out_shape=[jax.ShapeDtypeStruct((rows, width), kind) for kind in kinds],
        scratch_shapes=[
            pltpu.VMEM((SEL, depth), attention.dtype),
            pltpu.VMEM((SLOTS, depth, min(WIDTH_TILE, width)), jnp.bfloat16),
            pltpu.SemaphoreType.DMA((CUTS, SLOTS)),
        ],
        compiler_params=megabytes(16),
        cost_estimate=cost(2 * SEL * depth * width, 2 * depth * (width + SEL) + 4 * SEL * width),
        name="project_out",
    )(place, attention, w_out)


def per_device(
    hidden_in, norm_gain, w_query, w_keyval, w_out, pool_cache, doc_slot, doc_blocks, sel_pos
):
    tp_size = lax.axis_size("tp")
    req_size = lax.axis_size("req")
    me = lax.axis_index("tp")
    rows, width = hidden_in.shape
    slots, tokens = pool_cache.shape[:2]
    heads_here = w_query.shape[1] // HD
    selected = sel_pos[0]
    lengths = doc_blocks[0] * BLOCK

    if tp_size == KVH:
        ring = [*range(0, tp_size, 2), *range(tp_size - 1, 0, -2)]
    else:
        ring = list(range(tp_size))
    far = tp_size // 2
    forth = [(ring[p], ring[(p + 1) % tp_size]) for p in range(tp_size)]
    back = [(dst, src) for src, dst in forth]
    steps = [0] + [sign * k for k in range(1, far) for sign in (-1, 1)] + [far]
    table = [[ring[(ring.index(i) + s) % tp_size] for s in steps] for i in range(tp_size)]
    place = jnp.array(table, jnp.int32)[me]

    widened = hidden_in.astype(jnp.float32)
    normed = (
        widened
        * lax.rsqrt(jnp.mean(widened * widened, axis=-1, keepdims=True) + EPSILON)
        * norm_gain
    ).astype(jnp.bfloat16)
    normed, pool_cache = lax.optimization_barrier((normed, pool_cache))
    w_query, w_keyval, w_out = (
        pltpu.with_memory_space_constraint(w, pltpu.HBM) for w in (w_query, w_keyval, w_out)
    )
    middle = tp_size // 2
    order = jnp.arange(middle, dtype=jnp.int32)
    offsets = jnp.cumsum(lengths) - lengths
    first_slot = (me ^ order) * tokens
    slot_tokens = first_slot[:, None] + jnp.arange(tokens, dtype=jnp.int32)[None, :]
    cache_pos = offsets[:, None, None] + slot_tokens[None]
    is_valid = slot_tokens[None] < lengths[:, None, None]
    replaced = jnp.any(cache_pos[..., None] == selected, axis=-1)
    dead = jnp.where(is_valid & jnp.logical_not(replaced), 0.0, MASKED).astype(jnp.bfloat16)
    dead = jnp.broadcast_to(dead[..., None], (DOCS, middle, tokens, HD))
    dead = dead.reshape(DOCS, middle * tokens, HD)
    first_pos = jnp.where(
        first_slot[None] < lengths[:, None], offsets[:, None] + first_slot[None], FAR
    ).reshape(-1)
    cosine, sine_part = rotation_tables(selected)
    heads_here = w_query.shape[1] // HD
    tile_q = TILE_COLS // heads_here
    q_pos = jnp.tile(selected.reshape(SEL // tile_q, tile_q), (1, heads_here))
    q_pos = q_pos.reshape(SEL // tile_q, 1, TILE_COLS)

    part = width // CHUNKS
    streams = []
    for chunk in range(CHUNKS):
        own = normed[:, chunk * part : (chunk + 1) * part]
        streams.append({"before": [own], "behind": [own]})
    for k in range(1, far + 1):
        for chunk, held in enumerate(streams):
            if k < far or chunk % 2 == 0:
                held["before"].append(lax.ppermute(held["before"][-1], "tp", forth))
            if k < far or chunk % 2 == 1:
                held["behind"].append(lax.ppermute(held["behind"][-1], "tp", back))
        first = streams[0]["before"]
        if k == 1:
            by_kind = pool_cache.transpose(0, 2, 1, 3)
            sources = [by_kind]
            for shift in range(1, req_size):
                pairs = [((i + shift) % req_size, i) for i in range(req_size)]
                sources.append(lax.ppermute(by_kind, "req", pairs))
            holder = (doc_slot // slots - lax.axis_index("req")) % req_size
            slot = doc_slot % slots
            side = (me < middle).astype(jnp.int32)[None]
            takers = jnp.concatenate([me ^ order, me ^ order ^ middle]) * KVH // tp_size
        if k == 2:
            first[-1], dead, first_pos, cosine, sine_part, q_pos, takers, holder, slot, place, side = (
                lax.optimization_barrier(
                    (first[-1], dead, first_pos, cosine, sine_part, q_pos, takers, holder, slot)
                    + (place, side)
                )
            )
        if k == far - 1:
            sent = select_docs(sources, holder, slot, takers, tp_size)
            first[-1], *sent = lax.optimization_barrier((first[-1], *sent))
    weights = [w_keyval, w_query]
    sums = []
    for chunk, held in enumerate(streams):
        blocks = [held["before"][0]]
        for k in range(1, far):
            blocks += [held["before"][k], held["behind"][k]]
        blocks.append(held["behind" if chunk % 2 else "before"][far])
        if rows % 16:
            blocks = [jnp.concatenate(blocks, axis=0)]
        if chunk + 1 < CHUNKS:
            sums = project(place, blocks, weights, sums, chunk)
    across = [(i, i ^ middle) for i in range(tp_size)]
    (keyval,) = project(place, blocks, weights[:1], sums[:1], CHUNKS - 1)
    keyval, *blocks = lax.optimization_barrier((keyval, *blocks))
    their_keyval = lax.ppermute(keyval, "tp", across)
    (queries,) = project(
        place, blocks, weights[1:], sums[1:], CHUNKS - 1, (cosine, sine_part)
    )
    queries, their_keyval = lax.optimization_barrier((queries, their_keyval))

    def exchange(kept):
        return [
            lax.ppermute(kept[j], "tp", [(i, i ^ j) for i in range(tp_size)]) if j else kept[j]
            for j in range(middle)
        ]

    own, partners = sent[:middle], exchange(sent[middle:])
    own, *partners[1:3] = lax.optimization_barrier((own, *partners[1:3]))
    chunks = [exchange(own), partners]
    n_tiles = queries.shape[0]
    their_queries = lax.ppermute(queries, "tp", across)

    if tp_size == KVH:
        new = lax.ppermute(
            pick_new(side, keyval, their_keyval),
            "tp",
            [(i, 2 * i if i < middle else 2 * (i - middle) + 1) for i in range(tp_size)],
        )
    else:
        everyone = lax.all_gather(keyval, "tp", axis=1, tiled=True)
        my_head = me * KVH // tp_size
        new = jnp.concatenate(
            [
                lax.dynamic_slice_in_dim(everyone, (kind * KVH + my_head) * HD, HD, axis=1)
                for kind in range(2)
            ],
            axis=1,
        )

    metadata = (dead, first_pos, selected, q_pos)
    their_queries, new = lax.optimization_barrier((their_queries, new))
    (packed,) = attend(chunks[1], *metadata, their_queries, 0, n_tiles, [])
    theirs = lax.ppermute(packed, "tp", across)
    mine = attend(chunks[0], *metadata, queries, 0, n_tiles, [cosine, sine_part, new])
    attention = merge([mine], [theirs])

    finished = []
    for chunk in range(CHUNKS):
        kinds = [jnp.float32] * (tp_size - 1) + [jnp.bfloat16]
        pieces = project_out(place, attention, w_out, chunk, kinds)
        to_forth, to_back = list(pieces[2 : tp_size - 1 : 2]), list(pieces[1 : tp_size - 1 : 2])
        (to_back if chunk % 2 else to_forth).append(pieces[-1])
        total = pieces[0]
        for terms, pairs in ((to_forth, forth), (to_back, back)):
            held = None
            for term in reversed(terms):
                if held is not None:
                    term = term + held.astype(jnp.float32)
                held = lax.ppermute(term.astype(jnp.bfloat16), "tp", pairs)
            total = total + held.astype(jnp.float32)
        finished.append(total.astype(jnp.bfloat16))
    return jnp.concatenate(finished, axis=1)


def solution(mesh):
    placed = (
        P(("groups", "req", "tp"), None),
        P(),
        P(None, "tp"),
        P(None, "tp"),
        P("tp", None),
        P(("groups", "req"), "tp", None, None),
        P(("groups", "req")),
        P(("groups", "req"), None),
        P(("groups", "req"), None),
    )
    return jax.shard_map(
        per_device,
        mesh=mesh,
        in_specs=placed,
        out_specs=P(("groups", "req", "tp"), None),
        check_vma=False,
    )
```

```python
import functools
import math

import jax
import jax.numpy as jnp
from jax import lax
from jax.experimental import pallas as pl
from jax.experimental.pallas import tpu as pltpu
from jax.sharding import PartitionSpec as P

HEADS = 64
KVH = 8
HD = 128
DOCS = 4
BLOCK = 128
SEL = 256


EPSILON = 1e-05
ROPE_BASE = 500000.0
MASKED = -1e30
FAR = 1 << 30
CHUNKS = 2
TILE_COLS = 256
PAIR = 2
STATS = 16
HALVES = 1
DEPTH_TILE = 1024
WIDTH_TILE = 1024
SLOTS = 3
CUTS = 4


def cost(flops, bytes_accessed, transcendentals=0):
    return pl.CostEstimate(
        flops=int(flops), bytes_accessed=int(bytes_accessed), transcendentals=int(transcendentals)
    )


def rotation_tables(positions):
    half_dim = HD // 2
    inverse = ROPE_BASE ** (-(jnp.arange(half_dim, dtype=jnp.float32) * (2.0 / HD)))
    angles = positions.astype(jnp.float32)[:, None] * inverse[None, :]
    cosine = jnp.cos(angles)
    sine_part = jnp.sin(angles)
    return (
        jnp.concatenate([cosine, cosine], axis=-1),
        jnp.concatenate([-sine_part, sine_part], axis=-1),
    )


def rotate(values, cosine, sine_part):
    swapped = jnp.concatenate([values[:, HD // 2 :], values[:, : HD // 2]], axis=-1)
    return values * cosine + swapped * sine_part


def megabytes(count):
    return pltpu.CompilerParams(vmem_limit_bytes=count * 1024 * 1024)


def stream(sources, buffers, sems):
    def copies(step):
        slot = step % SLOTS
        made = []
        for i, (source, buffer) in enumerate(zip(sources, buffers)):
            rows = buffer.shape[1] // CUTS
            for cut in range(CUTS):
                here = pl.ds(cut * rows, rows)
                made.append(
                    pltpu.make_async_copy(
                        source(step).at[here], buffer.at[slot, here], sems.at[i * CUTS + cut, slot]
                    )
                )
        return made

    def start(step):
        for copy in copies(step):
            copy.start()

    def wait(step):
        for copy in copies(step):
            copy.wait()

    return start, wait


def project_kernel(n_blocks, n_weights, n_tables, chunk, is_last, place_ref, *refs):
    refs = list(refs)
    take = lambda count: [refs.pop(0) for _ in range(count)]
    blocks, weights = take(n_blocks), take(n_weights)
    prev = take(n_weights) if chunk else None
    if is_last:
        n_outs = len(refs) - 4 - n_tables
        tables, outs, (total, natural) = take(n_tables), take(n_outs), take(2)
        out, totals = outs[0], [total]
    else:
        totals = take(n_weights)
    buffers, sems = take(n_weights), refs[0]
    tile = buffers[0].shape[1]
    depth = blocks[0].shape[1]
    count = depth // tile
    rows_of = lambda ref: lambda step: ref.at[pl.ds(chunk * depth + step * tile, tile), :]
    start, wait = stream([rows_of(ref) for ref in weights], buffers, sems)

    for step in range(min(SLOTS, count)):
        start(step)
    for step in range(count):
        wait(step)
        cols = slice(step * tile, (step + 1) * tile)
        rows = jnp.concatenate([b[:, cols] for b in blocks], axis=0)
        for i, (buffer, total) in enumerate(zip(buffers, totals)):
            term = jnp.dot(rows, buffer[step % SLOTS], preferred_element_type=jnp.float32)
            if step:
                total[...] += term
            elif chunk:
                total[...] = prev[i][...] + term
            else:
                total[...] = term
        if step + SLOTS < count:
            start(step + SLOTS)

    if is_last:
        height = SEL // place_ref.shape[0]
        for block in range(SEL // height):
            here = slice(block * height, (block + 1) * height)
            there = pl.ds(pl.multiple_of(place_ref[block] * height, height), height)
            natural[there, :] = totals[0][here, :]
        if len(outs) == 2:
            side_ref = tables[0]
            for side in range(2):

                @pl.when(side_ref[0] == side)
                def _():
                    outs[1 - side][...] = natural[:, :HD].astype(out.dtype)
                    outs[side][...] = natural[:, HD:].astype(out.dtype)

            return
        if not tables:
            out[...] = natural[...].astype(out.dtype)
            return
        cos_ref, sin_ref = tables
        heads_here = natural.shape[1] // HD
        tile_q = TILE_COLS // heads_here
        for index in range(SEL // tile_q):
            here = slice(index * tile_q, (index + 1) * tile_q)
            stacked = jnp.concatenate(
                [
                    rotate(
                        natural[here, head * HD : (head + 1) * HD], cos_ref[here, :], sin_ref[here, :]
                    )
                    for head in range(heads_here)
                ],
                axis=0,
            )
            out[index] = stacked.T.astype(out.dtype)


def project(place, blocks, weights, prev, chunk, tables=(), side=()):
    depth = blocks[0].shape[1]
    widths = [w.shape[1] for w in weights]
    tile = min(DEPTH_TILE, depth)
    is_last = chunk + 1 == CHUNKS
    vmem = pl.BlockSpec(memory_space=pltpu.VMEM)
    hbm = pl.BlockSpec(memory_space=pltpu.HBM)
    totals = [((SEL, width), jnp.float32) for width in widths]
    if is_last:
        shape = (SEL * widths[0] // (HD * TILE_COLS), HD, TILE_COLS) if tables else (SEL, widths[0])
        outs, scratch = [(shape, jnp.bfloat16)], totals * 2
        if side:
            outs = [((SEL, HD), jnp.bfloat16)] * 2
    else:
        outs, scratch = totals, []
    return pl.pallas_call(
        functools.partial(
            project_kernel, len(blocks), len(weights), len(tables) + len(side), chunk, is_last
        ),
        in_specs=[pl.BlockSpec(memory_space=pltpu.SMEM)]
        + [vmem] * len(blocks)
        + [hbm] * len(weights)
        + [vmem] * (len(prev) + len(tables))
        + [pl.BlockSpec(memory_space=pltpu.SMEM)] * len(side),
        out_specs=[vmem] * len(outs),
        out_shape=[jax.ShapeDtypeStruct(*o) for o in outs],
        scratch_shapes=[pltpu.VMEM(*x) for x in scratch]
        + [pltpu.VMEM((SLOTS, tile, width), jnp.bfloat16) for width in widths]
        + [pltpu.SemaphoreType.DMA((len(weights) * CUTS, SLOTS))],
        compiler_params=megabytes(16),
        cost_estimate=cost(2 * SEL * depth * sum(widths), 2 * depth * (sum(widths) + SEL)),
        name="project",
    )(place, *blocks, *weights, *prev, *tables, *side)


def select_kernel(n_dest, n_src, place_ref, slot_ref, head_ref, *refs):
    sources = refs[:n_src]
    outs = refs[n_src : n_src + n_dest]
    sems = refs[n_src + n_dest]
    for doc in range(DOCS):
        for src in range(n_src):

            @pl.when(place_ref[doc] == src)
            def _():
                for dest in range(n_dest):
                    cols = pl.ds(pl.multiple_of(head_ref[dest] * HD, HD), HD)
                    pltpu.make_async_copy(
                        sources[src].at[slot_ref[doc], :, :, cols],
                        outs[dest].at[:, doc],
                        sems.at[dest, doc],
                    ).start()

    for dest in range(n_dest):
        for doc in range(DOCS):
            pltpu.make_async_copy(
                sources[0].at[0, :, :, 0:HD], outs[dest].at[:, doc], sems.at[dest, doc]
            ).wait()


def select_docs(sources, place, slot, heads, n_dest):
    tokens = sources[0].shape[2]
    shape = (2, DOCS, tokens, HD)
    smem = pl.BlockSpec(memory_space=pltpu.SMEM)
    return pl.pallas_call(
        functools.partial(select_kernel, n_dest, len(sources)),
        in_specs=[smem] * 3 + [pl.BlockSpec(memory_space=pl.ANY)] * len(sources),
        out_specs=[pl.BlockSpec(memory_space=pltpu.VMEM)] * n_dest,
        out_shape=[jax.ShapeDtypeStruct(shape, jnp.bfloat16)] * n_dest,
        scratch_shapes=[pltpu.SemaphoreType.DMA((n_dest, DOCS))],
        compiler_params=megabytes(8),
        cost_estimate=cost(0, 4 * n_dest * math.prod(shape)),
        name="select_docs",
    )(place, slot, heads, *sources)


def split_exact(value):
    pieces = []
    for _ in range(3):
        pieces.append(value.astype(jnp.bfloat16).astype(jnp.float32))
        value = value - pieces[-1]
    return pieces


def attend_kernel(n_chunks, with_new, n_tiles, tile_q, first_tile, first_ref, pos_ref, odd_ref, *refs):
    refs = list(refs)
    take = lambda count: [refs.pop(0) for _ in range(count)]
    chunks = take(n_chunks)
    dead_ref, qpos_ref, queries = take(3)
    if with_new:
        cos_ref, sin_ref, new_a, new_b = take(4)
    if with_new:
        top, total, summed, values, new_key, new_value = take(6)
    else:
        packed, top, total, summed, values = take(5)
    together = min(PAIR, n_tiles)
    n_pairs = n_tiles // together
    tokens = chunks[0].shape[2]
    scale = math.log2(math.e) / math.sqrt(HD)

    for chunk in range(n_chunks):
        for doc in range(DOCS):
            values[doc, :, chunk * tokens : (chunk + 1) * tokens] = chunks[chunk][1, doc].T
    if with_new:
        for odd, (key_ref, value_ref) in enumerate(((new_a, new_b), (new_b, new_a))):

            @pl.when(odd_ref[0] == odd)
            def _():
                new_key[...] = rotate(
                    key_ref[...].astype(jnp.float32), cos_ref[...], sin_ref[...]
                ).astype(jnp.bfloat16)
                new_value[...] = value_ref[...].T


    one_row = jnp.where(
        lax.broadcasted_iota(jnp.int32, (HD, TILE_COLS), 0) == 0, 1.0, 0.0
    ).astype(jnp.bfloat16)

    def update(tile, parts):
        best = functools.reduce(
            jnp.maximum, [jnp.max(scores, axis=0, keepdims=True) for scores, _ in parts]
        )
        old = top[tile]
        new = jnp.maximum(old, best)
        shrink = jnp.exp2((old - new) * scale)
        running = total[tile] * shrink
        mixed = summed[tile] * shrink
        for scores, value in parts:
            weights = jnp.exp2((scores - new) * scale)
            running += jnp.sum(weights, axis=0, keepdims=True)
            mixed += jnp.dot(
                value, weights.astype(jnp.bfloat16), preferred_element_type=jnp.float32
            )
        top[tile] = new
        total[tile] = running
        summed[tile] = mixed

    @pl.loop(0, n_pairs)
    def _(pair):
        tiles = [pair * together + i for i in range(together)]
        for tile in tiles:
            top[tile] = jnp.full(top.shape[1:], MASKED, jnp.float32)
            total[tile] = jnp.zeros(total.shape[1:], jnp.float32)
            summed[tile] = jnp.zeros(summed.shape[1:], jnp.float32)
        if with_new:
            fresh = []
            for tile in tiles:
                scores = jnp.dot(new_key[...], queries[tile], preferred_element_type=jnp.float32)
                key_index = lax.broadcasted_iota(jnp.int32, scores.shape, 0)
                q_index = (first_tile + tile) * tile_q + lax.broadcasted_iota(jnp.int32, scores.shape, 1) % tile_q
                fresh.append(jnp.where(key_index <= q_index, scores, MASKED))
            for tile, scores in zip(tiles, fresh):
                update(tile, [(scores, new_value[...])])

        @pl.loop(0, DOCS)
        def _(doc):
            firsts = [first_ref[doc * n_chunks + chunk] for chunk in range(n_chunks)]
            lowest = functools.reduce(jnp.minimum, firsts)
            reach = functools.reduce(jnp.maximum, firsts) + tokens - 1

            def visit(masked):
                found = []
                for tile in tiles:
                    extended = jnp.concatenate([queries[tile], one_row], axis=0)
                    parts = []
                    for chunk in range(n_chunks):
                        span = slice(chunk * tokens, (chunk + 1) * tokens)
                        keys = jnp.concatenate(
                            [chunks[chunk][0, doc], dead_ref[doc, span, :]], axis=1
                        )
                        scores = jnp.dot(keys, extended, preferred_element_type=jnp.float32)
                        if masked:
                            key_pos = firsts[chunk] + lax.broadcasted_iota(
                                jnp.int32, scores.shape, 0
                            )
                            scores = jnp.where(key_pos <= qpos_ref[first_tile + tile], scores, MASKED)
                        parts.append((scores, values[doc, :, span]))
                    found.append(parts)
                for tile, parts in zip(tiles, found):
                    update(tile, parts)

            start = first_tile * tile_q + pair * together * tile_q
            live = lowest <= pos_ref[start + together * tile_q - 1]
            whole = reach <= pos_ref[start]

            @pl.when(live & whole)
            def _():
                visit(False)

            @pl.when(live & jnp.logical_not(whole))
            def _():
                visit(True)

        if not with_new:
            for tile in tiles:
                extra = jnp.concatenate(
                    split_exact(top[tile])
                    + split_exact(total[tile])
                    + [jnp.zeros((STATS - 6, TILE_COLS), jnp.float32)],
                    axis=0,
                )
                packed[tile] = jnp.concatenate([summed[tile], extra], axis=0).astype(jnp.bfloat16)


def attend(chunks, dead, first_pos, selected, q_pos, odd, queries, first_tile, n_tiles, fresh):
    n_chunks = len(chunks)
    tokens = chunks[0].shape[2]
    tile_q = SEL // q_pos.shape[0]
    smem = pl.BlockSpec(memory_space=pltpu.SMEM)
    vmem = pl.BlockSpec(memory_space=pltpu.VMEM)
    operands = [first_pos, selected, odd, *chunks, dead, q_pos, queries, *fresh]
    state = [((n_tiles, 1, TILE_COLS), jnp.float32)] * 2
    state += [((n_tiles, HD, TILE_COLS), jnp.float32)]
    values = ((DOCS, HD, n_chunks * tokens), jnp.bfloat16)
    if fresh:
        outs = state
        scratch = [values, ((SEL, HD), jnp.bfloat16), ((HD, SEL), jnp.bfloat16)]
    else:
        outs = [((n_tiles, HD + STATS, TILE_COLS), jnp.bfloat16)]
        scratch = state + [values]
    pairs = n_tiles * TILE_COLS * DOCS * n_chunks * tokens // 2
    return pl.pallas_call(
        functools.partial(
            attend_kernel, n_chunks, bool(fresh), n_tiles, tile_q, first_tile
        ),
        in_specs=[smem] * 3 + [vmem] * (len(operands) - 3),
        out_specs=[vmem] * len(outs),
        out_shape=[jax.ShapeDtypeStruct(*s) for s in outs],
        scratch_shapes=[pltpu.VMEM(*s) for s in scratch],
        compiler_params=megabytes(16),
        cost_estimate=cost(4 * pairs * HD, 4 * DOCS * n_chunks * tokens * HD, pairs),
        name="attend",
    )(*operands)


def merge_kernel(*refs):
    out_ref = refs[-1]
    scale = math.log2(math.e) / math.sqrt(HD)
    for half in range(HALVES):
        top_a, total_a, mixed_a, packed = refs[4 * half : 4 * half + 4]
        n_tiles = top_a.shape[0]
        tile_q = SEL // HALVES // n_tiles
        for tile in range(n_tiles):
            extra = packed[tile, HD:, :].astype(jnp.float32)
            top_b = extra[0:1] + (extra[1:2] + extra[2:3])
            total_b = extra[3:4] + (extra[4:5] + extra[5:6])
            new = jnp.maximum(top_a[tile], top_b)
            part_a = jnp.exp2((top_a[tile] - new) * scale)
            part_b = jnp.exp2((top_b - new) * scale)
            total = total_a[tile] * part_a + total_b * part_b
            mixed = mixed_a[tile] * part_a + packed[tile, :HD, :].astype(jnp.float32) * part_b
            finished = (mixed / total).T.astype(jnp.bfloat16)
            here = slice((half * n_tiles + tile) * tile_q, (half * n_tiles + tile + 1) * tile_q)
            for head in range(TILE_COLS // tile_q):
                out_ref[here, head * HD : (head + 1) * HD] = finished[
                    head * tile_q : (head + 1) * tile_q, :
                ]


def merge(mine, theirs):
    n_tiles = mine[0][0].shape[0] * HALVES
    shape = (SEL, TILE_COLS * n_tiles // SEL * HD)
    operands = [a for state, packed in zip(mine, theirs) for a in (*state, packed)]
    return pl.pallas_call(
        merge_kernel,
        out_shape=jax.ShapeDtypeStruct(shape, jnp.bfloat16),
        compiler_params=megabytes(16),
        cost_estimate=cost(4 * math.prod(shape), 8 * math.prod(shape)),
        name="merge",
    )(*operands)


def out_kernel(n_blocks, first_col, place_ref, x_ref, w_ref, *refs):
    outs = refs[:n_blocks]
    ordered, slots, sems = refs[n_blocks:]
    rows = SEL // n_blocks
    tile = slots.shape[2]
    count = outs[0].shape[1] // tile
    start, wait = stream(
        [lambda step: w_ref.at[:, pl.ds(first_col + step * tile, tile)]], [slots], sems
    )

    for step in range(min(SLOTS, count)):
        start(step)
    for block in range(n_blocks):
        there = pl.ds(pl.multiple_of(place_ref[block] * rows, rows), rows)
        ordered[block * rows : (block + 1) * rows, :] = x_ref[there, :]
    for step in range(count):
        wait(step)
        product = jnp.dot(
            ordered[...].astype(jnp.bfloat16),
            slots[step % SLOTS],
            preferred_element_type=jnp.float32,
        )
        cols = slice(step * tile, (step + 1) * tile)
        for block, out in enumerate(outs):
            out[:, cols] = product[block * rows : (block + 1) * rows, :].astype(out.dtype)
        if step + SLOTS < count:
            start(step + SLOTS)


def project_out(place, attention, w_out, chunk, kinds):
    depth = w_out.shape[0]
    n_blocks = len(kinds)
    width = w_out.shape[1] // CHUNKS
    rows = SEL // n_blocks
    if rows % 16:
        attention = attention.astype(jnp.float32)
    vmem = pl.BlockSpec(memory_space=pltpu.VMEM)
    return pl.pallas_call(
        functools.partial(out_kernel, n_blocks, chunk * width),
        in_specs=[
            pl.BlockSpec(memory_space=pltpu.SMEM),
            vmem,
            pl.BlockSpec(memory_space=pltpu.HBM),
        ],
        out_specs=[vmem] * n_blocks,
        out_shape=[jax.ShapeDtypeStruct((rows, width), kind) for kind in kinds],
        scratch_shapes=[
            pltpu.VMEM((SEL, depth), attention.dtype),
            pltpu.VMEM((SLOTS, depth, min(WIDTH_TILE, width)), jnp.bfloat16),
            pltpu.SemaphoreType.DMA((CUTS, SLOTS)),
        ],
        compiler_params=megabytes(16),
        cost_estimate=cost(2 * SEL * depth * width, 2 * depth * (width + SEL) + 4 * SEL * width),
        name="project_out",
    )(place, attention, w_out)


def per_device(
    hidden_in, norm_gain, w_query, w_keyval, w_out, pool_cache, doc_slot, doc_blocks, sel_pos
):
    tp_size = lax.axis_size("tp")
    req_size = lax.axis_size("req")
    me = lax.axis_index("tp")
    rows, width = hidden_in.shape
    slots, tokens = pool_cache.shape[:2]
    heads_here = w_query.shape[1] // HD
    selected = sel_pos[0]
    lengths = doc_blocks[0] * BLOCK

    if tp_size == KVH:
        ring = [*range(0, tp_size, 2), *range(tp_size - 1, 0, -2)]
    else:
        ring = list(range(tp_size))
    far = tp_size // 2
    forth = [(ring[p], ring[(p + 1) % tp_size]) for p in range(tp_size)]
    back = [(dst, src) for src, dst in forth]
    steps = [0] + [sign * k for k in range(1, far) for sign in (-1, 1)] + [far]
    table = [[ring[(ring.index(i) + s) % tp_size] for s in steps] for i in range(tp_size)]
    place = jnp.array(table, jnp.int32)[me]

    widened = hidden_in.astype(jnp.float32)
    normed = (
        widened
        * lax.rsqrt(jnp.mean(widened * widened, axis=-1, keepdims=True) + EPSILON)
        * norm_gain
    ).astype(jnp.bfloat16)
    normed, pool_cache = lax.optimization_barrier((normed, pool_cache))
    w_query, w_keyval, w_out = (
        pltpu.with_memory_space_constraint(w, pltpu.HBM) for w in (w_query, w_keyval, w_out)
    )
    middle = tp_size // 2
    order = jnp.arange(middle, dtype=jnp.int32)
    offsets = jnp.cumsum(lengths) - lengths
    first_slot = (me ^ order) * tokens
    slot_tokens = first_slot[:, None] + jnp.arange(tokens, dtype=jnp.int32)[None, :]
    cache_pos = offsets[:, None, None] + slot_tokens[None]
    is_valid = slot_tokens[None] < lengths[:, None, None]
    replaced = jnp.any(cache_pos[..., None] == selected, axis=-1)
    dead = jnp.where(is_valid & jnp.logical_not(replaced), 0.0, MASKED).astype(jnp.bfloat16)
    dead = jnp.broadcast_to(dead[..., None], (DOCS, middle, tokens, HD))
    dead = dead.reshape(DOCS, middle * tokens, HD)
    first_pos = jnp.where(
        first_slot[None] < lengths[:, None], offsets[:, None] + first_slot[None], FAR
    ).reshape(-1)
    cosine, sine_part = rotation_tables(selected)
    heads_here = w_query.shape[1] // HD
    tile_q = TILE_COLS // heads_here
    q_pos = jnp.tile(selected.reshape(SEL // tile_q, tile_q), (1, heads_here))
    q_pos = q_pos.reshape(SEL // tile_q, 1, TILE_COLS)

    part = width // CHUNKS
    streams = []
    for chunk in range(CHUNKS):
        own = normed[:, chunk * part : (chunk + 1) * part]
        streams.append({"before": [own], "behind": [own]})
    for k in range(1, far + 1):
        for chunk, held in enumerate(streams):
            if k < far or chunk % 2 == 0:
                held["before"].append(lax.ppermute(held["before"][-1], "tp", forth))
            if k < far or chunk % 2 == 1:
                held["behind"].append(lax.ppermute(held["behind"][-1], "tp", back))
        first = streams[0]["before"]
        if k == 1:
            by_kind = pool_cache.transpose(0, 2, 1, 3)
            sources = [by_kind]
            for shift in range(1, req_size):
                pairs = [((i + shift) % req_size, i) for i in range(req_size)]
                sources.append(lax.ppermute(by_kind, "req", pairs))
            holder = (doc_slot // slots - lax.axis_index("req")) % req_size
            slot = doc_slot % slots
            side = (me < middle).astype(jnp.int32)[None]
            odd = (me % 2 if tp_size == KVH else me * 0)[None]
            takers = jnp.concatenate([me ^ order, me ^ order ^ middle]) * KVH // tp_size
        if k == 2:
            first[-1], dead, first_pos, cosine, sine_part, q_pos, takers, holder, slot, place, side, odd = (
                lax.optimization_barrier(
                    (first[-1], dead, first_pos, cosine, sine_part, q_pos, takers, holder, slot)
                    + (place, side, odd)
                )
            )
        if k == far - 1:
            sent = select_docs(sources, holder, slot, takers, tp_size)
            first[-1], *sent = lax.optimization_barrier((first[-1], *sent))
    weights = [w_keyval, w_query]
    sums = []
    for chunk, held in enumerate(streams):
        blocks = [held["before"][0]]
        for k in range(1, far):
            blocks += [held["before"][k], held["behind"][k]]
        blocks.append(held["behind" if chunk % 2 else "before"][far])
        if rows % 16:
            blocks = [jnp.concatenate(blocks, axis=0)]
        if chunk + 1 < CHUNKS:
            sums = project(place, blocks, weights, sums, chunk)
    across = [(i, i ^ middle) for i in range(tp_size)]
    if tp_size == KVH:
        first, second = project(place, blocks, weights[:1], sums[:1], CHUNKS - 1, (), (side,))
        first, second, *blocks = lax.optimization_barrier((first, second, *blocks))
        keys_to_even = [(i, 2 * i if i < middle else 2 * (i - middle) + 1) for i in range(tp_size)]
        keys_to_odd = [(i, 2 * i + 1 if i < middle else 2 * (i - middle)) for i in range(tp_size)]
        new = [lax.ppermute(first, "tp", keys_to_even), lax.ppermute(second, "tp", keys_to_odd)]
    else:
        (keyval,) = project(place, blocks, weights[:1], sums[:1], CHUNKS - 1)
        everyone = lax.all_gather(keyval, "tp", axis=1, tiled=True)
        my_head = me * KVH // tp_size
        new = [
            lax.dynamic_slice_in_dim(everyone, (kind * KVH + my_head) * HD, HD, axis=1)
            for kind in range(2)
        ]
    (queries,) = project(
        place, blocks, weights[1:], sums[1:], CHUNKS - 1, (cosine, sine_part)
    )
    queries, new = lax.optimization_barrier((queries, new))

    def exchange(kept):
        got = {
            j: lax.ppermute(kept[j], "tp", [(i, i ^ j) for i in range(tp_size)])
            for j in range(middle - 1, 0, -1)
        }
        return [kept[0]] + [got[j] for j in range(1, middle)]

    own, partners = sent[:middle], exchange(sent[middle:])
    own, *partners[2:] = lax.optimization_barrier((own, *partners[2:]))
    chunks = [exchange(own), partners]
    n_tiles = queries.shape[0]
    their_queries = lax.ppermute(queries, "tp", across)

    metadata = (dead, first_pos, selected, q_pos, odd)
    (packed,) = attend(chunks[1], *metadata, their_queries, 0, n_tiles, [])
    theirs = lax.ppermute(packed, "tp", across)
    mine = attend(chunks[0], *metadata, queries, 0, n_tiles, [cosine, sine_part, *new])
    attention = merge([mine], [theirs])

    finished = []
    for chunk in range(CHUNKS):
        kinds = [jnp.float32] * (tp_size - 1) + [jnp.bfloat16]
        pieces = project_out(place, attention, w_out, chunk, kinds)
        to_forth, to_back = list(pieces[2 : tp_size - 1 : 2]), list(pieces[1 : tp_size - 1 : 2])
        (to_back if chunk % 2 else to_forth).append(pieces[-1])
        total = pieces[0]
        for terms, pairs in ((to_forth, forth), (to_back, back)):
            held = None
            for term in reversed(terms):
                if held is not None:
                    term = term + held.astype(jnp.float32)
                held = lax.ppermute(term.astype(jnp.bfloat16), "tp", pairs)
            total = total + held.astype(jnp.float32)
        finished.append(total.astype(jnp.bfloat16))
    return jnp.concatenate(finished, axis=1)


def solution(mesh):
    placed = (
        P(("groups", "req", "tp"), None),
        P(),
        P(None, "tp"),
        P(None, "tp"),
        P("tp", None),
        P(("groups", "req"), "tp", None, None),
        P(("groups", "req")),
        P(("groups", "req"), None),
        P(("groups", "req"), None),
    )
    return jax.shard_map(
        per_device,
        mesh=mesh,
        in_specs=placed,
        out_specs=P(("groups", "req", "tp"), None),
        check_vma=False,
    )
```

```python
import functools
import math

import jax
import jax.numpy as jnp
from jax import lax
from jax.experimental import pallas as pl
from jax.experimental.pallas import tpu as pltpu
from jax.sharding import PartitionSpec as P

HEADS = 64
KVH = 8
HD = 128
DOCS = 4
BLOCK = 128
SEL = 256


EPSILON = 1e-05
ROPE_BASE = 500000.0
MASKED = -1e30
FAR = 1 << 30
CHUNKS = 2
TILE_COLS = 256
PAIR = 2
STATS = 16
HALVES = 2
DEPTH_TILE = 1024
WIDTH_TILE = 1024
SLOTS = 3
CUTS = 4


def cost(flops, bytes_accessed, transcendentals=0):
    return pl.CostEstimate(
        flops=int(flops), bytes_accessed=int(bytes_accessed), transcendentals=int(transcendentals)
    )


def rotation_tables(positions):
    half_dim = HD // 2
    inverse = ROPE_BASE ** (-(jnp.arange(half_dim, dtype=jnp.float32) * (2.0 / HD)))
    angles = positions.astype(jnp.float32)[:, None] * inverse[None, :]
    cosine = jnp.cos(angles)
    sine_part = jnp.sin(angles)
    return (
        jnp.concatenate([cosine, cosine], axis=-1),
        jnp.concatenate([-sine_part, sine_part], axis=-1),
    )


def rotate(values, cosine, sine_part):
    swapped = jnp.concatenate([values[:, HD // 2 :], values[:, : HD // 2]], axis=-1)
    return values * cosine + swapped * sine_part


def megabytes(count):
    return pltpu.CompilerParams(vmem_limit_bytes=count * 1024 * 1024)


def stream(sources, buffers, sems):
    def copies(step):
        slot = step % SLOTS
        made = []
        for i, (source, buffer) in enumerate(zip(sources, buffers)):
            rows = buffer.shape[1] // CUTS
            for cut in range(CUTS):
                here = pl.ds(cut * rows, rows)
                made.append(
                    pltpu.make_async_copy(
                        source(step).at[here], buffer.at[slot, here], sems.at[i * CUTS + cut, slot]
                    )
                )
        return made

    def start(step):
        for copy in copies(step):
            copy.start()

    def wait(step):
        for copy in copies(step):
            copy.wait()

    return start, wait


def project_kernel(n_blocks, n_weights, n_tables, chunk, is_last, place_ref, *refs):
    refs = list(refs)
    take = lambda count: [refs.pop(0) for _ in range(count)]
    blocks, weights = take(n_blocks), take(n_weights)
    prev = take(n_weights) if chunk else None
    if is_last:
        n_outs = len(refs) - 4 - n_tables
        tables, outs, (total, natural) = take(n_tables), take(n_outs), take(2)
        out, totals = outs[0], [total]
    else:
        totals = take(n_weights)
    buffers, sems = take(n_weights), refs[0]
    tile = buffers[0].shape[1]
    depth = blocks[0].shape[1]
    count = depth // tile
    rows_of = lambda ref: lambda step: ref.at[pl.ds(chunk * depth + step * tile, tile), :]
    start, wait = stream([rows_of(ref) for ref in weights], buffers, sems)

    for step in range(min(SLOTS, count)):
        start(step)
    for step in range(count):
        wait(step)
        cols = slice(step * tile, (step + 1) * tile)
        rows = jnp.concatenate([b[:, cols] for b in blocks], axis=0)
        for i, (buffer, total) in enumerate(zip(buffers, totals)):
            term = jnp.dot(rows, buffer[step % SLOTS], preferred_element_type=jnp.float32)
            if step:
                total[...] += term
            elif chunk:
                total[...] = prev[i][...] + term
            else:
                total[...] = term
        if step + SLOTS < count:
            start(step + SLOTS)

    if is_last:
        height = SEL // place_ref.shape[0]
        for block in range(SEL // height):
            here = slice(block * height, (block + 1) * height)
            there = pl.ds(pl.multiple_of(place_ref[block] * height, height), height)
            natural[there, :] = totals[0][here, :]
        if len(outs) == 2:
            side_ref = tables[0]
            for side in range(2):

                @pl.when(side_ref[0] == side)
                def _():
                    outs[1 - side][...] = natural[:, :HD].astype(out.dtype)
                    outs[side][...] = natural[:, HD:].astype(out.dtype)

            return
        if not tables:
            out[...] = natural[...].astype(out.dtype)
            return
        cos_ref, sin_ref = tables
        heads_here = natural.shape[1] // HD
        tile_q = TILE_COLS // heads_here
        for index in range(SEL // tile_q):
            here = slice(index * tile_q, (index + 1) * tile_q)
            stacked = jnp.concatenate(
                [
                    rotate(
                        natural[here, head * HD : (head + 1) * HD], cos_ref[here, :], sin_ref[here, :]
                    )
                    for head in range(heads_here)
                ],
                axis=0,
            )
            out[index] = stacked.T.astype(out.dtype)


def project(place, blocks, weights, prev, chunk, tables=(), side=()):
    depth = blocks[0].shape[1]
    widths = [w.shape[1] for w in weights]
    tile = min(DEPTH_TILE, depth)
    is_last = chunk + 1 == CHUNKS
    vmem = pl.BlockSpec(memory_space=pltpu.VMEM)
    hbm = pl.BlockSpec(memory_space=pltpu.HBM)
    totals = [((SEL, width), jnp.float32) for width in widths]
    if is_last:
        shape = (SEL * widths[0] // (HD * TILE_COLS), HD, TILE_COLS) if tables else (SEL, widths[0])
        outs, scratch = [(shape, jnp.bfloat16)], totals * 2
        if side:
            outs = [((SEL, HD), jnp.bfloat16)] * 2
    else:
        outs, scratch = totals, []
    return pl.pallas_call(
        functools.partial(
            project_kernel, len(blocks), len(weights), len(tables) + len(side), chunk, is_last
        ),
        in_specs=[pl.BlockSpec(memory_space=pltpu.SMEM)]
        + [vmem] * len(blocks)
        + [hbm] * len(weights)
        + [vmem] * (len(prev) + len(tables))
        + [pl.BlockSpec(memory_space=pltpu.SMEM)] * len(side),
        out_specs=[vmem] * len(outs),
        out_shape=[jax.ShapeDtypeStruct(*o) for o in outs],
        scratch_shapes=[pltpu.VMEM(*x) for x in scratch]
        + [pltpu.VMEM((SLOTS, tile, width), jnp.bfloat16) for width in widths]
        + [pltpu.SemaphoreType.DMA((len(weights) * CUTS, SLOTS))],
        compiler_params=megabytes(16),
        cost_estimate=cost(2 * SEL * depth * sum(widths), 2 * depth * (sum(widths) + SEL)),
        name="project",
    )(place, *blocks, *weights, *prev, *tables, *side)


def select_kernel(n_dest, n_src, place_ref, slot_ref, head_ref, *refs):
    sources = refs[:n_src]
    outs = refs[n_src : n_src + n_dest]
    sems = refs[n_src + n_dest]
    for doc in range(DOCS):
        for src in range(n_src):

            @pl.when(place_ref[doc] == src)
            def _():
                for dest in range(n_dest):
                    cols = pl.ds(pl.multiple_of(head_ref[dest] * HD, HD), HD)
                    pltpu.make_async_copy(
                        sources[src].at[slot_ref[doc], :, :, cols],
                        outs[dest].at[:, doc],
                        sems.at[dest, doc],
                    ).start()

    for dest in range(n_dest):
        for doc in range(DOCS):
            pltpu.make_async_copy(
                sources[0].at[0, :, :, 0:HD], outs[dest].at[:, doc], sems.at[dest, doc]
            ).wait()


def select_docs(sources, place, slot, heads, n_dest):
    tokens = sources[0].shape[2]
    shape = (2, DOCS, tokens, HD)
    smem = pl.BlockSpec(memory_space=pltpu.SMEM)
    return pl.pallas_call(
        functools.partial(select_kernel, n_dest, len(sources)),
        in_specs=[smem] * 3 + [pl.BlockSpec(memory_space=pl.ANY)] * len(sources),
        out_specs=[pl.BlockSpec(memory_space=pltpu.VMEM)] * n_dest,
        out_shape=[jax.ShapeDtypeStruct(shape, jnp.bfloat16)] * n_dest,
        scratch_shapes=[pltpu.SemaphoreType.DMA((n_dest, DOCS))],
        compiler_params=megabytes(8),
        cost_estimate=cost(0, 4 * n_dest * math.prod(shape)),
        name="select_docs",
    )(place, slot, heads, *sources)


def split_exact(value):
    pieces = []
    for _ in range(3):
        pieces.append(value.astype(jnp.bfloat16).astype(jnp.float32))
        value = value - pieces[-1]
    return pieces


def attend_kernel(n_chunks, with_new, n_tiles, tile_q, first_tile, first_ref, pos_ref, odd_ref, *refs):
    refs = list(refs)
    take = lambda count: [refs.pop(0) for _ in range(count)]
    chunks = take(n_chunks)
    dead_ref, qpos_ref, queries = take(3)
    if with_new:
        cos_ref, sin_ref, new_a, new_b = take(4)
    if with_new:
        top, total, summed, values, new_key, new_value = take(6)
    else:
        packed, top, total, summed, values = take(5)
    together = min(PAIR, n_tiles)
    n_pairs = n_tiles // together
    tokens = chunks[0].shape[2]
    scale = math.log2(math.e) / math.sqrt(HD)

    for chunk in range(n_chunks):
        for doc in range(DOCS):
            values[doc, :, chunk * tokens : (chunk + 1) * tokens] = chunks[chunk][1, doc].T
    if with_new:
        for odd, (key_ref, value_ref) in enumerate(((new_a, new_b), (new_b, new_a))):

            @pl.when(odd_ref[0] == odd)
            def _():
                new_key[...] = rotate(
                    key_ref[...].astype(jnp.float32), cos_ref[...], sin_ref[...]
                ).astype(jnp.bfloat16)
                new_value[...] = value_ref[...].T


    one_row = jnp.where(
        lax.broadcasted_iota(jnp.int32, (HD, TILE_COLS), 0) == 0, 1.0, 0.0
    ).astype(jnp.bfloat16)

    def update(tile, parts):
        best = functools.reduce(
            jnp.maximum, [jnp.max(scores, axis=0, keepdims=True) for scores, _ in parts]
        )
        old = top[tile]
        new = jnp.maximum(old, best)
        shrink = jnp.exp2((old - new) * scale)
        running = total[tile] * shrink
        mixed = summed[tile] * shrink
        for scores, value in parts:
            weights = jnp.exp2((scores - new) * scale)
            running += jnp.sum(weights, axis=0, keepdims=True)
            mixed += jnp.dot(
                value, weights.astype(jnp.bfloat16), preferred_element_type=jnp.float32
            )
        top[tile] = new
        total[tile] = running
        summed[tile] = mixed

    @pl.loop(0, n_pairs)
    def _(pair):
        tiles = [pair * together + i for i in range(together)]
        for tile in tiles:
            top[tile] = jnp.full(top.shape[1:], MASKED, jnp.float32)
            total[tile] = jnp.zeros(total.shape[1:], jnp.float32)
            summed[tile] = jnp.zeros(summed.shape[1:], jnp.float32)
        if with_new:
            fresh = []
            for tile in tiles:
                scores = jnp.dot(
                    new_key[...], queries[first_tile + tile], preferred_element_type=jnp.float32
                )
                key_index = lax.broadcasted_iota(jnp.int32, scores.shape, 0)
                q_index = (first_tile + tile) * tile_q + lax.broadcasted_iota(jnp.int32, scores.shape, 1) % tile_q
                fresh.append(jnp.where(key_index <= q_index, scores, MASKED))
            for tile, scores in zip(tiles, fresh):
                update(tile, [(scores, new_value[...])])

        @pl.loop(0, DOCS)
        def _(doc):
            firsts = [first_ref[doc * n_chunks + chunk] for chunk in range(n_chunks)]
            lowest = functools.reduce(jnp.minimum, firsts)
            highest = functools.reduce(jnp.maximum, firsts)
            reach = highest + tokens - 1

            def visit(masked, members):
                found = []
                for tile in tiles:
                    extended = jnp.concatenate([queries[first_tile + tile], one_row], axis=0)
                    parts = []
                    for chunk in members:
                        span = slice(chunk * tokens, (chunk + 1) * tokens)
                        keys = jnp.concatenate(
                            [chunks[chunk][0, doc], dead_ref[doc, span, :]], axis=1
                        )
                        scores = jnp.dot(keys, extended, preferred_element_type=jnp.float32)
                        if masked:
                            key_pos = firsts[chunk] + lax.broadcasted_iota(
                                jnp.int32, scores.shape, 0
                            )
                            scores = jnp.where(key_pos <= qpos_ref[first_tile + tile], scores, MASKED)
                        parts.append((scores, values[doc, :, span]))
                    found.append(parts)
                for tile, parts in zip(tiles, found):
                    update(tile, parts)

            start = first_tile * tile_q + pair * together * tile_q
            first_here = pos_ref[start]
            last_here = pos_ref[start + together * tile_q - 1]
            whole = reach <= first_here
            spread = jnp.logical_not(whole) & (highest <= last_here)
            ragged = (lowest <= last_here) & (highest > last_here)

            @pl.when(whole)
            def _():
                visit(False, range(n_chunks))

            @pl.when(spread)
            def _():
                visit(True, range(n_chunks))

            for chunk in range(n_chunks):

                @pl.when(ragged & (firsts[chunk] <= last_here))
                def _():
                    visit(True, [chunk])

        if not with_new:
            for tile in tiles:
                extra = jnp.concatenate(
                    split_exact(top[tile])
                    + split_exact(total[tile])
                    + [jnp.zeros((STATS - 6, TILE_COLS), jnp.float32)],
                    axis=0,
                )
                packed[tile] = jnp.concatenate([summed[tile], extra], axis=0).astype(jnp.bfloat16)


def attend(chunks, dead, first_pos, selected, q_pos, odd, queries, first_tile, n_tiles, fresh):
    n_chunks = len(chunks)
    tokens = chunks[0].shape[2]
    tile_q = SEL // q_pos.shape[0]
    smem = pl.BlockSpec(memory_space=pltpu.SMEM)
    vmem = pl.BlockSpec(memory_space=pltpu.VMEM)
    operands = [first_pos, selected, odd, *chunks, dead, q_pos, queries, *fresh]
    state = [((n_tiles, 1, TILE_COLS), jnp.float32)] * 2
    state += [((n_tiles, HD, TILE_COLS), jnp.float32)]
    values = ((DOCS, HD, n_chunks * tokens), jnp.bfloat16)
    if fresh:
        outs = state
        scratch = [values, ((SEL, HD), jnp.bfloat16), ((HD, SEL), jnp.bfloat16)]
    else:
        outs = [((n_tiles, HD + STATS, TILE_COLS), jnp.bfloat16)]
        scratch = state + [values]
    pairs = n_tiles * TILE_COLS * DOCS * n_chunks * tokens // 2
    return pl.pallas_call(
        functools.partial(
            attend_kernel, n_chunks, bool(fresh), n_tiles, tile_q, first_tile
        ),
        in_specs=[smem] * 3 + [vmem] * (len(operands) - 3),
        out_specs=[vmem] * len(outs),
        out_shape=[jax.ShapeDtypeStruct(*s) for s in outs],
        scratch_shapes=[pltpu.VMEM(*s) for s in scratch],
        compiler_params=megabytes(16),
        cost_estimate=cost(1, 1) if fresh else cost(4 * pairs * HD, 0, pairs),
        name="attend",
    )(*operands)


def merge_kernel(top_a, total_a, mixed_a, *refs):
    packs, out_ref = refs[:-1], refs[-1]
    scale = math.log2(math.e) / math.sqrt(HD)
    n_tiles = top_a.shape[0]
    tile_q = SEL // n_tiles
    for tile in range(n_tiles):
        packed = packs[tile * len(packs) // n_tiles].at[tile % (n_tiles // len(packs))]
        extra = packed[HD:, :].astype(jnp.float32)
        top_b = extra[0:1] + (extra[1:2] + extra[2:3])
        total_b = extra[3:4] + (extra[4:5] + extra[5:6])
        new = jnp.maximum(top_a[tile], top_b)
        part_a = jnp.exp2((top_a[tile] - new) * scale)
        part_b = jnp.exp2((top_b - new) * scale)
        total = total_a[tile] * part_a + total_b * part_b
        mixed = mixed_a[tile] * part_a + packed[:HD, :].astype(jnp.float32) * part_b
        finished = (mixed / total).T.astype(jnp.bfloat16)
        for head in range(TILE_COLS // tile_q):
            out_ref[tile * tile_q : (tile + 1) * tile_q, head * HD : (head + 1) * HD] = finished[
                head * tile_q : (head + 1) * tile_q, :
            ]


def merge(mine, theirs):
    n_tiles = mine[0].shape[0]
    shape = (SEL, TILE_COLS * n_tiles // SEL * HD)
    return pl.pallas_call(
        merge_kernel,
        out_shape=jax.ShapeDtypeStruct(shape, jnp.bfloat16),
        compiler_params=megabytes(16),
        cost_estimate=cost(4 * math.prod(shape), 8 * math.prod(shape)),
        name="merge",
    )(*mine, *theirs)


def out_kernel(n_blocks, first_col, place_ref, x_ref, w_ref, *refs):
    outs = refs[:n_blocks]
    ordered, slots, sems = refs[n_blocks:]
    rows = SEL // n_blocks
    tile = slots.shape[2]
    count = outs[0].shape[1] // tile
    start, wait = stream(
        [lambda step: w_ref.at[:, pl.ds(first_col + step * tile, tile)]], [slots], sems
    )

    for step in range(min(SLOTS, count)):
        start(step)
    for block in range(n_blocks):
        there = pl.ds(pl.multiple_of(place_ref[block] * rows, rows), rows)
        ordered[block * rows : (block + 1) * rows, :] = x_ref[there, :]
    for step in range(count):
        wait(step)
        product = jnp.dot(
            ordered[...].astype(jnp.bfloat16),
            slots[step % SLOTS],
            preferred_element_type=jnp.float32,
        )
        cols = slice(step * tile, (step + 1) * tile)
        for block, out in enumerate(outs):
            out[:, cols] = product[block * rows : (block + 1) * rows, :].astype(out.dtype)
        if step + SLOTS < count:
            start(step + SLOTS)


def project_out(place, attention, w_out, chunk, kinds):
    depth = w_out.shape[0]
    n_blocks = len(kinds)
    width = w_out.shape[1] // CHUNKS
    rows = SEL // n_blocks
    if rows % 16:
        attention = attention.astype(jnp.float32)
    vmem = pl.BlockSpec(memory_space=pltpu.VMEM)
    return pl.pallas_call(
        functools.partial(out_kernel, n_blocks, chunk * width),
        in_specs=[
            pl.BlockSpec(memory_space=pltpu.SMEM),
            vmem,
            pl.BlockSpec(memory_space=pltpu.HBM),
        ],
        out_specs=[vmem] * n_blocks,
        out_shape=[jax.ShapeDtypeStruct((rows, width), kind) for kind in kinds],
        scratch_shapes=[
            pltpu.VMEM((SEL, depth), attention.dtype),
            pltpu.VMEM((SLOTS, depth, min(WIDTH_TILE, width)), jnp.bfloat16),
            pltpu.SemaphoreType.DMA((CUTS, SLOTS)),
        ],
        compiler_params=megabytes(16),
        cost_estimate=cost(2 * SEL * depth * width, 2 * depth * (width + SEL) + 4 * SEL * width),
        name="project_out",
    )(place, attention, w_out)


def per_device(
    hidden_in, norm_gain, w_query, w_keyval, w_out, pool_cache, doc_slot, doc_blocks, sel_pos
):
    tp_size = lax.axis_size("tp")
    req_size = lax.axis_size("req")
    me = lax.axis_index("tp")
    rows, width = hidden_in.shape
    slots, tokens = pool_cache.shape[:2]
    heads_here = w_query.shape[1] // HD
    selected = sel_pos[0]
    lengths = doc_blocks[0] * BLOCK

    if tp_size == KVH:
        ring = [*range(0, tp_size, 2), *range(tp_size - 1, 0, -2)]
    else:
        ring = list(range(tp_size))
    far = tp_size // 2
    forth = [(ring[p], ring[(p + 1) % tp_size]) for p in range(tp_size)]
    back = [(dst, src) for src, dst in forth]
    steps = [0] + [sign * k for k in range(1, far) for sign in (-1, 1)] + [far]
    table = [[ring[(ring.index(i) + s) % tp_size] for s in steps] for i in range(tp_size)]
    place = jnp.array(table, jnp.int32)[me]

    widened = hidden_in.astype(jnp.float32)
    normed = (
        widened
        * lax.rsqrt(jnp.mean(widened * widened, axis=-1, keepdims=True) + EPSILON)
        * norm_gain
    ).astype(jnp.bfloat16)
    w_query, w_keyval, w_out = (
        pltpu.with_memory_space_constraint(w, pltpu.HBM) for w in (w_query, w_keyval, w_out)
    )
    middle = tp_size // 2
    order = jnp.arange(middle, dtype=jnp.int32)
    offsets = jnp.cumsum(lengths) - lengths
    first_slot = (me ^ order) * tokens
    slot_tokens = first_slot[:, None] + jnp.arange(tokens, dtype=jnp.int32)[None, :]
    cache_pos = offsets[:, None, None] + slot_tokens[None]
    is_valid = slot_tokens[None] < lengths[:, None, None]
    replaced = jnp.any(cache_pos[..., None] == selected, axis=-1)
    dead = jnp.where(is_valid & jnp.logical_not(replaced), 0.0, MASKED).astype(jnp.bfloat16)
    dead = jnp.broadcast_to(dead[..., None], (DOCS, middle, tokens, HD))
    dead = dead.reshape(DOCS, middle * tokens, HD)
    first_pos = jnp.where(
        first_slot[None] < lengths[:, None], offsets[:, None] + first_slot[None], FAR
    ).reshape(-1)
    cosine, sine_part = rotation_tables(selected)
    heads_here = w_query.shape[1] // HD
    tile_q = TILE_COLS // heads_here
    q_pos = jnp.tile(selected.reshape(SEL // tile_q, tile_q), (1, heads_here))
    q_pos = q_pos.reshape(SEL // tile_q, 1, TILE_COLS)

    part = width // CHUNKS
    streams = []
    for chunk in range(CHUNKS):
        own = normed[:, chunk * part : (chunk + 1) * part]
        streams.append({"before": [own], "behind": [own]})
    for k in range(1, far + 1):
        for chunk, held in enumerate(streams):
            if k < far or chunk % 2 == 0:
                held["before"].append(lax.ppermute(held["before"][-1], "tp", forth))
            if k < far or chunk % 2 == 1:
                held["behind"].append(lax.ppermute(held["behind"][-1], "tp", back))
        first = streams[0]["before"]
        if k == 1:
            heads_of = [held[side] for held in streams for side in ("before", "behind")]
            pool_cache, *firsts = lax.optimization_barrier(
                (pool_cache, *[held[-1] for held in heads_of])
            )
            for held, value in zip(heads_of, firsts):
                held[-1] = value
            by_kind = pool_cache.transpose(0, 2, 1, 3)
            sources = [by_kind]
            for shift in range(1, req_size):
                pairs = [((i + shift) % req_size, i) for i in range(req_size)]
                sources.append(lax.ppermute(by_kind, "req", pairs))
            holder = (doc_slot // slots - lax.axis_index("req")) % req_size
            slot = doc_slot % slots
            side = (me < middle).astype(jnp.int32)[None]
            odd = (me % 2 if tp_size == KVH else me * 0)[None]
            takers = jnp.concatenate([me ^ order, me ^ order ^ middle]) * KVH // tp_size
        if k == 2:
            first[-1], dead, first_pos, cosine, sine_part, q_pos, takers, holder, slot, place, side, odd = (
                lax.optimization_barrier(
                    (first[-1], dead, first_pos, cosine, sine_part, q_pos, takers, holder, slot)
                    + (place, side, odd)
                )
            )
        if k == far - 1:
            sent = select_docs(sources, holder, slot, takers, tp_size)
            first[-1], *sent = lax.optimization_barrier((first[-1], *sent))
    weights = [w_keyval, w_query]
    sums = []
    for chunk, held in enumerate(streams):
        blocks = [held["before"][0]]
        for k in range(1, far):
            blocks += [held["before"][k], held["behind"][k]]
        blocks.append(held["behind" if chunk % 2 else "before"][far])
        if rows % 16:
            blocks = [jnp.concatenate(blocks, axis=0)]
        if chunk + 1 < CHUNKS:
            sums = project(place, blocks, weights, sums, chunk)
    across = [(i, i ^ middle) for i in range(tp_size)]
    if tp_size == KVH:
        first, second = project(place, blocks, weights[:1], sums[:1], CHUNKS - 1, (), (side,))
        first, second, *blocks = lax.optimization_barrier((first, second, *blocks))
        keys_to_even = [(i, 2 * i if i < middle else 2 * (i - middle) + 1) for i in range(tp_size)]
        keys_to_odd = [(i, 2 * i + 1 if i < middle else 2 * (i - middle)) for i in range(tp_size)]
        new = [lax.ppermute(first, "tp", keys_to_even), lax.ppermute(second, "tp", keys_to_odd)]
    else:
        (keyval,) = project(place, blocks, weights[:1], sums[:1], CHUNKS - 1)
        everyone = lax.all_gather(keyval, "tp", axis=1, tiled=True)
        my_head = me * KVH // tp_size
        new = [
            lax.dynamic_slice_in_dim(everyone, (kind * KVH + my_head) * HD, HD, axis=1)
            for kind in range(2)
        ]
    (queries,) = project(
        place, blocks, weights[1:], sums[1:], CHUNKS - 1, (cosine, sine_part)
    )
    queries, new = lax.optimization_barrier((queries, new))

    def exchange(kept):
        got = {
            j: lax.ppermute(kept[j], "tp", [(i, i ^ j) for i in range(tp_size)])
            for j in range(middle - 1, 0, -1)
        }
        return [kept[0]] + [got[j] for j in range(1, middle)]

    own, partners = sent[:middle], exchange(sent[middle:])
    own, *partners[2:] = lax.optimization_barrier((own, *partners[2:]))
    chunks = [exchange(own), partners]
    n_tiles = queries.shape[0]
    their_queries = lax.ppermute(queries, "tp", across)

    metadata = (dead, first_pos, selected, q_pos, odd)
    share = n_tiles // min(HALVES, n_tiles)
    theirs = [
        lax.ppermute(
            attend(chunks[1], *metadata, their_queries, first, share, [])[0], "tp", across
        )
        for first in range(n_tiles - share, -1, -share)
    ][::-1]
    mine = attend(chunks[0], *metadata, queries, 0, n_tiles, [cosine, sine_part, *new])
    attention = merge(mine, theirs)

    finished = []
    for chunk in range(CHUNKS):
        kinds = [jnp.float32] * (tp_size - 1) + [jnp.bfloat16]
        pieces = project_out(place, attention, w_out, chunk, kinds)
        to_forth, to_back = list(pieces[2 : tp_size - 1 : 2]), list(pieces[1 : tp_size - 1 : 2])
        (to_back if chunk % 2 else to_forth).append(pieces[-1])
        total = pieces[0]
        for terms, pairs in ((to_forth, forth), (to_back, back)):
            held = None
            for term in reversed(terms):
                if held is not None:
                    term = term + held.astype(jnp.float32)
                held = lax.ppermute(term.astype(jnp.bfloat16), "tp", pairs)
            total = total + held.astype(jnp.float32)
        finished.append(total.astype(jnp.bfloat16))
    return jnp.concatenate(finished, axis=1)


def solution(mesh):
    placed = (
        P(("groups", "req", "tp"), None),
        P(),
        P(None, "tp"),
        P(None, "tp"),
        P("tp", None),
        P(("groups", "req"), "tp", None, None),
        P(("groups", "req")),
        P(("groups", "req"), None),
        P(("groups", "req"), None),
    )
    return jax.shard_map(
        per_device,
        mesh=mesh,
        in_specs=placed,
        out_specs=P(("groups", "req", "tp"), None),
        check_vma=False,
    )
```

```python
import functools
import math

import jax
import jax.numpy as jnp
from jax import lax
from jax.experimental import pallas as pl
from jax.experimental.pallas import tpu as pltpu
from jax.sharding import PartitionSpec as P

HEADS = 64
KVH = 8
HD = 128
DOCS = 4
BLOCK = 128
SEL = 256


EPSILON = 1e-05
ROPE_BASE = 500000.0
MASKED = -1e30
FAR = 1 << 30
CHUNKS = 2
TILE_COLS = 256
PAIR = 2
STATS = 16
HALVES = 2
DEPTH_TILE = 1024
WIDTH_TILE = 1024
SLOTS = 3
CUTS = 4


def cost(flops, bytes_accessed, transcendentals=0):
    return pl.CostEstimate(
        flops=int(flops), bytes_accessed=int(bytes_accessed), transcendentals=int(transcendentals)
    )


def rotation_tables(positions):
    half_dim = HD // 2
    inverse = ROPE_BASE ** (-(jnp.arange(half_dim, dtype=jnp.float32) * (2.0 / HD)))
    angles = positions.astype(jnp.float32)[:, None] * inverse[None, :]
    cosine = jnp.cos(angles)
    sine_part = jnp.sin(angles)
    return (
        jnp.concatenate([cosine, cosine], axis=-1),
        jnp.concatenate([-sine_part, sine_part], axis=-1),
    )


def rotate(values, cosine, sine_part):
    swapped = jnp.concatenate([values[:, HD // 2 :], values[:, : HD // 2]], axis=-1)
    return values * cosine + swapped * sine_part


def megabytes(count):
    return pltpu.CompilerParams(vmem_limit_bytes=count * 1024 * 1024)


def stream(sources, buffers, sems):
    def copies(step):
        slot = step % SLOTS
        made = []
        for i, (source, buffer) in enumerate(zip(sources, buffers)):
            rows = buffer.shape[1] // CUTS
            for cut in range(CUTS):
                here = pl.ds(cut * rows, rows)
                made.append(
                    pltpu.make_async_copy(
                        source(step).at[here], buffer.at[slot, here], sems.at[i * CUTS + cut, slot]
                    )
                )
        return made

    def start(step):
        for copy in copies(step):
            copy.start()

    def wait(step):
        for copy in copies(step):
            copy.wait()

    return start, wait


def project_kernel(n_blocks, chunk, is_last, split, place_ref, *refs):
    refs = list(refs)
    take = lambda count: [refs.pop(0) for _ in range(count)]
    blocks, weights = take(n_blocks), take(2)
    prev = take(2) if chunk else None
    if is_last:
        cos_ref, sin_ref, side_ref = take(3)
        out_kv, (out_q,) = take(2 if split else 1), take(1)
        totals, (natural_kv, natural_q) = take(2), take(2)
    else:
        totals = take(2)
    buffers, sems = take(2), refs[0]
    tile = buffers[0].shape[1]
    depth = blocks[0].shape[1]
    count = depth // tile
    rows_of = lambda ref: lambda step: ref.at[pl.ds(chunk * depth + step * tile, tile), :]
    start, wait = stream([rows_of(ref) for ref in weights], buffers, sems)

    for step in range(min(SLOTS, count)):
        start(step)
    for step in range(count):
        wait(step)
        cols = slice(step * tile, (step + 1) * tile)
        rows = jnp.concatenate([b[:, cols] for b in blocks], axis=0)
        for i, (buffer, total) in enumerate(zip(buffers, totals)):
            term = jnp.dot(rows, buffer[step % SLOTS], preferred_element_type=jnp.float32)
            if step:
                total[...] += term
            elif chunk:
                total[...] = prev[i][...] + term
            else:
                total[...] = term
        if step + SLOTS < count:
            start(step + SLOTS)

    if is_last:
        height = SEL // place_ref.shape[0]
        for block in range(SEL // height):
            here = slice(block * height, (block + 1) * height)
            there = pl.ds(pl.multiple_of(place_ref[block] * height, height), height)
            natural_kv[there, :] = totals[0][here, :]
            natural_q[there, :] = totals[1][here, :]
        if split:
            for side in range(2):

                @pl.when(side_ref[0] == side)
                def _():
                    out_kv[1 - side][...] = natural_kv[:, :HD].astype(jnp.bfloat16)
                    out_kv[side][...] = natural_kv[:, HD:].astype(jnp.bfloat16)

        else:
            out_kv[0][...] = natural_kv[...].astype(jnp.bfloat16)
        heads_here = natural_q.shape[1] // HD
        tile_q = TILE_COLS // heads_here
        for index in range(SEL // tile_q):
            here = slice(index * tile_q, (index + 1) * tile_q)
            stacked = jnp.concatenate(
                [
                    rotate(
                        natural_q[here, head * HD : (head + 1) * HD], cos_ref[here, :], sin_ref[here, :]
                    )
                    for head in range(heads_here)
                ],
                axis=0,
            )
            out_q[index] = stacked.T.astype(jnp.bfloat16)


def project(place, blocks, weights, prev, chunk, tables, side, split):
    depth = blocks[0].shape[1]
    widths = [w.shape[1] for w in weights]
    tile = min(DEPTH_TILE, depth)
    is_last = chunk + 1 == CHUNKS
    smem = pl.BlockSpec(memory_space=pltpu.SMEM)
    vmem = pl.BlockSpec(memory_space=pltpu.VMEM)
    hbm = pl.BlockSpec(memory_space=pltpu.HBM)
    totals = [((SEL, width), jnp.float32) for width in widths]
    operands, specs = [place, *blocks, *weights, *prev], [smem] + [vmem] * len(blocks) + [hbm] * 2
    specs += [vmem] * len(prev)
    outs, scratch = totals, []
    if is_last:
        operands += [*tables, side]
        specs += [vmem] * 2 + [smem]
        outs = [(SEL, HD)] * 2 if split else [(SEL, widths[0])]
        outs = outs + [(SEL * widths[1] // (HD * TILE_COLS), HD, TILE_COLS)]
        outs, scratch = [(shape, jnp.bfloat16) for shape in outs], totals * 2
    return pl.pallas_call(
        functools.partial(project_kernel, len(blocks), chunk, is_last, split),
        in_specs=specs,
        out_specs=[vmem] * len(outs),
        out_shape=[jax.ShapeDtypeStruct(*o) for o in outs],
        scratch_shapes=[pltpu.VMEM(*x) for x in scratch]
        + [pltpu.VMEM((SLOTS, tile, width), jnp.bfloat16) for width in widths]
        + [pltpu.SemaphoreType.DMA((2 * CUTS, SLOTS))],
        compiler_params=megabytes(16),
        cost_estimate=cost(2 * SEL * depth * sum(widths), 2 * depth * (sum(widths) + SEL)),
        name="project",
    )(*operands)


def select_kernel(n_dest, n_src, place_ref, slot_ref, head_ref, *refs):
    sources = refs[:n_src]
    outs = refs[n_src : n_src + n_dest]
    sems = refs[n_src + n_dest]
    for doc in range(DOCS):
        for src in range(n_src):

            @pl.when(place_ref[doc] == src)
            def _():
                for dest in range(n_dest):
                    cols = pl.ds(pl.multiple_of(head_ref[dest] * HD, HD), HD)
                    pltpu.make_async_copy(
                        sources[src].at[slot_ref[doc], :, :, cols],
                        outs[dest].at[:, doc],
                        sems.at[dest, doc],
                    ).start()

    for dest in range(n_dest):
        for doc in range(DOCS):
            pltpu.make_async_copy(
                sources[0].at[0, :, :, 0:HD], outs[dest].at[:, doc], sems.at[dest, doc]
            ).wait()


def select_docs(sources, place, slot, heads, n_dest):
    tokens = sources[0].shape[2]
    shape = (2, DOCS, tokens, HD)
    smem = pl.BlockSpec(memory_space=pltpu.SMEM)
    return pl.pallas_call(
        functools.partial(select_kernel, n_dest, len(sources)),
        in_specs=[smem] * 3 + [pl.BlockSpec(memory_space=pl.ANY)] * len(sources),
        out_specs=[pl.BlockSpec(memory_space=pltpu.VMEM)] * n_dest,
        out_shape=[jax.ShapeDtypeStruct(shape, jnp.bfloat16)] * n_dest,
        scratch_shapes=[pltpu.SemaphoreType.DMA((n_dest, DOCS))],
        compiler_params=megabytes(8),
        cost_estimate=cost(0, 4 * n_dest * math.prod(shape)),
        name="select_docs",
    )(place, slot, heads, *sources)


def split_exact(value):
    pieces = []
    for _ in range(3):
        pieces.append(value.astype(jnp.bfloat16).astype(jnp.float32))
        value = value - pieces[-1]
    return pieces


def attend_kernel(n_chunks, with_new, n_tiles, tile_q, first_tile, first_ref, pos_ref, odd_ref, *refs):
    refs = list(refs)
    take = lambda count: [refs.pop(0) for _ in range(count)]
    chunks = take(n_chunks)
    dead_ref, qpos_ref, queries = take(3)
    if with_new:
        cos_ref, sin_ref, new_a, new_b = take(4)
    if with_new:
        top, total, summed, values, new_key, new_value = take(6)
    else:
        packed, top, total, summed, values = take(5)
    together = min(PAIR, n_tiles)
    n_pairs = n_tiles // together
    tokens = chunks[0].shape[2]
    scale = math.log2(math.e) / math.sqrt(HD)

    for chunk in range(n_chunks):
        for doc in range(DOCS):
            values[doc, :, chunk * tokens : (chunk + 1) * tokens] = chunks[chunk][1, doc].T
    if with_new:
        for odd, (key_ref, value_ref) in enumerate(((new_a, new_b), (new_b, new_a))):

            @pl.when(odd_ref[0] == odd)
            def _():
                new_key[...] = rotate(
                    key_ref[...].astype(jnp.float32), cos_ref[...], sin_ref[...]
                ).astype(jnp.bfloat16)
                new_value[...] = value_ref[...].T


    one_row = jnp.where(
        lax.broadcasted_iota(jnp.int32, (HD, TILE_COLS), 0) == 0, 1.0, 0.0
    ).astype(jnp.bfloat16)

    def update(tile, parts):
        best = functools.reduce(
            jnp.maximum, [jnp.max(scores, axis=0, keepdims=True) for scores, _ in parts]
        )
        old = top[tile]
        new = jnp.maximum(old, best)
        shrink = jnp.exp2((old - new) * scale)
        running = total[tile] * shrink
        mixed = summed[tile] * shrink
        for scores, value in parts:
            weights = jnp.exp2((scores - new) * scale)
            running += jnp.sum(weights, axis=0, keepdims=True)
            mixed += jnp.dot(
                value, weights.astype(jnp.bfloat16), preferred_element_type=jnp.float32
            )
        top[tile] = new
        total[tile] = running
        summed[tile] = mixed

    @pl.loop(0, n_pairs)
    def _(pair):
        tiles = [pair * together + i for i in range(together)]
        for tile in tiles:
            top[tile] = jnp.full(top.shape[1:], MASKED, jnp.float32)
            total[tile] = jnp.zeros(total.shape[1:], jnp.float32)
            summed[tile] = jnp.zeros(summed.shape[1:], jnp.float32)
        if with_new:
            fresh = []
            for tile in tiles:
                scores = jnp.dot(
                    new_key[...], queries[first_tile + tile], preferred_element_type=jnp.float32
                )
                key_index = lax.broadcasted_iota(jnp.int32, scores.shape, 0)
                q_index = (first_tile + tile) * tile_q + lax.broadcasted_iota(jnp.int32, scores.shape, 1) % tile_q
                fresh.append(jnp.where(key_index <= q_index, scores, MASKED))
            for tile, scores in zip(tiles, fresh):
                update(tile, [(scores, new_value[...])])

        @pl.loop(0, DOCS)
        def _(doc):
            firsts = [first_ref[doc * n_chunks + chunk] for chunk in range(n_chunks)]
            lowest = functools.reduce(jnp.minimum, firsts)
            highest = functools.reduce(jnp.maximum, firsts)
            reach = highest + tokens - 1

            def visit(masked, members):
                found = []
                for tile in tiles:
                    extended = jnp.concatenate([queries[first_tile + tile], one_row], axis=0)
                    parts = []
                    for chunk in members:
                        span = slice(chunk * tokens, (chunk + 1) * tokens)
                        keys = jnp.concatenate(
                            [chunks[chunk][0, doc], dead_ref[doc, span, :]], axis=1
                        )
                        scores = jnp.dot(keys, extended, preferred_element_type=jnp.float32)
                        if masked:
                            key_pos = firsts[chunk] + lax.broadcasted_iota(
                                jnp.int32, scores.shape, 0
                            )
                            scores = jnp.where(key_pos <= qpos_ref[first_tile + tile], scores, MASKED)
                        parts.append((scores, values[doc, :, span]))
                    found.append(parts)
                for tile, parts in zip(tiles, found):
                    update(tile, parts)

            start = first_tile * tile_q + pair * together * tile_q
            first_here = pos_ref[start]
            last_here = pos_ref[start + together * tile_q - 1]
            whole = reach <= first_here
            spread = jnp.logical_not(whole) & (highest <= last_here)
            ragged = (lowest <= last_here) & (highest > last_here)

            @pl.when(whole)
            def _():
                visit(False, range(n_chunks))

            @pl.when(spread)
            def _():
                visit(True, range(n_chunks))

            for chunk in range(n_chunks):

                @pl.when(ragged & (firsts[chunk] <= last_here))
                def _():
                    visit(True, [chunk])

        if not with_new:
            for tile in tiles:
                extra = jnp.concatenate(
                    split_exact(top[tile])
                    + split_exact(total[tile])
                    + [jnp.zeros((STATS - 6, TILE_COLS), jnp.float32)],
                    axis=0,
                )
                packed[tile] = jnp.concatenate([summed[tile], extra], axis=0).astype(jnp.bfloat16)


def attend(chunks, dead, first_pos, selected, q_pos, odd, queries, first_tile, n_tiles, fresh):
    n_chunks = len(chunks)
    tokens = chunks[0].shape[2]
    tile_q = SEL // q_pos.shape[0]
    smem = pl.BlockSpec(memory_space=pltpu.SMEM)
    vmem = pl.BlockSpec(memory_space=pltpu.VMEM)
    operands = [first_pos, selected, odd, *chunks, dead, q_pos, queries, *fresh]
    state = [((n_tiles, 1, TILE_COLS), jnp.float32)] * 2
    state += [((n_tiles, HD, TILE_COLS), jnp.float32)]
    values = ((DOCS, HD, n_chunks * tokens), jnp.bfloat16)
    if fresh:
        outs = state
        scratch = [values, ((SEL, HD), jnp.bfloat16), ((HD, SEL), jnp.bfloat16)]
    else:
        outs = [((n_tiles, HD + STATS, TILE_COLS), jnp.bfloat16)]
        scratch = state + [values]
    pairs = n_tiles * TILE_COLS * DOCS * n_chunks * tokens // 2
    return pl.pallas_call(
        functools.partial(
            attend_kernel, n_chunks, bool(fresh), n_tiles, tile_q, first_tile
        ),
        in_specs=[smem] * 3 + [vmem] * (len(operands) - 3),
        out_specs=[vmem] * len(outs),
        out_shape=[jax.ShapeDtypeStruct(*s) for s in outs],
        scratch_shapes=[pltpu.VMEM(*s) for s in scratch],
        compiler_params=megabytes(16),
        cost_estimate=cost(1, 1) if fresh else cost(4 * pairs * HD, 0, pairs),
        name="attend",
    )(*operands)


def merge_kernel(top_a, total_a, mixed_a, *refs):
    packs, out_ref = refs[:-1], refs[-1]
    scale = math.log2(math.e) / math.sqrt(HD)
    n_tiles = top_a.shape[0]
    tile_q = SEL // n_tiles
    for tile in range(n_tiles):
        packed = packs[tile * len(packs) // n_tiles].at[tile % (n_tiles // len(packs))]
        extra = packed[HD:, :].astype(jnp.float32)
        top_b = extra[0:1] + (extra[1:2] + extra[2:3])
        total_b = extra[3:4] + (extra[4:5] + extra[5:6])
        new = jnp.maximum(top_a[tile], top_b)
        part_a = jnp.exp2((top_a[tile] - new) * scale)
        part_b = jnp.exp2((top_b - new) * scale)
        total = total_a[tile] * part_a + total_b * part_b
        mixed = mixed_a[tile] * part_a + packed[:HD, :].astype(jnp.float32) * part_b
        finished = (mixed / total).T.astype(jnp.bfloat16)
        for head in range(TILE_COLS // tile_q):
            out_ref[tile * tile_q : (tile + 1) * tile_q, head * HD : (head + 1) * HD] = finished[
                head * tile_q : (head + 1) * tile_q, :
            ]


def merge(mine, theirs):
    n_tiles = mine[0].shape[0]
    shape = (SEL, TILE_COLS * n_tiles // SEL * HD)
    return pl.pallas_call(
        merge_kernel,
        out_shape=jax.ShapeDtypeStruct(shape, jnp.bfloat16),
        compiler_params=megabytes(16),
        cost_estimate=cost(4 * math.prod(shape), 8 * math.prod(shape)),
        name="merge",
    )(*mine, *theirs)


def out_kernel(n_blocks, first_col, place_ref, x_ref, w_ref, *refs):
    outs = refs[:n_blocks]
    ordered, slots, sems = refs[n_blocks:]
    rows = SEL // n_blocks
    tile = slots.shape[2]
    count = outs[0].shape[1] // tile
    start, wait = stream(
        [lambda step: w_ref.at[:, pl.ds(first_col + step * tile, tile)]], [slots], sems
    )

    for step in range(min(SLOTS, count)):
        start(step)
    for block in range(n_blocks):
        there = pl.ds(pl.multiple_of(place_ref[block] * rows, rows), rows)
        ordered[block * rows : (block + 1) * rows, :] = x_ref[there, :]
    for step in range(count):
        wait(step)
        product = jnp.dot(
            ordered[...].astype(jnp.bfloat16),
            slots[step % SLOTS],
            preferred_element_type=jnp.float32,
        )
        cols = slice(step * tile, (step + 1) * tile)
        for block, out in enumerate(outs):
            out[:, cols] = product[block * rows : (block + 1) * rows, :].astype(out.dtype)
        if step + SLOTS < count:
            start(step + SLOTS)


def project_out(place, attention, w_out, chunk, kinds):
    depth = w_out.shape[0]
    n_blocks = len(kinds)
    width = w_out.shape[1] // CHUNKS
    rows = SEL // n_blocks
    if rows % 16:
        attention = attention.astype(jnp.float32)
    vmem = pl.BlockSpec(memory_space=pltpu.VMEM)
    return pl.pallas_call(
        functools.partial(out_kernel, n_blocks, chunk * width),
        in_specs=[
            pl.BlockSpec(memory_space=pltpu.SMEM),
            vmem,
            pl.BlockSpec(memory_space=pltpu.HBM),
        ],
        out_specs=[vmem] * n_blocks,
        out_shape=[jax.ShapeDtypeStruct((rows, width), kind) for kind in kinds],
        scratch_shapes=[
            pltpu.VMEM((SEL, depth), attention.dtype),
            pltpu.VMEM((SLOTS, depth, min(WIDTH_TILE, width)), jnp.bfloat16),
            pltpu.SemaphoreType.DMA((CUTS, SLOTS)),
        ],
        compiler_params=megabytes(16),
        cost_estimate=cost(2 * SEL * depth * width, 2 * depth * (width + SEL) + 4 * SEL * width),
        name="project_out",
    )(place, attention, w_out)


def per_device(
    hidden_in, norm_gain, w_query, w_keyval, w_out, pool_cache, doc_slot, doc_blocks, sel_pos
):
    tp_size = lax.axis_size("tp")
    req_size = lax.axis_size("req")
    me = lax.axis_index("tp")
    rows, width = hidden_in.shape
    slots, tokens = pool_cache.shape[:2]
    heads_here = w_query.shape[1] // HD
    selected = sel_pos[0]
    lengths = doc_blocks[0] * BLOCK

    if tp_size == KVH:
        ring = [*range(0, tp_size, 2), *range(tp_size - 1, 0, -2)]
    else:
        ring = list(range(tp_size))
    far = tp_size // 2
    forth = [(ring[p], ring[(p + 1) % tp_size]) for p in range(tp_size)]
    back = [(dst, src) for src, dst in forth]
    steps = [0] + [sign * k for k in range(1, far) for sign in (-1, 1)] + [far]
    table = [[ring[(ring.index(i) + s) % tp_size] for s in steps] for i in range(tp_size)]
    place = jnp.array(table, jnp.int32)[me]

    widened = hidden_in.astype(jnp.float32)
    normed = (
        widened
        * lax.rsqrt(jnp.mean(widened * widened, axis=-1, keepdims=True) + EPSILON)
        * norm_gain
    ).astype(jnp.bfloat16)
    normed, pool_cache = lax.optimization_barrier((normed, pool_cache))
    w_query, w_keyval, w_out = (
        pltpu.with_memory_space_constraint(w, pltpu.HBM) for w in (w_query, w_keyval, w_out)
    )
    middle = tp_size // 2
    order = jnp.arange(middle, dtype=jnp.int32)
    offsets = jnp.cumsum(lengths) - lengths
    first_slot = (me ^ order) * tokens
    slot_tokens = first_slot[:, None] + jnp.arange(tokens, dtype=jnp.int32)[None, :]
    cache_pos = offsets[:, None, None] + slot_tokens[None]
    is_valid = slot_tokens[None] < lengths[:, None, None]
    replaced = jnp.any(cache_pos[..., None] == selected, axis=-1)
    dead = jnp.where(is_valid & jnp.logical_not(replaced), 0.0, MASKED).astype(jnp.bfloat16)
    dead = jnp.broadcast_to(dead[..., None], (DOCS, middle, tokens, HD))
    dead = dead.reshape(DOCS, middle * tokens, HD)
    first_pos = jnp.where(
        first_slot[None] < lengths[:, None], offsets[:, None] + first_slot[None], FAR
    ).reshape(-1)
    cosine, sine_part = rotation_tables(selected)
    heads_here = w_query.shape[1] // HD
    tile_q = TILE_COLS // heads_here
    q_pos = jnp.tile(selected.reshape(SEL // tile_q, tile_q), (1, heads_here))
    q_pos = q_pos.reshape(SEL // tile_q, 1, TILE_COLS)

    part = width // CHUNKS
    streams = []
    for chunk in range(CHUNKS):
        own = normed[:, chunk * part : (chunk + 1) * part]
        streams.append({"before": [own], "behind": [own]})
    for k in range(1, far + 1):
        for chunk, held in enumerate(streams):
            if k < far or chunk % 2 == 0:
                held["before"].append(lax.ppermute(held["before"][-1], "tp", forth))
            if k < far or chunk % 2 == 1:
                held["behind"].append(lax.ppermute(held["behind"][-1], "tp", back))
        first = streams[0]["before"]
        if k == 1:
            by_kind = pool_cache.transpose(0, 2, 1, 3)
            sources = [by_kind]
            for shift in range(1, req_size):
                pairs = [((i + shift) % req_size, i) for i in range(req_size)]
                sources.append(lax.ppermute(by_kind, "req", pairs))
            holder = (doc_slot // slots - lax.axis_index("req")) % req_size
            slot = doc_slot % slots
            side = (me < middle).astype(jnp.int32)[None]
            odd = (me % 2 if tp_size == KVH else me * 0)[None]
            takers = jnp.concatenate([me ^ order, me ^ order ^ middle]) * KVH // tp_size
        if k == 2:
            first[-1], dead, first_pos, cosine, sine_part, q_pos, takers, holder, slot, place, side, odd = (
                lax.optimization_barrier(
                    (first[-1], dead, first_pos, cosine, sine_part, q_pos, takers, holder, slot)
                    + (place, side, odd)
                )
            )
        if k == far - 1:
            sent = select_docs(sources, holder, slot, takers, tp_size)
            first[-1], *sent = lax.optimization_barrier((first[-1], *sent))
    weights = [w_keyval, w_query]
    sums = []
    for chunk, held in enumerate(streams):
        blocks = [held["before"][0]]
        for k in range(1, far):
            blocks += [held["before"][k], held["behind"][k]]
        blocks.append(held["behind" if chunk % 2 else "before"][far])
        if rows % 16:
            blocks = [jnp.concatenate(blocks, axis=0)]
        sums = project(
            place, blocks, weights, sums, chunk, (cosine, sine_part), side, tp_size == KVH
        )
    across = [(i, i ^ middle) for i in range(tp_size)]
    *keyval, queries = sums
    their_queries = lax.ppermute(queries, "tp", across)
    if tp_size == KVH:
        first, second = keyval
        keys_to_even = [(i, 2 * i if i < middle else 2 * (i - middle) + 1) for i in range(tp_size)]
        keys_to_odd = [(i, 2 * i + 1 if i < middle else 2 * (i - middle)) for i in range(tp_size)]
        new = [lax.ppermute(first, "tp", keys_to_even), lax.ppermute(second, "tp", keys_to_odd)]
    else:
        everyone = lax.all_gather(keyval[0], "tp", axis=1, tiled=True)
        my_head = me * KVH // tp_size
        new = [
            lax.dynamic_slice_in_dim(everyone, (kind * KVH + my_head) * HD, HD, axis=1)
            for kind in range(2)
        ]

    def exchange(kept):
        got = {
            j: lax.ppermute(kept[j], "tp", [(i, i ^ j) for i in range(tp_size)])
            for j in range(1, middle)
        }
        return [kept[0]] + [got[j] for j in range(1, middle)]

    kept = list(sent[middle:])
    kept[-1], queries = lax.optimization_barrier((kept[-1], queries))
    own, partners = sent[:middle], exchange(kept)
    own, *partners[1:-1] = lax.optimization_barrier((own, *partners[1:-1]))
    chunks = [exchange(own), partners]
    n_tiles = queries.shape[0]

    metadata = (dead, first_pos, selected, q_pos, odd)
    their_queries, new = lax.optimization_barrier((their_queries, new))
    share = n_tiles // min(HALVES, n_tiles)
    theirs = [
        lax.ppermute(
            attend(chunks[1], *metadata, their_queries, first, share, [])[0], "tp", across
        )
        for first in range(n_tiles - share, -1, -share)
    ][::-1]
    mine = attend(chunks[0], *metadata, queries, 0, n_tiles, [cosine, sine_part, *new])
    attention = merge(mine, theirs)

    finished = []
    for chunk in range(CHUNKS):
        kinds = [jnp.float32] * (tp_size - 1) + [jnp.bfloat16]
        pieces = project_out(place, attention, w_out, chunk, kinds)
        to_forth, to_back = list(pieces[2 : tp_size - 1 : 2]), list(pieces[1 : tp_size - 1 : 2])
        (to_back if chunk % 2 else to_forth).append(pieces[-1])
        total = pieces[0]
        for terms, pairs in ((to_forth, forth), (to_back, back)):
            held = None
            for term in reversed(terms):
                if held is not None:
                    term = term + held.astype(jnp.float32)
                held = lax.ppermute(term.astype(jnp.bfloat16), "tp", pairs)
            total = total + held.astype(jnp.float32)
        finished.append(total.astype(jnp.bfloat16))
    return jnp.concatenate(finished, axis=1)


def solution(mesh):
    placed = (
        P(("groups", "req", "tp"), None),
        P(),
        P(None, "tp"),
        P(None, "tp"),
        P("tp", None),
        P(("groups", "req"), "tp", None, None),
        P(("groups", "req")),
        P(("groups", "req"), None),
        P(("groups", "req"), None),
    )
    return jax.shard_map(
        per_device,
        mesh=mesh,
        in_specs=placed,
        out_specs=P(("groups", "req", "tp"), None),
        check_vma=False,
    )
```

```python
import functools
import math

import jax
import jax.numpy as jnp
from jax import lax
from jax.experimental import pallas as pl
from jax.experimental.pallas import tpu as pltpu
from jax.sharding import PartitionSpec as P

HEADS = 64
KVH = 8
HD = 128
DOCS = 4
BLOCK = 128
SEL = 256


EPSILON = 1e-05
ROPE_BASE = 500000.0
MASKED = -1e30
FAR = 1 << 30
CHUNKS = 2
TILE_COLS = 256
PAIR = 2
STATS = 16
HALVES = 2
DEPTH_TILE = 1024
WIDTH_TILE = 1024
SLOTS = 3
CUTS = 4


def cost(flops, bytes_accessed, transcendentals=0):
    return pl.CostEstimate(
        flops=int(flops), bytes_accessed=int(bytes_accessed), transcendentals=int(transcendentals)
    )


def rotation_tables(positions):
    half_dim = HD // 2
    inverse = ROPE_BASE ** (-(jnp.arange(half_dim, dtype=jnp.float32) * (2.0 / HD)))
    angles = positions.astype(jnp.float32)[:, None] * inverse[None, :]
    cosine = jnp.cos(angles)
    sine_part = jnp.sin(angles)
    return (
        jnp.concatenate([cosine, cosine], axis=-1),
        jnp.concatenate([-sine_part, sine_part], axis=-1),
    )


def rotate(values, cosine, sine_part):
    swapped = jnp.concatenate([values[:, HD // 2 :], values[:, : HD // 2]], axis=-1)
    return values * cosine + swapped * sine_part


def megabytes(count):
    return pltpu.CompilerParams(vmem_limit_bytes=count * 1024 * 1024)


def stream(sources, buffers, sems):
    def copies(step):
        slot = step % SLOTS
        made = []
        for i, (source, buffer) in enumerate(zip(sources, buffers)):
            rows = buffer.shape[1] // CUTS
            for cut in range(CUTS):
                here = pl.ds(cut * rows, rows)
                made.append(
                    pltpu.make_async_copy(
                        source(step).at[here], buffer.at[slot, here], sems.at[i * CUTS + cut, slot]
                    )
                )
        return made

    def start(step):
        for copy in copies(step):
            copy.start()

    def wait(step):
        for copy in copies(step):
            copy.wait()

    return start, wait


def project_kernel(n_blocks, chunk, is_last, split, place_ref, *refs):
    refs = list(refs)
    take = lambda count: [refs.pop(0) for _ in range(count)]
    blocks, weights = take(n_blocks), take(2)
    prev = take(2) if chunk else None
    if is_last:
        cos_ref, sin_ref, side_ref = take(3)
        out_kv, (out_q,) = take(2 if split else 1), take(1)
        totals, (natural_kv, natural_q) = take(2), take(2)
    else:
        totals = take(2)
    buffers, sems = take(2), refs[0]
    tile = buffers[0].shape[1]
    depth = blocks[0].shape[1]
    count = depth // tile
    rows_of = lambda ref: lambda step: ref.at[pl.ds(chunk * depth + step * tile, tile), :]
    start, wait = stream([rows_of(ref) for ref in weights], buffers, sems)

    for step in range(min(SLOTS, count)):
        start(step)
    for step in range(count):
        wait(step)
        cols = slice(step * tile, (step + 1) * tile)
        rows = jnp.concatenate([b[:, cols] for b in blocks], axis=0)
        for i, (buffer, total) in enumerate(zip(buffers, totals)):
            term = jnp.dot(rows, buffer[step % SLOTS], preferred_element_type=jnp.float32)
            if step:
                total[...] += term
            elif chunk:
                total[...] = prev[i][...] + term
            else:
                total[...] = term
        if step + SLOTS < count:
            start(step + SLOTS)

    if is_last:
        height = SEL // place_ref.shape[0]
        for block in range(SEL // height):
            here = slice(block * height, (block + 1) * height)
            there = pl.ds(pl.multiple_of(place_ref[block] * height, height), height)
            natural_kv[there, :] = totals[0][here, :]
            natural_q[there, :] = totals[1][here, :]
        if split:
            for side in range(2):

                @pl.when(side_ref[0] == side)
                def _():
                    out_kv[1 - side][...] = natural_kv[:, :HD].astype(jnp.bfloat16)
                    out_kv[side][...] = natural_kv[:, HD:].astype(jnp.bfloat16)

        else:
            out_kv[0][...] = natural_kv[...].astype(jnp.bfloat16)
        heads_here = natural_q.shape[1] // HD
        tile_q = TILE_COLS // heads_here
        for index in range(SEL // tile_q):
            here = slice(index * tile_q, (index + 1) * tile_q)
            stacked = jnp.concatenate(
                [
                    rotate(
                        natural_q[here, head * HD : (head + 1) * HD], cos_ref[here, :], sin_ref[here, :]
                    )
                    for head in range(heads_here)
                ],
                axis=0,
            )
            out_q[index] = stacked.T.astype(jnp.bfloat16)


def project(place, blocks, weights, prev, chunk, tables, side, split):
    depth = blocks[0].shape[1]
    widths = [w.shape[1] for w in weights]
    tile = min(DEPTH_TILE, depth)
    is_last = chunk + 1 == CHUNKS
    smem = pl.BlockSpec(memory_space=pltpu.SMEM)
    vmem = pl.BlockSpec(memory_space=pltpu.VMEM)
    hbm = pl.BlockSpec(memory_space=pltpu.HBM)
    totals = [((SEL, width), jnp.float32) for width in widths]
    operands, specs = [place, *blocks, *weights, *prev], [smem] + [vmem] * len(blocks) + [hbm] * 2
    specs += [vmem] * len(prev)
    outs, scratch = totals, []
    if is_last:
        operands += [*tables, side]
        specs += [vmem] * 2 + [smem]
        outs = [(SEL, HD)] * 2 if split else [(SEL, widths[0])]
        outs = outs + [(SEL * widths[1] // (HD * TILE_COLS), HD, TILE_COLS)]
        outs, scratch = [(shape, jnp.bfloat16) for shape in outs], totals * 2
    return pl.pallas_call(
        functools.partial(project_kernel, len(blocks), chunk, is_last, split),
        in_specs=specs,
        out_specs=[vmem] * len(outs),
        out_shape=[jax.ShapeDtypeStruct(*o) for o in outs],
        scratch_shapes=[pltpu.VMEM(*x) for x in scratch]
        + [pltpu.VMEM((SLOTS, tile, width), jnp.bfloat16) for width in widths]
        + [pltpu.SemaphoreType.DMA((2 * CUTS, SLOTS))],
        compiler_params=megabytes(16),
        cost_estimate=cost(2 * SEL * depth * sum(widths), 2 * depth * (sum(widths) + SEL)),
        name="project",
    )(*operands)


def select_kernel(n_dest, n_src, place_ref, slot_ref, head_ref, *refs):
    sources = refs[:n_src]
    outs = refs[n_src : n_src + n_dest]
    sems = refs[n_src + n_dest]
    for doc in range(DOCS):
        for src in range(n_src):

            @pl.when(place_ref[doc] == src)
            def _():
                for dest in range(n_dest):
                    cols = pl.ds(pl.multiple_of(head_ref[dest] * HD, HD), HD)
                    pltpu.make_async_copy(
                        sources[src].at[slot_ref[doc], :, :, cols],
                        outs[dest].at[:, doc],
                        sems.at[dest, doc],
                    ).start()

    for dest in range(n_dest):
        for doc in range(DOCS):
            pltpu.make_async_copy(
                sources[0].at[0, :, :, 0:HD], outs[dest].at[:, doc], sems.at[dest, doc]
            ).wait()


def select_docs(sources, place, slot, heads, n_dest):
    tokens = sources[0].shape[2]
    shape = (2, DOCS, tokens, HD)
    smem = pl.BlockSpec(memory_space=pltpu.SMEM)
    return pl.pallas_call(
        functools.partial(select_kernel, n_dest, len(sources)),
        in_specs=[smem] * 3 + [pl.BlockSpec(memory_space=pl.ANY)] * len(sources),
        out_specs=[pl.BlockSpec(memory_space=pltpu.VMEM)] * n_dest,
        out_shape=[jax.ShapeDtypeStruct(shape, jnp.bfloat16)] * n_dest,
        scratch_shapes=[pltpu.SemaphoreType.DMA((n_dest, DOCS))],
        compiler_params=megabytes(8),
        cost_estimate=cost(0, 4 * n_dest * math.prod(shape)),
        name="select_docs",
    )(place, slot, heads, *sources)


def split_exact(value):
    pieces = []
    for _ in range(3):
        pieces.append(value.astype(jnp.bfloat16).astype(jnp.float32))
        value = value - pieces[-1]
    return pieces


def attend_kernel(
    n_chunks, offset, packs, has_state, with_new, n_tiles, tile_q, first_tile, first_ref, pos_ref, odd_ref, *refs
):
    refs = list(refs)
    take = lambda count: [refs.pop(0) for _ in range(count)]
    chunks = take(n_chunks)
    dead_ref, qpos_ref, queries = take(3)
    if has_state:
        old_top, old_total, old_summed = take(3)
    if with_new:
        cos_ref, sin_ref, new_a, new_b = take(4)
    if packs:
        (packed,) = take(1)
    top, total, summed, values = take(4)
    if with_new:
        new_key, new_value = take(2)
    together = min(PAIR, n_tiles)
    n_pairs = n_tiles // together
    tokens = chunks[0].shape[2]
    all_chunks = dead_ref.shape[1] // tokens
    scale = math.log2(math.e) / math.sqrt(HD)

    for chunk in range(n_chunks):
        for doc in range(DOCS):
            values[doc, :, chunk * tokens : (chunk + 1) * tokens] = chunks[chunk][1, doc].T
    if with_new:
        for odd, (key_ref, value_ref) in enumerate(((new_a, new_b), (new_b, new_a))):

            @pl.when(odd_ref[0] == odd)
            def _():
                new_key[...] = rotate(
                    key_ref[...].astype(jnp.float32), cos_ref[...], sin_ref[...]
                ).astype(jnp.bfloat16)
                new_value[...] = value_ref[...].T


    one_row = jnp.where(
        lax.broadcasted_iota(jnp.int32, (HD, TILE_COLS), 0) == 0, 1.0, 0.0
    ).astype(jnp.bfloat16)

    def update(tile, parts):
        best = functools.reduce(
            jnp.maximum, [jnp.max(scores, axis=0, keepdims=True) for scores, _ in parts]
        )
        old = top[tile]
        new = jnp.maximum(old, best)
        shrink = jnp.exp2((old - new) * scale)
        running = total[tile] * shrink
        mixed = summed[tile] * shrink
        for scores, value in parts:
            weights = jnp.exp2((scores - new) * scale)
            running += jnp.sum(weights, axis=0, keepdims=True)
            mixed += jnp.dot(
                value, weights.astype(jnp.bfloat16), preferred_element_type=jnp.float32
            )
        top[tile] = new
        total[tile] = running
        summed[tile] = mixed

    @pl.loop(0, n_pairs)
    def _(pair):
        tiles = [pair * together + i for i in range(together)]
        for tile in tiles:
            if has_state:
                top[tile] = old_top[tile]
                total[tile] = old_total[tile]
                summed[tile] = old_summed[tile]
            else:
                top[tile] = jnp.full(top.shape[1:], MASKED, jnp.float32)
                total[tile] = jnp.zeros(total.shape[1:], jnp.float32)
                summed[tile] = jnp.zeros(summed.shape[1:], jnp.float32)
        if with_new:
            fresh = []
            for tile in tiles:
                scores = jnp.dot(
                    new_key[...], queries[first_tile + tile], preferred_element_type=jnp.float32
                )
                key_index = lax.broadcasted_iota(jnp.int32, scores.shape, 0)
                q_index = (first_tile + tile) * tile_q + lax.broadcasted_iota(jnp.int32, scores.shape, 1) % tile_q
                fresh.append(jnp.where(key_index <= q_index, scores, MASKED))
            for tile, scores in zip(tiles, fresh):
                update(tile, [(scores, new_value[...])])

        @pl.loop(0, DOCS)
        def _(doc):
            firsts = [first_ref[doc * all_chunks + offset + chunk] for chunk in range(n_chunks)]
            lowest = functools.reduce(jnp.minimum, firsts)
            highest = functools.reduce(jnp.maximum, firsts)
            reach = highest + tokens - 1

            def visit(masked, members):
                found = []
                for tile in tiles:
                    extended = jnp.concatenate([queries[first_tile + tile], one_row], axis=0)
                    parts = []
                    for chunk in members:
                        span = slice(chunk * tokens, (chunk + 1) * tokens)
                        dead_span = slice((offset + chunk) * tokens, (offset + chunk + 1) * tokens)
                        keys = jnp.concatenate(
                            [chunks[chunk][0, doc], dead_ref[doc, dead_span, :]], axis=1
                        )
                        scores = jnp.dot(keys, extended, preferred_element_type=jnp.float32)
                        if masked:
                            key_pos = firsts[chunk] + lax.broadcasted_iota(
                                jnp.int32, scores.shape, 0
                            )
                            scores = jnp.where(key_pos <= qpos_ref[first_tile + tile], scores, MASKED)
                        parts.append((scores, values[doc, :, span]))
                    found.append(parts)
                for tile, parts in zip(tiles, found):
                    update(tile, parts)

            start = first_tile * tile_q + pair * together * tile_q
            first_here = pos_ref[start]
            last_here = pos_ref[start + together * tile_q - 1]
            whole = reach <= first_here
            spread = jnp.logical_not(whole) & (highest <= last_here)
            ragged = (lowest <= last_here) & (highest > last_here)

            @pl.when(whole)
            def _():
                visit(False, range(n_chunks))

            @pl.when(spread)
            def _():
                visit(True, range(n_chunks))

            for chunk in range(n_chunks):

                @pl.when(ragged & (firsts[chunk] <= last_here))
                def _():
                    visit(True, [chunk])

        if packs:
            for tile in tiles:
                extra = jnp.concatenate(
                    split_exact(top[tile])
                    + split_exact(total[tile])
                    + [jnp.zeros((STATS - 6, TILE_COLS), jnp.float32)],
                    axis=0,
                )
                packed[tile] = jnp.concatenate([summed[tile], extra], axis=0).astype(jnp.bfloat16)


def attend(chunks, offset, metadata, queries, first_tile, n_tiles, state=(), fresh=(), packs=False):
    dead, first_pos, selected, q_pos, odd = metadata
    n_chunks = len(chunks)
    tokens = chunks[0].shape[2]
    tile_q = SEL // q_pos.shape[0]
    smem = pl.BlockSpec(memory_space=pltpu.SMEM)
    vmem = pl.BlockSpec(memory_space=pltpu.VMEM)
    operands = [first_pos, selected, odd, *chunks, dead, q_pos, queries, *state, *fresh]
    outs = [((n_tiles, 1, TILE_COLS), jnp.float32)] * 2
    outs += [((n_tiles, HD, TILE_COLS), jnp.float32)]
    scratch = [((DOCS, HD, n_chunks * tokens), jnp.bfloat16)]
    if packs:
        outs, scratch = [((n_tiles, HD + STATS, TILE_COLS), jnp.bfloat16)], outs + scratch
    if fresh:
        scratch += [((SEL, HD), jnp.bfloat16), ((HD, SEL), jnp.bfloat16)]
    pairs = n_tiles * TILE_COLS * DOCS * n_chunks * tokens // 2
    return pl.pallas_call(
        functools.partial(
            attend_kernel,
            n_chunks,
            offset,
            packs,
            bool(state),
            bool(fresh),
            n_tiles,
            tile_q,
            first_tile,
        ),
        in_specs=[smem] * 3 + [vmem] * (len(operands) - 3),
        out_specs=[vmem] * len(outs),
        out_shape=[jax.ShapeDtypeStruct(*s) for s in outs],
        scratch_shapes=[pltpu.VMEM(*s) for s in scratch],
        compiler_params=megabytes(16),
        cost_estimate=cost(4 * pairs * HD, 0, pairs) if packs else cost(1, 1),
        name="attend",
    )(*operands)


def merge_kernel(top_a, total_a, mixed_a, *refs):
    packs, out_ref = refs[:-1], refs[-1]
    scale = math.log2(math.e) / math.sqrt(HD)
    n_tiles = top_a.shape[0]
    tile_q = SEL // n_tiles
    for tile in range(n_tiles):
        packed = packs[tile * len(packs) // n_tiles].at[tile % (n_tiles // len(packs))]
        extra = packed[HD:, :].astype(jnp.float32)
        top_b = extra[0:1] + (extra[1:2] + extra[2:3])
        total_b = extra[3:4] + (extra[4:5] + extra[5:6])
        new = jnp.maximum(top_a[tile], top_b)
        part_a = jnp.exp2((top_a[tile] - new) * scale)
        part_b = jnp.exp2((top_b - new) * scale)
        total = total_a[tile] * part_a + total_b * part_b
        mixed = mixed_a[tile] * part_a + packed[:HD, :].astype(jnp.float32) * part_b
        finished = (mixed / total).T.astype(jnp.bfloat16)
        for head in range(TILE_COLS // tile_q):
            out_ref[tile * tile_q : (tile + 1) * tile_q, head * HD : (head + 1) * HD] = finished[
                head * tile_q : (head + 1) * tile_q, :
            ]


def merge(mine, theirs):
    n_tiles = mine[0].shape[0]
    shape = (SEL, TILE_COLS * n_tiles // SEL * HD)
    return pl.pallas_call(
        merge_kernel,
        out_shape=jax.ShapeDtypeStruct(shape, jnp.bfloat16),
        compiler_params=megabytes(16),
        cost_estimate=cost(4 * math.prod(shape), 8 * math.prod(shape)),
        name="merge",
    )(*mine, *theirs)


def out_kernel(n_blocks, first_col, place_ref, x_ref, w_ref, *refs):
    outs = refs[:n_blocks]
    ordered, slots, sems = refs[n_blocks:]
    rows = SEL // n_blocks
    tile = slots.shape[2]
    count = outs[0].shape[1] // tile
    start, wait = stream(
        [lambda step: w_ref.at[:, pl.ds(first_col + step * tile, tile)]], [slots], sems
    )

    for step in range(min(SLOTS, count)):
        start(step)
    for block in range(n_blocks):
        there = pl.ds(pl.multiple_of(place_ref[block] * rows, rows), rows)
        ordered[block * rows : (block + 1) * rows, :] = x_ref[there, :]
    for step in range(count):
        wait(step)
        product = jnp.dot(
            ordered[...].astype(jnp.bfloat16),
            slots[step % SLOTS],
            preferred_element_type=jnp.float32,
        )
        cols = slice(step * tile, (step + 1) * tile)
        for block, out in enumerate(outs):
            out[:, cols] = product[block * rows : (block + 1) * rows, :].astype(out.dtype)
        if step + SLOTS < count:
            start(step + SLOTS)


def project_out(place, attention, w_out, chunk, kinds):
    depth = w_out.shape[0]
    n_blocks = len(kinds)
    width = w_out.shape[1] // CHUNKS
    rows = SEL // n_blocks
    if rows % 16:
        attention = attention.astype(jnp.float32)
    vmem = pl.BlockSpec(memory_space=pltpu.VMEM)
    return pl.pallas_call(
        functools.partial(out_kernel, n_blocks, chunk * width),
        in_specs=[
            pl.BlockSpec(memory_space=pltpu.SMEM),
            vmem,
            pl.BlockSpec(memory_space=pltpu.HBM),
        ],
        out_specs=[vmem] * n_blocks,
        out_shape=[jax.ShapeDtypeStruct((rows, width), kind) for kind in kinds],
        scratch_shapes=[
            pltpu.VMEM((SEL, depth), attention.dtype),
            pltpu.VMEM((SLOTS, depth, min(WIDTH_TILE, width)), jnp.bfloat16),
            pltpu.SemaphoreType.DMA((CUTS, SLOTS)),
        ],
        compiler_params=megabytes(16),
        cost_estimate=cost(2 * SEL * depth * width, 2 * depth * (width + SEL) + 4 * SEL * width),
        name="project_out",
    )(place, attention, w_out)


def per_device(
    hidden_in, norm_gain, w_query, w_keyval, w_out, pool_cache, doc_slot, doc_blocks, sel_pos
):
    tp_size = lax.axis_size("tp")
    req_size = lax.axis_size("req")
    me = lax.axis_index("tp")
    rows, width = hidden_in.shape
    slots, tokens = pool_cache.shape[:2]
    heads_here = w_query.shape[1] // HD
    selected = sel_pos[0]
    lengths = doc_blocks[0] * BLOCK

    if tp_size == KVH:
        ring = [*range(0, tp_size, 2), *range(tp_size - 1, 0, -2)]
    else:
        ring = list(range(tp_size))
    far = tp_size // 2
    forth = [(ring[p], ring[(p + 1) % tp_size]) for p in range(tp_size)]
    back = [(dst, src) for src, dst in forth]
    steps = [0] + [sign * k for k in range(1, far) for sign in (-1, 1)] + [far]
    table = [[ring[(ring.index(i) + s) % tp_size] for s in steps] for i in range(tp_size)]
    place = jnp.array(table, jnp.int32)[me]

    widened = hidden_in.astype(jnp.float32)
    normed = (
        widened
        * lax.rsqrt(jnp.mean(widened * widened, axis=-1, keepdims=True) + EPSILON)
        * norm_gain
    ).astype(jnp.bfloat16)
    normed, pool_cache = lax.optimization_barrier((normed, pool_cache))
    w_query, w_keyval, w_out = (
        pltpu.with_memory_space_constraint(w, pltpu.HBM) for w in (w_query, w_keyval, w_out)
    )
    middle = tp_size // 2
    order = jnp.arange(middle, dtype=jnp.int32)
    offsets = jnp.cumsum(lengths) - lengths
    first_slot = (me ^ order) * tokens
    slot_tokens = first_slot[:, None] + jnp.arange(tokens, dtype=jnp.int32)[None, :]
    cache_pos = offsets[:, None, None] + slot_tokens[None]
    is_valid = slot_tokens[None] < lengths[:, None, None]
    replaced = jnp.any(cache_pos[..., None] == selected, axis=-1)
    dead = jnp.where(is_valid & jnp.logical_not(replaced), 0.0, MASKED).astype(jnp.bfloat16)
    dead = jnp.broadcast_to(dead[..., None], (DOCS, middle, tokens, HD))
    dead = dead.reshape(DOCS, middle * tokens, HD)
    first_pos = jnp.where(
        first_slot[None] < lengths[:, None], offsets[:, None] + first_slot[None], FAR
    ).reshape(-1)
    cosine, sine_part = rotation_tables(selected)
    heads_here = w_query.shape[1] // HD
    tile_q = TILE_COLS // heads_here
    q_pos = jnp.tile(selected.reshape(SEL // tile_q, tile_q), (1, heads_here))
    q_pos = q_pos.reshape(SEL // tile_q, 1, TILE_COLS)

    part = width // CHUNKS
    streams = []
    for chunk in range(CHUNKS):
        own = normed[:, chunk * part : (chunk + 1) * part]
        streams.append({"before": [own], "behind": [own]})
    for k in range(1, far + 1):
        for chunk, held in enumerate(streams):
            if k < far or chunk % 2 == 0:
                held["before"].append(lax.ppermute(held["before"][-1], "tp", forth))
            if k < far or chunk % 2 == 1:
                held["behind"].append(lax.ppermute(held["behind"][-1], "tp", back))
        first = streams[0]["before"]
        if k == 1:
            by_kind = pool_cache.transpose(0, 2, 1, 3)
            sources = [by_kind]
            for shift in range(1, req_size):
                pairs = [((i + shift) % req_size, i) for i in range(req_size)]
                sources.append(lax.ppermute(by_kind, "req", pairs))
            holder = (doc_slot // slots - lax.axis_index("req")) % req_size
            slot = doc_slot % slots
            side = (me < middle).astype(jnp.int32)[None]
            odd = (me % 2 if tp_size == KVH else me * 0)[None]
            takers = jnp.concatenate([me ^ order, me ^ order ^ middle]) * KVH // tp_size
        if k == 2:
            first[-1], dead, first_pos, cosine, sine_part, q_pos, takers, holder, slot, place, side, odd = (
                lax.optimization_barrier(
                    (first[-1], dead, first_pos, cosine, sine_part, q_pos, takers, holder, slot)
                    + (place, side, odd)
                )
            )
        if k == far - 1:
            sent = select_docs(sources, holder, slot, takers, tp_size)
            first[-1], *sent = lax.optimization_barrier((first[-1], *sent))
    weights = [w_keyval, w_query]
    sums = []
    for chunk, held in enumerate(streams):
        blocks = [held["before"][0]]
        for k in range(1, far):
            blocks += [held["before"][k], held["behind"][k]]
        blocks.append(held["behind" if chunk % 2 else "before"][far])
        if rows % 16:
            blocks = [jnp.concatenate(blocks, axis=0)]
        sums = project(
            place, blocks, weights, sums, chunk, (cosine, sine_part), side, tp_size == KVH
        )
    across = [(i, i ^ middle) for i in range(tp_size)]
    *keyval, queries = sums
    their_queries = lax.ppermute(queries, "tp", across)
    if tp_size == KVH:
        first, second = keyval
        keys_to_even = [(i, 2 * i if i < middle else 2 * (i - middle) + 1) for i in range(tp_size)]
        keys_to_odd = [(i, 2 * i + 1 if i < middle else 2 * (i - middle)) for i in range(tp_size)]
        new = [lax.ppermute(first, "tp", keys_to_even), lax.ppermute(second, "tp", keys_to_odd)]
    else:
        everyone = lax.all_gather(keyval[0], "tp", axis=1, tiled=True)
        my_head = me * KVH // tp_size
        new = [
            lax.dynamic_slice_in_dim(everyone, (kind * KVH + my_head) * HD, HD, axis=1)
            for kind in range(2)
        ]

    def exchange(keys, j):
        return lax.ppermute(keys, "tp", [(i, i ^ j) for i in range(tp_size)])

    n_tiles = queries.shape[0]
    metadata = (dead, first_pos, selected, q_pos, odd)
    own, kept = list(sent[:middle]), list(sent[middle:])
    kept[-1], queries = lax.optimization_barrier((kept[-1], queries))
    partners = [kept[0]] + [exchange(kept[j], j) for j in range(1, middle)]
    near = attend([own[0], exchange(own[1], 1)], 0, metadata, queries, 0, n_tiles)
    near, own, *partners[1:-1] = lax.optimization_barrier((near, own, *partners[1:-1]))
    rest = [exchange(own[j], j) for j in range(2, middle)]
    their_queries, new = lax.optimization_barrier((their_queries, new))
    share = n_tiles // min(HALVES, n_tiles)
    theirs = [
        lax.ppermute(
            attend(partners, 0, metadata, their_queries, first, share, packs=True)[0], "tp", across
        )
        for first in range(n_tiles - share, -1, -share)
    ][::-1]
    mine = attend(
        rest, 2, metadata, queries, 0, n_tiles, near, (cosine, sine_part, *new)
    )
    attention = merge(mine, theirs)

    finished = []
    for chunk in range(CHUNKS):
        kinds = [jnp.float32] * (tp_size - 1) + [jnp.bfloat16]
        pieces = project_out(place, attention, w_out, chunk, kinds)
        to_forth, to_back = list(pieces[2 : tp_size - 1 : 2]), list(pieces[1 : tp_size - 1 : 2])
        (to_back if chunk % 2 else to_forth).append(pieces[-1])
        total = pieces[0]
        for terms, pairs in ((to_forth, forth), (to_back, back)):
            held = None
            for term in reversed(terms):
                if held is not None:
                    term = term + held.astype(jnp.float32)
                held = lax.ppermute(term.astype(jnp.bfloat16), "tp", pairs)
            total = total + held.astype(jnp.float32)
        finished.append(total.astype(jnp.bfloat16))
    return jnp.concatenate(finished, axis=1)


def solution(mesh):
    placed = (
        P(("groups", "req", "tp"), None),
        P(),
        P(None, "tp"),
        P(None, "tp"),
        P("tp", None),
        P(("groups", "req"), "tp", None, None),
        P(("groups", "req")),
        P(("groups", "req"), None),
        P(("groups", "req"), None),
    )
    return jax.shard_map(
        per_device,
        mesh=mesh,
        in_specs=placed,
        out_specs=P(("groups", "req", "tp"), None),
        check_vma=False,
    )
```

```python
import functools
import math

import jax
import jax.numpy as jnp
from jax import lax
from jax.experimental import pallas as pl
from jax.experimental.pallas import tpu as pltpu
from jax.sharding import PartitionSpec as P

HEADS = 64
KVH = 8
HD = 128
DOCS = 4
BLOCK = 128
SEL = 256


EPSILON = 1e-05
ROPE_BASE = 500000.0
MASKED = -1e30
FAR = 1 << 30
CHUNKS = 2
TILE_COLS = 256
PAIR = 2
STATS = 16
HALVES = 2
DEPTH_TILE = 1024
WIDTH_TILE = 1024
SLOTS = 3
CUTS = 4


def cost(flops, bytes_accessed, transcendentals=0):
    return pl.CostEstimate(
        flops=int(flops), bytes_accessed=int(bytes_accessed), transcendentals=int(transcendentals)
    )


def rotation_tables(positions):
    half_dim = HD // 2
    inverse = ROPE_BASE ** (-(jnp.arange(half_dim, dtype=jnp.float32) * (2.0 / HD)))
    angles = positions.astype(jnp.float32)[:, None] * inverse[None, :]
    cosine = jnp.cos(angles)
    sine_part = jnp.sin(angles)
    return (
        jnp.concatenate([cosine, cosine], axis=-1),
        jnp.concatenate([-sine_part, sine_part], axis=-1),
    )


def rotate(values, cosine, sine_part):
    swapped = jnp.concatenate([values[:, HD // 2 :], values[:, : HD // 2]], axis=-1)
    return values * cosine + swapped * sine_part


def megabytes(count):
    return pltpu.CompilerParams(vmem_limit_bytes=count * 1024 * 1024)


def stream(sources, buffers, sems):
    def copies(step):
        slot = step % SLOTS
        made = []
        for i, (source, buffer) in enumerate(zip(sources, buffers)):
            rows = buffer.shape[1] // CUTS
            for cut in range(CUTS):
                here = pl.ds(cut * rows, rows)
                made.append(
                    pltpu.make_async_copy(
                        source(step).at[here], buffer.at[slot, here], sems.at[i * CUTS + cut, slot]
                    )
                )
        return made

    def start(step):
        for copy in copies(step):
            copy.start()

    def wait(step):
        for copy in copies(step):
            copy.wait()

    return start, wait


def project_kernel(n_blocks, chunk, is_last, split, place_ref, *refs):
    refs = list(refs)
    take = lambda count: [refs.pop(0) for _ in range(count)]
    blocks, weights = take(n_blocks), take(2)
    prev = take(2) if chunk else None
    if is_last:
        cos_ref, sin_ref, side_ref = take(3)
        out_kv, (out_q,) = take(2 if split else 1), take(1)
        totals, (natural_kv, natural_q) = take(2), take(2)
    else:
        totals = take(2)
    buffers, sems = take(2), refs[0]
    tile = buffers[0].shape[1]
    depth = blocks[0].shape[1]
    count = depth // tile
    rows_of = lambda ref: lambda step: ref.at[pl.ds(chunk * depth + step * tile, tile), :]
    start, wait = stream([rows_of(ref) for ref in weights], buffers, sems)

    for step in range(min(SLOTS, count)):
        start(step)
    for step in range(count):
        wait(step)
        cols = slice(step * tile, (step + 1) * tile)
        rows = jnp.concatenate([b[:, cols] for b in blocks], axis=0)
        for i, (buffer, total) in enumerate(zip(buffers, totals)):
            term = jnp.dot(rows, buffer[step % SLOTS], preferred_element_type=jnp.float32)
            if step:
                total[...] += term
            elif chunk:
                total[...] = prev[i][...] + term
            else:
                total[...] = term
        if step + SLOTS < count:
            start(step + SLOTS)

    if is_last:
        height = SEL // place_ref.shape[0]
        for block in range(SEL // height):
            here = slice(block * height, (block + 1) * height)
            there = pl.ds(pl.multiple_of(place_ref[block] * height, height), height)
            natural_kv[there, :] = totals[0][here, :]
            natural_q[there, :] = totals[1][here, :]
        if split:
            for side in range(2):

                @pl.when(side_ref[0] == side)
                def _():
                    out_kv[1 - side][...] = natural_kv[:, :HD].astype(jnp.bfloat16)
                    out_kv[side][...] = natural_kv[:, HD:].astype(jnp.bfloat16)

        else:
            out_kv[0][...] = natural_kv[...].astype(jnp.bfloat16)
        heads_here = natural_q.shape[1] // HD
        tile_q = TILE_COLS // heads_here
        for index in range(SEL // tile_q):
            here = slice(index * tile_q, (index + 1) * tile_q)
            stacked = jnp.concatenate(
                [
                    rotate(
                        natural_q[here, head * HD : (head + 1) * HD], cos_ref[here, :], sin_ref[here, :]
                    )
                    for head in range(heads_here)
                ],
                axis=0,
            )
            out_q[index] = stacked.T.astype(jnp.bfloat16)


def project(place, blocks, weights, prev, chunk, tables, side, split):
    depth = blocks[0].shape[1]
    widths = [w.shape[1] for w in weights]
    tile = min(DEPTH_TILE, depth)
    is_last = chunk + 1 == CHUNKS
    smem = pl.BlockSpec(memory_space=pltpu.SMEM)
    vmem = pl.BlockSpec(memory_space=pltpu.VMEM)
    hbm = pl.BlockSpec(memory_space=pltpu.HBM)
    totals = [((SEL, width), jnp.float32) for width in widths]
    operands, specs = [place, *blocks, *weights, *prev], [smem] + [vmem] * len(blocks) + [hbm] * 2
    specs += [vmem] * len(prev)
    outs, scratch = totals, []
    if is_last:
        operands += [*tables, side]
        specs += [vmem] * 2 + [smem]
        outs = [(SEL, HD)] * 2 if split else [(SEL, widths[0])]
        outs = outs + [(SEL * widths[1] // (HD * TILE_COLS), HD, TILE_COLS)]
        outs, scratch = [(shape, jnp.bfloat16) for shape in outs], totals * 2
    return pl.pallas_call(
        functools.partial(project_kernel, len(blocks), chunk, is_last, split),
        in_specs=specs,
        out_specs=[vmem] * len(outs),
        out_shape=[jax.ShapeDtypeStruct(*o) for o in outs],
        scratch_shapes=[pltpu.VMEM(*x) for x in scratch]
        + [pltpu.VMEM((SLOTS, tile, width), jnp.bfloat16) for width in widths]
        + [pltpu.SemaphoreType.DMA((2 * CUTS, SLOTS))],
        compiler_params=megabytes(16),
        cost_estimate=cost(2 * SEL * depth * sum(widths), 2 * depth * (sum(widths) + SEL)),
        name="project",
    )(*operands)


def select_kernel(n_dest, n_src, place_ref, slot_ref, head_ref, *refs):
    sources = refs[:n_src]
    outs = refs[n_src : n_src + n_dest]
    sems = refs[n_src + n_dest]
    for doc in range(DOCS):
        for src in range(n_src):

            @pl.when(place_ref[doc] == src)
            def _():
                for dest in range(n_dest):
                    cols = pl.ds(pl.multiple_of(head_ref[dest] * HD, HD), HD)
                    pltpu.make_async_copy(
                        sources[src].at[slot_ref[doc], :, :, cols],
                        outs[dest].at[:, doc],
                        sems.at[dest, doc],
                    ).start()

    for dest in range(n_dest):
        for doc in range(DOCS):
            pltpu.make_async_copy(
                sources[0].at[0, :, :, 0:HD], outs[dest].at[:, doc], sems.at[dest, doc]
            ).wait()


def select_docs(sources, place, slot, heads, n_dest):
    tokens = sources[0].shape[2]
    shape = (2, DOCS, tokens, HD)
    smem = pl.BlockSpec(memory_space=pltpu.SMEM)
    return pl.pallas_call(
        functools.partial(select_kernel, n_dest, len(sources)),
        in_specs=[smem] * 3 + [pl.BlockSpec(memory_space=pl.ANY)] * len(sources),
        out_specs=[pl.BlockSpec(memory_space=pltpu.VMEM)] * n_dest,
        out_shape=[jax.ShapeDtypeStruct(shape, jnp.bfloat16)] * n_dest,
        scratch_shapes=[pltpu.SemaphoreType.DMA((n_dest, DOCS))],
        compiler_params=megabytes(8),
        cost_estimate=cost(0, 4 * n_dest * math.prod(shape)),
        name="select_docs",
    )(place, slot, heads, *sources)


def split_exact(value):
    pieces = []
    for _ in range(3):
        pieces.append(value.astype(jnp.bfloat16).astype(jnp.float32))
        value = value - pieces[-1]
    return pieces


def attend_kernel(
    n_chunks, offset, packs, has_state, with_new, n_tiles, tile_q, first_tile, first_ref, pos_ref, odd_ref, *refs
):
    refs = list(refs)
    take = lambda count: [refs.pop(0) for _ in range(count)]
    chunks = take(n_chunks)
    dead_ref, qpos_ref, queries = take(3)
    if has_state:
        old_top, old_total, old_summed = take(3)
    if with_new:
        cos_ref, sin_ref, new_a, new_b = take(4)
    if packs:
        (packed,) = take(1)
    top, total, summed, values = take(4)
    if with_new:
        new_key, new_value = take(2)
    together = min(PAIR, n_tiles)
    n_pairs = n_tiles // together
    tokens = chunks[0].shape[2]
    all_chunks = dead_ref.shape[1] // tokens
    scale = math.log2(math.e) / math.sqrt(HD)

    for chunk in range(n_chunks):
        for doc in range(DOCS):
            values[doc, :, chunk * tokens : (chunk + 1) * tokens] = chunks[chunk][1, doc].T
    if with_new:
        for odd, (key_ref, value_ref) in enumerate(((new_a, new_b), (new_b, new_a))):

            @pl.when(odd_ref[0] == odd)
            def _():
                new_key[...] = rotate(
                    key_ref[...].astype(jnp.float32), cos_ref[...], sin_ref[...]
                ).astype(jnp.bfloat16)
                new_value[...] = value_ref[...].T


    one_row = jnp.where(
        lax.broadcasted_iota(jnp.int32, (HD, TILE_COLS), 0) == 0, 1.0, 0.0
    ).astype(jnp.bfloat16)

    def update(tile, parts):
        best = functools.reduce(
            jnp.maximum, [jnp.max(scores, axis=0, keepdims=True) for scores, _ in parts]
        )
        old = top[tile]
        new = jnp.maximum(old, best)
        shrink = jnp.exp2((old - new) * scale)
        running = total[tile] * shrink
        mixed = summed[tile] * shrink
        for scores, value in parts:
            weights = jnp.exp2((scores - new) * scale)
            running += jnp.sum(weights, axis=0, keepdims=True)
            mixed += jnp.dot(
                value, weights.astype(jnp.bfloat16), preferred_element_type=jnp.float32
            )
        top[tile] = new
        total[tile] = running
        summed[tile] = mixed

    @pl.loop(0, n_pairs)
    def _(pair):
        tiles = [pair * together + i for i in range(together)]
        for tile in tiles:
            if has_state:
                top[tile] = old_top[tile]
                total[tile] = old_total[tile]
                summed[tile] = old_summed[tile]
            else:
                top[tile] = jnp.full(top.shape[1:], MASKED, jnp.float32)
                total[tile] = jnp.zeros(total.shape[1:], jnp.float32)
                summed[tile] = jnp.zeros(summed.shape[1:], jnp.float32)
        if with_new:
            fresh = []
            for tile in tiles:
                scores = jnp.dot(
                    new_key[...], queries[first_tile + tile], preferred_element_type=jnp.float32
                )
                key_index = lax.broadcasted_iota(jnp.int32, scores.shape, 0)
                q_index = (first_tile + tile) * tile_q + lax.broadcasted_iota(jnp.int32, scores.shape, 1) % tile_q
                fresh.append(jnp.where(key_index <= q_index, scores, MASKED))
            for tile, scores in zip(tiles, fresh):
                update(tile, [(scores, new_value[...])])

        @pl.loop(0, DOCS)
        def _(doc):
            firsts = [first_ref[doc * all_chunks + offset + chunk] for chunk in range(n_chunks)]
            lowest = functools.reduce(jnp.minimum, firsts)
            highest = functools.reduce(jnp.maximum, firsts)
            reach = highest + tokens - 1

            def visit(masked, members):
                found = []
                for tile in tiles:
                    extended = jnp.concatenate([queries[first_tile + tile], one_row], axis=0)
                    parts = []
                    for chunk in members:
                        span = slice(chunk * tokens, (chunk + 1) * tokens)
                        dead_span = slice((offset + chunk) * tokens, (offset + chunk + 1) * tokens)
                        keys = jnp.concatenate(
                            [chunks[chunk][0, doc], dead_ref[doc, dead_span, :]], axis=1
                        )
                        scores = jnp.dot(keys, extended, preferred_element_type=jnp.float32)
                        if masked:
                            key_pos = firsts[chunk] + lax.broadcasted_iota(
                                jnp.int32, scores.shape, 0
                            )
                            scores = jnp.where(key_pos <= qpos_ref[first_tile + tile], scores, MASKED)
                        parts.append((scores, values[doc, :, span]))
                    found.append(parts)
                for tile, parts in zip(tiles, found):
                    update(tile, parts)

            start = first_tile * tile_q + pair * together * tile_q
            first_here = pos_ref[start]
            last_here = pos_ref[start + together * tile_q - 1]
            whole = reach <= first_here
            spread = jnp.logical_not(whole) & (highest <= last_here)
            ragged = (lowest <= last_here) & (highest > last_here)

            @pl.when(whole)
            def _():
                visit(False, range(n_chunks))

            @pl.when(spread)
            def _():
                visit(True, range(n_chunks))

            for chunk in range(n_chunks):

                @pl.when(ragged & (firsts[chunk] <= last_here))
                def _():
                    visit(True, [chunk])

        if packs:
            for tile in tiles:
                extra = jnp.concatenate(
                    split_exact(top[tile])
                    + split_exact(total[tile])
                    + [jnp.zeros((STATS - 6, TILE_COLS), jnp.float32)],
                    axis=0,
                )
                packed[tile] = jnp.concatenate([summed[tile], extra], axis=0).astype(jnp.bfloat16)


def attend(chunks, offset, metadata, queries, first_tile, n_tiles, state=(), fresh=(), packs=False):
    dead, first_pos, selected, q_pos, odd = metadata
    n_chunks = len(chunks)
    tokens = chunks[0].shape[2]
    tile_q = SEL // q_pos.shape[0]
    smem = pl.BlockSpec(memory_space=pltpu.SMEM)
    vmem = pl.BlockSpec(memory_space=pltpu.VMEM)
    operands = [first_pos, selected, odd, *chunks, dead, q_pos, queries, *state, *fresh]
    outs = [((n_tiles, 1, TILE_COLS), jnp.float32)] * 2
    outs += [((n_tiles, HD, TILE_COLS), jnp.float32)]
    scratch = [((DOCS, HD, n_chunks * tokens), jnp.bfloat16)]
    if packs:
        outs, scratch = [((n_tiles, HD + STATS, TILE_COLS), jnp.bfloat16)], outs + scratch
    if fresh:
        scratch += [((SEL, HD), jnp.bfloat16), ((HD, SEL), jnp.bfloat16)]
    pairs = n_tiles * TILE_COLS * DOCS * n_chunks * tokens // 2
    return pl.pallas_call(
        functools.partial(
            attend_kernel,
            n_chunks,
            offset,
            packs,
            bool(state),
            bool(fresh),
            n_tiles,
            tile_q,
            first_tile,
        ),
        in_specs=[smem] * 3 + [vmem] * (len(operands) - 3),
        out_specs=[vmem] * len(outs),
        out_shape=[jax.ShapeDtypeStruct(*s) for s in outs],
        scratch_shapes=[pltpu.VMEM(*s) for s in scratch],
        compiler_params=megabytes(16),
        cost_estimate=cost(4 * pairs * HD, 0, pairs) if packs else cost(1, 1),
        name="attend",
    )(*operands)


def merge_kernel(top_a, total_a, mixed_a, *refs):
    packs, out_ref = refs[:-1], refs[-1]
    scale = math.log2(math.e) / math.sqrt(HD)
    n_tiles = top_a.shape[0]
    tile_q = SEL // n_tiles
    for tile in range(n_tiles):
        packed = packs[tile * len(packs) // n_tiles].at[tile % (n_tiles // len(packs))]
        extra = packed[HD:, :].astype(jnp.float32)
        top_b = extra[0:1] + (extra[1:2] + extra[2:3])
        total_b = extra[3:4] + (extra[4:5] + extra[5:6])
        new = jnp.maximum(top_a[tile], top_b)
        part_a = jnp.exp2((top_a[tile] - new) * scale)
        part_b = jnp.exp2((top_b - new) * scale)
        total = total_a[tile] * part_a + total_b * part_b
        mixed = mixed_a[tile] * part_a + packed[:HD, :].astype(jnp.float32) * part_b
        finished = (mixed / total).T.astype(jnp.bfloat16)
        for head in range(TILE_COLS // tile_q):
            out_ref[tile * tile_q : (tile + 1) * tile_q, head * HD : (head + 1) * HD] = finished[
                head * tile_q : (head + 1) * tile_q, :
            ]


def merge(mine, theirs):
    n_tiles = mine[0].shape[0]
    shape = (SEL, TILE_COLS * n_tiles // SEL * HD)
    return pl.pallas_call(
        merge_kernel,
        out_shape=jax.ShapeDtypeStruct(shape, jnp.bfloat16),
        compiler_params=megabytes(16),
        cost_estimate=cost(4 * math.prod(shape), 8 * math.prod(shape)),
        name="merge",
    )(*mine, *theirs)


def out_kernel(n_blocks, first_col, place_ref, x_ref, w_ref, *refs):
    outs = refs[:n_blocks]
    ordered, slots, sems = refs[n_blocks:]
    rows = SEL // n_blocks
    tile = slots.shape[2]
    count = outs[0].shape[1] // tile
    start, wait = stream(
        [lambda step: w_ref.at[:, pl.ds(first_col + step * tile, tile)]], [slots], sems
    )

    for step in range(min(SLOTS, count)):
        start(step)
    for block in range(n_blocks):
        there = pl.ds(pl.multiple_of(place_ref[block] * rows, rows), rows)
        ordered[block * rows : (block + 1) * rows, :] = x_ref[there, :]
    for step in range(count):
        wait(step)
        product = jnp.dot(
            ordered[...].astype(jnp.bfloat16),
            slots[step % SLOTS],
            preferred_element_type=jnp.float32,
        )
        cols = slice(step * tile, (step + 1) * tile)
        for block, out in enumerate(outs):
            out[:, cols] = product[block * rows : (block + 1) * rows, :].astype(out.dtype)
        if step + SLOTS < count:
            start(step + SLOTS)


def project_out(place, attention, w_out, chunk, kinds):
    depth = w_out.shape[0]
    n_blocks = len(kinds)
    width = w_out.shape[1] // CHUNKS
    rows = SEL // n_blocks
    if rows % 16:
        attention = attention.astype(jnp.float32)
    vmem = pl.BlockSpec(memory_space=pltpu.VMEM)
    return pl.pallas_call(
        functools.partial(out_kernel, n_blocks, chunk * width),
        in_specs=[
            pl.BlockSpec(memory_space=pltpu.SMEM),
            vmem,
            pl.BlockSpec(memory_space=pltpu.HBM),
        ],
        out_specs=[vmem] * n_blocks,
        out_shape=[jax.ShapeDtypeStruct((rows, width), kind) for kind in kinds],
        scratch_shapes=[
            pltpu.VMEM((SEL, depth), attention.dtype),
            pltpu.VMEM((SLOTS, depth, min(WIDTH_TILE, width)), jnp.bfloat16),
            pltpu.SemaphoreType.DMA((CUTS, SLOTS)),
        ],
        compiler_params=megabytes(16),
        cost_estimate=cost(2 * SEL * depth * width, 2 * depth * (width + SEL) + 4 * SEL * width),
        name="project_out",
    )(place, attention, w_out)


def per_device(
    hidden_in, norm_gain, w_query, w_keyval, w_out, pool_cache, doc_slot, doc_blocks, sel_pos
):
    tp_size = lax.axis_size("tp")
    req_size = lax.axis_size("req")
    me = lax.axis_index("tp")
    rows, width = hidden_in.shape
    slots, tokens = pool_cache.shape[:2]
    heads_here = w_query.shape[1] // HD
    selected = sel_pos[0]
    lengths = doc_blocks[0] * BLOCK

    if tp_size == KVH:
        ring = [*range(0, tp_size, 2), *range(tp_size - 1, 0, -2)]
    else:
        ring = list(range(tp_size))
    far = tp_size // 2
    forth = [(ring[p], ring[(p + 1) % tp_size]) for p in range(tp_size)]
    back = [(dst, src) for src, dst in forth]
    steps = [0] + [sign * k for k in range(1, far) for sign in (-1, 1)] + [far]
    table = [[ring[(ring.index(i) + s) % tp_size] for s in steps] for i in range(tp_size)]
    place = jnp.array(table, jnp.int32)[me]

    widened = hidden_in.astype(jnp.float32)
    normed = (
        widened
        * lax.rsqrt(jnp.mean(widened * widened, axis=-1, keepdims=True) + EPSILON)
        * norm_gain
    ).astype(jnp.bfloat16)
    normed, pool_cache = lax.optimization_barrier((normed, pool_cache))
    w_query, w_keyval, w_out = (
        pltpu.with_memory_space_constraint(w, pltpu.HBM) for w in (w_query, w_keyval, w_out)
    )
    middle = tp_size // 2
    order = jnp.arange(middle, dtype=jnp.int32)
    offsets = jnp.cumsum(lengths) - lengths
    first_slot = (me ^ order) * tokens
    slot_tokens = first_slot[:, None] + jnp.arange(tokens, dtype=jnp.int32)[None, :]
    cache_pos = offsets[:, None, None] + slot_tokens[None]
    is_valid = slot_tokens[None] < lengths[:, None, None]
    replaced = jnp.any(cache_pos[..., None] == selected, axis=-1)
    dead = jnp.where(is_valid & jnp.logical_not(replaced), 0.0, MASKED).astype(jnp.bfloat16)
    dead = jnp.broadcast_to(dead[..., None], (DOCS, middle, tokens, HD))
    dead = dead.reshape(DOCS, middle * tokens, HD)
    first_pos = jnp.where(
        first_slot[None] < lengths[:, None], offsets[:, None] + first_slot[None], FAR
    ).reshape(-1)
    cosine, sine_part = rotation_tables(selected)
    heads_here = w_query.shape[1] // HD
    tile_q = TILE_COLS // heads_here
    q_pos = jnp.tile(selected.reshape(SEL // tile_q, tile_q), (1, heads_here))
    q_pos = q_pos.reshape(SEL // tile_q, 1, TILE_COLS)

    part = width // CHUNKS
    streams = []
    for chunk in range(CHUNKS):
        own = normed[:, chunk * part : (chunk + 1) * part]
        streams.append({"before": [own], "behind": [own]})
    for k in range(1, far + 1):
        for chunk, held in enumerate(streams):
            if k < far or chunk % 2 == 0:
                held["before"].append(lax.ppermute(held["before"][-1], "tp", forth))
            if k < far or chunk % 2 == 1:
                held["behind"].append(lax.ppermute(held["behind"][-1], "tp", back))
        first = streams[0]["before"]
        if k == 1:
            by_kind = pool_cache.transpose(0, 2, 1, 3)
            sources = [by_kind]
            for shift in range(1, req_size):
                pairs = [((i + shift) % req_size, i) for i in range(req_size)]
                sources.append(lax.ppermute(by_kind, "req", pairs))
            holder = (doc_slot // slots - lax.axis_index("req")) % req_size
            slot = doc_slot % slots
            side = (me < middle).astype(jnp.int32)[None]
            odd = (me % 2 if tp_size == KVH else me * 0)[None]
            takers = jnp.concatenate([me ^ order, me ^ order ^ middle]) * KVH // tp_size
        if k == 2:
            first[-1], dead, first_pos, cosine, sine_part, q_pos, takers, holder, slot, place, side, odd = (
                lax.optimization_barrier(
                    (first[-1], dead, first_pos, cosine, sine_part, q_pos, takers, holder, slot)
                    + (place, side, odd)
                )
            )
        if k == far - 1:
            sent = select_docs(sources, holder, slot, takers, tp_size)
            first[-1], *sent = lax.optimization_barrier((first[-1], *sent))
    weights = [w_keyval, w_query]
    sums = []
    for chunk, held in enumerate(streams):
        blocks = [held["before"][0]]
        for k in range(1, far):
            blocks += [held["before"][k], held["behind"][k]]
        blocks.append(held["behind" if chunk % 2 else "before"][far])
        if rows % 16:
            blocks = [jnp.concatenate(blocks, axis=0)]
        sums = project(
            place, blocks, weights, sums, chunk, (cosine, sine_part), side, tp_size == KVH
        )
    across = [(i, i ^ middle) for i in range(tp_size)]
    *keyval, queries = sums
    their_queries = lax.ppermute(queries, "tp", across)
    if tp_size == KVH:
        first, second = keyval
        keys_to_even = [(i, 2 * i if i < middle else 2 * (i - middle) + 1) for i in range(tp_size)]
        keys_to_odd = [(i, 2 * i + 1 if i < middle else 2 * (i - middle)) for i in range(tp_size)]
        new = [lax.ppermute(first, "tp", keys_to_even), lax.ppermute(second, "tp", keys_to_odd)]
    else:
        everyone = lax.all_gather(keyval[0], "tp", axis=1, tiled=True)
        my_head = me * KVH // tp_size
        new = [
            lax.dynamic_slice_in_dim(everyone, (kind * KVH + my_head) * HD, HD, axis=1)
            for kind in range(2)
        ]

    def exchange(keys, j):
        return lax.ppermute(keys, "tp", [(i, i ^ j) for i in range(tp_size)])

    n_tiles = queries.shape[0]
    metadata = (dead, first_pos, selected, q_pos, odd)
    own, kept = list(sent[:middle]), list(sent[middle:])
    kept[-1], queries = lax.optimization_barrier((kept[-1], queries))
    partners = [kept[0]] + [exchange(kept[j], j) for j in range(1, middle)]
    own, *partners[1:-1] = lax.optimization_barrier((own, *partners[1:-1]))
    own = [own[0]] + [exchange(own[j], j) for j in range(1, middle)]
    their_queries, new = lax.optimization_barrier((their_queries, new))
    share = n_tiles // min(HALVES, n_tiles)
    theirs = []
    for first in range(n_tiles - share, -1, -share):
        (packed,) = attend(partners, 0, metadata, their_queries, first, share, packs=True)
        theirs.insert(0, lax.ppermute(packed, "tp", across))
    queries, _ = lax.optimization_barrier((queries, packed))
    near = attend(
        own[:2], 0, metadata, queries, 0, n_tiles, fresh=(cosine, sine_part, *new)
    )
    mine = attend(own[2:], 2, metadata, queries, 0, n_tiles, near)
    attention = merge(mine, theirs)

    finished = []
    for chunk in range(CHUNKS):
        kinds = [jnp.float32] * (tp_size - 1) + [jnp.bfloat16]
        pieces = project_out(place, attention, w_out, chunk, kinds)
        to_forth, to_back = list(pieces[2 : tp_size - 1 : 2]), list(pieces[1 : tp_size - 1 : 2])
        (to_back if chunk % 2 else to_forth).append(pieces[-1])
        total = pieces[0]
        for terms, pairs in ((to_forth, forth), (to_back, back)):
            held = None
            for term in reversed(terms):
                if held is not None:
                    term = term + held.astype(jnp.float32)
                held = lax.ppermute(term.astype(jnp.bfloat16), "tp", pairs)
            total = total + held.astype(jnp.float32)
        finished.append(total.astype(jnp.bfloat16))
    return jnp.concatenate(finished, axis=1)


def solution(mesh):
    placed = (
        P(("groups", "req", "tp"), None),
        P(),
        P(None, "tp"),
        P(None, "tp"),
        P("tp", None),
        P(("groups", "req"), "tp", None, None),
        P(("groups", "req")),
        P(("groups", "req"), None),
        P(("groups", "req"), None),
    )
    return jax.shard_map(
        per_device,
        mesh=mesh,
        in_specs=placed,
        out_specs=P(("groups", "req", "tp"), None),
        check_vma=False,
    )
```

```python
import functools
import math

import jax
import jax.numpy as jnp
from jax import lax
from jax.experimental import pallas as pl
from jax.experimental.pallas import tpu as pltpu
from jax.sharding import PartitionSpec as P

HEADS = 64
KVH = 8
HD = 128
DOCS = 4
BLOCK = 128
SEL = 256


EPSILON = 1e-05
ROPE_BASE = 500000.0
MASKED = -1e30
FAR = 1 << 30
CHUNKS = 2
TILE_COLS = 256
PAIR = 2
STATS = 16
HALVES = 2
DEPTH_TILE = 1024
WIDTH_TILE = 1024
SLOTS = 3
CUTS = 4


def cost(flops, bytes_accessed, transcendentals=0):
    return pl.CostEstimate(
        flops=int(flops), bytes_accessed=int(bytes_accessed), transcendentals=int(transcendentals)
    )


def norm_kernel(rows_ref, gain_ref, *outs):
    widened = rows_ref[...].astype(jnp.float32)
    mean = jnp.mean(widened * widened, axis=-1, keepdims=True)
    normed = (widened * lax.rsqrt(mean + EPSILON) * gain_ref[...]).astype(jnp.bfloat16)
    part = outs[0].shape[1]
    for index, out in enumerate(outs):
        out[...] = normed[:, index * part : (index + 1) * part]


def norm(rows, gain):
    height, width = rows.shape
    return pl.pallas_call(
        norm_kernel,
        out_shape=[jax.ShapeDtypeStruct((height, width // CHUNKS), jnp.bfloat16)] * CHUNKS,
        compiler_params=megabytes(8),
        cost_estimate=cost(4 * height * width, 4 * height * width),
        name="norm",
    )(rows, gain[None, :])


def rotation_tables(positions):
    half_dim = HD // 2
    inverse = ROPE_BASE ** (-(jnp.arange(half_dim, dtype=jnp.float32) * (2.0 / HD)))
    angles = positions.astype(jnp.float32)[:, None] * inverse[None, :]
    cosine = jnp.cos(angles)
    sine_part = jnp.sin(angles)
    return (
        jnp.concatenate([cosine, cosine], axis=-1),
        jnp.concatenate([-sine_part, sine_part], axis=-1),
    )


def rotate(values, cosine, sine_part):
    swapped = jnp.concatenate([values[:, HD // 2 :], values[:, : HD // 2]], axis=-1)
    return values * cosine + swapped * sine_part


def megabytes(count):
    return pltpu.CompilerParams(vmem_limit_bytes=count * 1024 * 1024)


def stream(sources, buffers, sems):
    def copies(step):
        slot = step % SLOTS
        made = []
        for i, (source, buffer) in enumerate(zip(sources, buffers)):
            rows = buffer.shape[1] // CUTS
            for cut in range(CUTS):
                here = pl.ds(cut * rows, rows)
                made.append(
                    pltpu.make_async_copy(
                        source(step).at[here], buffer.at[slot, here], sems.at[i * CUTS + cut, slot]
                    )
                )
        return made

    def start(step):
        for copy in copies(step):
            copy.start()

    def wait(step):
        for copy in copies(step):
            copy.wait()

    return start, wait


def project_kernel(n_blocks, chunk, is_last, split, place_ref, *refs):
    refs = list(refs)
    take = lambda count: [refs.pop(0) for _ in range(count)]
    blocks, weights = take(n_blocks), take(2)
    prev = take(2) if chunk else None
    if is_last:
        cos_ref, sin_ref, side_ref = take(3)
        out_kv, (out_q,) = take(2 if split else 1), take(1)
        totals, (natural_kv, natural_q) = take(2), take(2)
    else:
        totals = take(2)
    buffers, sems = take(2), refs[0]
    tile = buffers[0].shape[1]
    depth = blocks[0].shape[1]
    count = depth // tile
    rows_of = lambda ref: lambda step: ref.at[pl.ds(chunk * depth + step * tile, tile), :]
    start, wait = stream([rows_of(ref) for ref in weights], buffers, sems)

    for step in range(min(SLOTS, count)):
        start(step)
    for step in range(count):
        wait(step)
        cols = slice(step * tile, (step + 1) * tile)
        rows = jnp.concatenate([b[:, cols] for b in blocks], axis=0)
        for i, (buffer, total) in enumerate(zip(buffers, totals)):
            term = jnp.dot(rows, buffer[step % SLOTS], preferred_element_type=jnp.float32)
            if step:
                total[...] += term
            elif chunk:
                total[...] = prev[i][...] + term
            else:
                total[...] = term
        if step + SLOTS < count:
            start(step + SLOTS)

    if is_last:
        height = SEL // place_ref.shape[0]
        for block in range(SEL // height):
            here = slice(block * height, (block + 1) * height)
            there = pl.ds(pl.multiple_of(place_ref[block] * height, height), height)
            natural_kv[there, :] = totals[0][here, :]
            natural_q[there, :] = totals[1][here, :]
        if split:
            for side in range(2):

                @pl.when(side_ref[0] == side)
                def _():
                    out_kv[1 - side][...] = natural_kv[:, :HD].astype(jnp.bfloat16)
                    out_kv[side][...] = natural_kv[:, HD:].astype(jnp.bfloat16)

        else:
            out_kv[0][...] = natural_kv[...].astype(jnp.bfloat16)
        heads_here = natural_q.shape[1] // HD
        tile_q = TILE_COLS // heads_here
        for index in range(SEL // tile_q):
            here = slice(index * tile_q, (index + 1) * tile_q)
            stacked = jnp.concatenate(
                [
                    rotate(
                        natural_q[here, head * HD : (head + 1) * HD], cos_ref[here, :], sin_ref[here, :]
                    )
                    for head in range(heads_here)
                ],
                axis=0,
            )
            out_q[index] = stacked.T.astype(jnp.bfloat16)


def project(place, blocks, weights, prev, chunk, tables, side, split):
    depth = blocks[0].shape[1]
    widths = [w.shape[1] for w in weights]
    tile = min(DEPTH_TILE, depth)
    is_last = chunk + 1 == CHUNKS
    smem = pl.BlockSpec(memory_space=pltpu.SMEM)
    vmem = pl.BlockSpec(memory_space=pltpu.VMEM)
    hbm = pl.BlockSpec(memory_space=pltpu.HBM)
    totals = [((SEL, width), jnp.float32) for width in widths]
    operands, specs = [place, *blocks, *weights, *prev], [smem] + [vmem] * len(blocks) + [hbm] * 2
    specs += [vmem] * len(prev)
    outs, scratch = totals, []
    if is_last:
        operands += [*tables, side]
        specs += [vmem] * 2 + [smem]
        outs = [(SEL, HD)] * 2 if split else [(SEL, widths[0])]
        outs = outs + [(SEL * widths[1] // (HD * TILE_COLS), HD, TILE_COLS)]
        outs, scratch = [(shape, jnp.bfloat16) for shape in outs], totals * 2
    return pl.pallas_call(
        functools.partial(project_kernel, len(blocks), chunk, is_last, split),
        in_specs=specs,
        out_specs=[vmem] * len(outs),
        out_shape=[jax.ShapeDtypeStruct(*o) for o in outs],
        scratch_shapes=[pltpu.VMEM(*x) for x in scratch]
        + [pltpu.VMEM((SLOTS, tile, width), jnp.bfloat16) for width in widths]
        + [pltpu.SemaphoreType.DMA((2 * CUTS, SLOTS))],
        compiler_params=megabytes(16),
        cost_estimate=cost(2 * SEL * depth * sum(widths), 2 * depth * (sum(widths) + SEL)),
        name="project",
    )(*operands)


def select_kernel(n_dest, n_src, place_ref, slot_ref, head_ref, *refs):
    sources = refs[:n_src]
    outs = refs[n_src : n_src + n_dest]
    sems = refs[n_src + n_dest]
    for doc in range(DOCS):
        for src in range(n_src):

            @pl.when(place_ref[doc] == src)
            def _():
                for dest in range(n_dest):
                    cols = pl.ds(pl.multiple_of(head_ref[dest] * HD, HD), HD)
                    pltpu.make_async_copy(
                        sources[src].at[slot_ref[doc], :, :, cols],
                        outs[dest].at[:, doc],
                        sems.at[dest, doc],
                    ).start()

    for dest in range(n_dest):
        for doc in range(DOCS):
            pltpu.make_async_copy(
                sources[0].at[0, :, :, 0:HD], outs[dest].at[:, doc], sems.at[dest, doc]
            ).wait()


def select_docs(sources, place, slot, heads, n_dest):
    tokens = sources[0].shape[2]
    shape = (2, DOCS, tokens, HD)
    smem = pl.BlockSpec(memory_space=pltpu.SMEM)
    return pl.pallas_call(
        functools.partial(select_kernel, n_dest, len(sources)),
        in_specs=[smem] * 3 + [pl.BlockSpec(memory_space=pl.ANY)] * len(sources),
        out_specs=[pl.BlockSpec(memory_space=pltpu.VMEM)] * n_dest,
        out_shape=[jax.ShapeDtypeStruct(shape, jnp.bfloat16)] * n_dest,
        scratch_shapes=[pltpu.SemaphoreType.DMA((n_dest, DOCS))],
        compiler_params=megabytes(8),
        cost_estimate=cost(0, 4 * n_dest * math.prod(shape)),
        name="select_docs",
    )(place, slot, heads, *sources)


def split_exact(value):
    pieces = []
    for _ in range(3):
        pieces.append(value.astype(jnp.bfloat16).astype(jnp.float32))
        value = value - pieces[-1]
    return pieces


def attend_kernel(
    n_chunks, offset, packs, has_state, with_new, n_tiles, tile_q, first_tile, first_ref, pos_ref, odd_ref, *refs
):
    refs = list(refs)
    take = lambda count: [refs.pop(0) for _ in range(count)]
    chunks = take(n_chunks)
    dead_ref, qpos_ref, queries = take(3)
    if has_state:
        old_top, old_total, old_summed = take(3)
    if with_new:
        cos_ref, sin_ref, new_a, new_b = take(4)
    if packs:
        (packed,) = take(1)
    top, total, summed, values = take(4)
    if with_new:
        new_key, new_value = take(2)
    together = min(PAIR, n_tiles)
    n_pairs = n_tiles // together
    tokens = chunks[0].shape[2]
    all_chunks = dead_ref.shape[1] // tokens
    scale = math.log2(math.e) / math.sqrt(HD)

    for chunk in range(n_chunks):
        for doc in range(DOCS):
            values[doc, :, chunk * tokens : (chunk + 1) * tokens] = chunks[chunk][1, doc].T
    if with_new:
        for odd, (key_ref, value_ref) in enumerate(((new_a, new_b), (new_b, new_a))):

            @pl.when(odd_ref[0] == odd)
            def _():
                new_key[...] = rotate(
                    key_ref[...].astype(jnp.float32), cos_ref[...], sin_ref[...]
                ).astype(jnp.bfloat16)
                new_value[...] = value_ref[...].T


    one_row = jnp.where(
        lax.broadcasted_iota(jnp.int32, (HD, TILE_COLS), 0) == 0, 1.0, 0.0
    ).astype(jnp.bfloat16)

    def update(tile, parts):
        best = functools.reduce(
            jnp.maximum, [jnp.max(scores, axis=0, keepdims=True) for scores, _ in parts]
        )
        old = top[tile]
        new = jnp.maximum(old, best)
        shrink = jnp.exp2((old - new) * scale)
        running = total[tile] * shrink
        mixed = summed[tile] * shrink
        for scores, value in parts:
            weights = jnp.exp2((scores - new) * scale)
            running += jnp.sum(weights, axis=0, keepdims=True)
            mixed += jnp.dot(
                value, weights.astype(jnp.bfloat16), preferred_element_type=jnp.float32
            )
        top[tile] = new
        total[tile] = running
        summed[tile] = mixed

    @pl.loop(0, n_pairs)
    def _(pair):
        tiles = [pair * together + i for i in range(together)]
        for tile in tiles:
            if has_state:
                top[tile] = old_top[tile]
                total[tile] = old_total[tile]
                summed[tile] = old_summed[tile]
            else:
                top[tile] = jnp.full(top.shape[1:], MASKED, jnp.float32)
                total[tile] = jnp.zeros(total.shape[1:], jnp.float32)
                summed[tile] = jnp.zeros(summed.shape[1:], jnp.float32)
        if with_new:
            fresh = []
            for tile in tiles:
                scores = jnp.dot(
                    new_key[...], queries[first_tile + tile], preferred_element_type=jnp.float32
                )
                key_index = lax.broadcasted_iota(jnp.int32, scores.shape, 0)
                q_index = (first_tile + tile) * tile_q + lax.broadcasted_iota(jnp.int32, scores.shape, 1) % tile_q
                fresh.append(jnp.where(key_index <= q_index, scores, MASKED))
            for tile, scores in zip(tiles, fresh):
                update(tile, [(scores, new_value[...])])

        @pl.loop(0, DOCS)
        def _(doc):
            firsts = [first_ref[doc * all_chunks + offset + chunk] for chunk in range(n_chunks)]
            lowest = functools.reduce(jnp.minimum, firsts)
            highest = functools.reduce(jnp.maximum, firsts)
            reach = highest + tokens - 1

            def visit(masked, members):
                found = []
                for tile in tiles:
                    extended = jnp.concatenate([queries[first_tile + tile], one_row], axis=0)
                    parts = []
                    for chunk in members:
                        span = slice(chunk * tokens, (chunk + 1) * tokens)
                        dead_span = slice((offset + chunk) * tokens, (offset + chunk + 1) * tokens)
                        keys = jnp.concatenate(
                            [chunks[chunk][0, doc], dead_ref[doc, dead_span, :]], axis=1
                        )
                        scores = jnp.dot(keys, extended, preferred_element_type=jnp.float32)
                        if masked:
                            key_pos = firsts[chunk] + lax.broadcasted_iota(
                                jnp.int32, scores.shape, 0
                            )
                            scores = jnp.where(key_pos <= qpos_ref[first_tile + tile], scores, MASKED)
                        parts.append((scores, values[doc, :, span]))
                    found.append(parts)
                for tile, parts in zip(tiles, found):
                    update(tile, parts)

            start = first_tile * tile_q + pair * together * tile_q
            first_here = pos_ref[start]
            last_here = pos_ref[start + together * tile_q - 1]
            whole = reach <= first_here
            spread = jnp.logical_not(whole) & (highest <= last_here)
            ragged = (lowest <= last_here) & (highest > last_here)

            @pl.when(whole)
            def _():
                visit(False, range(n_chunks))

            @pl.when(spread)
            def _():
                visit(True, range(n_chunks))

            for chunk in range(n_chunks):

                @pl.when(ragged & (firsts[chunk] <= last_here))
                def _():
                    visit(True, [chunk])

        if packs:
            for tile in tiles:
                extra = jnp.concatenate(
                    split_exact(top[tile])
                    + split_exact(total[tile])
                    + [jnp.zeros((STATS - 6, TILE_COLS), jnp.float32)],
                    axis=0,
                )
                packed[tile] = jnp.concatenate([summed[tile], extra], axis=0).astype(jnp.bfloat16)


def attend(chunks, offset, metadata, queries, first_tile, n_tiles, state=(), fresh=(), packs=False):
    dead, first_pos, selected, q_pos, odd = metadata
    n_chunks = len(chunks)
    tokens = chunks[0].shape[2]
    tile_q = SEL // q_pos.shape[0]
    smem = pl.BlockSpec(memory_space=pltpu.SMEM)
    vmem = pl.BlockSpec(memory_space=pltpu.VMEM)
    operands = [first_pos, selected, odd, *chunks, dead, q_pos, queries, *state, *fresh]
    outs = [((n_tiles, 1, TILE_COLS), jnp.float32)] * 2
    outs += [((n_tiles, HD, TILE_COLS), jnp.float32)]
    scratch = [((DOCS, HD, n_chunks * tokens), jnp.bfloat16)]
    if packs:
        outs, scratch = [((n_tiles, HD + STATS, TILE_COLS), jnp.bfloat16)], outs + scratch
    if fresh:
        scratch += [((SEL, HD), jnp.bfloat16), ((HD, SEL), jnp.bfloat16)]
    pairs = n_tiles * TILE_COLS * DOCS * n_chunks * tokens // 2
    return pl.pallas_call(
        functools.partial(
            attend_kernel,
            n_chunks,
            offset,
            packs,
            bool(state),
            bool(fresh),
            n_tiles,
            tile_q,
            first_tile,
        ),
        in_specs=[smem] * 3 + [vmem] * (len(operands) - 3),
        out_specs=[vmem] * len(outs),
        out_shape=[jax.ShapeDtypeStruct(*s) for s in outs],
        scratch_shapes=[pltpu.VMEM(*s) for s in scratch],
        compiler_params=megabytes(16),
        cost_estimate=cost(4 * pairs * HD, 0, pairs) if packs else cost(1, 1),
        name="attend",
    )(*operands)


def merge_kernel(top_a, total_a, mixed_a, *refs):
    packs, out_ref = refs[:-1], refs[-1]
    scale = math.log2(math.e) / math.sqrt(HD)
    n_tiles = top_a.shape[0]
    tile_q = SEL // n_tiles
    for tile in range(n_tiles):
        packed = packs[tile * len(packs) // n_tiles].at[tile % (n_tiles // len(packs))]
        extra = packed[HD:, :].astype(jnp.float32)
        top_b = extra[0:1] + (extra[1:2] + extra[2:3])
        total_b = extra[3:4] + (extra[4:5] + extra[5:6])
        new = jnp.maximum(top_a[tile], top_b)
        part_a = jnp.exp2((top_a[tile] - new) * scale)
        part_b = jnp.exp2((top_b - new) * scale)
        total = total_a[tile] * part_a + total_b * part_b
        mixed = mixed_a[tile] * part_a + packed[:HD, :].astype(jnp.float32) * part_b
        finished = (mixed / total).T.astype(jnp.bfloat16)
        for head in range(TILE_COLS // tile_q):
            out_ref[tile * tile_q : (tile + 1) * tile_q, head * HD : (head + 1) * HD] = finished[
                head * tile_q : (head + 1) * tile_q, :
            ]


def merge(mine, theirs):
    n_tiles = mine[0].shape[0]
    shape = (SEL, TILE_COLS * n_tiles // SEL * HD)
    return pl.pallas_call(
        merge_kernel,
        out_shape=jax.ShapeDtypeStruct(shape, jnp.bfloat16),
        compiler_params=megabytes(16),
        cost_estimate=cost(4 * math.prod(shape), 8 * math.prod(shape)),
        name="merge",
    )(*mine, *theirs)


def out_kernel(n_blocks, first_col, place_ref, x_ref, w_ref, *refs):
    outs = refs[:n_blocks]
    ordered, slots, sems = refs[n_blocks:]
    rows = SEL // n_blocks
    tile = slots.shape[2]
    count = outs[0].shape[1] // tile
    start, wait = stream(
        [lambda step: w_ref.at[:, pl.ds(first_col + step * tile, tile)]], [slots], sems
    )

    for step in range(min(SLOTS, count)):
        start(step)
    for block in range(n_blocks):
        there = pl.ds(pl.multiple_of(place_ref[block] * rows, rows), rows)
        ordered[block * rows : (block + 1) * rows, :] = x_ref[there, :]
    for step in range(count):
        wait(step)
        product = jnp.dot(
            ordered[...].astype(jnp.bfloat16),
            slots[step % SLOTS],
            preferred_element_type=jnp.float32,
        )
        cols = slice(step * tile, (step + 1) * tile)
        for block, out in enumerate(outs):
            out[:, cols] = product[block * rows : (block + 1) * rows, :].astype(out.dtype)
        if step + SLOTS < count:
            start(step + SLOTS)


def project_out(place, attention, w_out, chunk, kinds):
    depth = w_out.shape[0]
    n_blocks = len(kinds)
    width = w_out.shape[1] // CHUNKS
    rows = SEL // n_blocks
    if rows % 16:
        attention = attention.astype(jnp.float32)
    vmem = pl.BlockSpec(memory_space=pltpu.VMEM)
    return pl.pallas_call(
        functools.partial(out_kernel, n_blocks, chunk * width),
        in_specs=[
            pl.BlockSpec(memory_space=pltpu.SMEM),
            vmem,
            pl.BlockSpec(memory_space=pltpu.HBM),
        ],
        out_specs=[vmem] * n_blocks,
        out_shape=[jax.ShapeDtypeStruct((rows, width), kind) for kind in kinds],
        scratch_shapes=[
            pltpu.VMEM((SEL, depth), attention.dtype),
            pltpu.VMEM((SLOTS, depth, min(WIDTH_TILE, width)), jnp.bfloat16),
            pltpu.SemaphoreType.DMA((CUTS, SLOTS)),
        ],
        compiler_params=megabytes(16),
        cost_estimate=cost(2 * SEL * depth * width, 2 * depth * (width + SEL) + 4 * SEL * width),
        name="project_out",
    )(place, attention, w_out)


def per_device(
    hidden_in, norm_gain, w_query, w_keyval, w_out, pool_cache, doc_slot, doc_blocks, sel_pos
):
    tp_size = lax.axis_size("tp")
    req_size = lax.axis_size("req")
    me = lax.axis_index("tp")
    rows, width = hidden_in.shape
    slots, tokens = pool_cache.shape[:2]
    heads_here = w_query.shape[1] // HD
    selected = sel_pos[0]
    lengths = doc_blocks[0] * BLOCK

    if tp_size == KVH:
        ring = [*range(0, tp_size, 2), *range(tp_size - 1, 0, -2)]
    else:
        ring = list(range(tp_size))
    far = tp_size // 2
    forth = [(ring[p], ring[(p + 1) % tp_size]) for p in range(tp_size)]
    back = [(dst, src) for src, dst in forth]
    steps = [0] + [sign * k for k in range(1, far) for sign in (-1, 1)] + [far]
    table = [[ring[(ring.index(i) + s) % tp_size] for s in steps] for i in range(tp_size)]
    place = jnp.array(table, jnp.int32)[me]

    normed = norm(hidden_in, norm_gain)
    *normed, pool_cache = lax.optimization_barrier((*normed, pool_cache))
    w_query, w_keyval, w_out = (
        pltpu.with_memory_space_constraint(w, pltpu.HBM) for w in (w_query, w_keyval, w_out)
    )
    middle = tp_size // 2
    order = jnp.arange(middle, dtype=jnp.int32)
    offsets = jnp.cumsum(lengths) - lengths
    first_slot = (me ^ order) * tokens
    slot_tokens = first_slot[:, None] + jnp.arange(tokens, dtype=jnp.int32)[None, :]
    cache_pos = offsets[:, None, None] + slot_tokens[None]
    is_valid = slot_tokens[None] < lengths[:, None, None]
    replaced = jnp.any(cache_pos[..., None] == selected, axis=-1)
    dead = jnp.where(is_valid & jnp.logical_not(replaced), 0.0, MASKED).astype(jnp.bfloat16)
    dead = jnp.broadcast_to(dead[..., None], (DOCS, middle, tokens, HD))
    dead = dead.reshape(DOCS, middle * tokens, HD)
    first_pos = jnp.where(
        first_slot[None] < lengths[:, None], offsets[:, None] + first_slot[None], FAR
    ).reshape(-1)
    cosine, sine_part = rotation_tables(selected)
    heads_here = w_query.shape[1] // HD
    tile_q = TILE_COLS // heads_here
    q_pos = jnp.tile(selected.reshape(SEL // tile_q, tile_q), (1, heads_here))
    q_pos = q_pos.reshape(SEL // tile_q, 1, TILE_COLS)

    streams = []
    for chunk in range(CHUNKS):
        own = normed[chunk]
        streams.append({"before": [own], "behind": [own]})
    for k in range(1, far + 1):
        for chunk, held in enumerate(streams):
            if k < far or chunk % 2 == 0:
                held["before"].append(lax.ppermute(held["before"][-1], "tp", forth))
            if k < far or chunk % 2 == 1:
                held["behind"].append(lax.ppermute(held["behind"][-1], "tp", back))
        first = streams[0]["before"]
        if k == 1:
            by_kind = pool_cache.transpose(0, 2, 1, 3)
            sources = [by_kind]
            for shift in range(1, req_size):
                pairs = [((i + shift) % req_size, i) for i in range(req_size)]
                sources.append(lax.ppermute(by_kind, "req", pairs))
            holder = (doc_slot // slots - lax.axis_index("req")) % req_size
            slot = doc_slot % slots
            side = (me < middle).astype(jnp.int32)[None]
            odd = (me % 2 if tp_size == KVH else me * 0)[None]
            takers = jnp.concatenate([me ^ order, me ^ order ^ middle]) * KVH // tp_size
        if k == 2:
            first[-1], dead, first_pos, cosine, sine_part, q_pos, takers, holder, slot, place, side, odd = (
                lax.optimization_barrier(
                    (first[-1], dead, first_pos, cosine, sine_part, q_pos, takers, holder, slot)
                    + (place, side, odd)
                )
            )
            sent = select_docs(sources, holder, slot, takers, tp_size)
            first[-1], *sent = lax.optimization_barrier((first[-1], *sent))
        if k == far - 1:
            first[-1], *sent = lax.optimization_barrier((first[-1], *sent))
    weights = [w_keyval, w_query]
    sums = []
    for chunk, held in enumerate(streams):
        blocks = [held["before"][0]]
        for k in range(1, far):
            blocks += [held["before"][k], held["behind"][k]]
        blocks.append(held["behind" if chunk % 2 else "before"][far])
        if rows % 16:
            blocks = [jnp.concatenate(blocks, axis=0)]
        sums = project(
            place, blocks, weights, sums, chunk, (cosine, sine_part), side, tp_size == KVH
        )
    across = [(i, i ^ middle) for i in range(tp_size)]
    *keyval, queries = sums
    their_queries = lax.ppermute(queries, "tp", across)
    if tp_size == KVH:
        first, second = keyval
        keys_to_even = [(i, 2 * i if i < middle else 2 * (i - middle) + 1) for i in range(tp_size)]
        keys_to_odd = [(i, 2 * i + 1 if i < middle else 2 * (i - middle)) for i in range(tp_size)]
        new = [lax.ppermute(first, "tp", keys_to_even), lax.ppermute(second, "tp", keys_to_odd)]
    else:
        everyone = lax.all_gather(keyval[0], "tp", axis=1, tiled=True)
        my_head = me * KVH // tp_size
        new = [
            lax.dynamic_slice_in_dim(everyone, (kind * KVH + my_head) * HD, HD, axis=1)
            for kind in range(2)
        ]

    def exchange(keys, j):
        return lax.ppermute(keys, "tp", [(i, i ^ j) for i in range(tp_size)])

    n_tiles = queries.shape[0]
    metadata = (dead, first_pos, selected, q_pos, odd)
    own, kept = list(sent[:middle]), list(sent[middle:])
    kept[-1], queries = lax.optimization_barrier((kept[-1], queries))
    partners = [kept[0]] + [exchange(kept[j], j) for j in range(1, middle)]
    own, *partners[1:-1] = lax.optimization_barrier((own, *partners[1:-1]))
    own = [own[0]] + [exchange(own[j], j) for j in range(1, middle)]
    their_queries, new = lax.optimization_barrier((their_queries, new))
    share = n_tiles // min(HALVES, n_tiles)
    theirs = []
    for first in range(n_tiles - share, -1, -share):
        (packed,) = attend(partners, 0, metadata, their_queries, first, share, packs=True)
        theirs.insert(0, lax.ppermute(packed, "tp", across))
    queries, _ = lax.optimization_barrier((queries, packed))
    near = attend(
        own[:2], 0, metadata, queries, 0, n_tiles, fresh=(cosine, sine_part, *new)
    )
    mine = attend(own[2:], 2, metadata, queries, 0, n_tiles, near)
    attention = merge(mine, theirs)

    finished = []
    for chunk in range(CHUNKS):
        kinds = [jnp.float32] * (tp_size - 1) + [jnp.bfloat16]
        pieces = project_out(place, attention, w_out, chunk, kinds)
        to_forth, to_back = list(pieces[2 : tp_size - 1 : 2]), list(pieces[1 : tp_size - 1 : 2])
        (to_back if chunk % 2 else to_forth).append(pieces[-1])
        total = pieces[0]
        for terms, pairs in ((to_forth, forth), (to_back, back)):
            held = None
            for term in reversed(terms):
                if held is not None:
                    term = term + held.astype(jnp.float32)
                held = lax.ppermute(term.astype(jnp.bfloat16), "tp", pairs)
            total = total + held.astype(jnp.float32)
        finished.append(total.astype(jnp.bfloat16))
    return jnp.concatenate(finished, axis=1)


def solution(mesh):
    placed = (
        P(("groups", "req", "tp"), None),
        P(),
        P(None, "tp"),
        P(None, "tp"),
        P("tp", None),
        P(("groups", "req"), "tp", None, None),
        P(("groups", "req")),
        P(("groups", "req"), None),
        P(("groups", "req"), None),
    )
    return jax.shard_map(
        per_device,
        mesh=mesh,
        in_specs=placed,
        out_specs=P(("groups", "req", "tp"), None),
        check_vma=False,
    )
```
